32 devices in a mesh: groups: 2 (over y), dp: 4 (over z), tensor: 4 (over x, core).
Axes of the slice: x: 2, y: 2, z: 4, core: 2. Of those that a mesh axis runs over, the one named last changes fastest.
Arguments:
- tokens: bfloat16 [3072, 8192], P(('groups', 'dp'), 'tensor'), parts along dimension 0, may hold values from -6 to 6
- cotangent: bfloat16 [1024, 16384], P(('groups', 'tensor'), 'dp'), parts along dimension 0, may hold values from -6 to 6
- frozen_up_weight: bfloat16 [8192, 16384], P('tensor', 'dp'), may hold values from -0.0625 to 0.0625
- adapter_down_factor: bfloat16 [8, 8192, 64], P(('groups', 'dp'), 'tensor'), parts along dimension 0, may hold values from -0.0625 to 0.0625
- adapter_up_factor: bfloat16 [8, 64, 16384], P('groups', None, 'dp'), parts along dimension 0, may hold values from -0.75 to 0.75
- tokens_per_adapter: int32 [8], P('groups'), parts along dimension 0, may hold values from 0 to 384, as said below
- adapter_of_block: int32 [8], P('groups'), parts along dimension 0, may hold values from 0 to 3, as said below
- slot_of_block: int32 [8], P('groups'), parts along dimension 0, may hold values from 0 to 2, as said below
Outputs:
- projected: bfloat16 [1024, 16384], P(('groups', 'tensor'), 'dp'), parts along dimension 0
- adapter_down_gradient: float32 [8, 8192, 64], P(('groups', 'dp'), 'tensor'), parts along dimension 0
- adapter_up_gradient: float32 [8, 64, 16384], P('groups', None, 'dp'), parts along dimension 0
The draws below stay inside these ranges and needn't reach their ends.
There are 2 independent parts, one for each index of `groups`. The reference program is written for one: setup_inputs(seed, part) draws one part's arguments, and reference() takes and returns one part's arrays. A program takes and returns all parts, laid end to end along the dimension named above; an argument that names none is the same for every part. Nothing has to cross between parts.
Inputs may be any that keep to these rules, and one draw needn't show every extreme that they name: Adapter a uses ceil(tokens_per_adapter[a] / 128) blocks, at most 3; these numbers sum to 4. One adapter holds exactly 384 tokens. `adapter_of_block`: Non-decreasing; adapter a holds ceil(tokens_per_adapter[a] / 128) consecutive entries; the last entry is 3. `slot_of_block`: blocks of one adapter sit in distinct slots of that adapter's owner.
All inputs are finite; a program needn't handle non-finite values.
Results may differ from the reference program's by a relative error of at most 0.0031.
Values may be sent and summed in bfloat16 or wider, within the bound.
No kernel may reach another device: no remote copies, remote signals or barrier semaphores. Data moves between devices by JAX's collectives and lax.ppermute only.
A program may use at most 128 MiB of HBM per device.

```python
import jax
import jax.numpy as jnp
from jax import lax

MODEL_WIDTH = 8192
HIDDEN_UNITS = 16384
ADAPTER_RANK = 64
BLK = 128
CAP = 3
TOKENS = 512
N_DP = 4


def block_layout(key, part):
    adapter_count = N_DP
    heavy_adapter = jax.random.randint(jax.random.fold_in(key, 11), (), 0, adapter_count)
    slot_ranks = jax.random.permutation(jax.random.fold_in(key, 12), adapter_count * CAP).astype(jnp.int32)
    slot_ids = jnp.arange(adapter_count * CAP, dtype=jnp.int32)
    slot_owner = slot_ids // CAP
    scores = slot_ranks + jnp.where(slot_owner == heavy_adapter, adapter_count * CAP, 0)
    forced = (slot_ids == (adapter_count - 1) * CAP) & (heavy_adapter != adapter_count - 1)
    scores = jnp.where(forced, -1, scores)
    ordered = jnp.argsort(scores, stable=True)
    taken = jnp.zeros(adapter_count * CAP, jnp.int32).at[ordered[:adapter_count - CAP]].set(1)
    adapter_ids = jnp.arange(adapter_count, dtype=jnp.int32)
    block_counts = jnp.sum(taken.reshape(adapter_count, CAP), axis=1)
    block_counts = jnp.where(adapter_ids == heavy_adapter, CAP, block_counts)
    tails = jax.random.randint(jax.random.fold_in(key, 13), (adapter_count,), 1, BLK + 1)
    tails = jnp.where(adapter_ids == heavy_adapter, BLK, tails)
    token_counts = jnp.where(block_counts > 0, (block_counts - 1) * BLK + tails, 0)
    block_ends = jnp.cumsum(block_counts)
    block_index = jnp.arange(adapter_count, dtype=jnp.int32)
    adapter_of_block = jnp.sum((block_ends[None, :] <= block_index[:, None]).astype(jnp.int32), axis=1)
    block_starts = block_ends - block_counts
    position = block_index - block_starts[adapter_of_block]
    shifts = jax.random.randint(jax.random.fold_in(key, 14), (adapter_count,), 0, CAP)
    shifts = jnp.where(adapter_ids == adapter_of_block[0], 0, shifts)
    part_shift = jnp.asarray(part, jnp.int32) % CAP
    slot_of_block = (position + shifts[adapter_of_block] + part_shift) % CAP
    return (token_counts.astype(jnp.int32), adapter_of_block.astype(jnp.int32), slot_of_block.astype(jnp.int32))


def draw_tokens_per_adapter(key, part):
    return block_layout(key, part)[0]


def draw_adapter_of_block(key, part):
    return block_layout(key, part)[1]


def draw_slot_of_block(key, part):
    return block_layout(key, part)[2]


def shard_levels(key, shape, pieces, smallest, high):
    gain = 1.0
    for dim, blocks in pieces:
        steps = jax.random.uniform(jax.random.fold_in(jax.random.fold_in(key, 6), dim), (blocks,), jnp.float32, smallest / len(pieces), high / len(pieces))
        gain = gain * jnp.repeat(jnp.exp(steps), shape[dim] // blocks).reshape((-1,) + (1,) * (len(shape) - 1 - dim))
    return gain


def gaussian(rng, dims, scale, reach, pieces=(), kind=jnp.bfloat16):
    values = jax.random.normal(rng, dims, jnp.float32) * scale
    if len(pieces) > 0:
        values = shard_levels(rng, dims, pieces, -0.22, 0.18) * values
    return jnp.clip(values, min=-reach, max=reach).astype(kind)


def setup_inputs(seed: int = 0, part: int = 0) -> dict:
    streams_of = jax.random.split(jax.random.key(seed), 9)
    part_keys = jax.random.split(jax.random.fold_in(streams_of[8], part), 9)
    return {
        "tokens": gaussian(part_keys[0], (N_DP * CAP * BLK, MODEL_WIDTH), 1.0, 6.0, ((0, 4), (1, 4))),
        "cotangent": gaussian(part_keys[1], (TOKENS, HIDDEN_UNITS), 1.0, 6.0, ((0, 4), (1, 4))),
        "frozen_up_weight": gaussian(streams_of[2], (MODEL_WIDTH, HIDDEN_UNITS), MODEL_WIDTH ** -0.5, 0.0625, ((0, 4), (1, 4))),
        "adapter_down_factor": gaussian(part_keys[3], (N_DP, MODEL_WIDTH, ADAPTER_RANK), MODEL_WIDTH ** -0.5, 0.0625, ((0, 4), (1, 4))),
        "adapter_up_factor": gaussian(part_keys[4], (N_DP, ADAPTER_RANK, HIDDEN_UNITS), ADAPTER_RANK ** -0.5, 0.75, ((2, 4),)),
        "tokens_per_adapter": draw_tokens_per_adapter(jax.random.fold_in(jax.random.fold_in(streams_of[8], part), 71), part),
        "adapter_of_block": draw_adapter_of_block(jax.random.fold_in(jax.random.fold_in(streams_of[8], part), 71), part),
        "slot_of_block": draw_slot_of_block(jax.random.fold_in(jax.random.fold_in(streams_of[8], part), 71), part),
    }


adapter_scale = 0.5


def block_live(tokens_per_adapter, adapter_of_block, block_rows):
    adapter_count = tokens_per_adapter.shape[0]
    nblocks = (tokens_per_adapter + block_rows - 1) // block_rows
    first_block = jnp.cumsum(nblocks) - nblocks
    membership_mask = (adapter_of_block[:, None] == jnp.arange(adapter_count, dtype=jnp.int32)[None, :]).astype(jnp.int32)
    begin_block = jnp.sum(membership_mask * first_block[None, :], axis=1)
    total_rows = jnp.sum(membership_mask * tokens_per_adapter[None, :], axis=1)
    block_place = jnp.arange(adapter_of_block.shape[0], dtype=jnp.int32) - begin_block
    offset = block_place[:, None] * block_rows + jnp.arange(block_rows, dtype=jnp.int32)[None, :]
    return (offset < total_rows[:, None]).astype(jnp.float32)


def reference(tokens, cotangent, frozen_up_weight, adapter_down_factor, adapter_up_factor, tokens_per_adapter, adapter_of_block, slot_of_block):
    live_rows = block_live(tokens_per_adapter, adapter_of_block, BLK)
    row_mask = live_rows[:, :, None]
    rows_per_slot = tokens.reshape(N_DP * CAP, BLK, MODEL_WIDTH)
    selected_factor = rows_per_slot[(adapter_of_block * CAP + slot_of_block).astype(jnp.int32)]
    complete_down_factor = jnp.einsum("pxq,pqf->pxf", selected_factor.astype(jnp.float32), adapter_down_factor[adapter_of_block].astype(jnp.float32))
    lowered = (complete_down_factor * row_mask).astype(jnp.bfloat16)
    rows_in = (selected_factor * row_mask.astype(jnp.bfloat16)).reshape(N_DP * BLK, MODEL_WIDTH)
    frozen_contribution = jnp.dot(rows_in, frozen_up_weight, preferred_element_type=jnp.float32)
    selected_rows = adapter_up_factor[adapter_of_block].astype(jnp.float32)
    adapter_side_term = jnp.einsum("azs,asg->azg", lowered.astype(jnp.float32), selected_rows).reshape(N_DP * BLK, HIDDEN_UNITS)
    projected = (frozen_contribution + adapter_scale * adapter_side_term).astype(jnp.bfloat16)
    masked = cotangent.reshape(N_DP, BLK, HIDDEN_UNITS) * row_mask.astype(jnp.bfloat16)
    returned_rows = jnp.einsum("bkf,brf->bkr", masked.astype(jnp.float32), selected_rows).astype(jnp.bfloat16)
    membership_mask = (adapter_of_block[:, None] == jnp.arange(N_DP, dtype=jnp.int32)[None, :]).astype(jnp.float32)
    up_factor_pieces = jnp.einsum("bkr,bkf->brf", lowered.astype(jnp.float32), masked.astype(jnp.float32))
    adapter_up_gradient = adapter_scale * jnp.einsum("dg,dwq->gwq", membership_mask, up_factor_pieces, precision=lax.Precision.HIGHEST)
    down_factor_pieces = jnp.einsum("wic,win->wcn", selected_factor.astype(jnp.float32), returned_rows.astype(jnp.float32))
    adapter_down_gradient = adapter_scale * jnp.einsum("it,ikf->tkf", membership_mask, down_factor_pieces, precision=lax.Precision.HIGHEST)
    return (projected, adapter_down_gradient, adapter_up_gradient)
```

```python
import functools

import jax
import jax.numpy as jnp
from jax import lax
from jax.experimental import pallas as pl
from jax.experimental.pallas import tpu as pltpu
from jax.sharding import PartitionSpec as P

BLK = 128
CAP = 3
CORES = 2
UNIT_ROWS = 64
SKEW = 1

adapter_scale = 0.5


def block_live(tokens_per_adapter, adapter_of_block, block_rows):
    adapter_count = tokens_per_adapter.shape[0]
    nblocks = (tokens_per_adapter + block_rows - 1) // block_rows
    first_block = jnp.cumsum(nblocks) - nblocks
    membership_mask = (
        adapter_of_block[:, None] == jnp.arange(adapter_count, dtype=jnp.int32)[None, :]
    ).astype(jnp.int32)
    begin_block = jnp.sum(membership_mask * first_block[None, :], axis=1)
    total_rows = jnp.sum(membership_mask * tokens_per_adapter[None, :], axis=1)
    block_place = jnp.arange(adapter_of_block.shape[0], dtype=jnp.int32) - begin_block
    offset = block_place[:, None] * block_rows + jnp.arange(block_rows, dtype=jnp.int32)[None, :]
    return offset < total_rows[:, None]


def split_product_kernel(x_ref, w_ref, send_ref, keep_ref):
    half = x_ref.shape[0] // 2
    total = jnp.dot(x_ref[...], w_ref[...], preferred_element_type=jnp.float32)
    send_ref[...] = total[:half].astype(send_ref.dtype)
    keep_ref[...] = total[half:]


def split_product(rows, weight):
    count, depth = rows.shape
    width = weight.shape[1]
    tile = 512
    return pl.pallas_call(
        split_product_kernel,
        grid=(width // tile,),
        in_specs=[
            pl.BlockSpec((count, depth), lambda n: (0, 0)),
            pl.BlockSpec((depth, tile), lambda n: (0, n)),
        ],
        out_specs=[
            pl.BlockSpec((count // 2, tile), lambda n: (0, n)),
            pl.BlockSpec((count // 2, tile), lambda n: (0, n)),
        ],
        out_shape=[
            jax.ShapeDtypeStruct((count // 2, width), jnp.bfloat16),
            jax.ShapeDtypeStruct((count // 2, width), jnp.float32),
        ],
        compiler_params=pltpu.CompilerParams(vmem_limit_bytes=24 * 2**20),
        cost_estimate=pl.CostEstimate(
            flops=2 * count * depth * width,
            bytes_accessed=2 * (count * depth + depth * width) + 3 * count * width,
            transcendentals=0,
        ),
        name="split_product",
    )(rows, weight)


def per_device(
    tokens,
    cotangent,
    frozen_up_weight,
    adapter_down_factor,
    adapter_up_factor,
    tokens_per_adapter,
    adapter_of_block,
    slot_of_block,
):
    owners = lax.axis_size("dp")
    parts = lax.axis_size("tensor")
    chips = parts // CORES
    place = lax.axis_index("dp")
    part = lax.axis_index("tensor")
    chip, core = part // CORES, part % CORES
    block_count = adapter_of_block.shape[0]
    per_part = block_count // parts
    width_dev = tokens.shape[1]
    hidden_dev = cotangent.shape[1]
    rank = adapter_up_factor.shape[1]
    adapter_count = adapter_up_factor.shape[0]

    def to_other_core(value):
        return lax.ppermute(value, "tensor", [(i, i ^ 1) for i in range(parts)])

    def to_chip(value, k):
        return lax.ppermute(value, "tensor", [(i, i ^ (k * CORES)) for i in range(parts)])

    def across_dp(value, k):
        return lax.ppermute(value, "dp", [(i, i ^ k) for i in range(owners)])

    rel_core = jnp.arange(CORES, dtype=jnp.int32)[:, None, None]
    rel_chip = jnp.arange(chips, dtype=jnp.int32)[None, :, None]
    rel_block = jnp.arange(per_part, dtype=jnp.int32)[None, None, :]
    block_rel = ((chip ^ rel_chip) * CORES + (core ^ rel_core)) * per_part + rel_block
    owner_rel = adapter_of_block[block_rel]
    slot_rel = slot_of_block[block_rel]
    mine_rel = owner_rel == place
    live = block_live(tokens_per_adapter, adapter_of_block, BLK)
    keep_here = lax.dynamic_slice_in_dim(live, part * per_part, per_part, 0)[:, :, None]
    adapter_here = lax.dynamic_slice_in_dim(adapter_of_block, part * per_part, per_part, 0)

    units_per_chunk = parts * per_part
    chunks = BLK // UNIT_ROWS
    units = chunks * units_per_chunk
    order = jnp.flip(owner_rel, 0).reshape(-1), jnp.flip(slot_rel, 0).reshape(-1)
    unit_owner = jnp.tile(order[0], chunks)
    unit_start = jnp.tile(order[1], chunks) * BLK + jnp.repeat(
        jnp.arange(chunks, dtype=jnp.int32) * UNIT_ROWS, units_per_chunk
    )

    def own_rows(unit):
        return lax.dynamic_slice(tokens, (unit_start[unit], 0), (UNIT_ROWS, width_dev))

    def relay(step_in_line, perm):
        arrived = []
        for step in range(units + SKEW * (owners - 2)):
            unit = jnp.clip(step - SKEW * step_in_line, 0, units - 1)
            value = own_rows(unit)
            if step >= SKEW:
                value = jnp.where(unit_owner[unit] == place, value, arrived[step - SKEW])
            arrived.append(lax.ppermute(value, "dp", perm))
        return arrived

    down_line = relay(owners - 1 - place, [(i, i - 1) for i in range(1, owners)])
    up_line = relay(place, [(i, i + 1) for i in range(owners - 1)])

    def unit_rows(unit):
        value = own_rows(unit)
        above = down_line[unit]
        below = up_line[unit]
        for hop in range(1, owners - 1):
            above = jnp.where(place == owners - 2 - hop, down_line[unit + SKEW * hop], above)
            below = jnp.where(place == 1 + hop, up_line[unit + SKEW * hop], below)
        owner = unit_owner[unit]
        return jnp.where(owner == place, value, jnp.where(owner > place, above, below))

    rows_per_slot = tokens.reshape(CAP, BLK, width_dev)
    partial_low = jnp.einsum(
        "mgh,hx->mgx", rows_per_slot, adapter_down_factor[0], preferred_element_type=jnp.float32
    )
    in_slot = (
        slot_rel[..., None] == jnp.arange(CAP, dtype=jnp.int32)
    ) & mine_rel[..., None]
    low_rel = jnp.sum(
        jnp.where(in_slot[..., None, None], partial_low, 0.0), axis=3
    )
    low_chip = low_rel[0] + to_other_core(low_rel[1])
    low_part = low_chip[0]
    for k in range(1, chips):
        low_part = low_part + to_chip(low_chip[k], k)
    blocks_here = cotangent.reshape(per_part, BLK, hidden_dev)
    up_here = adapter_up_factor[adapter_here]
    partial_back = jnp.einsum(
        "bkf,brf->bkr", blocks_here, up_here, preferred_element_type=jnp.float32
    )
    both = jnp.concatenate([low_part, partial_back], axis=-1)
    k = 1
    while k < owners:
        both = both + across_dp(both, k)
        k *= 2
    both = jnp.where(keep_here, both, 0.0).astype(jnp.bfloat16)
    lowered, back_rows = both[..., :rank], both[..., rank:]

    def every_part(value):
        same_core = jnp.stack([value] + [to_chip(value, k) for k in range(1, chips)])
        return same_core, to_other_core(same_core)

    back_rel = jnp.stack(every_part(back_rows))
    back_slots = jnp.sum(
        jnp.where(in_slot[..., None, None], back_rel[:, :, :, None], 0), axis=(0, 1, 2)
    ).astype(jnp.bfloat16)
    down_gradient = adapter_scale * jnp.einsum(
        "skd,skr->dr", rows_per_slot, back_slots, preferred_element_type=jnp.float32
    )

    pieces = jnp.einsum(
        "bkr,bkf->brf", lowered, blocks_here, preferred_element_type=jnp.float32
    ).astype(jnp.bfloat16)
    pieces_rel = every_part(pieces)
    adapters = jnp.arange(adapter_count, dtype=jnp.int32)[:, None, None]

    def of_adapter(core_index, chip_index):
        total = None
        for i in range(per_part):
            piece = pieces_rel[core_index][chip_index, i].astype(jnp.float32)
            term = jnp.where(owner_rel[core_index, chip_index, i] == adapters, piece[None], 0.0)
            total = term if total is None else total + term
        return total

    level = [of_adapter(0, j) + of_adapter(1, j) for j in range(chips)]
    while len(level) > 1:
        level = [level[j] + level[j + 1] for j in range(0, len(level), 2)]
    up_gradient = adapter_scale * level[0]

    projected = []
    for chunk in range(chunks):
        first = chunk * units_per_chunk
        rows = jnp.concatenate([unit_rows(first + u) for u in range(units_per_chunk)], axis=0)
        send, keep = split_product(rows, frozen_up_weight)
        chip_sum = (keep + to_other_core(send).astype(jnp.float32)).reshape(
            chips, per_part, UNIT_ROWS, hidden_dev
        )
        low_chunk = lowered[:, chunk * UNIT_ROWS : (chunk + 1) * UNIT_ROWS]
        keep_chunk = keep_here[:, chunk * UNIT_ROWS : (chunk + 1) * UNIT_ROWS]
        total = chip_sum[0] + adapter_scale * jnp.einsum(
            "azs,asg->azg", low_chunk, up_here, preferred_element_type=jnp.float32
        )
        for k in range(1, chips):
            total = total + to_chip(chip_sum[k].astype(jnp.bfloat16), k).astype(jnp.float32)
        projected.append(jnp.where(keep_chunk, total, 0.0).astype(jnp.bfloat16))
    projected = jnp.concatenate(projected, axis=1).reshape(per_part * BLK, hidden_dev)
    return (projected, down_gradient[None], up_gradient)


def solution(mesh):
    return jax.shard_map(
        per_device,
        mesh=mesh,
        in_specs=(
            P(("groups", "dp"), "tensor"),
            P(("groups", "tensor"), "dp"),
            P("tensor", "dp"),
            P(("groups", "dp"), "tensor", None),
            P("groups", None, "dp"),
            P("groups"),
            P("groups"),
            P("groups"),
        ),
        out_specs=(
            P(("groups", "tensor"), "dp"),
            P(("groups", "dp"), "tensor", None),
            P("groups", None, "dp"),
        ),
        check_vma=False,
    )
```

```python
import functools

import jax
import jax.numpy as jnp
from jax import lax
from jax.experimental import pallas as pl
from jax.experimental.pallas import tpu as pltpu
from jax.sharding import PartitionSpec as P

BLK = 128
CAP = 3
CORES = 2
CHUNK_ROWS = (64, 64)
MIB = 2**20

adapter_scale = 0.5

LAST = (((1,), (1,)), ((), ()))


class Index:
    def __init__(self, ref, block_count, adapter_count, parts):
        self.ref = ref
        self.blocks, self.adapters, self.parts = block_count, adapter_count, parts
        self.chips = parts // CORES
        self.per_part = block_count // parts

    @staticmethod
    def pack(adapter_of_block, slot_of_block, tokens_per_adapter):
        place = jnp.stack([lax.axis_index("dp"), lax.axis_index("tensor")]).astype(jnp.int32)
        return jnp.concatenate([adapter_of_block, slot_of_block, tokens_per_adapter, place])

    def owner(self, block):
        return self.ref[block]

    def slot(self, block):
        return self.ref[self.blocks + block]

    def tokens(self, adapter):
        return self.ref[2 * self.blocks + adapter]

    @property
    def place(self):
        return self.ref[2 * self.blocks + self.adapters]

    @property
    def part(self):
        return self.ref[2 * self.blocks + self.adapters + 1]

    def block(self, core_bit, chip_bits, i):
        return (self.part ^ (chip_bits * CORES + core_bit)) * self.per_part + i

    def live_rows(self, block):
        adapter = self.owner(block)
        first = jnp.int32(0)
        for a in range(self.adapters):
            count = (self.tokens(a) + BLK - 1) // BLK
            first = first + jnp.where(a < adapter, count, 0)
        return self.tokens(adapter) - (block - first) * BLK


def whole(shape):
    return pl.BlockSpec(shape, lambda *_: (0,) * len(shape))


def shape_of(shape, dtype):
    return jax.ShapeDtypeStruct(shape, dtype)


def cost(flops, bytes_accessed):
    return pl.CostEstimate(flops=flops, bytes_accessed=bytes_accessed, transcendentals=0)


def copy_all(copies):
    for copy in copies:
        copy.start()
    for copy in copies:
        copy.wait()


def first_hop_kernel(index_of, starts, rows, index_ref, tokens_ref, *refs):
    outs, sems = refs[:-1], refs[-1]
    index = index_of(index_ref)
    place = index.place
    inward = jnp.where(place == 0, 2, 1)
    copies = []
    for c, (start, count) in enumerate(zip(starts, rows)):
        for j, block in enumerate((inward, 0)):
            at = pl.multiple_of(index.slot(block) * BLK + start, 16)
            copies.append(
                pltpu.make_async_copy(
                    tokens_ref.at[pl.ds(at, count)], outs[2 * c + j], sems.at[2 * c + j]
                )
            )
    copy_all(copies)


def pick_copy(choices, out_ref, sem):
    for condition, source in choices:

        @pl.when(condition)
        def _(source=source):
            copy = pltpu.make_async_copy(source, out_ref, sem)
            copy.start()
            copy.wait()


def second_hop_kernel(index_of, start, count, index_ref, tokens_ref, a_ref, b_ref, x_ref, y_ref, sems):
    index = index_of(index_ref)
    place = index.place

    def own(block):
        at = pl.multiple_of(index.slot(block) * BLK + start, 16)
        return tokens_ref.at[pl.ds(at, count)]

    outer = jnp.where(place == 0, 1, jnp.where(place == 1, 0, 2))
    passed = (place == 1) & (index.owner(0) != 1)
    pick_copy(
        [(jnp.logical_not(passed), own(outer)), (passed, b_ref)], x_ref, sems.at[0]
    )
    middle = jnp.where(place == 1, 2, 1)
    passed = ((place == 1) | (place == 2)) & (index.owner(middle) != place)
    pick_copy(
        [(jnp.logical_not(passed), own(middle)), (passed, a_ref)], y_ref, sems.at[1]
    )


def settle_kernel(index_of, start, count, index_ref, tokens_ref, x_ref, y_ref, out_ref, sems):
    index = index_of(index_ref)
    place = index.place
    owner = index.owner(place)
    mine = owner == place
    edge = (place == 0) | ((place == 1) & (owner == 0)) | ((place == 2) & (owner == 3))
    at = pl.multiple_of(index.slot(place) * BLK + start, 16)
    pick_copy(
        [
            (mine, tokens_ref.at[pl.ds(at, count)]),
            (jnp.logical_not(mine) & edge, x_ref),
            (jnp.logical_not(mine | edge), y_ref),
        ],
        out_ref,
        sems.at[0],
    )


def blocks_at_home(index_of, index, tokens):
    width = tokens.shape[1]
    starts = [sum(CHUNK_ROWS[:c]) for c in range(len(CHUNK_ROWS))]
    hbm = pl.BlockSpec(memory_space=pl.ANY)

    def call(kernel, outs, copies, operands, name):
        return pl.pallas_call(
            kernel,
            grid_spec=pltpu.PrefetchScalarGridSpec(
                num_scalar_prefetch=1,
                grid=(),
                in_specs=[hbm] * len(operands),
                out_specs=[hbm] * len(outs),
                scratch_shapes=[pltpu.SemaphoreType.DMA((copies,))],
            ),
            out_shape=outs,
            cost_estimate=cost(0, 4 * sum(o.size for o in outs)),
            name=name,
        )(index, *operands)

    sends = call(
        functools.partial(first_hop_kernel, index_of, starts, CHUNK_ROWS),
        [shape_of((count, width), tokens.dtype) for count in CHUNK_ROWS for _ in range(2)],
        2 * len(CHUNK_ROWS),
        (tokens,),
        "first_hop",
    )
    homes = []
    for c, (start, count) in enumerate(zip(starts, CHUNK_ROWS)):
        unit = shape_of((count, width), tokens.dtype)
        inward = lax.ppermute(sends[2 * c], "dp", [(3, 2), (0, 1)])
        left = lax.ppermute(sends[2 * c + 1], "dp", [(2, 1)])
        outer, middle = call(
            functools.partial(second_hop_kernel, index_of, start, count),
            [unit, unit],
            2,
            (tokens, inward, left),
            "second_hop",
        )
        outer = lax.ppermute(outer, "dp", [(1, 0), (0, 1), (3, 2)])
        middle = lax.ppermute(middle, "dp", [(2, 1), (1, 2)])
        (home,) = call(
            functools.partial(settle_kernel, index_of, start, count),
            [unit],
            1,
            (tokens, outer, middle),
            "settle",
        )
        homes.append(home)
    return homes


def split_product_kernel(index_of, index_ref, x_ref, w_ref, send_ref, other_ref, own_ref):
    index = index_of(index_ref)
    each = index.per_part * x_ref.shape[1]
    rows = [
        x_ref[index.block(core_bit, chip_bits, i)]
        for core_bit in (1, 0)
        for chip_bits in range(index.chips)
        for i in range(index.per_part)
    ]
    total = jnp.dot(
        jnp.concatenate(rows, axis=0), w_ref[...], preferred_element_type=jnp.float32
    )
    half = index.chips * each
    send_ref[...] = total[:half].astype(send_ref.dtype)
    own_ref[...] = total[half : half + each]
    other_ref[...] = total[half + each :]


def split_product(index_of, index, shape, rows, weight):
    block_count, count, depth = rows.shape
    width = weight.shape[1]
    tile = 512
    each = shape.per_part * count
    half = block_count * count // 2

    def columns(height):
        return pl.BlockSpec((height, tile), lambda n, _: (0, n))

    return pl.pallas_call(
        functools.partial(split_product_kernel, index_of),
        grid_spec=pltpu.PrefetchScalarGridSpec(
            num_scalar_prefetch=1,
            grid=(width // tile,),
            in_specs=[whole(rows.shape), columns(depth)],
            out_specs=[columns(half), columns(half - each), columns(each)],
        ),
        out_shape=[
            shape_of((half, width), jnp.bfloat16),
            shape_of((half - each, width), jnp.float32),
            shape_of((each, width), jnp.float32),
        ],
        compiler_params=pltpu.CompilerParams(vmem_limit_bytes=24 * MIB),
        cost_estimate=cost(
            4 * half * depth * width, 2 * depth * (2 * half + width) + 6 * half * width
        ),
        name="split_product",
    )(index, rows, weight)


def narrow_kernel(index_of, index_ref, tokens_ref, down_ref, cot_ref, up_ref, send_ref, keep_ref, back_ref, low):
    index = index_of(index_ref)
    for m in range(CAP):
        low[m] = lax.dot_general(
            down_ref[0],
            tokens_ref[m * BLK : (m + 1) * BLK],
            LAST,
            preferred_element_type=jnp.float32,
        )
    for core_bit, out_ref in ((1, send_ref), (0, keep_ref)):
        for chip_bits in range(index.chips):
            for i in range(index.per_part):
                block = index.block(core_bit, chip_bits, i)
                mine = index.owner(block) == index.place
                out_ref[chip_bits, i] = jnp.where(mine, low[index.slot(block)], 0.0)
    for i in range(index.per_part):
        adapter = index.owner(index.block(0, 0, i))
        back_ref[i] = lax.dot_general(
            up_ref[adapter],
            cot_ref[i * BLK : (i + 1) * BLK],
            LAST,
            preferred_element_type=jnp.float32,
        )


def narrow(index_of, index, shape, tokens, down, cotangent, up):
    rank = up.shape[1]
    one = (shape.per_part, rank, BLK)
    outs = [(shape.chips,) + one, (shape.chips,) + one, one]
    operands = (tokens, down, cotangent, up)
    return pl.pallas_call(
        functools.partial(narrow_kernel, index_of),
        grid_spec=pltpu.PrefetchScalarGridSpec(
            num_scalar_prefetch=1,
            grid=(1,),
            in_specs=[whole(o.shape) for o in operands],
            out_specs=[whole(o) for o in outs],
            scratch_shapes=[pltpu.VMEM((CAP, rank, BLK), jnp.float32)],
        ),
        out_shape=[shape_of(o, jnp.float32) for o in outs],
        compiler_params=pltpu.CompilerParams(vmem_limit_bytes=24 * MIB),
        cost_estimate=cost(2 * rank * (tokens.size + cotangent.size), 2 * sum(o.size for o in operands)),
        name="narrow",
    )(index, *operands)


def pieces_kernel(index_of, index_ref, sum_ref, more_ref, cot_ref, low_ref, back_ref, piece_ref):
    index = index_of(index_ref)
    for i in range(index.per_part):
        live = index.live_rows(index.block(0, 0, i))
        keep = lax.broadcasted_iota(jnp.int32, low_ref.shape[1:], 1) < live
        lowered = jnp.where(keep, sum_ref[0, i] + more_ref[0, i], 0.0).astype(low_ref.dtype)
        back = jnp.where(keep, sum_ref[1, i] + more_ref[1, i], 0.0)
        low_ref[i] = lowered
        back_ref[i] = back.astype(back_ref.dtype)
        piece_ref[i] = jnp.dot(
            lowered, cot_ref[i * BLK : (i + 1) * BLK], preferred_element_type=jnp.float32
        ).astype(piece_ref.dtype)


def make_pieces(index_of, index, shape, total, more, cotangent):
    _, per_part, rank, _ = total.shape
    width = cotangent.shape[1]
    outs = [(per_part, rank, BLK), (per_part, rank, BLK), (per_part, rank, width)]
    operands = (total, more, cotangent)
    return pl.pallas_call(
        functools.partial(pieces_kernel, index_of),
        grid_spec=pltpu.PrefetchScalarGridSpec(
            num_scalar_prefetch=1,
            grid=(1,),
            in_specs=[whole(o.shape) for o in operands],
            out_specs=[whole(o) for o in outs],
        ),
        out_shape=[shape_of(o, jnp.bfloat16) for o in outs],
        compiler_params=pltpu.CompilerParams(vmem_limit_bytes=24 * MIB),
        cost_estimate=cost(2 * rank * cotangent.size, 3 * cotangent.size),
        name="pieces",
    )(index, *operands)


def down_gradient_kernel(index_of, index_ref, tokens_ref, *refs):
    back_refs, out_ref = refs[:-1], refs[-1]
    index = index_of(index_ref)
    out_ref[...] = jnp.zeros_like(out_ref)
    for core_bit in range(CORES):
        for chip_bits in range(index.chips):
            for i in range(index.per_part):
                block = index.block(core_bit, chip_bits, i)
                back_ref = back_refs[core_bit * index.chips + chip_bits]

                @pl.when(index.owner(block) == index.place)
                def _(block=block, back_ref=back_ref, i=i):
                    at = pl.multiple_of(index.slot(block) * BLK, BLK)
                    out_ref[0] += adapter_scale * jnp.dot(
                        back_ref[i],
                        tokens_ref[pl.ds(at, BLK)],
                        preferred_element_type=jnp.float32,
                    )


def down_gradient(index_of, index, tokens, backs):
    out = (1, backs[0].shape[1], tokens.shape[1])
    operands = (tokens, *backs)
    return pl.pallas_call(
        functools.partial(down_gradient_kernel, index_of),
        grid_spec=pltpu.PrefetchScalarGridSpec(
            num_scalar_prefetch=1,
            grid=(1,),
            in_specs=[whole(o.shape) for o in operands],
            out_specs=whole(out),
        ),
        out_shape=shape_of(out, jnp.float32),
        compiler_params=pltpu.CompilerParams(vmem_limit_bytes=24 * MIB),
        cost_estimate=cost(2 * out[1] * tokens.size, 2 * tokens.size),
        name="down_gradient",
    )(index, *operands)


def up_gradient_kernel(index_of, index_ref, *refs):
    piece_refs, out_ref = refs[:-1], refs[-1]
    index = index_of(index_ref)

    def of_device(core_bit, chip_bits, adapter):
        total = None
        for i in range(index.per_part):
            mine = index.owner(index.block(core_bit, chip_bits, i)) == adapter
            piece = piece_refs[core_bit * index.chips + chip_bits][i].astype(jnp.float32)
            term = jnp.where(mine, piece, 0.0)
            total = term if total is None else total + term
        return total

    for adapter in range(index.adapters):
        level = [
            of_device(0, j, adapter) + of_device(1, j, adapter) for j in range(index.chips)
        ]
        while len(level) > 1:
            level = [level[j] + level[j + 1] for j in range(0, len(level), 2)]
        out_ref[adapter] = adapter_scale * level[0]


def up_gradient(index_of, index, adapter_count, pieces):
    per_part, rank, width = pieces[0].shape
    tile = 512
    out = (adapter_count, rank, width)
    return pl.pallas_call(
        functools.partial(up_gradient_kernel, index_of),
        grid_spec=pltpu.PrefetchScalarGridSpec(
            num_scalar_prefetch=1,
            grid=(width // tile,),
            in_specs=[pl.BlockSpec((per_part, rank, tile), lambda n, _: (0, 0, n))] * len(pieces),
            out_specs=pl.BlockSpec((adapter_count, rank, tile), lambda n, _: (0, 0, n)),
        ),
        out_shape=shape_of(out, jnp.float32),
        compiler_params=pltpu.CompilerParams(vmem_limit_bytes=24 * MIB),
        cost_estimate=cost(0, 4 * adapter_count * rank * width + 2 * len(pieces) * pieces[0].size),
        name="up_gradient",
    )(index, *pieces)


def finish_kernel(index_of, counts, index_ref, low_ref, up_ref, *refs):
    sum_refs, out_ref = refs[:-1], refs[-1]
    index = index_of(index_ref)
    per_chunk = len(sum_refs) // len(counts)
    for i in range(index.per_part):
        block = index.block(0, 0, i)
        live = index.live_rows(block)
        side = lax.dot_general(
            low_ref[i],
            up_ref[index.owner(block)],
            (((0,), (0,)), ((), ())),
            preferred_element_type=jnp.float32,
        )
        start = 0
        for c, count in enumerate(counts):
            total = adapter_scale * side[start : start + count]
            for ref in sum_refs[c * per_chunk : (c + 1) * per_chunk]:
                total = total + ref[i * count : (i + 1) * count].astype(jnp.float32)
            keep = start + lax.broadcasted_iota(jnp.int32, total.shape, 0) < live
            at = i * BLK + start
            out_ref[at : at + count] = jnp.where(keep, total, 0.0).astype(out_ref.dtype)
            start += count


def finish(index_of, index, lowered, up, sums):
    per_part = lowered.shape[0]
    adapter_count, rank, width = up.shape
    tile = 1024
    flat = [s for chunk in sums for s in chunk]
    heights = [per_part * count for chunk, count in zip(sums, CHUNK_ROWS) for _ in chunk]
    out = (per_part * BLK, width)
    return pl.pallas_call(
        functools.partial(finish_kernel, index_of, CHUNK_ROWS),
        grid_spec=pltpu.PrefetchScalarGridSpec(
            num_scalar_prefetch=1,
            grid=(width // tile,),
            in_specs=[
                whole(lowered.shape),
                pl.BlockSpec((adapter_count, rank, tile), lambda n, _: (0, 0, n)),
            ]
            + [pl.BlockSpec((height, tile), lambda n, _: (0, n)) for height in heights],
            out_specs=pl.BlockSpec((out[0], tile), lambda n, _: (0, n)),
        ),
        out_shape=shape_of(out, jnp.bfloat16),
        compiler_params=pltpu.CompilerParams(vmem_limit_bytes=24 * MIB),
        cost_estimate=cost(2 * rank * out[0] * width, 10 * out[0] * width + 2 * up.size),
        name="finish",
    )(index, lowered, up, *flat)


def per_device(
    tokens,
    cotangent,
    frozen_up_weight,
    adapter_down_factor,
    adapter_up_factor,
    tokens_per_adapter,
    adapter_of_block,
    slot_of_block,
):
    owners = lax.axis_size("dp")
    parts = lax.axis_size("tensor")
    chips = parts // CORES
    block_count = adapter_of_block.shape[0]
    adapter_count = adapter_up_factor.shape[0]
    width_dev = tokens.shape[1]
    index_of = functools.partial(
        Index, block_count=block_count, adapter_count=adapter_count, parts=parts
    )
    shape = index_of(None)
    index = Index.pack(adapter_of_block, slot_of_block, tokens_per_adapter)

    def to_other_core(value):
        return lax.ppermute(value, "tensor", [(i, i ^ 1) for i in range(parts)])

    def to_chip(value, k):
        return lax.ppermute(value, "tensor", [(i, i ^ (k * CORES)) for i in range(parts)])

    def across_dp(value, k):
        return lax.ppermute(value, "dp", [(i, i ^ k) for i in range(owners)])

    def every_part(value):
        same_core = [value] + [to_chip(value, k) for k in range(1, chips)]
        return same_core + [to_other_core(v) for v in same_core]

    if owners == 4 and block_count == 4:
        homes = blocks_at_home(index_of, index, tokens)
        chunks = [lax.all_gather(home, "dp", axis=0) for home in homes]
    else:
        every_slot = lax.all_gather(
            tokens.reshape(CAP, BLK, width_dev), "dp", axis=0, tiled=True
        )
        picked = every_slot[adapter_of_block * CAP + slot_of_block]
        starts = [sum(CHUNK_ROWS[:c]) for c in range(len(CHUNK_ROWS))]
        chunks = [picked[:, s : s + count] for s, count in zip(starts, CHUNK_ROWS)]

    send, keep, back = narrow(
        index_of,
        index,
        shape,
        tokens,
        jnp.swapaxes(adapter_down_factor, 1, 2),
        cotangent,
        adapter_up_factor,
    )
    low_chip = keep + to_other_core(send)
    low_part = low_chip[0]
    for k in range(1, chips):
        low_part = low_part + to_chip(low_chip[k], k)
    total = jnp.stack([low_part, back])
    k = 1
    while 2 * k < owners:
        total = total + across_dp(total, k)
        k *= 2
    more = across_dp(total, k)
    lowered, back_rows, pieces = make_pieces(index_of, index, shape, total, more, cotangent)
    up_grad = up_gradient(index_of, index, adapter_count, every_part(pieces))
    down_grad = down_gradient(index_of, index, tokens, every_part(back_rows))

    sums = []
    for rows in chunks:
        count = rows.shape[1]
        each = shape.per_part * count
        send, other, own = split_product(index_of, index, shape, rows, frozen_up_weight)
        arrived = to_other_core(send)
        outgoing = (other + arrived[each:].astype(jnp.float32)).astype(jnp.bfloat16)
        sums.append(
            [own, arrived]
            + [to_chip(outgoing[(k - 1) * each : k * each], k) for k in range(1, chips)]
        )
    projected = finish(index_of, index, lowered, adapter_up_factor, sums)
    return (projected, jnp.swapaxes(down_grad, 1, 2), up_grad)


def solution(mesh):
    return jax.shard_map(
        per_device,
        mesh=mesh,
        in_specs=(
            P(("groups", "dp"), "tensor"),
            P(("groups", "tensor"), "dp"),
            P("tensor", "dp"),
            P(("groups", "dp"), "tensor", None),
            P("groups", None, "dp"),
            P("groups"),
            P("groups"),
            P("groups"),
        ),
        out_specs=(
            P(("groups", "tensor"), "dp"),
            P(("groups", "dp"), "tensor", None),
            P("groups", None, "dp"),
        ),
        check_vma=False,
    )
```

```python
import functools

import jax
import jax.numpy as jnp
from jax import lax
from jax.experimental import pallas as pl
from jax.experimental.pallas import tpu as pltpu
from jax.sharding import PartitionSpec as P

BLK = 128
CAP = 3
CORES = 2
CHUNK_ROWS = (64, 64)
MIB = 2**20

adapter_scale = 0.5

LAST = (((1,), (1,)), ((), ()))


class Index:
    def __init__(self, ref, block_count, adapter_count, parts):
        self.ref = ref
        self.blocks, self.adapters, self.parts = block_count, adapter_count, parts
        self.chips = parts // CORES
        self.per_part = block_count // parts

    @staticmethod
    def pack(adapter_of_block, slot_of_block, tokens_per_adapter):
        place = jnp.stack([lax.axis_index("dp"), lax.axis_index("tensor")]).astype(jnp.int32)
        return jnp.concatenate([adapter_of_block, slot_of_block, tokens_per_adapter, place])

    def owner(self, block):
        return self.ref[block]

    def slot(self, block):
        return self.ref[self.blocks + block]

    def tokens(self, adapter):
        return self.ref[2 * self.blocks + adapter]

    @property
    def place(self):
        return self.ref[2 * self.blocks + self.adapters]

    @property
    def part(self):
        return self.ref[2 * self.blocks + self.adapters + 1]

    def block(self, core_bit, chip_bits, i):
        return (self.part ^ (chip_bits * CORES + core_bit)) * self.per_part + i

    def live_rows(self, block):
        adapter = self.owner(block)
        first = jnp.int32(0)
        for a in range(self.adapters):
            count = (self.tokens(a) + BLK - 1) // BLK
            first = first + jnp.where(a < adapter, count, 0)
        return self.tokens(adapter) - (block - first) * BLK


def whole(shape):
    return pl.BlockSpec(shape, lambda *_: (0,) * len(shape))


def shape_of(shape, dtype):
    return jax.ShapeDtypeStruct(shape, dtype)


def cost(flops, bytes_accessed):
    return pl.CostEstimate(flops=flops, bytes_accessed=bytes_accessed, transcendentals=0)


def own_copy(index, block, start, tokens_ref, out_ref, sem):
    at = pl.multiple_of(index.slot(block) * BLK + start, 16)
    return pltpu.make_async_copy(tokens_ref.at[pl.ds(at, out_ref.shape[0])], out_ref, sem)


def run_all(copies):
    for copy in copies:
        copy.start()
    for copy in copies:
        copy.wait()


def first_hop_kernel(index_of, starts, index_ref, tokens_ref, *refs):
    outs, sems = refs[:-1], refs[-1]
    index = index_of(index_ref)
    inward = jnp.where(index.place == 0, 2, 1)
    run_all(
        [
            own_copy(index, block, start, tokens_ref, outs[2 * c + j], sems.at[2 * c + j])
            for c, start in enumerate(starts)
            for j, block in enumerate((inward, 0))
        ]
    )


def second_hop_kernel(index_of, start, index_ref, tokens_ref, a_ref, b_ref, *refs):
    x_ref, y_ref, sems = refs[-3:]
    index = index_of(index_ref)
    place = index.place
    outer = jnp.where(place == 0, 1, jnp.where(place == 1, 0, 2))
    middle = jnp.where(place == 1, 2, 1)
    run_all(
        [
            own_copy(index, outer, start, tokens_ref, x_ref, sems.at[0]),
            own_copy(index, middle, start, tokens_ref, y_ref, sems.at[1]),
        ]
    )

    @pl.when((place == 1) & (index.owner(0) != 1))
    def _():
        x_ref[...] = b_ref[...]

    @pl.when(((place == 1) | (place == 2)) & (index.owner(middle) != place))
    def _():
        y_ref[...] = a_ref[...]


def settle_kernel(index_of, start, index_ref, tokens_ref, x_ref, y_ref, *refs):
    out_ref, sems = refs[-2:]
    index = index_of(index_ref)
    place = index.place
    owner = index.owner(place)
    mine = owner == place
    edge = (place == 0) | ((place == 1) & (owner == 0)) | ((place == 2) & (owner == 3))
    run_all([own_copy(index, place, start, tokens_ref, out_ref, sems.at[0])])

    @pl.when(jnp.logical_not(mine) & edge)
    def _():
        out_ref[...] = x_ref[...]

    @pl.when(jnp.logical_not(mine | edge))
    def _():
        out_ref[...] = y_ref[...]


def blocks_at_home(index_of, index, tokens, beside):
    width = tokens.shape[1]
    starts = [sum(CHUNK_ROWS[:c]) for c in range(len(CHUNK_ROWS))]
    hbm = pl.BlockSpec(memory_space=pl.ANY)
    vmem = pl.BlockSpec(memory_space=pltpu.VMEM)
    beside = list(beside)

    def call(kernel, outs, received, name):
        extra = tuple(beside.pop(0)()) if beside and received else ()
        return pl.pallas_call(
            kernel,
            grid_spec=pltpu.PrefetchScalarGridSpec(
                num_scalar_prefetch=1,
                grid=(),
                in_specs=[hbm] + [vmem] * len(received) + [hbm] * len(extra),
                out_specs=[vmem] * len(outs),
                scratch_shapes=[pltpu.SemaphoreType.DMA((len(outs),))],
            ),
            out_shape=outs,
            cost_estimate=cost(0, 4 * sum(o.size for o in outs)),
            name=name,
        )(index, tokens, *received, *extra)

    sends = call(
        functools.partial(first_hop_kernel, index_of, starts),
        [shape_of((count, width), tokens.dtype) for count in CHUNK_ROWS for _ in range(2)],
        (),
        "first_hop",
    )
    homes = []
    for c, (start, count) in enumerate(zip(starts, CHUNK_ROWS)):
        unit = shape_of((count, width), tokens.dtype)
        inward = lax.ppermute(sends[2 * c], "dp", [(3, 2), (0, 1)])
        left = lax.ppermute(sends[2 * c + 1], "dp", [(2, 1)])
        outer, middle = call(
            functools.partial(second_hop_kernel, index_of, start),
            [unit, unit],
            (inward, left),
            "second_hop",
        )
        outer = lax.ppermute(outer, "dp", [(1, 0), (0, 1), (3, 2)])
        middle = lax.ppermute(middle, "dp", [(2, 1), (1, 2)])
        (home,) = call(
            functools.partial(settle_kernel, index_of, start),
            [unit],
            (outer, middle),
            "settle",
        )
        homes.append(home)
    return homes


def split_product_kernel(index_of, index_ref, x_ref, w_ref, send_ref, other_ref, own_ref):
    index = index_of(index_ref)
    each = index.per_part * x_ref.shape[1]
    rows = [
        x_ref[index.block(core_bit, chip_bits, i)]
        for core_bit in (1, 0)
        for chip_bits in range(index.chips)
        for i in range(index.per_part)
    ]
    total = jnp.dot(
        jnp.concatenate(rows, axis=0), w_ref[...], preferred_element_type=jnp.float32
    )
    half = index.chips * each
    send_ref[...] = total[:half].astype(send_ref.dtype)
    own_ref[...] = total[half : half + each]
    other_ref[...] = total[half + each :]


def split_product(index_of, index, shape, rows, weight):
    block_count, count, depth = rows.shape
    width = weight.shape[1]
    tile = 512
    each = shape.per_part * count
    half = block_count * count // 2

    def columns(height):
        return pl.BlockSpec((height, tile), lambda n, _: (0, n))

    return pl.pallas_call(
        functools.partial(split_product_kernel, index_of),
        grid_spec=pltpu.PrefetchScalarGridSpec(
            num_scalar_prefetch=1,
            grid=(width // tile,),
            in_specs=[whole(rows.shape), columns(depth)],
            out_specs=[columns(half), columns(half - each), columns(each)],
        ),
        out_shape=[
            shape_of((half, width), jnp.bfloat16),
            shape_of((half - each, width), jnp.float32),
            shape_of((each, width), jnp.float32),
        ],
        compiler_params=pltpu.CompilerParams(vmem_limit_bytes=48 * MIB),
        cost_estimate=cost(
            4 * half * depth * width, 2 * depth * (2 * half + width) + 6 * half * width
        ),
        name="split_product",
    )(index, rows, weight)


def narrow_kernel(index_of, index_ref, tokens_ref, down_ref, cot_ref, up_ref, send_ref, keep_ref, back_ref, low):
    index = index_of(index_ref)
    for m in range(CAP):
        low[m] = lax.dot_general(
            down_ref[0],
            tokens_ref[m * BLK : (m + 1) * BLK],
            LAST,
            preferred_element_type=jnp.float32,
        )
    for core_bit, out_ref in ((1, send_ref), (0, keep_ref)):
        for chip_bits in range(index.chips):
            for i in range(index.per_part):
                block = index.block(core_bit, chip_bits, i)
                mine = index.owner(block) == index.place
                out_ref[chip_bits, i] = jnp.where(mine, low[index.slot(block)], 0.0)
    for i in range(index.per_part):
        adapter = index.owner(index.block(0, 0, i))
        back_ref[i] = lax.dot_general(
            up_ref[adapter],
            cot_ref[i * BLK : (i + 1) * BLK],
            LAST,
            preferred_element_type=jnp.float32,
        )


def narrow(index_of, index, shape, tokens, down, cotangent, up):
    rank = up.shape[1]
    one = (shape.per_part, rank, BLK)
    outs = [(shape.chips,) + one, (shape.chips,) + one, one]
    operands = (tokens, down, cotangent, up)
    return pl.pallas_call(
        functools.partial(narrow_kernel, index_of),
        grid_spec=pltpu.PrefetchScalarGridSpec(
            num_scalar_prefetch=1,
            grid=(1,),
            in_specs=[whole(o.shape) for o in operands],
            out_specs=[whole(o) for o in outs],
            scratch_shapes=[pltpu.VMEM((CAP, rank, BLK), jnp.float32)],
        ),
        out_shape=[shape_of(o, jnp.float32) for o in outs],
        compiler_params=pltpu.CompilerParams(vmem_limit_bytes=24 * MIB),
        cost_estimate=cost(2 * rank * (tokens.size + cotangent.size), 2 * sum(o.size for o in operands)),
        name="narrow",
    )(index, *operands)


def pieces_kernel(index_of, index_ref, sum_ref, more_ref, cot_ref, low_ref, back_ref, piece_ref):
    index = index_of(index_ref)
    for i in range(index.per_part):
        live = index.live_rows(index.block(0, 0, i))
        keep = lax.broadcasted_iota(jnp.int32, low_ref.shape[1:], 1) < live
        lowered = jnp.where(keep, sum_ref[0, i] + more_ref[0, i], 0.0).astype(low_ref.dtype)
        back = jnp.where(keep, sum_ref[1, i] + more_ref[1, i], 0.0)
        low_ref[i] = lowered
        back_ref[i] = back.astype(back_ref.dtype)
        piece_ref[i] = jnp.dot(
            lowered, cot_ref[i * BLK : (i + 1) * BLK], preferred_element_type=jnp.float32
        ).astype(piece_ref.dtype)


def make_pieces(index_of, index, shape, total, more, cotangent):
    _, per_part, rank, _ = total.shape
    width = cotangent.shape[1]
    outs = [(per_part, rank, BLK), (per_part, rank, BLK), (per_part, rank, width)]
    operands = (total, more, cotangent)
    return pl.pallas_call(
        functools.partial(pieces_kernel, index_of),
        grid_spec=pltpu.PrefetchScalarGridSpec(
            num_scalar_prefetch=1,
            grid=(1,),
            in_specs=[whole(o.shape) for o in operands],
            out_specs=[whole(o) for o in outs],
        ),
        out_shape=[shape_of(o, jnp.bfloat16) for o in outs],
        compiler_params=pltpu.CompilerParams(vmem_limit_bytes=24 * MIB),
        cost_estimate=cost(2 * rank * cotangent.size, 3 * cotangent.size),
        name="pieces",
    )(index, *operands)


def down_gradient_kernel(index_of, index_ref, tokens_ref, *refs):
    back_refs, out_ref = refs[:-1], refs[-1]
    index = index_of(index_ref)
    out_ref[...] = jnp.zeros_like(out_ref)
    for core_bit in range(CORES):
        for chip_bits in range(index.chips):
            for i in range(index.per_part):
                block = index.block(core_bit, chip_bits, i)
                back_ref = back_refs[core_bit * index.chips + chip_bits]

                @pl.when(index.owner(block) == index.place)
                def _(block=block, back_ref=back_ref, i=i):
                    at = pl.multiple_of(index.slot(block) * BLK, BLK)
                    out_ref[0] += adapter_scale * jnp.dot(
                        back_ref[i],
                        tokens_ref[pl.ds(at, BLK)],
                        preferred_element_type=jnp.float32,
                    )


def down_gradient(index_of, index, tokens, backs):
    out = (1, backs[0].shape[1], tokens.shape[1])
    operands = (tokens, *backs)
    return pl.pallas_call(
        functools.partial(down_gradient_kernel, index_of),
        grid_spec=pltpu.PrefetchScalarGridSpec(
            num_scalar_prefetch=1,
            grid=(1,),
            in_specs=[whole(o.shape) for o in operands],
            out_specs=whole(out),
        ),
        out_shape=shape_of(out, jnp.float32),
        compiler_params=pltpu.CompilerParams(vmem_limit_bytes=24 * MIB),
        cost_estimate=cost(2 * out[1] * tokens.size, 2 * tokens.size),
        name="down_gradient",
    )(index, *operands)


def up_gradient_kernel(index_of, index_ref, *refs):
    piece_refs, out_ref = refs[:-1], refs[-1]
    index = index_of(index_ref)

    def of_device(core_bit, chip_bits, adapter):
        total = None
        for i in range(index.per_part):
            mine = index.owner(index.block(core_bit, chip_bits, i)) == adapter
            piece = piece_refs[core_bit * index.chips + chip_bits][i].astype(jnp.float32)
            term = jnp.where(mine, piece, 0.0)
            total = term if total is None else total + term
        return total

    for adapter in range(index.adapters):
        level = [
            of_device(0, j, adapter) + of_device(1, j, adapter) for j in range(index.chips)
        ]
        while len(level) > 1:
            level = [level[j] + level[j + 1] for j in range(0, len(level), 2)]
        out_ref[adapter] = adapter_scale * level[0]


def up_gradient(index_of, index, adapter_count, pieces):
    per_part, rank, width = pieces[0].shape
    tile = 512
    out = (adapter_count, rank, width)
    return pl.pallas_call(
        functools.partial(up_gradient_kernel, index_of),
        grid_spec=pltpu.PrefetchScalarGridSpec(
            num_scalar_prefetch=1,
            grid=(width // tile,),
            in_specs=[pl.BlockSpec((per_part, rank, tile), lambda n, _: (0, 0, n))] * len(pieces),
            out_specs=pl.BlockSpec((adapter_count, rank, tile), lambda n, _: (0, 0, n)),
        ),
        out_shape=shape_of(out, jnp.float32),
        compiler_params=pltpu.CompilerParams(vmem_limit_bytes=24 * MIB),
        cost_estimate=cost(0, 4 * adapter_count * rank * width + 2 * len(pieces) * pieces[0].size),
        name="up_gradient",
    )(index, *pieces)


def finish_kernel(index_of, counts, index_ref, low_ref, *refs):
    index = index_of(index_ref)
    up_refs, sum_refs, out_ref = refs[: index.per_part], refs[index.per_part : -1], refs[-1]
    per_chunk = len(sum_refs) // len(counts)
    for i in range(index.per_part):
        block = index.block(0, 0, i)
        live = index.live_rows(block)
        side = lax.dot_general(
            low_ref[i],
            up_refs[i][0],
            (((0,), (0,)), ((), ())),
            preferred_element_type=jnp.float32,
        )
        start = 0
        for c, count in enumerate(counts):
            total = adapter_scale * side[start : start + count]
            for ref in sum_refs[c * per_chunk : (c + 1) * per_chunk]:
                total = total + ref[i * count : (i + 1) * count].astype(jnp.float32)
            keep = start + lax.broadcasted_iota(jnp.int32, total.shape, 0) < live
            at = i * BLK + start
            out_ref[at : at + count] = jnp.where(keep, total, 0.0).astype(out_ref.dtype)
            start += count


def finish(index_of, index, lowered, up, sums):
    per_part = lowered.shape[0]
    adapter_count, rank, width = up.shape
    tile = 1024
    flat = [s for chunk in sums for s in chunk]
    heights = [per_part * count for chunk, count in zip(sums, CHUNK_ROWS) for _ in chunk]
    out = (per_part * BLK, width)

    def factor(i):
        def at(n, index_ref):
            index = index_of(index_ref)
            return (index.owner(index.block(0, 0, i)), 0, n)

        return pl.BlockSpec((1, rank, tile), at)

    return pl.pallas_call(
        functools.partial(finish_kernel, index_of, CHUNK_ROWS),
        grid_spec=pltpu.PrefetchScalarGridSpec(
            num_scalar_prefetch=1,
            grid=(width // tile,),
            in_specs=[whole(lowered.shape)]
            + [factor(i) for i in range(per_part)]
            + [pl.BlockSpec((height, tile), lambda n, _: (0, n)) for height in heights],
            out_specs=pl.BlockSpec((out[0], tile), lambda n, _: (0, n)),
        ),
        out_shape=shape_of(out, jnp.bfloat16),
        compiler_params=pltpu.CompilerParams(vmem_limit_bytes=24 * MIB),
        cost_estimate=cost(2 * rank * out[0] * width, 10 * out[0] * width + 2 * up.size),
        name="finish",
    )(index, lowered, *[up] * per_part, *flat)


def per_device(
    tokens,
    cotangent,
    frozen_up_weight,
    adapter_down_factor,
    adapter_up_factor,
    tokens_per_adapter,
    adapter_of_block,
    slot_of_block,
):
    owners = lax.axis_size("dp")
    parts = lax.axis_size("tensor")
    chips = parts // CORES
    block_count = adapter_of_block.shape[0]
    adapter_count = adapter_up_factor.shape[0]
    width_dev = tokens.shape[1]
    index_of = functools.partial(
        Index, block_count=block_count, adapter_count=adapter_count, parts=parts
    )
    shape = index_of(None)
    index = Index.pack(adapter_of_block, slot_of_block, tokens_per_adapter)

    def to_other_core(value):
        return lax.ppermute(value, "tensor", [(i, i ^ 1) for i in range(parts)])

    def to_chip(value, k):
        return lax.ppermute(value, "tensor", [(i, i ^ (k * CORES)) for i in range(parts)])

    def across_dp(value, k):
        return lax.ppermute(value, "dp", [(i, i ^ k) for i in range(owners)])

    def every_part(value):
        same_core = [value] + [to_chip(value, k) for k in range(1, chips)]
        return same_core + [to_other_core(v) for v in same_core]

    steps = {}

    def first_step():
        steps["send"], steps["keep"], steps["back"] = narrow(
            index_of,
            index,
            shape,
            tokens,
            jnp.swapaxes(adapter_down_factor, 1, 2),
            cotangent,
            adapter_up_factor,
        )
        return [steps["send"]]

    def second_step():
        low_chip = steps["keep"] + to_other_core(steps["send"])
        low_part = low_chip[0]
        for k in range(1, chips):
            low_part = low_part + to_chip(low_chip[k], k)
        steps["total"] = jnp.stack([low_part, steps["back"]])
        return [steps["total"]]

    def third_step():
        total, k = steps["total"], 1
        while 2 * k < owners:
            total = total + across_dp(total, k)
            k *= 2
        steps["small"] = make_pieces(
            index_of, index, shape, total, across_dp(total, k), cotangent
        )
        return [steps["small"][0]]

    if owners == 4 and block_count == 4:
        homes = blocks_at_home(index_of, index, tokens, [first_step, second_step, third_step])
        chunks = [lax.all_gather(home, "dp", axis=0) for home in homes]
    else:
        first_step(), second_step(), third_step()
        every_slot = lax.all_gather(
            tokens.reshape(CAP, BLK, width_dev), "dp", axis=0, tiled=True
        )
        picked = every_slot[adapter_of_block * CAP + slot_of_block]
        starts = [sum(CHUNK_ROWS[:c]) for c in range(len(CHUNK_ROWS))]
        chunks = [picked[:, s : s + count] for s, count in zip(starts, CHUNK_ROWS)]
    lowered, back_rows, pieces = steps["small"]
    up_grad = up_gradient(index_of, index, adapter_count, every_part(pieces))
    down_grad = down_gradient(index_of, index, tokens, every_part(back_rows))

    sums = []
    for rows in chunks:
        count = rows.shape[1]
        each = shape.per_part * count
        send, other, own = split_product(index_of, index, shape, rows, frozen_up_weight)
        arrived = to_other_core(send)
        outgoing = (other + arrived[each:].astype(jnp.float32)).astype(jnp.bfloat16)
        sums.append(
            [own, arrived]
            + [to_chip(outgoing[(k - 1) * each : k * each], k) for k in range(1, chips)]
        )
    projected = finish(index_of, index, lowered, adapter_up_factor, sums)
    return (projected, jnp.swapaxes(down_grad, 1, 2), up_grad)


def solution(mesh):
    return jax.shard_map(
        per_device,
        mesh=mesh,
        in_specs=(
            P(("groups", "dp"), "tensor"),
            P(("groups", "tensor"), "dp"),
            P("tensor", "dp"),
            P(("groups", "dp"), "tensor", None),
            P("groups", None, "dp"),
            P("groups"),
            P("groups"),
            P("groups"),
        ),
        out_specs=(
            P(("groups", "tensor"), "dp"),
            P(("groups", "dp"), "tensor", None),
            P("groups", None, "dp"),
        ),
        check_vma=False,
    )
```

```python
import functools

import jax
import jax.numpy as jnp
from jax import lax
from jax.experimental import pallas as pl
from jax.experimental.pallas import tpu as pltpu
from jax.sharding import PartitionSpec as P

BLK = 128
CAP = 3
CORES = 2
CHUNK_ROWS = (64, 64)
PARTS = 2
MIB = 2**20

adapter_scale = 0.5

LAST = (((1,), (1,)), ((), ()))


class Index:
    def __init__(self, ref, block_count, adapter_count, parts):
        self.ref = ref
        self.blocks, self.adapters, self.parts = block_count, adapter_count, parts
        self.chips = parts // CORES
        self.per_part = block_count // parts

    @staticmethod
    def pack(adapter_of_block, slot_of_block, tokens_per_adapter):
        place = jnp.stack([lax.axis_index("dp"), lax.axis_index("tensor")]).astype(jnp.int32)
        return jnp.concatenate([adapter_of_block, slot_of_block, tokens_per_adapter, place])

    def owner(self, block):
        return self.ref[block]

    def slot(self, block):
        return self.ref[self.blocks + block]

    def tokens(self, adapter):
        return self.ref[2 * self.blocks + adapter]

    @property
    def place(self):
        return self.ref[2 * self.blocks + self.adapters]

    @property
    def part(self):
        return self.ref[2 * self.blocks + self.adapters + 1]

    def block(self, core_bit, chip_bits, i):
        return (self.part ^ (chip_bits * CORES + core_bit)) * self.per_part + i

    def live_rows(self, block):
        adapter = self.owner(block)
        first = jnp.int32(0)
        for a in range(self.adapters):
            count = (self.tokens(a) + BLK - 1) // BLK
            first = first + jnp.where(a < adapter, count, 0)
        return self.tokens(adapter) - (block - first) * BLK


def whole(shape):
    return pl.BlockSpec(shape, lambda *_: (0,) * len(shape))


def shape_of(shape, dtype):
    return jax.ShapeDtypeStruct(shape, dtype)


def cost(flops, bytes_accessed):
    return pl.CostEstimate(flops=flops, bytes_accessed=bytes_accessed, transcendentals=0)


def own_copy(index, block, start, tokens_ref, out_ref, sem):
    at = pl.multiple_of(index.slot(block) * BLK + start, 16)
    return pltpu.make_async_copy(tokens_ref.at[pl.ds(at, out_ref.shape[0])], out_ref, sem)


def run_all(copies):
    for copy in copies:
        copy.start()
    for copy in copies:
        copy.wait()


def first_hop_kernel(index_of, start, index_ref, tokens_ref, *refs):
    a_ref, b_ref, sems = refs[-3:]
    index = index_of(index_ref)
    inward = jnp.where(index.place == 0, 2, 1)
    run_all(
        [
            own_copy(index, inward, start, tokens_ref, a_ref, sems.at[0]),
            own_copy(index, 0, start, tokens_ref, b_ref, sems.at[1]),
        ]
    )


def second_hop_kernel(index_of, start, index_ref, tokens_ref, a_ref, b_ref, *refs):
    x_ref, y_ref, sems = refs[-3:]
    index = index_of(index_ref)
    place = index.place
    outer = jnp.where(place == 0, 1, jnp.where(place == 1, 0, 2))
    middle = jnp.where(place == 1, 2, 1)
    run_all(
        [
            own_copy(index, outer, start, tokens_ref, x_ref, sems.at[0]),
            own_copy(index, middle, start, tokens_ref, y_ref, sems.at[1]),
        ]
    )

    @pl.when((place == 1) & (index.owner(0) != 1))
    def _():
        x_ref[...] = b_ref[...]

    @pl.when(((place == 1) | (place == 2)) & (index.owner(middle) != place))
    def _():
        y_ref[...] = a_ref[...]


def settle_kernel(index_of, start, index_ref, tokens_ref, x_ref, y_ref, *refs):
    out_ref, sems = refs[-2:]
    index = index_of(index_ref)
    place = index.place
    owner = index.owner(place)
    mine = owner == place
    edge = (place == 0) | ((place == 1) & (owner == 0)) | ((place == 2) & (owner == 3))
    run_all([own_copy(index, place, start, tokens_ref, out_ref, sems.at[0])])

    @pl.when(jnp.logical_not(mine) & edge)
    def _():
        out_ref[...] = x_ref[...]

    @pl.when(jnp.logical_not(mine | edge))
    def _():
        out_ref[...] = y_ref[...]


def after(values):
    specs = [
        pl.BlockSpec((1,) * (v.ndim - 2) + (16, 128), lambda *_, n=v.ndim: (0,) * n) for v in values
    ]
    return specs, list(values)


def hop_call(kernel, index, tokens, outs, received, waits, name):
    specs, extra = after(waits)
    return pl.pallas_call(
        kernel,
        grid_spec=pltpu.PrefetchScalarGridSpec(
            num_scalar_prefetch=1,
            grid=(1,),
            in_specs=[pl.BlockSpec(memory_space=pl.ANY)]
            + [whole(r.shape) for r in received]
            + specs,
            out_specs=[whole(o.shape) for o in outs],
            scratch_shapes=[pltpu.SemaphoreType.DMA((len(outs),))],
        ),
        out_shape=outs,
        cost_estimate=cost(0, 4 * sum(o.size for o in outs)),
        name=name,
    )(index, tokens, *received, *extra)


class Homing:
    def __init__(self, index_of, index, tokens, chunk):
        self.index_of, self.index, self.tokens = index_of, index, tokens
        self.start = sum(CHUNK_ROWS[:chunk])
        self.unit = shape_of((CHUNK_ROWS[chunk], tokens.shape[1]), tokens.dtype)

    def call(self, kernel, count, received, waits, name):
        return hop_call(
            functools.partial(kernel, self.index_of, self.start),
            self.index,
            self.tokens,
            [self.unit] * count,
            received,
            waits,
            name,
        )

    def first(self, waits=()):
        inward, left = self.call(first_hop_kernel, 2, (), waits, "first_hop")
        self.sent = inward
        self.received = (
            lax.ppermute(inward, "dp", [(3, 2), (0, 1)]),
            lax.ppermute(left, "dp", [(2, 1)]),
        )

    def second(self, waits=()):
        outer, middle = self.call(second_hop_kernel, 2, self.received, waits, "second_hop")
        self.sent = outer
        self.received = (
            lax.ppermute(outer, "dp", [(1, 0), (0, 1), (3, 2)]),
            lax.ppermute(middle, "dp", [(2, 1), (1, 2)]),
        )

    def settle(self, waits=()):
        (self.sent,) = self.call(settle_kernel, 1, self.received, waits, "settle")
        return self.sent


STREAMS = 4


def split_product_kernel(index_of, index_ref, x_ref, *refs):
    w_refs, (send_ref, other_ref, own_ref) = refs[:STREAMS], refs[-3:]
    index = index_of(index_ref)
    each = index.per_part * x_ref.shape[1]
    rows = [
        x_ref[index.block(core_bit, chip_bits, i)]
        for core_bit in (1, 0)
        for chip_bits in range(index.chips)
        for i in range(index.per_part)
    ]
    total = jnp.dot(
        jnp.concatenate(rows, axis=0),
        jnp.concatenate([w[...] for w in w_refs], axis=0),
        preferred_element_type=jnp.float32,
    )
    half = index.chips * each
    send_ref[...] = total[:half].astype(send_ref.dtype)
    own_ref[...] = total[half : half + each]
    other_ref[...] = total[half + each :]


def split_product(index_of, index, shape, rows, weight, part, part_count, waits):
    block_count, count, depth = rows.shape
    width = weight.shape[1] // part_count
    tile = 512
    each = shape.per_part * count
    half = block_count * count // 2
    specs, extra = after(waits)

    def columns(height):
        return pl.BlockSpec((height, tile), lambda n, _: (0, n))

    def stream(i):
        first = part * (width // tile)
        return pl.BlockSpec((depth // STREAMS, tile), lambda n, _: (i, first + n))

    return pl.pallas_call(
        functools.partial(split_product_kernel, index_of),
        grid_spec=pltpu.PrefetchScalarGridSpec(
            num_scalar_prefetch=1,
            grid=(width // tile,),
            in_specs=[whole(rows.shape)] + [stream(i) for i in range(STREAMS)] + specs,
            out_specs=[columns(half), columns(half - each), columns(each)],
        ),
        out_shape=[
            shape_of((half, width), jnp.bfloat16),
            shape_of((half - each, width), jnp.float32),
            shape_of((each, width), jnp.float32),
        ],
        compiler_params=pltpu.CompilerParams(vmem_limit_bytes=48 * MIB),
        cost_estimate=cost(
            4 * half * depth * width, 2 * depth * (2 * half + width) + 6 * half * width
        ),
        name="split_product",
    )(index, rows, *[weight] * STREAMS, *extra)


def narrow_kernel(index_of, index_ref, tokens_ref, down_ref, cot_ref, up_ref, *refs):
    send_ref, keep_ref, back_ref, low = refs[-4:]
    index = index_of(index_ref)
    for m in range(CAP):
        low[m] = lax.dot_general(
            down_ref[0],
            tokens_ref[m * BLK : (m + 1) * BLK],
            LAST,
            preferred_element_type=jnp.float32,
        )
    for core_bit, out_ref in ((1, send_ref), (0, keep_ref)):
        for chip_bits in range(index.chips):
            for i in range(index.per_part):
                block = index.block(core_bit, chip_bits, i)
                mine = index.owner(block) == index.place
                out_ref[chip_bits, i] = jnp.where(mine, low[index.slot(block)], 0.0)
    for i in range(index.per_part):
        adapter = index.owner(index.block(0, 0, i))
        back_ref[i] = lax.dot_general(
            up_ref[adapter],
            cot_ref[i * BLK : (i + 1) * BLK],
            LAST,
            preferred_element_type=jnp.float32,
        )


def narrow(index_of, index, shape, tokens, down, cotangent, up, waits):
    rank = up.shape[1]
    one = (shape.per_part, rank, BLK)
    outs = [(shape.chips,) + one, (shape.chips,) + one, one]
    operands = (tokens, down, cotangent, up)
    specs, extra = after(waits)
    return pl.pallas_call(
        functools.partial(narrow_kernel, index_of),
        grid_spec=pltpu.PrefetchScalarGridSpec(
            num_scalar_prefetch=1,
            grid=(1,),
            in_specs=[whole(o.shape) for o in operands] + specs,
            out_specs=[whole(o) for o in outs],
            scratch_shapes=[pltpu.VMEM((CAP, rank, BLK), jnp.float32)],
        ),
        out_shape=[shape_of(o, jnp.float32) for o in outs],
        compiler_params=pltpu.CompilerParams(vmem_limit_bytes=24 * MIB),
        cost_estimate=cost(2 * rank * (tokens.size + cotangent.size), 2 * sum(o.size for o in operands)),
        name="narrow",
    )(index, *operands, *extra)


def pieces_kernel(index_of, index_ref, sum_ref, more_ref, cot_ref, low_ref, back_ref, piece_ref):
    index = index_of(index_ref)
    for i in range(index.per_part):
        live = index.live_rows(index.block(0, 0, i))
        keep = lax.broadcasted_iota(jnp.int32, low_ref.shape[1:], 1) < live
        lowered = jnp.where(keep, sum_ref[0, i] + more_ref[0, i], 0.0).astype(low_ref.dtype)
        back = jnp.where(keep, sum_ref[1, i] + more_ref[1, i], 0.0)
        low_ref[i] = lowered
        back_ref[i] = back.astype(back_ref.dtype)
        piece_ref[i] = jnp.dot(
            lowered, cot_ref[i * BLK : (i + 1) * BLK], preferred_element_type=jnp.float32
        ).astype(piece_ref.dtype)


def make_pieces(index_of, index, shape, total, more, cotangent):
    _, per_part, rank, _ = total.shape
    width = cotangent.shape[1]
    outs = [(per_part, rank, BLK), (per_part, rank, BLK), (per_part, rank, width)]
    operands = (total, more, cotangent)
    return pl.pallas_call(
        functools.partial(pieces_kernel, index_of),
        grid_spec=pltpu.PrefetchScalarGridSpec(
            num_scalar_prefetch=1,
            grid=(1,),
            in_specs=[whole(o.shape) for o in operands],
            out_specs=[whole(o) for o in outs],
        ),
        out_shape=[shape_of(o, jnp.bfloat16) for o in outs],
        compiler_params=pltpu.CompilerParams(vmem_limit_bytes=24 * MIB),
        cost_estimate=cost(2 * rank * cotangent.size, 3 * cotangent.size),
        name="pieces",
    )(index, *operands)


def down_gradient_kernel(index_of, index_ref, tokens_ref, *refs):
    back_refs, out_ref = refs[:-1], refs[-1]
    index = index_of(index_ref)
    out_ref[...] = jnp.zeros_like(out_ref)
    for core_bit in range(CORES):
        for chip_bits in range(index.chips):
            for i in range(index.per_part):
                block = index.block(core_bit, chip_bits, i)
                back_ref = back_refs[core_bit * index.chips + chip_bits]

                @pl.when(index.owner(block) == index.place)
                def _(block=block, back_ref=back_ref, i=i):
                    at = pl.multiple_of(index.slot(block) * BLK, BLK)
                    out_ref[0] += adapter_scale * jnp.dot(
                        back_ref[i],
                        tokens_ref[pl.ds(at, BLK)],
                        preferred_element_type=jnp.float32,
                    )


def down_gradient(index_of, index, tokens, backs):
    out = (1, backs[0].shape[1], tokens.shape[1])
    operands = (tokens, *backs)
    return pl.pallas_call(
        functools.partial(down_gradient_kernel, index_of),
        grid_spec=pltpu.PrefetchScalarGridSpec(
            num_scalar_prefetch=1,
            grid=(1,),
            in_specs=[whole(o.shape) for o in operands],
            out_specs=whole(out),
        ),
        out_shape=shape_of(out, jnp.float32),
        compiler_params=pltpu.CompilerParams(vmem_limit_bytes=24 * MIB),
        cost_estimate=cost(2 * out[1] * tokens.size, 2 * tokens.size),
        name="down_gradient",
    )(index, *operands)


def up_gradient_kernel(index_of, index_ref, *refs):
    piece_refs, out_ref = refs[:-1], refs[-1]
    index = index_of(index_ref)

    def of_device(core_bit, chip_bits, adapter):
        total = None
        for i in range(index.per_part):
            mine = index.owner(index.block(core_bit, chip_bits, i)) == adapter
            piece = piece_refs[core_bit * index.chips + chip_bits][i].astype(jnp.float32)
            term = jnp.where(mine, piece, 0.0)
            total = term if total is None else total + term
        return total

    for adapter in range(index.adapters):
        level = [
            of_device(0, j, adapter) + of_device(1, j, adapter) for j in range(index.chips)
        ]
        while len(level) > 1:
            level = [level[j] + level[j + 1] for j in range(0, len(level), 2)]
        out_ref[adapter] = adapter_scale * level[0]


def up_gradient(index_of, index, adapter_count, pieces):
    per_part, rank, width = pieces[0].shape
    tile = 1024
    out = (adapter_count, rank, width)
    return pl.pallas_call(
        functools.partial(up_gradient_kernel, index_of),
        grid_spec=pltpu.PrefetchScalarGridSpec(
            num_scalar_prefetch=1,
            grid=(width // tile,),
            in_specs=[pl.BlockSpec((per_part, rank, tile), lambda n, _: (0, 0, n))] * len(pieces),
            out_specs=pl.BlockSpec((adapter_count, rank, tile), lambda n, _: (0, 0, n)),
        ),
        out_shape=shape_of(out, jnp.float32),
        compiler_params=pltpu.CompilerParams(vmem_limit_bytes=24 * MIB),
        cost_estimate=cost(0, 4 * adapter_count * rank * width + 2 * len(pieces) * pieces[0].size),
        name="up_gradient",
    )(index, *pieces)


def finish_kernel(index_of, counts, index_ref, low_ref, *refs):
    index = index_of(index_ref)
    up_refs, sum_refs, out_ref = refs[: index.per_part], refs[index.per_part : -1], refs[-1]
    per_chunk = len(sum_refs) // len(counts)
    for i in range(index.per_part):
        block = index.block(0, 0, i)
        live = index.live_rows(block)
        side = lax.dot_general(
            low_ref[i],
            up_refs[i][0],
            (((0,), (0,)), ((), ())),
            preferred_element_type=jnp.float32,
        )
        start = 0
        for c, count in enumerate(counts):
            total = adapter_scale * side[start : start + count]
            for ref in sum_refs[c * per_chunk : (c + 1) * per_chunk]:
                total = total + ref[i * count : (i + 1) * count].astype(jnp.float32)
            keep = start + lax.broadcasted_iota(jnp.int32, total.shape, 0) < live
            at = i * BLK + start
            out_ref[at : at + count] = jnp.where(keep, total, 0.0).astype(out_ref.dtype)
            start += count


def finish(index_of, index, lowered, up, sums, part, part_count, projected):
    per_part = lowered.shape[0]
    _, rank, width = up.shape
    tile = min(1024, width // part_count)
    tiles = width // part_count // tile
    first = part * tiles
    out = (per_part * BLK, width)

    def factor(i):
        def at(n, index_ref):
            index = index_of(index_ref)
            return (index.owner(index.block(0, 0, i)), 0, first + n)

        return pl.BlockSpec((1, rank, tile), at)

    specs, flat = [], []
    for chunk, count in zip(sums, CHUNK_ROWS):
        for value in chunk:
            begin = first if value.shape[1] == width else 0
            specs.append(
                pl.BlockSpec((per_part * count, tile), lambda n, _, begin=begin: (0, begin + n))
            )
            flat.append(value)
    kernel = functools.partial(finish_kernel, index_of, CHUNK_ROWS)
    operands = [index, lowered, *[up] * per_part, *flat]
    aliases = {}
    if projected is not None:
        aliases = {len(operands): 0}
        operands.append(projected)
        specs.append(pl.BlockSpec(memory_space=pl.ANY))

        def kernel(*refs):
            finish_kernel(index_of, CHUNK_ROWS, *refs[:-2], refs[-1])

    return pl.pallas_call(
        kernel,
        grid_spec=pltpu.PrefetchScalarGridSpec(
            num_scalar_prefetch=1,
            grid=(tiles,),
            in_specs=[whole(lowered.shape)] + [factor(i) for i in range(per_part)] + specs,
            out_specs=pl.BlockSpec((out[0], tile), lambda n, _: (0, first + n)),
        ),
        out_shape=shape_of(out, jnp.bfloat16),
        input_output_aliases=aliases,
        compiler_params=pltpu.CompilerParams(vmem_limit_bytes=24 * MIB),
        cost_estimate=cost(
            2 * rank * out[0] * tiles * tile, (10 * out[0] + 2 * rank) * tiles * tile
        ),
        name="finish",
    )(*operands)


def per_device(
    tokens,
    cotangent,
    frozen_up_weight,
    adapter_down_factor,
    adapter_up_factor,
    tokens_per_adapter,
    adapter_of_block,
    slot_of_block,
):
    owners = lax.axis_size("dp")
    parts = lax.axis_size("tensor")
    chips = parts // CORES
    block_count = adapter_of_block.shape[0]
    adapter_count = adapter_up_factor.shape[0]
    width_dev = tokens.shape[1]
    index_of = functools.partial(
        Index, block_count=block_count, adapter_count=adapter_count, parts=parts
    )
    shape = index_of(None)
    index = Index.pack(adapter_of_block, slot_of_block, tokens_per_adapter)

    def to_other_core(value):
        return lax.ppermute(value, "tensor", [(i, i ^ 1) for i in range(parts)])

    def to_chip(value, k):
        return lax.ppermute(value, "tensor", [(i, i ^ (k * CORES)) for i in range(parts)])

    def across_dp(value, k):
        return lax.ppermute(value, "dp", [(i, i ^ k) for i in range(owners)])

    def every_part(value):
        same_core = [value] + [to_chip(value, k) for k in range(1, chips)]
        return same_core + [to_other_core(v) for v in same_core]

    def small_products(waits):
        return narrow(
            index_of,
            index,
            shape,
            tokens,
            jnp.swapaxes(adapter_down_factor, 1, 2),
            cotangent,
            adapter_up_factor,
            waits,
        )

    def over_parts(send, keep):
        low_chip = keep + to_other_core(send)
        low_part = low_chip[0]
        for k in range(1, chips):
            low_part = low_part + to_chip(low_chip[k], k)
        return low_part

    def over_dp(low_part, back):
        total, k = jnp.stack([low_part, back]), 1
        while 2 * k < owners:
            total = total + across_dp(total, k)
            k *= 2
        return make_pieces(index_of, index, shape, total, across_dp(total, k), cotangent)

    if owners == 4 and block_count == 4:
        head = Homing(index_of, index, tokens, 0)
        tail = [Homing(index_of, index, tokens, c) for c in range(1, len(CHUNK_ROWS))]
        head.first()
        send, keep, back = small_products([head.sent])
        head.second([send])
        low_part = over_parts(send, keep)
        homes = [head.settle([low_part])]
        for homing in tail:
            homing.first([homes[-1]])
            homing.second()
            homes.append(homing.settle())
        lowered, back_rows, pieces = over_dp(low_part, back)
        chunks = [lax.all_gather(home, "dp", axis=0) for home in homes]
    else:
        send, keep, back = small_products([])
        lowered, back_rows, pieces = over_dp(over_parts(send, keep), back)
        every_slot = lax.all_gather(
            tokens.reshape(CAP, BLK, width_dev), "dp", axis=0, tiled=True
        )
        picked = every_slot[adapter_of_block * CAP + slot_of_block]
        starts = [sum(CHUNK_ROWS[:c]) for c in range(len(CHUNK_ROWS))]
        chunks = [picked[:, s : s + count] for s, count in zip(starts, CHUNK_ROWS)]

    def summed(rows, part, part_count, waits):
        each = shape.per_part * rows.shape[1]
        send, other, own = split_product(
            index_of, index, shape, rows, frozen_up_weight, part, part_count, waits
        )
        arrived = to_other_core(send)
        outgoing = (other + arrived[each:].astype(jnp.float32)).astype(jnp.bfloat16)
        return [own, arrived] + [
            to_chip(outgoing[(k - 1) * each : k * each], k) for k in range(1, chips)
        ]

    sums = [summed(rows, 0, 1, [pieces]) for rows in chunks[:-1]]
    up_grad = up_gradient(index_of, index, adapter_count, every_part(pieces))
    down_grad = down_gradient(index_of, index, tokens, every_part(back_rows))
    waits = [up_grad, down_grad] + [chunk[-1] for chunk in sums]
    last = []
    for part in range(PARTS):
        last.append(summed(chunks[-1], part, PARTS, waits))
        waits = []
    projected = None
    for part in range(PARTS):
        projected = finish(
            index_of,
            index,
            lowered,
            adapter_up_factor,
            sums + [last[part]],
            part,
            PARTS,
            projected,
        )
    return (projected, jnp.swapaxes(down_grad, 1, 2), up_grad)


def solution(mesh):
    return jax.shard_map(
        per_device,
        mesh=mesh,
        in_specs=(
            P(("groups", "dp"), "tensor"),
            P(("groups", "tensor"), "dp"),
            P("tensor", "dp"),
            P(("groups", "dp"), "tensor", None),
            P("groups", None, "dp"),
            P("groups"),
            P("groups"),
            P("groups"),
        ),
        out_specs=(
            P(("groups", "tensor"), "dp"),
            P(("groups", "dp"), "tensor", None),
            P("groups", None, "dp"),
        ),
        check_vma=False,
    )
```

```python
import functools

import jax
import jax.numpy as jnp
from jax import lax
from jax.experimental import pallas as pl
from jax.experimental.pallas import tpu as pltpu
from jax.sharding import PartitionSpec as P

BLK = 128
CAP = 3
CORES = 2
CHUNK_ROWS = (64, 64)
PARTS = 4
SMALL = pltpu.CompilerParams(vmem_limit_bytes=12 * 2**20)

adapter_scale = 0.5

LAST = (((1,), (1,)), ((), ()))


class Index:
    def __init__(self, ref, block_count, adapter_count, parts):
        self.ref = ref
        self.blocks, self.adapters, self.parts = block_count, adapter_count, parts
        self.chips = parts // CORES
        self.per_part = block_count // parts

    @staticmethod
    def pack(adapter_of_block, slot_of_block, tokens_per_adapter):
        place = jnp.stack([lax.axis_index("dp"), lax.axis_index("tensor")]).astype(jnp.int32)
        return jnp.concatenate([adapter_of_block, slot_of_block, tokens_per_adapter, place])

    def owner(self, block):
        return self.ref[block]

    def slot(self, block):
        return self.ref[self.blocks + block]

    def tokens(self, adapter):
        return self.ref[2 * self.blocks + adapter]

    @property
    def place(self):
        return self.ref[2 * self.blocks + self.adapters]

    @property
    def part(self):
        return self.ref[2 * self.blocks + self.adapters + 1]

    def block(self, core_bit, chip_bits, i):
        return (self.part ^ (chip_bits * CORES + core_bit)) * self.per_part + i

    def live_rows(self, block):
        adapter = self.owner(block)
        first = jnp.int32(0)
        for a in range(self.adapters):
            count = (self.tokens(a) + BLK - 1) // BLK
            first = first + jnp.where(a < adapter, count, 0)
        return self.tokens(adapter) - (block - first) * BLK


def in_vmem(value):
    return pltpu.with_memory_space_constraint(value, pltpu.VMEM)


def in_hbm(value):
    return pltpu.with_memory_space_constraint(value, pltpu.HBM)


def held():
    return pl.BlockSpec(memory_space=pltpu.VMEM)


def whole(shape):
    return pl.BlockSpec(shape, lambda *_: (0,) * len(shape))


def shape_of(shape, dtype):
    return jax.ShapeDtypeStruct(shape, dtype)


BRIEF = pl.CostEstimate(flops=1, bytes_accessed=1, transcendentals=0)


def own_rows(index, block, start, tokens_ref, out_ref):
    at = pl.multiple_of(index.slot(block) * BLK + start, 16)
    out_ref[...] = tokens_ref[pl.ds(at, out_ref.shape[0])]


def first_hop_kernel(index_of, start, index_ref, tokens_ref, *refs):
    a_ref, b_ref = refs[-2:]
    index = index_of(index_ref)
    own_rows(index, jnp.where(index.place == 0, 2, 1), start, tokens_ref, a_ref)
    own_rows(index, 0, start, tokens_ref, b_ref)


def second_hop_kernel(index_of, start, index_ref, tokens_ref, a_ref, b_ref, *refs):
    x_ref, y_ref = refs[-2:]
    index = index_of(index_ref)
    place = index.place
    outer = jnp.where(place == 0, 1, jnp.where(place == 1, 0, 2))
    middle = jnp.where(place == 1, 2, 1)
    own_rows(index, outer, start, tokens_ref, x_ref)
    own_rows(index, middle, start, tokens_ref, y_ref)

    @pl.when((place == 1) & (index.owner(0) != 1))
    def _():
        x_ref[...] = b_ref[...]

    @pl.when(((place == 1) | (place == 2)) & (index.owner(middle) != place))
    def _():
        y_ref[...] = a_ref[...]


def settle_kernel(index_of, start, index_ref, tokens_ref, x_ref, y_ref, *refs):
    out_ref = refs[-1]
    index = index_of(index_ref)
    place = index.place
    owner = index.owner(place)
    mine = owner == place
    edge = (place == 0) | ((place == 1) & (owner == 0)) | ((place == 2) & (owner == 3))
    own_rows(index, place, start, tokens_ref, out_ref)

    @pl.when(jnp.logical_not(mine) & edge)
    def _():
        out_ref[...] = x_ref[...]

    @pl.when(jnp.logical_not(mine | edge))
    def _():
        out_ref[...] = y_ref[...]


def after(values, far=()):
    specs = [
        pl.BlockSpec((1,) * (v.ndim - 2) + (16, 128), lambda *_, n=v.ndim: (0,) * n) for v in values
    ] + [pl.BlockSpec(memory_space=pl.ANY)] * len(far)
    return specs, [*values, *(in_hbm(v) for v in far)]


def hop_call(kernel, index, tokens, unit, count, stay, received, waits, name):
    specs, extra = after((), waits) if waits and waits[0].shape == unit.shape else after(waits)
    out = pltpu.VMEM(unit.shape, unit.dtype) if stay else unit
    return pl.pallas_call(
        kernel,
        grid_spec=pltpu.PrefetchScalarGridSpec(
            num_scalar_prefetch=1,
            grid=(1,),
            in_specs=[held()] * (1 + len(received)) + specs,
            out_specs=[held() if stay else whole(unit.shape)] * count,
        ),
        out_shape=[out] * count,
        compiler_params=SMALL,
        cost_estimate=BRIEF,
        name=name,
    )(index, tokens, *[in_vmem(r) for r in received], *extra)


class Homing:
    def __init__(self, index_of, index, tokens, chunk):
        self.index_of, self.index, self.tokens = index_of, index, tokens
        self.start = sum(CHUNK_ROWS[:chunk])
        self.unit = shape_of((CHUNK_ROWS[chunk], tokens.shape[1]), tokens.dtype)

    def call(self, kernel, count, stay, received, waits, name):
        return hop_call(
            functools.partial(kernel, self.index_of, self.start),
            self.index,
            self.tokens,
            self.unit,
            count,
            stay,
            received,
            waits,
            name,
        )

    def first(self, waits=()):
        inward, left = self.call(first_hop_kernel, 2, True, (), waits, "first_hop")
        self.sent = inward
        self.received = (
            lax.ppermute(inward, "dp", [(3, 2), (0, 1)]),
            lax.ppermute(left, "dp", [(2, 1)]),
        )

    def second(self, waits=()):
        outer, middle = self.call(second_hop_kernel, 2, True, self.received, waits, "second_hop")
        self.sent = outer
        self.received = (
            lax.ppermute(outer, "dp", [(1, 0), (0, 1), (3, 2)]),
            lax.ppermute(middle, "dp", [(2, 1), (1, 2)]),
        )

    def settle(self, waits=()):
        (self.sent,) = self.call(settle_kernel, 1, False, self.received, waits, "settle")
        return self.sent


def split_product_kernel(index_of, tile, index_ref, x_ref, w_ref, *refs):
    send_ref, other_ref, own_ref, sent = refs[-4:]
    index = index_of(index_ref)
    step = pl.program_id(0)
    each = index.per_part * x_ref.shape[1]
    half = index.chips * each
    rows = jnp.concatenate(
        [
            x_ref[index.block(core_bit, chip_bits, i)]
            for core_bit in (1, 0)
            for chip_bits in range(index.chips)
            for i in range(index.per_part)
        ],
        axis=0,
    )
    for n in range(w_ref.shape[1] // tile):
        columns = slice(n * tile, (n + 1) * tile)
        total = jnp.dot(rows, w_ref[:, columns], preferred_element_type=jnp.float32)
        parts = (
            (sent, total[:half]),
            (own_ref, total[half : half + each]),
            (other_ref, total[half + each :]),
        )

        @pl.when(step == 0)
        def _():
            for ref, value in parts:
                ref[:, columns] = value

        @pl.when(step > 0)
        def _():
            for ref, value in parts:
                ref[:, columns] += value

    @pl.when(step == pl.num_programs(0) - 1)
    def _():
        send_ref[...] = sent[...].astype(send_ref.dtype)


def split_product(index_of, index, shape, rows, weight, part, part_count, waits, far):
    block_count, count, depth = rows.shape
    width = weight.shape[1] // part_count
    deep = min(512, depth)
    each = shape.per_part * count
    half = block_count * count // 2
    specs, extra = after(waits, far)
    return pl.pallas_call(
        functools.partial(split_product_kernel, index_of, min(512, width)),
        grid_spec=pltpu.PrefetchScalarGridSpec(
            num_scalar_prefetch=1,
            grid=(depth // deep,),
            in_specs=[
                pl.BlockSpec((block_count, count, deep), lambda k, _: (0, 0, k)),
                pl.BlockSpec((deep, width), lambda k, _: (k, part)),
            ]
            + specs,
            out_specs=[whole((half, width)), whole((half - each, width)), whole((each, width))],
            scratch_shapes=[pltpu.VMEM((half, width), jnp.float32)],
        ),
        out_shape=[
            shape_of((half, width), jnp.bfloat16),
            shape_of((half - each, width), jnp.float32),
            shape_of((each, width), jnp.float32),
        ],
        compiler_params=pltpu.CompilerParams(vmem_limit_bytes=32 * 2**20),
        cost_estimate=BRIEF,
        name="split_product",
    )(index, in_hbm(rows), in_hbm(weight), *extra)


def narrow_kernel(index_of, index_ref, tokens_ref, down_ref, cot_ref, up_ref, *refs):
    send_ref, keep_ref, back_ref, low = refs[-4:]
    index = index_of(index_ref)
    for m in range(CAP):
        low[m] = lax.dot_general(
            down_ref[0],
            tokens_ref[m * BLK : (m + 1) * BLK],
            LAST,
            preferred_element_type=jnp.float32,
        )
    for core_bit, out_ref in ((1, send_ref), (0, keep_ref)):
        for chip_bits in range(index.chips):
            for i in range(index.per_part):
                block = index.block(core_bit, chip_bits, i)
                mine = index.owner(block) == index.place
                out_ref[chip_bits, i] = jnp.where(mine, low[index.slot(block)], 0.0)
    for i in range(index.per_part):
        adapter = index.owner(index.block(0, 0, i))
        back_ref[i] = lax.dot_general(
            up_ref[adapter],
            cot_ref[i * BLK : (i + 1) * BLK],
            LAST,
            preferred_element_type=jnp.float32,
        )


def narrow(index_of, index, shape, tokens, down, cotangent, up, waits):
    rank = up.shape[1]
    one = (shape.per_part, rank, BLK)
    outs = [(shape.chips,) + one, (shape.chips,) + one, one]
    operands = (tokens, down, cotangent, up)
    specs, extra = after(waits)
    return pl.pallas_call(
        functools.partial(narrow_kernel, index_of),
        grid_spec=pltpu.PrefetchScalarGridSpec(
            num_scalar_prefetch=1,
            grid=(1,),
            in_specs=[held()] + [whole(o.shape) for o in operands[1:]] + specs,
            out_specs=[whole(o) for o in outs],
            scratch_shapes=[pltpu.VMEM((CAP, rank, BLK), jnp.float32)],
        ),
        out_shape=[shape_of(o, jnp.float32) for o in outs],
        compiler_params=SMALL,
        cost_estimate=BRIEF,
        name="narrow",
    )(index, *operands, *extra)


def merge_kernel(keep_ref, arrived_ref, back_ref, *refs):
    out_ref = refs[-1]
    total = keep_ref[0] + arrived_ref[0]
    for ref in refs[:-1][: keep_ref.shape[0] - 1]:
        total = total + ref[...]
    out_ref[0] = total
    out_ref[1] = back_ref[...]


def merge(keep, arrived, back, others, waits):
    specs, extra = after(waits)
    operands = (keep, arrived, back, *others)
    out = (2,) + back.shape
    return pl.pallas_call(
        merge_kernel,
        grid=(1,),
        in_specs=[whole(o.shape) for o in operands] + specs,
        out_specs=whole(out),
        out_shape=shape_of(out, jnp.float32),
        compiler_params=SMALL,
        cost_estimate=BRIEF,
        name="merge",
    )(*operands, *extra)


def pieces_kernel(index_of, index_ref, sum_ref, more_ref, cot_ref, low_ref, back_ref, piece_ref):
    index = index_of(index_ref)
    for i in range(index.per_part):
        live = index.live_rows(index.block(0, 0, i))
        keep = lax.broadcasted_iota(jnp.int32, low_ref.shape[1:], 1) < live
        lowered = jnp.where(keep, sum_ref[0, i] + more_ref[0, i], 0.0).astype(low_ref.dtype)
        back = jnp.where(keep, sum_ref[1, i] + more_ref[1, i], 0.0)
        low_ref[i] = lowered
        back_ref[i] = back.astype(back_ref.dtype)
        piece_ref[i] = jnp.dot(
            lowered, cot_ref[i * BLK : (i + 1) * BLK], preferred_element_type=jnp.float32
        ).astype(piece_ref.dtype)


def make_pieces(index_of, index, shape, total, more, cotangent):
    _, per_part, rank, _ = total.shape
    width = cotangent.shape[1]
    outs = [(per_part, rank, BLK), (per_part, rank, BLK), (per_part, rank, width)]
    operands = (total, more, cotangent)
    return pl.pallas_call(
        functools.partial(pieces_kernel, index_of),
        grid_spec=pltpu.PrefetchScalarGridSpec(
            num_scalar_prefetch=1,
            grid=(1,),
            in_specs=[whole(o.shape) for o in operands],
            out_specs=[whole(o) for o in outs],
        ),
        out_shape=[shape_of(o, jnp.bfloat16) for o in outs],
        compiler_params=SMALL,
        cost_estimate=BRIEF,
        name="pieces",
    )(index, *operands)


def down_gradient_kernel(index_of, index_ref, tokens_ref, *refs):
    back_refs, out_ref = refs[:-1], refs[-1]
    index = index_of(index_ref)
    out_ref[...] = jnp.zeros_like(out_ref)
    for core_bit in range(CORES):
        for chip_bits in range(index.chips):
            for i in range(index.per_part):
                block = index.block(core_bit, chip_bits, i)
                back_ref = back_refs[core_bit * index.chips + chip_bits]

                @pl.when(index.owner(block) == index.place)
                def _(block=block, back_ref=back_ref, i=i):
                    at = pl.multiple_of(index.slot(block) * BLK, BLK)
                    out_ref[0] += adapter_scale * jnp.dot(
                        back_ref[i],
                        tokens_ref[pl.ds(at, BLK)],
                        preferred_element_type=jnp.float32,
                    )


def down_gradient(index_of, index, tokens, backs):
    out = (1, backs[0].shape[1], tokens.shape[1])
    operands = (tokens, *backs)
    return pl.pallas_call(
        functools.partial(down_gradient_kernel, index_of),
        grid_spec=pltpu.PrefetchScalarGridSpec(
            num_scalar_prefetch=1,
            grid=(1,),
            in_specs=[held()] + [whole(o.shape) for o in backs],
            out_specs=whole(out),
        ),
        out_shape=shape_of(out, jnp.float32),
        compiler_params=SMALL,
        cost_estimate=BRIEF,
        name="down_gradient",
    )(index, *operands)


def up_gradient_kernel(index_of, index_ref, *refs):
    piece_refs, out_ref = refs[:-1], refs[-1]
    index = index_of(index_ref)

    def of_device(core_bit, chip_bits, adapter):
        total = None
        for i in range(index.per_part):
            mine = index.owner(index.block(core_bit, chip_bits, i)) == adapter
            piece = piece_refs[core_bit * index.chips + chip_bits][i].astype(jnp.float32)
            term = jnp.where(mine, piece, 0.0)
            total = term if total is None else total + term
        return total

    for adapter in range(index.adapters):
        level = [
            of_device(0, j, adapter) + of_device(1, j, adapter) for j in range(index.chips)
        ]
        while len(level) > 1:
            level = [level[j] + level[j + 1] for j in range(0, len(level), 2)]
        out_ref[adapter] = adapter_scale * level[0]


def up_gradient(index_of, index, adapter_count, pieces):
    per_part, rank, width = pieces[0].shape
    tile = 1024
    out = (adapter_count, rank, width)
    return pl.pallas_call(
        functools.partial(up_gradient_kernel, index_of),
        grid_spec=pltpu.PrefetchScalarGridSpec(
            num_scalar_prefetch=1,
            grid=(width // tile,),
            in_specs=[pl.BlockSpec((per_part, rank, tile), lambda n, _: (0, 0, n))] * len(pieces),
            out_specs=pl.BlockSpec((adapter_count, rank, tile), lambda n, _: (0, 0, n)),
        ),
        out_shape=shape_of(out, jnp.float32),
        compiler_params=SMALL,
        cost_estimate=BRIEF,
        name="up_gradient",
    )(index, *pieces)


def finish_kernel(index_of, counts, index_ref, low_ref, *refs):
    index = index_of(index_ref)
    up_refs, sum_refs, out_ref = refs[: index.per_part], refs[index.per_part : -1], refs[-1]
    per_chunk = len(sum_refs) // len(counts)
    for i in range(index.per_part):
        block = index.block(0, 0, i)
        live = index.live_rows(block)
        side = lax.dot_general(
            low_ref[i],
            up_refs[i][0],
            (((0,), (0,)), ((), ())),
            preferred_element_type=jnp.float32,
        )
        start = 0
        for c, count in enumerate(counts):
            total = adapter_scale * side[start : start + count]
            for ref in sum_refs[c * per_chunk : (c + 1) * per_chunk]:
                total = total + ref[i * count : (i + 1) * count].astype(jnp.float32)
            keep = start + lax.broadcasted_iota(jnp.int32, total.shape, 0) < live
            at = i * BLK + start
            out_ref[at : at + count] = jnp.where(keep, total, 0.0).astype(out_ref.dtype)
            start += count


def finish(index_of, index, lowered, up, sums, part, part_count, projected, far):
    per_part = lowered.shape[0]
    _, rank, width = up.shape
    tile = min(1024, width // part_count)
    tiles = width // part_count // tile
    first = part * tiles
    out = (per_part * BLK, width)

    def factor(i):
        def at(n, index_ref):
            index = index_of(index_ref)
            return (index.owner(index.block(0, 0, i)), 0, first + n)

        return pl.BlockSpec((1, rank, tile), at)

    specs, flat = [], []
    for chunk, count in zip(sums, CHUNK_ROWS):
        for value in chunk:
            begin = first if value.shape[1] == width else 0
            specs.append(
                pl.BlockSpec((per_part * count, tile), lambda n, _, begin=begin: (0, begin + n))
            )
            flat.append(value)
    operands = [index, lowered, *[up] * per_part, *flat]
    aliases = {}
    if projected is not None:
        aliases = {len(operands): 0}
        far = [projected]
    more, extra = after((), far)
    if projected is not None:
        extra = [projected]

    def kernel(*refs):
        finish_kernel(index_of, CHUNK_ROWS, *refs[: len(operands)], refs[-1])

    return pl.pallas_call(
        kernel,
        grid_spec=pltpu.PrefetchScalarGridSpec(
            num_scalar_prefetch=1,
            grid=(tiles,),
            in_specs=[whole(lowered.shape)] + [factor(i) for i in range(per_part)] + specs + more,
            out_specs=pl.BlockSpec((out[0], tile), lambda n, _: (0, first + n)),
        ),
        out_shape=shape_of(out, jnp.bfloat16),
        input_output_aliases=aliases,
        compiler_params=SMALL,
        cost_estimate=BRIEF,
        name="finish",
    )(*operands, *extra)


def per_device(
    tokens,
    cotangent,
    frozen_up_weight,
    adapter_down_factor,
    adapter_up_factor,
    tokens_per_adapter,
    adapter_of_block,
    slot_of_block,
):
    owners = lax.axis_size("dp")
    parts = lax.axis_size("tensor")
    chips = parts // CORES
    block_count = adapter_of_block.shape[0]
    adapter_count = adapter_up_factor.shape[0]
    width_dev = tokens.shape[1]
    index_of = functools.partial(
        Index, block_count=block_count, adapter_count=adapter_count, parts=parts
    )
    shape = index_of(None)
    index = Index.pack(adapter_of_block, slot_of_block, tokens_per_adapter)

    def to_other_core(value):
        return lax.ppermute(value, "tensor", [(i, i ^ 1) for i in range(parts)])

    def to_chip(value, k):
        return lax.ppermute(value, "tensor", [(i, i ^ (k * CORES)) for i in range(parts)])

    def across_dp(value, k):
        return lax.ppermute(value, "dp", [(i, i ^ k) for i in range(owners)])

    def every_part(value):
        same_core = [value] + [to_chip(value, k) for k in range(1, chips)]
        return same_core + [to_other_core(v) for v in same_core]

    rows_here = in_vmem(tokens)

    def small_products(waits):
        return narrow(
            index_of,
            index,
            shape,
            rows_here,
            jnp.swapaxes(adapter_down_factor, 1, 2),
            cotangent,
            adapter_up_factor,
            waits,
        )

    def over_parts(send, keep):
        arrived = to_other_core(send)
        return arrived, [to_chip(keep[k] + arrived[k], k) for k in range(1, chips)]

    def over_dp(total):
        k = 1
        while 2 * k < owners:
            total = total + across_dp(total, k)
            k *= 2
        return make_pieces(index_of, index, shape, total, across_dp(total, k), cotangent)

    if owners == 4 and block_count == 4:
        head = Homing(index_of, index, rows_here, 0)
        tail = [Homing(index_of, index, rows_here, c) for c in range(1, len(CHUNK_ROWS))]
        head.first()
        send, keep, back = small_products([head.sent])
        head.second([send])
        arrived, others = over_parts(send, keep)
        homes = [head.settle(others)]
        tail[0].first([homes[-1]])
        total = merge(keep, arrived, back, others, [tail[0].sent])
        tail[0].second()
        homes.append(tail[0].settle())
        for homing in tail[1:]:
            homing.first([homes[-1]])
            homing.second()
            homes.append(homing.settle())
        lowered, back_rows, pieces = over_dp(total)
        chunks = [lax.all_gather(home, "dp", axis=0) for home in homes]
    else:
        send, keep, back = small_products([])
        arrived, others = over_parts(send, keep)
        lowered, back_rows, pieces = over_dp(merge(keep, arrived, back, others, []))
        homes = []
        every_slot = lax.all_gather(
            tokens.reshape(CAP, BLK, width_dev), "dp", axis=0, tiled=True
        )
        picked = every_slot[adapter_of_block * CAP + slot_of_block]
        starts = [sum(CHUNK_ROWS[:c]) for c in range(len(CHUNK_ROWS))]
        chunks = [picked[:, s : s + count] for s, count in zip(starts, CHUNK_ROWS)]

    pieces_same_core = [pieces] + [to_chip(pieces, k) for k in range(1, chips)]

    def summed(rows, part, waits, far):
        each = shape.per_part * rows.shape[1]
        send, other, own = split_product(
            index_of, index, shape, rows, frozen_up_weight, part, PARTS, waits, far
        )
        arrived = to_other_core(send)
        outgoing = (other + arrived[each:].astype(jnp.float32)).astype(jnp.bfloat16)
        return [own, arrived] + [
            to_chip(outgoing[(k - 1) * each : k * each], k) for k in range(1, chips)
        ]

    waits, far = pieces_same_core[1:], homes[1:]
    sums = [[] for _ in range(PARTS)]
    for rows in chunks:
        for part in range(PARTS):
            sums[part].append(summed(rows, part, waits, far))
            waits, far = [], []
        waits = [v for part in sums for v in part[-1][2:]]
    pieces_all = pieces_same_core + [to_other_core(p) for p in pieces_same_core]
    up_grad = up_gradient(index_of, index, adapter_count, pieces_all)
    down_grad = down_gradient(index_of, index, rows_here, every_part(back_rows))
    projected = None
    for part in range(PARTS):
        projected = finish(
            index_of,
            index,
            lowered,
            adapter_up_factor,
            sums[part],
            part,
            PARTS,
            projected,
            [up_grad, down_grad],
        )
    return (projected, jnp.swapaxes(down_grad, 1, 2), up_grad)


def solution(mesh):
    return jax.shard_map(
        per_device,
        mesh=mesh,
        in_specs=(
            P(("groups", "dp"), "tensor"),
            P(("groups", "tensor"), "dp"),
            P("tensor", "dp"),
            P(("groups", "dp"), "tensor", None),
            P("groups", None, "dp"),
            P("groups"),
            P("groups"),
            P("groups"),
        ),
        out_specs=(
            P(("groups", "tensor"), "dp"),
            P(("groups", "dp"), "tensor", None),
            P("groups", None, "dp"),
        ),
        check_vma=False,
    )
```

```python
import functools

import jax
import jax.numpy as jnp
from jax import lax
from jax.experimental import pallas as pl
from jax.experimental.pallas import tpu as pltpu
from jax.sharding import PartitionSpec as P

BLK = 128
CAP = 3
CORES = 2
CHUNK_ROWS = (64, 64)
PARTS = (4, 2)
SMALL = pltpu.CompilerParams(vmem_limit_bytes=12 * 2**20)

adapter_scale = 0.5

LAST = (((1,), (1,)), ((), ()))


class Index:
    def __init__(self, ref, block_count, adapter_count, parts):
        self.ref = ref
        self.blocks, self.adapters, self.parts = block_count, adapter_count, parts
        self.chips = parts // CORES
        self.per_part = block_count // parts

    @staticmethod
    def pack(adapter_of_block, slot_of_block, tokens_per_adapter):
        place = jnp.stack([lax.axis_index("dp"), lax.axis_index("tensor")]).astype(jnp.int32)
        return jnp.concatenate([adapter_of_block, slot_of_block, tokens_per_adapter, place])

    def owner(self, block):
        return self.ref[block]

    def slot(self, block):
        return self.ref[self.blocks + block]

    def tokens(self, adapter):
        return self.ref[2 * self.blocks + adapter]

    @property
    def place(self):
        return self.ref[2 * self.blocks + self.adapters]

    @property
    def part(self):
        return self.ref[2 * self.blocks + self.adapters + 1]

    def block(self, core_bit, chip_bits, i):
        return (self.part ^ (chip_bits * CORES + core_bit)) * self.per_part + i

    def live_rows(self, block):
        adapter = self.owner(block)
        first = jnp.int32(0)
        for a in range(self.adapters):
            count = (self.tokens(a) + BLK - 1) // BLK
            first = first + jnp.where(a < adapter, count, 0)
        return self.tokens(adapter) - (block - first) * BLK


def in_vmem(value):
    return pltpu.with_memory_space_constraint(value, pltpu.VMEM)


def in_hbm(value):
    return pltpu.with_memory_space_constraint(value, pltpu.HBM)


def held():
    return pl.BlockSpec(memory_space=pltpu.VMEM)


def whole(shape):
    return pl.BlockSpec(shape, lambda *_: (0,) * len(shape))


def shape_of(shape, dtype):
    return jax.ShapeDtypeStruct(shape, dtype)


BRIEF = pl.CostEstimate(flops=1, bytes_accessed=1, transcendentals=0)


def own_rows(index, block, start, tokens_ref, out_ref):
    at = pl.multiple_of(index.slot(block) * BLK + start, 16)
    out_ref[...] = tokens_ref[pl.ds(at, out_ref.shape[0])]


def first_hop_kernel(index_of, start, index_ref, tokens_ref, *refs):
    a_ref, b_ref = refs[-2:]
    index = index_of(index_ref)
    own_rows(index, jnp.where(index.place == 0, 2, 1), start, tokens_ref, a_ref)
    own_rows(index, 0, start, tokens_ref, b_ref)


def second_hop_kernel(index_of, start, index_ref, tokens_ref, a_ref, b_ref, *refs):
    x_ref, y_ref = refs[-2:]
    index = index_of(index_ref)
    place = index.place
    outer = jnp.where(place == 0, 1, jnp.where(place == 1, 0, 2))
    middle = jnp.where(place == 1, 2, 1)
    own_rows(index, outer, start, tokens_ref, x_ref)
    own_rows(index, middle, start, tokens_ref, y_ref)

    @pl.when((place == 1) & (index.owner(0) != 1))
    def _():
        x_ref[...] = b_ref[...]

    @pl.when(((place == 1) | (place == 2)) & (index.owner(middle) != place))
    def _():
        y_ref[...] = a_ref[...]


def settle_kernel(index_of, start, index_ref, tokens_ref, x_ref, y_ref, *refs):
    out_ref = refs[-1]
    index = index_of(index_ref)
    place = index.place
    owner = index.owner(place)
    mine = owner == place
    edge = (place == 0) | ((place == 1) & (owner == 0)) | ((place == 2) & (owner == 3))
    own_rows(index, place, start, tokens_ref, out_ref)

    @pl.when(jnp.logical_not(mine) & edge)
    def _():
        out_ref[...] = x_ref[...]

    @pl.when(jnp.logical_not(mine | edge))
    def _():
        out_ref[...] = y_ref[...]


def after(values, far=()):
    specs = [
        pl.BlockSpec((1,) * (v.ndim - 2) + (16, 128), lambda *_, n=v.ndim: (0,) * n) for v in values
    ] + [pl.BlockSpec(memory_space=pl.ANY)] * len(far)
    return specs, [*values, *(in_hbm(v) for v in far)]


def hop_call(kernel, index, tokens, unit, count, stay, received, waits, name, declared):
    specs, extra = after((), waits) if waits and waits[0].shape == unit.shape else after(waits)
    out = pltpu.VMEM(unit.shape, unit.dtype) if stay else unit
    return pl.pallas_call(
        kernel,
        grid_spec=pltpu.PrefetchScalarGridSpec(
            num_scalar_prefetch=1,
            grid=(1,),
            in_specs=[held()] * (1 + len(received)) + specs,
            out_specs=[held() if stay else whole(unit.shape)] * count,
        ),
        out_shape=[out] * count,
        compiler_params=SMALL,
        cost_estimate=declared,
        name=name,
    )(index, tokens, *[in_vmem(r) for r in received], *extra)


class Homing:
    def __init__(self, index_of, index, tokens, chunk):
        self.index_of, self.index, self.tokens = index_of, index, tokens
        self.start = sum(CHUNK_ROWS[:chunk])
        self.unit = shape_of((CHUNK_ROWS[chunk], tokens.shape[1]), tokens.dtype)

    def call(self, kernel, count, stay, received, waits, name, declared=BRIEF):
        return hop_call(
            functools.partial(kernel, self.index_of, self.start),
            self.index,
            self.tokens,
            self.unit,
            count,
            stay,
            received,
            waits,
            name,
            declared,
        )

    def first(self, waits=()):
        inward, left = self.call(first_hop_kernel, 2, True, (), waits, "first_hop")
        self.sent = inward
        self.received = (
            lax.ppermute(inward, "dp", [(3, 2), (0, 1)]),
            lax.ppermute(left, "dp", [(2, 1)]),
        )

    def second(self, waits=()):
        outer, middle = self.call(second_hop_kernel, 2, True, self.received, waits, "second_hop")
        self.sent = outer
        self.received = (
            lax.ppermute(outer, "dp", [(1, 0), (0, 1), (3, 2)]),
            lax.ppermute(middle, "dp", [(2, 1), (1, 2)]),
        )

    def settle(self, waits=(), declared=BRIEF):
        (self.sent,) = self.call(
            settle_kernel, 1, False, self.received, waits, "settle", declared
        )
        return self.sent


def split_product_kernel(index_of, first, index_ref, x_ref, w_ref, *refs):
    send_ref, other_ref, own_ref, rows, tiles, rows_sems, tile_sems = refs[-7:]
    index = index_of(index_ref)
    count, tile = x_ref.shape[1], tiles.shape[2]
    each = index.per_part * count
    half = index.chips * each
    buffers, steps = tiles.shape[0], own_ref.shape[1] // tile

    def weight_copy(n):
        return pltpu.make_async_copy(
            w_ref.at[:, pl.ds(first + n * tile, tile)],
            tiles.at[n % buffers],
            tile_sems.at[n % buffers],
        )

    order = [
        index.block(core_bit, chip_bits, i)
        for core_bit in (1, 0)
        for chip_bits in range(index.chips)
        for i in range(index.per_part)
    ]
    row_copies = [
        pltpu.make_async_copy(
            x_ref.at[block], rows.at[pl.ds(j * count, count)], rows_sems.at[j]
        )
        for j, block in enumerate(order)
    ]
    weight_copy(0).start()
    for copy in row_copies:
        copy.start()
    for n in range(1, min(buffers, steps)):
        weight_copy(n).start()
    for copy in row_copies:
        copy.wait()
    for n in range(steps):
        weight_copy(n).wait()
        total = jnp.dot(rows[...], tiles[n % buffers], preferred_element_type=jnp.float32)
        columns = slice(n * tile, (n + 1) * tile)
        send_ref[:, columns] = total[:half].astype(send_ref.dtype)
        own_ref[:, columns] = total[half : half + each]
        other_ref[:, columns] = total[half + each :]
        if n + buffers < steps:
            weight_copy(n + buffers).start()


def split_product(index_of, index, shape, rows, weight, part, part_count, waits, far):
    block_count, count, depth = rows.shape
    width = weight.shape[1] // part_count
    tile = min(512, width)
    buffers = min(4, width // tile)
    each = shape.per_part * count
    half = block_count * count // 2
    specs, extra = after(waits, far)
    hbm = pl.BlockSpec(memory_space=pl.ANY)
    return pl.pallas_call(
        functools.partial(split_product_kernel, index_of, part * width),
        grid_spec=pltpu.PrefetchScalarGridSpec(
            num_scalar_prefetch=1,
            grid=(1,),
            in_specs=[hbm, hbm] + specs,
            out_specs=[held()] * 3,
            scratch_shapes=[
                pltpu.VMEM((block_count * count, depth), rows.dtype),
                pltpu.VMEM((buffers, depth, tile), weight.dtype),
                pltpu.SemaphoreType.DMA((block_count,)),
                pltpu.SemaphoreType.DMA((buffers,)),
            ],
        ),
        out_shape=[
            pltpu.VMEM((half, width), jnp.bfloat16),
            pltpu.VMEM((half - each, width), jnp.float32),
            pltpu.VMEM((each, width), jnp.float32),
        ],
        compiler_params=pltpu.CompilerParams(vmem_limit_bytes=20 * 2**20),
        cost_estimate=BRIEF,
        name="split_product",
    )(index, in_hbm(rows), in_hbm(weight), *extra)


def narrow_kernel(index_of, index_ref, tokens_ref, down_ref, cot_ref, up_ref, *refs):
    send_ref, keep_ref, back_ref, low = refs[-4:]
    index = index_of(index_ref)
    for m in range(CAP):
        low[m] = lax.dot_general(
            down_ref[0],
            tokens_ref[m * BLK : (m + 1) * BLK],
            LAST,
            preferred_element_type=jnp.float32,
        )
    for core_bit, out_ref in ((1, send_ref), (0, keep_ref)):
        for chip_bits in range(index.chips):
            for i in range(index.per_part):
                block = index.block(core_bit, chip_bits, i)
                mine = index.owner(block) == index.place
                out_ref[chip_bits, i] = jnp.where(mine, low[index.slot(block)], 0.0)
    for i in range(index.per_part):
        adapter = index.owner(index.block(0, 0, i))
        back_ref[i] = lax.dot_general(
            up_ref[adapter],
            cot_ref[i * BLK : (i + 1) * BLK],
            LAST,
            preferred_element_type=jnp.float32,
        )


def narrow(index_of, index, shape, tokens, down, cotangent, up, waits):
    rank = up.shape[1]
    one = (shape.per_part, rank, BLK)
    outs = [(shape.chips,) + one, (shape.chips,) + one, one]
    operands = (tokens, down, cotangent, up)
    specs, extra = after(waits)
    return pl.pallas_call(
        functools.partial(narrow_kernel, index_of),
        grid_spec=pltpu.PrefetchScalarGridSpec(
            num_scalar_prefetch=1,
            grid=(1,),
            in_specs=[held()] + [whole(o.shape) for o in operands[1:]] + specs,
            out_specs=[whole(o) for o in outs],
            scratch_shapes=[pltpu.VMEM((CAP, rank, BLK), jnp.float32)],
        ),
        out_shape=[shape_of(o, jnp.float32) for o in outs],
        compiler_params=SMALL,
        cost_estimate=BRIEF,
        name="narrow",
    )(index, *operands, *extra)


def merge_kernel(keep_ref, arrived_ref, back_ref, *refs):
    out_ref = refs[-1]
    total = keep_ref[0] + arrived_ref[0]
    for ref in refs[:-1][: keep_ref.shape[0] - 1]:
        total = total + ref[...]
    out_ref[0] = total
    out_ref[1] = back_ref[...]


def merge(keep, arrived, back, others, waits):
    specs, extra = after(waits)
    operands = (keep, arrived, back, *others)
    out = (2,) + back.shape
    return pl.pallas_call(
        merge_kernel,
        grid=(1,),
        in_specs=[whole(o.shape) for o in operands] + specs,
        out_specs=whole(out),
        out_shape=shape_of(out, jnp.float32),
        compiler_params=SMALL,
        cost_estimate=BRIEF,
        name="merge",
    )(*operands, *extra)


def pieces_kernel(index_of, index_ref, sum_ref, more_ref, cot_ref, low_ref, back_ref, piece_ref):
    index = index_of(index_ref)
    for i in range(index.per_part):
        live = index.live_rows(index.block(0, 0, i))
        keep = lax.broadcasted_iota(jnp.int32, low_ref.shape[1:], 1) < live
        lowered = jnp.where(keep, sum_ref[0, i] + more_ref[0, i], 0.0).astype(low_ref.dtype)
        back = jnp.where(keep, sum_ref[1, i] + more_ref[1, i], 0.0)
        low_ref[i] = lowered
        back_ref[i] = back.astype(back_ref.dtype)
        piece_ref[i] = jnp.dot(
            lowered, cot_ref[i * BLK : (i + 1) * BLK], preferred_element_type=jnp.float32
        ).astype(piece_ref.dtype)


def make_pieces(index_of, index, shape, total, more, cotangent):
    _, per_part, rank, _ = total.shape
    width = cotangent.shape[1]
    outs = [(per_part, rank, BLK), (per_part, rank, BLK), (per_part, rank, width)]
    operands = (total, more, cotangent)
    return pl.pallas_call(
        functools.partial(pieces_kernel, index_of),
        grid_spec=pltpu.PrefetchScalarGridSpec(
            num_scalar_prefetch=1,
            grid=(1,),
            in_specs=[whole(o.shape) for o in operands],
            out_specs=[whole(o) for o in outs],
        ),
        out_shape=[shape_of(o, jnp.bfloat16) for o in outs],
        compiler_params=SMALL,
        cost_estimate=BRIEF,
        name="pieces",
    )(index, *operands)


def down_gradient_kernel(index_of, index_ref, tokens_ref, *refs):
    back_refs, out_ref = refs[:-1], refs[-1]
    index = index_of(index_ref)
    out_ref[...] = jnp.zeros_like(out_ref)
    for core_bit in range(CORES):
        for chip_bits in range(index.chips):
            for i in range(index.per_part):
                block = index.block(core_bit, chip_bits, i)
                back_ref = back_refs[core_bit * index.chips + chip_bits]

                @pl.when(index.owner(block) == index.place)
                def _(block=block, back_ref=back_ref, i=i):
                    at = pl.multiple_of(index.slot(block) * BLK, BLK)
                    out_ref[0] += adapter_scale * jnp.dot(
                        back_ref[i],
                        tokens_ref[pl.ds(at, BLK)],
                        preferred_element_type=jnp.float32,
                    )


def down_gradient(index_of, index, tokens, backs):
    out = (1, backs[0].shape[1], tokens.shape[1])
    operands = (tokens, *backs)
    return pl.pallas_call(
        functools.partial(down_gradient_kernel, index_of),
        grid_spec=pltpu.PrefetchScalarGridSpec(
            num_scalar_prefetch=1,
            grid=(1,),
            in_specs=[held()] + [whole(o.shape) for o in backs],
            out_specs=whole(out),
        ),
        out_shape=shape_of(out, jnp.float32),
        compiler_params=SMALL,
        cost_estimate=BRIEF,
        name="down_gradient",
    )(index, *operands)


def up_gradient_kernel(index_of, index_ref, *refs):
    piece_refs, out_ref = refs[:-1], refs[-1]
    index = index_of(index_ref)

    def of_device(core_bit, chip_bits, adapter):
        total = None
        for i in range(index.per_part):
            mine = index.owner(index.block(core_bit, chip_bits, i)) == adapter
            piece = piece_refs[core_bit * index.chips + chip_bits][i].astype(jnp.float32)
            term = jnp.where(mine, piece, 0.0)
            total = term if total is None else total + term
        return total

    for adapter in range(index.adapters):
        level = [
            of_device(0, j, adapter) + of_device(1, j, adapter) for j in range(index.chips)
        ]
        while len(level) > 1:
            level = [level[j] + level[j + 1] for j in range(0, len(level), 2)]
        out_ref[adapter] = adapter_scale * level[0]


def up_gradient(index_of, index, adapter_count, pieces):
    per_part, rank, width = pieces[0].shape
    tile = 1024
    out = (adapter_count, rank, width)
    return pl.pallas_call(
        functools.partial(up_gradient_kernel, index_of),
        grid_spec=pltpu.PrefetchScalarGridSpec(
            num_scalar_prefetch=1,
            grid=(width // tile,),
            in_specs=[pl.BlockSpec((per_part, rank, tile), lambda n, _: (0, 0, n))] * len(pieces),
            out_specs=pl.BlockSpec((adapter_count, rank, tile), lambda n, _: (0, 0, n)),
        ),
        out_shape=shape_of(out, jnp.float32),
        compiler_params=SMALL,
        cost_estimate=BRIEF,
        name="up_gradient",
    )(index, *pieces)


def finish_kernel(index_of, layout, tiles, terms, index_ref, low_ref, *refs):
    index = index_of(index_ref)
    up_refs, sum_refs, out_ref = refs[: index.per_part], refs[index.per_part : -1], refs[-1]
    step = pl.program_id(0)
    for i in range(index.per_part):
        block = index.block(0, 0, i)
        live = index.live_rows(block)
        side = lax.dot_general(
            low_ref[i],
            up_refs[i][0],
            (((0,), (0,)), ((), ())),
            preferred_element_type=jnp.float32,
        )
        start, at_ref = 0, 0
        for count, spans in layout:
            for p in range(tiles // spans):
                parts = sum_refs[at_ref : at_ref + terms]
                at_ref += terms

                @pl.when(step // spans == p)
                def _(parts=parts, start=start, count=count):
                    total = adapter_scale * side[start : start + count]
                    for ref in parts:
                        total = total + ref[i * count : (i + 1) * count].astype(jnp.float32)
                    keep = start + lax.broadcasted_iota(jnp.int32, total.shape, 0) < live
                    at = i * BLK + start
                    out_ref[at : at + count] = jnp.where(keep, total, 0.0).astype(out_ref.dtype)

            start += count


def finish(index_of, index, lowered, up, sums, part, part_count, projected, far):
    per_part = lowered.shape[0]
    _, rank, width = up.shape
    tile = width // max(PARTS)
    tiles = width // part_count // tile
    first = part * tiles
    out = (per_part * BLK, width)

    def factor(i):
        def at(n, index_ref):
            index = index_of(index_ref)
            return (index.owner(index.block(0, 0, i)), 0, first + n)

        return pl.BlockSpec((1, rank, tile), at)

    specs, flat, layout = [], [], []
    for chunk, count in zip(sums, CHUNK_ROWS):
        each = max(1, len(chunk) // part_count)
        begin = part * len(chunk) // part_count
        spans = tiles // each
        layout.append((count, spans))
        for p in range(each):
            offset = first - begin * (width // len(chunk) // tile) - p * spans
            limit = width // len(chunk) // tile - 1
            for value in chunk[begin + p]:
                specs.append(
                    pl.BlockSpec(
                        (per_part * count, tile),
                        lambda n, _, o=offset, m=limit: (0, jnp.clip(o + n, 0, m)),
                    )
                )
                flat.append(value)
    terms = len(sums[0][0])
    operands = [index, lowered, *[up] * per_part, *flat]
    aliases = {}
    if projected is not None:
        aliases = {len(operands): 0}
        far = [projected]
    more, extra = after((), far)
    if projected is not None:
        extra = [projected]

    def kernel(*refs):
        finish_kernel(index_of, layout, tiles, terms, *refs[: len(operands)], refs[-1])

    return pl.pallas_call(
        kernel,
        grid_spec=pltpu.PrefetchScalarGridSpec(
            num_scalar_prefetch=1,
            grid=(tiles,),
            in_specs=[whole(lowered.shape)] + [factor(i) for i in range(per_part)] + specs + more,
            out_specs=pl.BlockSpec((out[0], tile), lambda n, _: (0, first + n)),
        ),
        out_shape=shape_of(out, jnp.bfloat16),
        input_output_aliases=aliases,
        compiler_params=SMALL,
        cost_estimate=BRIEF,
        name="finish",
    )(*operands, *extra)


def per_device(
    tokens,
    cotangent,
    frozen_up_weight,
    adapter_down_factor,
    adapter_up_factor,
    tokens_per_adapter,
    adapter_of_block,
    slot_of_block,
):
    owners = lax.axis_size("dp")
    parts = lax.axis_size("tensor")
    chips = parts // CORES
    block_count = adapter_of_block.shape[0]
    adapter_count = adapter_up_factor.shape[0]
    width_dev = tokens.shape[1]
    index_of = functools.partial(
        Index, block_count=block_count, adapter_count=adapter_count, parts=parts
    )
    shape = index_of(None)
    index = Index.pack(adapter_of_block, slot_of_block, tokens_per_adapter)

    def to_other_core(value):
        return lax.ppermute(value, "tensor", [(i, i ^ 1) for i in range(parts)])

    def to_chip(value, k):
        return lax.ppermute(value, "tensor", [(i, i ^ (k * CORES)) for i in range(parts)])

    def across_dp(value, k):
        return lax.ppermute(value, "dp", [(i, i ^ k) for i in range(owners)])

    def every_part(value):
        same_core = [value] + [to_chip(value, k) for k in range(1, chips)]
        return same_core + [to_other_core(v) for v in same_core]

    rows_here = in_vmem(tokens)

    def small_products(waits):
        return narrow(
            index_of,
            index,
            shape,
            rows_here,
            jnp.swapaxes(adapter_down_factor, 1, 2),
            cotangent,
            adapter_up_factor,
            waits,
        )

    def over_parts(send, keep):
        arrived = to_other_core(send)
        return arrived, [to_chip(keep[k] + arrived[k], k) for k in range(1, chips)]

    def over_dp(total):
        k = 1
        while 2 * k < owners:
            total = total + across_dp(total, k)
            k *= 2
        return make_pieces(index_of, index, shape, total, across_dp(total, k), cotangent)

    if owners == 4 and block_count == 4:
        head = Homing(index_of, index, rows_here, 0)
        tail = [Homing(index_of, index, rows_here, c) for c in range(1, len(CHUNK_ROWS))]
        head.first()
        send, keep, back = small_products([head.sent])
        head.second([send])
        arrived, others = over_parts(send, keep)
        homes = [head.settle(others)]
        tail[0].first([homes[-1]])
        tail[0].second()
        total = merge(keep, arrived, back, others, [tail[0].sent])
        homes.append(tail[0].settle())
        for homing in tail[1:]:
            homing.first([homes[-1]])
            homing.second()
            homes.append(homing.settle())
        lowered, back_rows, pieces = over_dp(total)
        chunks = [lax.all_gather(home, "dp", axis=0) for home in homes]
    else:
        send, keep, back = small_products([])
        arrived, others = over_parts(send, keep)
        lowered, back_rows, pieces = over_dp(merge(keep, arrived, back, others, []))
        homes = []
        every_slot = lax.all_gather(
            tokens.reshape(CAP, BLK, width_dev), "dp", axis=0, tiled=True
        )
        picked = every_slot[adapter_of_block * CAP + slot_of_block]
        starts = [sum(CHUNK_ROWS[:c]) for c in range(len(CHUNK_ROWS))]
        chunks = [picked[:, s : s + count] for s, count in zip(starts, CHUNK_ROWS)]

    pieces_same_core = [pieces] + [to_chip(pieces, k) for k in range(1, chips)]

    def summed(rows, part, part_count, waits, far):
        each = shape.per_part * rows.shape[1]
        send, other, own = split_product(
            index_of, index, shape, rows, frozen_up_weight, part, part_count, waits, far
        )
        arrived = to_other_core(send)
        outgoing = (other + arrived[each:].astype(jnp.float32)).astype(jnp.bfloat16)
        return [own, arrived] + [
            to_chip(outgoing[(k - 1) * each : k * each], k) for k in range(1, chips)
        ]

    waits, far = [lowered], homes[1:]
    sums = []
    for rows, part_count in zip(chunks, PARTS):
        sums.append([])
        for part in range(part_count):
            sums[-1].append(summed(rows, part, part_count, waits, far))
            waits, far = [], []
        waits = pieces_same_core[1:] + [v for part in sums[-1] for v in part[2:]]
    pieces_all = pieces_same_core + [to_other_core(p) for p in pieces_same_core]
    up_grad = up_gradient(index_of, index, adapter_count, pieces_all)
    down_grad = down_gradient(index_of, index, rows_here, every_part(back_rows))
    projected = None
    for part in range(PARTS[-1]):
        projected = finish(
            index_of,
            index,
            lowered,
            adapter_up_factor,
            sums,
            part,
            PARTS[-1],
            projected,
            [up_grad, down_grad],
        )
    return (projected, jnp.swapaxes(down_grad, 1, 2), up_grad)


def solution(mesh):
    return jax.shard_map(
        per_device,
        mesh=mesh,
        in_specs=(
            P(("groups", "dp"), "tensor"),
            P(("groups", "tensor"), "dp"),
            P("tensor", "dp"),
            P(("groups", "dp"), "tensor", None),
            P("groups", None, "dp"),
            P("groups"),
            P("groups"),
            P("groups"),
        ),
        out_specs=(
            P(("groups", "tensor"), "dp"),
            P(("groups", "dp"), "tensor", None),
            P("groups", None, "dp"),
        ),
        check_vma=False,
    )
```

```python
import functools

import jax
import jax.numpy as jnp
from jax import lax
from jax.experimental import pallas as pl
from jax.experimental.pallas import tpu as pltpu
from jax.sharding import PartitionSpec as P

BLK = 128
CAP = 3
CORES = 2
CHUNK_ROWS = (64, 64)
PARTS = (2, 2)
SMALL = pltpu.CompilerParams(vmem_limit_bytes=12 * 2**20)

adapter_scale = 0.5

LAST = (((1,), (1,)), ((), ()))


class Index:
    def __init__(self, ref, block_count, adapter_count, parts):
        self.ref = ref
        self.blocks, self.adapters, self.parts = block_count, adapter_count, parts
        self.chips = parts // CORES
        self.per_part = block_count // parts

    @staticmethod
    def pack(adapter_of_block, slot_of_block, tokens_per_adapter):
        place = jnp.stack([lax.axis_index("dp"), lax.axis_index("tensor")]).astype(jnp.int32)
        return jnp.concatenate([adapter_of_block, slot_of_block, tokens_per_adapter, place])

    def owner(self, block):
        return self.ref[block]

    def slot(self, block):
        return self.ref[self.blocks + block]

    def tokens(self, adapter):
        return self.ref[2 * self.blocks + adapter]

    @property
    def place(self):
        return self.ref[2 * self.blocks + self.adapters]

    @property
    def part(self):
        return self.ref[2 * self.blocks + self.adapters + 1]

    def block(self, core_bit, chip_bits, i):
        return (self.part ^ (chip_bits * CORES + core_bit)) * self.per_part + i

    def position(self, block):
        bits = (block // self.per_part) ^ self.part
        half = (1 - bits % CORES) * self.chips + bits // CORES
        return half * self.per_part + block % self.per_part

    def live_rows(self, block):
        adapter = self.owner(block)
        first = jnp.int32(0)
        for a in range(self.adapters):
            count = (self.tokens(a) + BLK - 1) // BLK
            first = first + jnp.where(a < adapter, count, 0)
        return self.tokens(adapter) - (block - first) * BLK


def in_vmem(value):
    return pltpu.with_memory_space_constraint(value, pltpu.VMEM)


def in_hbm(value):
    return pltpu.with_memory_space_constraint(value, pltpu.HBM)


def held():
    return pl.BlockSpec(memory_space=pltpu.VMEM)


def whole(shape):
    return pl.BlockSpec(shape, lambda *_: (0,) * len(shape))


def shape_of(shape, dtype):
    return jax.ShapeDtypeStruct(shape, dtype)


BRIEF = pl.CostEstimate(flops=1, bytes_accessed=1, transcendentals=0)


def own_rows(index, block, start, tokens_ref, out_ref):
    at = pl.multiple_of(index.slot(block) * BLK + start, 16)
    out_ref[...] = tokens_ref[pl.ds(at, out_ref.shape[0])]


def first_hop_kernel(index_of, start, index_ref, tokens_ref, *refs):
    a_ref, b_ref = refs[-2:]
    index = index_of(index_ref)
    own_rows(index, jnp.where(index.place == 0, 2, 1), start, tokens_ref, a_ref)
    own_rows(index, 0, start, tokens_ref, b_ref)


def second_hop_kernel(index_of, start, index_ref, tokens_ref, a_ref, b_ref, *refs):
    x_ref, y_ref = refs[-2:]
    index = index_of(index_ref)
    place = index.place
    outer = jnp.where(place == 0, 1, jnp.where(place == 1, 0, 2))
    middle = jnp.where(place == 1, 2, 1)
    own_rows(index, outer, start, tokens_ref, x_ref)
    own_rows(index, middle, start, tokens_ref, y_ref)

    @pl.when((place == 1) & (index.owner(0) != 1))
    def _():
        x_ref[...] = b_ref[...]

    @pl.when(((place == 1) | (place == 2)) & (index.owner(middle) != place))
    def _():
        y_ref[...] = a_ref[...]


def settle_kernel(index_of, start, index_ref, tokens_ref, x_ref, y_ref, *refs):
    out_ref = refs[-1]
    index = index_of(index_ref)
    place = index.place
    owner = index.owner(place)
    mine = owner == place
    edge = (place == 0) | ((place == 1) & (owner == 0)) | ((place == 2) & (owner == 3))
    own_rows(index, place, start, tokens_ref, out_ref)

    @pl.when(jnp.logical_not(mine) & edge)
    def _():
        out_ref[...] = x_ref[...]

    @pl.when(jnp.logical_not(mine | edge))
    def _():
        out_ref[...] = y_ref[...]


def collect_kernel(index_of, count, index_ref, home_ref, outer_ref, *refs):
    inner_refs, outer_refs, out_ref = refs[:2], refs[2:4], refs[-1]
    index = index_of(index_ref)
    place = index.place

    def put(block, ref):
        at = pl.multiple_of(index.position(block) * count, 16)
        out_ref[pl.ds(at, count)] = ref[...]

    put(place, home_ref)
    put(place ^ 1, outer_ref)
    middle = (place == 1) | (place == 2)

    @pl.when(middle)
    def _():
        put(3 - place, inner_refs[0])
        put(place ^ 2, inner_refs[1])

    @pl.when(jnp.logical_not(middle))
    def _():
        put(place ^ 2, outer_refs[0])
        put(3 - place, outer_refs[1])


def after(values, far=()):
    specs = [
        pl.BlockSpec((1,) * (v.ndim - 2) + (16, 128), lambda *_, n=v.ndim: (0,) * n) for v in values
    ] + [pl.BlockSpec(memory_space=pl.ANY)] * len(far)
    return specs, [*values, *(in_hbm(v) for v in far)]


def hop_call(kernel, index, tokens, unit, count, stay, received, waits, name, declared):
    specs, extra = after(waits)
    out = pltpu.VMEM(unit.shape, unit.dtype) if stay else unit
    return pl.pallas_call(
        kernel,
        grid_spec=pltpu.PrefetchScalarGridSpec(
            num_scalar_prefetch=1,
            grid=(1,),
            in_specs=[held()] * (1 + len(received)) + specs,
            out_specs=[held() if stay else whole(unit.shape)] * count,
        ),
        out_shape=[out] * count,
        compiler_params=SMALL,
        cost_estimate=declared,
        name=name,
    )(index, tokens, *[in_vmem(r) for r in received], *extra)


class Homing:
    def __init__(self, index_of, index, tokens, chunk):
        self.index_of, self.index, self.tokens = index_of, index, tokens
        self.start = sum(CHUNK_ROWS[:chunk])
        self.unit = shape_of((CHUNK_ROWS[chunk], tokens.shape[1]), tokens.dtype)

    def call(self, kernel, count, stay, received, waits, name, declared=BRIEF):
        return hop_call(
            functools.partial(kernel, self.index_of, self.start),
            self.index,
            self.tokens,
            self.unit,
            count,
            stay,
            received,
            waits,
            name,
            declared,
        )

    def first(self, waits=()):
        inward, left = self.call(first_hop_kernel, 2, True, (), waits, "first_hop")
        self.sent = inward
        self.received = (
            lax.ppermute(inward, "dp", [(3, 2), (0, 1)]),
            lax.ppermute(left, "dp", [(2, 1)]),
        )

    def second(self, waits=()):
        outer, middle = self.call(second_hop_kernel, 2, True, self.received, waits, "second_hop")
        self.sent = outer
        self.received = (
            lax.ppermute(outer, "dp", [(1, 0), (0, 1), (3, 2)]),
            lax.ppermute(middle, "dp", [(2, 1), (1, 2)]),
        )

    def settle(self, waits=()):
        (home,) = self.call(settle_kernel, 1, True, self.received, waits, "settle")
        self.sent = home
        outer = lax.ppermute(home, "dp", [(0, 1), (1, 0), (2, 3), (3, 2)])
        inner = lax.ppermute(home, "dp", [(1, 2), (2, 1)])
        outer_2 = lax.ppermute(inner, "dp", [(1, 0), (2, 3)])
        inner_2 = lax.ppermute(outer, "dp", [(1, 2), (2, 1)])
        outer_3 = lax.ppermute(inner_2, "dp", [(1, 0), (2, 3)])
        self.arrived = home, outer, inner, inner_2, outer_2, outer_3

    def rows(self, waits=()):
        count, width = self.unit.shape
        specs, extra = after(waits)
        return pl.pallas_call(
            functools.partial(collect_kernel, self.index_of, count),
            grid_spec=pltpu.PrefetchScalarGridSpec(
                num_scalar_prefetch=1,
                grid=(1,),
                in_specs=[held()] * len(self.arrived) + specs,
                out_specs=held(),
            ),
            out_shape=pltpu.VMEM((4 * count, width), self.unit.dtype),
            compiler_params=SMALL,
            cost_estimate=BRIEF,
            name="collect",
        )(self.index, *[in_vmem(a) for a in self.arrived], *extra)


def load_weight_kernel(w_ref, *refs):
    out_ref, sems = refs[-2:]
    streams = sems.shape[0]
    depth = w_ref.shape[0] // streams
    copies = [
        pltpu.make_async_copy(
            w_ref.at[pl.ds(i * depth, depth)], out_ref.at[pl.ds(i * depth, depth)], sems.at[i]
        )
        for i in range(streams)
    ]
    for copy in copies:
        copy.start()
    for copy in copies:
        copy.wait()


def load_weight(weight, waits):
    specs, extra = after(waits)
    return pl.pallas_call(
        load_weight_kernel,
        grid=(1,),
        in_specs=[pl.BlockSpec(memory_space=pl.ANY)] + specs,
        out_specs=pl.BlockSpec(memory_space=pl.ANY),
        out_shape=pltpu.VMEM(weight.shape, weight.dtype),
        scratch_shapes=[pltpu.SemaphoreType.DMA((4,))],
        compiler_params=SMALL,
        cost_estimate=BRIEF,
        name="load_weight",
    )(in_hbm(weight), *extra)


def split_product_kernel(each, half, first, tile, rows_ref, w_ref, *refs):
    send_ref, other_ref, own_ref = refs[-3:]
    for n in range(own_ref.shape[1] // tile):
        total = jnp.dot(
            rows_ref[...],
            w_ref[:, first + n * tile : first + (n + 1) * tile],
            preferred_element_type=jnp.float32,
        )
        columns = slice(n * tile, (n + 1) * tile)
        send_ref[:, columns] = total[:half].astype(send_ref.dtype)
        own_ref[:, columns] = total[half : half + each]
        other_ref[:, columns] = total[half + each :]


def split_product(shape, rows, weight, part, part_count, waits):
    half = rows.shape[0] // 2
    each = half // shape.chips
    width = weight.shape[1] // part_count
    specs, extra = after(waits)
    return pl.pallas_call(
        functools.partial(split_product_kernel, each, half, part * width, min(512, width)),
        grid=(1,),
        in_specs=[held(), held()] + specs,
        out_specs=[held()] * 3,
        out_shape=[
            pltpu.VMEM((half, width), jnp.bfloat16),
            pltpu.VMEM((half - each, width), jnp.float32),
            pltpu.VMEM((each, width), jnp.float32),
        ],
        compiler_params=SMALL,
        cost_estimate=BRIEF,
        name="split_product",
    )(in_vmem(rows), in_vmem(weight), *extra)


def narrow_kernel(index_of, index_ref, tokens_ref, down_ref, cot_ref, up_ref, *refs):
    send_ref, keep_ref, back_ref, low = refs[-4:]
    index = index_of(index_ref)
    for m in range(CAP):
        low[m] = lax.dot_general(
            down_ref[0],
            tokens_ref[m * BLK : (m + 1) * BLK],
            LAST,
            preferred_element_type=jnp.float32,
        )
    for core_bit, out_ref in ((1, send_ref), (0, keep_ref)):
        for chip_bits in range(index.chips):
            for i in range(index.per_part):
                block = index.block(core_bit, chip_bits, i)
                mine = index.owner(block) == index.place
                out_ref[chip_bits, i] = jnp.where(mine, low[index.slot(block)], 0.0)
    for i in range(index.per_part):
        adapter = index.owner(index.block(0, 0, i))
        back_ref[i] = lax.dot_general(
            up_ref[adapter],
            cot_ref[i * BLK : (i + 1) * BLK],
            LAST,
            preferred_element_type=jnp.float32,
        )


def narrow(index_of, index, shape, tokens, down, cotangent, up, waits):
    rank = up.shape[1]
    one = (shape.per_part, rank, BLK)
    outs = [(shape.chips,) + one, (shape.chips,) + one, one]
    operands = (tokens, down, cotangent, up)
    specs, extra = after(waits)
    return pl.pallas_call(
        functools.partial(narrow_kernel, index_of),
        grid_spec=pltpu.PrefetchScalarGridSpec(
            num_scalar_prefetch=1,
            grid=(1,),
            in_specs=[held()] + [whole(o.shape) for o in operands[1:]] + specs,
            out_specs=[whole(o) for o in outs],
            scratch_shapes=[pltpu.VMEM((CAP, rank, BLK), jnp.float32)],
        ),
        out_shape=[shape_of(o, jnp.float32) for o in outs],
        compiler_params=SMALL,
        cost_estimate=BRIEF,
        name="narrow",
    )(index, *operands, *extra)


def merge_kernel(keep_ref, arrived_ref, back_ref, *refs):
    out_ref = refs[-1]
    total = keep_ref[0] + arrived_ref[0]
    for ref in refs[:-1][: keep_ref.shape[0] - 1]:
        total = total + ref[...]
    out_ref[0] = total
    out_ref[1] = back_ref[...]


def merge(keep, arrived, back, others, waits):
    specs, extra = after(waits)
    operands = (keep, arrived, back, *others)
    out = (2,) + back.shape
    return pl.pallas_call(
        merge_kernel,
        grid=(1,),
        in_specs=[whole(o.shape) for o in operands] + specs,
        out_specs=whole(out),
        out_shape=shape_of(out, jnp.float32),
        compiler_params=SMALL,
        cost_estimate=BRIEF,
        name="merge",
    )(*operands, *extra)


def pieces_kernel(index_of, index_ref, sum_ref, more_ref, cot_ref, low_ref, back_ref, piece_ref):
    index = index_of(index_ref)
    for i in range(index.per_part):
        live = index.live_rows(index.block(0, 0, i))
        keep = lax.broadcasted_iota(jnp.int32, low_ref.shape[1:], 1) < live
        lowered = jnp.where(keep, sum_ref[0, i] + more_ref[0, i], 0.0).astype(low_ref.dtype)
        back = jnp.where(keep, sum_ref[1, i] + more_ref[1, i], 0.0)
        low_ref[i] = lowered
        back_ref[i] = back.astype(back_ref.dtype)
        piece_ref[i] = jnp.dot(
            lowered, cot_ref[i * BLK : (i + 1) * BLK], preferred_element_type=jnp.float32
        ).astype(piece_ref.dtype)


def make_pieces(index_of, index, shape, total, more, cotangent):
    _, per_part, rank, _ = total.shape
    width = cotangent.shape[1]
    outs = [(per_part, rank, BLK), (per_part, rank, BLK), (per_part, rank, width)]
    operands = (total, more, cotangent)
    return pl.pallas_call(
        functools.partial(pieces_kernel, index_of),
        grid_spec=pltpu.PrefetchScalarGridSpec(
            num_scalar_prefetch=1,
            grid=(1,),
            in_specs=[whole(o.shape) for o in operands],
            out_specs=[whole(o) for o in outs],
        ),
        out_shape=[shape_of(o, jnp.bfloat16) for o in outs],
        compiler_params=SMALL,
        cost_estimate=BRIEF,
        name="pieces",
    )(index, *operands)


def down_gradient_kernel(index_of, index_ref, tokens_ref, *refs):
    back_refs, out_ref = refs[:-1], refs[-1]
    index = index_of(index_ref)
    out_ref[...] = jnp.zeros_like(out_ref)
    for core_bit in range(CORES):
        for chip_bits in range(index.chips):
            for i in range(index.per_part):
                block = index.block(core_bit, chip_bits, i)
                back_ref = back_refs[core_bit * index.chips + chip_bits]

                @pl.when(index.owner(block) == index.place)
                def _(block=block, back_ref=back_ref, i=i):
                    at = pl.multiple_of(index.slot(block) * BLK, BLK)
                    out_ref[0] += adapter_scale * jnp.dot(
                        back_ref[i],
                        tokens_ref[pl.ds(at, BLK)],
                        preferred_element_type=jnp.float32,
                    )


def down_gradient(index_of, index, tokens, backs):
    out = (1, backs[0].shape[1], tokens.shape[1])
    operands = (tokens, *backs)
    return pl.pallas_call(
        functools.partial(down_gradient_kernel, index_of),
        grid_spec=pltpu.PrefetchScalarGridSpec(
            num_scalar_prefetch=1,
            grid=(1,),
            in_specs=[held()] + [whole(o.shape) for o in backs],
            out_specs=whole(out),
        ),
        out_shape=shape_of(out, jnp.float32),
        compiler_params=SMALL,
        cost_estimate=BRIEF,
        name="down_gradient",
    )(index, *operands)


def up_gradient_kernel(index_of, index_ref, *refs):
    piece_refs, out_ref = refs[:-1], refs[-1]
    index = index_of(index_ref)

    def of_device(core_bit, chip_bits, adapter):
        total = None
        for i in range(index.per_part):
            mine = index.owner(index.block(core_bit, chip_bits, i)) == adapter
            piece = piece_refs[core_bit * index.chips + chip_bits][i].astype(jnp.float32)
            term = jnp.where(mine, piece, 0.0)
            total = term if total is None else total + term
        return total

    for adapter in range(index.adapters):
        level = [
            of_device(0, j, adapter) + of_device(1, j, adapter) for j in range(index.chips)
        ]
        while len(level) > 1:
            level = [level[j] + level[j + 1] for j in range(0, len(level), 2)]
        out_ref[adapter] = adapter_scale * level[0]


def up_gradient(index_of, index, adapter_count, pieces):
    per_part, rank, width = pieces[0].shape
    tile = 1024
    out = (adapter_count, rank, width)
    return pl.pallas_call(
        functools.partial(up_gradient_kernel, index_of),
        grid_spec=pltpu.PrefetchScalarGridSpec(
            num_scalar_prefetch=1,
            grid=(width // tile,),
            in_specs=[pl.BlockSpec((per_part, rank, tile), lambda n, _: (0, 0, n))] * len(pieces),
            out_specs=pl.BlockSpec((adapter_count, rank, tile), lambda n, _: (0, 0, n)),
        ),
        out_shape=shape_of(out, jnp.float32),
        compiler_params=SMALL,
        cost_estimate=BRIEF,
        name="up_gradient",
    )(index, *pieces)


def finish_kernel(index_of, layout, tiles, terms, index_ref, low_ref, *refs):
    index = index_of(index_ref)
    up_refs, sum_refs, out_ref = refs[: index.per_part], refs[index.per_part : -1], refs[-1]
    step = pl.program_id(0)
    for i in range(index.per_part):
        block = index.block(0, 0, i)
        live = index.live_rows(block)
        side = lax.dot_general(
            low_ref[i],
            up_refs[i][0],
            (((0,), (0,)), ((), ())),
            preferred_element_type=jnp.float32,
        )
        start, at_ref = 0, 0
        for count, spans in layout:
            for p in range(tiles // spans):
                parts = sum_refs[at_ref : at_ref + terms]
                at_ref += terms

                @pl.when(step // spans == p)
                def _(parts=parts, start=start, count=count):
                    total = adapter_scale * side[start : start + count]
                    for ref in parts:
                        total = total + ref[i * count : (i + 1) * count].astype(jnp.float32)
                    keep = start + lax.broadcasted_iota(jnp.int32, total.shape, 0) < live
                    at = i * BLK + start
                    out_ref[at : at + count] = jnp.where(keep, total, 0.0).astype(out_ref.dtype)

            start += count


def finish(index_of, index, lowered, up, sums, part, part_count, projected, far):
    per_part = lowered.shape[0]
    _, rank, width = up.shape
    tile = width // max(PARTS)
    tiles = width // part_count // tile
    first = part * tiles
    out = (per_part * BLK, width)

    def factor(i):
        def at(n, index_ref):
            index = index_of(index_ref)
            return (index.owner(index.block(0, 0, i)), 0, first + n)

        return pl.BlockSpec((1, rank, tile), at)

    specs, flat, layout = [], [], []
    for chunk, count in zip(sums, CHUNK_ROWS):
        each = max(1, len(chunk) // part_count)
        begin = part * len(chunk) // part_count
        spans = tiles // each
        layout.append((count, spans))
        for p in range(each):
            offset = first - begin * (width // len(chunk) // tile) - p * spans
            limit = width // len(chunk) // tile - 1
            for value in chunk[begin + p]:
                specs.append(
                    pl.BlockSpec(
                        (per_part * count, tile),
                        lambda n, _, o=offset, m=limit: (0, jnp.clip(o + n, 0, m)),
                    )
                )
                flat.append(value)
    terms = len(sums[0][0])
    operands = [index, lowered, *[up] * per_part, *flat]
    aliases = {}
    if projected is not None:
        aliases = {len(operands): 0}
        far = [projected]
    more, extra = after((), far)
    if projected is not None:
        extra = [projected]

    def kernel(*refs):
        finish_kernel(index_of, layout, tiles, terms, *refs[: len(operands)], refs[-1])

    return pl.pallas_call(
        kernel,
        grid_spec=pltpu.PrefetchScalarGridSpec(
            num_scalar_prefetch=1,
            grid=(tiles,),
            in_specs=[whole(lowered.shape)] + [factor(i) for i in range(per_part)] + specs + more,
            out_specs=pl.BlockSpec((out[0], tile), lambda n, _: (0, first + n)),
        ),
        out_shape=shape_of(out, jnp.bfloat16),
        input_output_aliases=aliases,
        compiler_params=SMALL,
        cost_estimate=BRIEF,
        name="finish",
    )(*operands, *extra)


def per_device(
    tokens,
    cotangent,
    frozen_up_weight,
    adapter_down_factor,
    adapter_up_factor,
    tokens_per_adapter,
    adapter_of_block,
    slot_of_block,
):
    owners = lax.axis_size("dp")
    parts = lax.axis_size("tensor")
    chips = parts // CORES
    block_count = adapter_of_block.shape[0]
    adapter_count = adapter_up_factor.shape[0]
    width_dev = tokens.shape[1]
    index_of = functools.partial(
        Index, block_count=block_count, adapter_count=adapter_count, parts=parts
    )
    shape = index_of(None)
    index = Index.pack(adapter_of_block, slot_of_block, tokens_per_adapter)

    def to_other_core(value):
        return lax.ppermute(value, "tensor", [(i, i ^ 1) for i in range(parts)])

    def to_chip(value, k):
        return lax.ppermute(value, "tensor", [(i, i ^ (k * CORES)) for i in range(parts)])

    def across_dp(value, k):
        return lax.ppermute(value, "dp", [(i, i ^ k) for i in range(owners)])

    def every_part(value):
        same_core = [value] + [to_chip(value, k) for k in range(1, chips)]
        return same_core + [to_other_core(v) for v in same_core]

    rows_here = in_vmem(tokens)

    def small_products(waits):
        return narrow(
            index_of,
            index,
            shape,
            rows_here,
            jnp.swapaxes(adapter_down_factor, 1, 2),
            cotangent,
            adapter_up_factor,
            waits,
        )

    def over_parts(send, keep):
        arrived = to_other_core(send)
        return arrived, [to_chip(keep[k] + arrived[k], k) for k in range(1, chips)]

    def over_dp(total):
        k = 1
        while 2 * k < owners:
            total = total + across_dp(total, k)
            k *= 2
        return make_pieces(index_of, index, shape, total, across_dp(total, k), cotangent)

    if owners == 4 and block_count == 4:
        head, tail = [Homing(index_of, index, rows_here, c) for c in range(2)]
        head.first()
        tail.first([head.sent])
        send, keep, back = small_products([tail.sent])
        head.second([send])
        arrived, others = over_parts(send, keep)
        tail.second([head.sent])
        head.settle([tail.sent])
        weight = load_weight(frozen_up_weight, [head.sent])
        total = merge(keep, arrived, back, others, [])
        tail.settle([total])
        lowered, back_rows, pieces = over_dp(total)
        chunks = [head.rows(), tail.rows()]
    else:
        weight = load_weight(frozen_up_weight, [])
        send, keep, back = small_products([])
        arrived, others = over_parts(send, keep)
        lowered, back_rows, pieces = over_dp(merge(keep, arrived, back, others, []))
        every_slot = lax.all_gather(
            tokens.reshape(CAP, BLK, width_dev), "dp", axis=0, tiled=True
        )
        part = lax.axis_index("tensor")
        devices = jnp.arange(parts, dtype=jnp.int32)
        order = (devices // chips ^ 1) + (devices % chips) * CORES ^ part
        blocks = (order[:, None] * shape.per_part + jnp.arange(shape.per_part)).reshape(-1)
        picked = every_slot[adapter_of_block[blocks] * CAP + slot_of_block[blocks]]
        starts = [sum(CHUNK_ROWS[:c]) for c in range(len(CHUNK_ROWS))]
        chunks = [
            picked[:, s : s + count].reshape(-1, width_dev)
            for s, count in zip(starts, CHUNK_ROWS)
        ]
    pieces_same_core = [pieces] + [to_chip(pieces, k) for k in range(1, chips)]

    def summed(rows, part, part_count, waits):
        each = rows.shape[0] // parts
        send, other, own = split_product(shape, rows, weight, part, part_count, waits)
        arrived = to_other_core(send)
        outgoing = (other + arrived[each:].astype(jnp.float32)).astype(jnp.bfloat16)
        across = [to_chip(outgoing[(k - 1) * each : k * each], k) for k in range(1, chips)]
        return [own, arrived] + across, outgoing

    waits = [lowered]
    sums = []
    for rows, part_count in zip(chunks, PARTS):
        sums.append([])
        sent = []
        for part in range(part_count):
            terms, outgoing = summed(rows, part, part_count, waits)
            sums[-1].append(terms)
            sent.append(outgoing)
            waits = []
        waits = sent
    pieces_all = pieces_same_core + [to_other_core(p) for p in pieces_same_core]
    up_grad = up_gradient(index_of, index, adapter_count, pieces_all)
    down_grad = down_gradient(index_of, index, rows_here, every_part(back_rows))
    projected = None
    for part in range(PARTS[-1]):
        projected = finish(
            index_of,
            index,
            lowered,
            adapter_up_factor,
            sums,
            part,
            PARTS[-1],
            projected,
            [up_grad, down_grad],
        )
    return (projected, jnp.swapaxes(down_grad, 1, 2), up_grad)


def solution(mesh):
    return jax.shard_map(
        per_device,
        mesh=mesh,
        in_specs=(
            P(("groups", "dp"), "tensor"),
            P(("groups", "tensor"), "dp"),
            P("tensor", "dp"),
            P(("groups", "dp"), "tensor", None),
            P("groups", None, "dp"),
            P("groups"),
            P("groups"),
            P("groups"),
        ),
        out_specs=(
            P(("groups", "tensor"), "dp"),
            P(("groups", "dp"), "tensor", None),
            P("groups", None, "dp"),
        ),
        check_vma=False,
    )
```

```python
import functools

import jax
import jax.numpy as jnp
from jax import lax
from jax.experimental import pallas as pl
from jax.experimental.pallas import tpu as pltpu
from jax.sharding import PartitionSpec as P

BLK = 128
CAP = 3
CORES = 2
CHUNK_ROWS = (64, 64)
PARTS = (2, 2)
SMALL = pltpu.CompilerParams(vmem_limit_bytes=12 * 2**20)

adapter_scale = 0.5

LAST = (((1,), (1,)), ((), ()))


class Index:
    def __init__(self, ref, block_count, adapter_count, parts):
        self.ref = ref
        self.blocks, self.adapters, self.parts = block_count, adapter_count, parts
        self.chips = parts // CORES
        self.per_part = block_count // parts

    @staticmethod
    def pack(adapter_of_block, slot_of_block, tokens_per_adapter):
        place = jnp.stack([lax.axis_index("dp"), lax.axis_index("tensor")]).astype(jnp.int32)
        return jnp.concatenate([adapter_of_block, slot_of_block, tokens_per_adapter, place])

    def owner(self, block):
        return self.ref[block]

    def slot(self, block):
        return self.ref[self.blocks + block]

    def tokens(self, adapter):
        return self.ref[2 * self.blocks + adapter]

    @property
    def place(self):
        return self.ref[2 * self.blocks + self.adapters]

    @property
    def part(self):
        return self.ref[2 * self.blocks + self.adapters + 1]

    def block(self, core_bit, chip_bits, i):
        return (self.part ^ (chip_bits * CORES + core_bit)) * self.per_part + i

    def position(self, block):
        bits = (block // self.per_part) ^ self.part
        half = (1 - bits % CORES) * self.chips + bits // CORES
        return half * self.per_part + block % self.per_part

    def live_rows(self, block):
        adapter = self.owner(block)
        first = jnp.int32(0)
        for a in range(self.adapters):
            count = (self.tokens(a) + BLK - 1) // BLK
            first = first + jnp.where(a < adapter, count, 0)
        return self.tokens(adapter) - (block - first) * BLK


def in_vmem(value):
    return pltpu.with_memory_space_constraint(value, pltpu.VMEM)


def in_hbm(value):
    return pltpu.with_memory_space_constraint(value, pltpu.HBM)


def held():
    return pl.BlockSpec(memory_space=pltpu.VMEM)


def whole(shape):
    return pl.BlockSpec(shape, lambda *_: (0,) * len(shape))


def shape_of(shape, dtype):
    return jax.ShapeDtypeStruct(shape, dtype)


BRIEF = pl.CostEstimate(flops=1, bytes_accessed=1, transcendentals=0)


def own_rows(index, block, tokens_ref, out_ref, start=0):
    at = pl.multiple_of(index.slot(block) * BLK + start, 16)
    out_ref[...] = tokens_ref[pl.ds(at, out_ref.shape[0])]


def first_hop_kernel(index_of, index_ref, tokens_ref, *refs):
    a_ref, b_ref = refs[-2:]
    index = index_of(index_ref)
    own_rows(index, jnp.where(index.place == 0, 2, 1), tokens_ref, a_ref)
    own_rows(index, 0, tokens_ref, b_ref)


def second_hop_kernel(index_of, index_ref, tokens_ref, a_ref, b_ref, *refs):
    x_ref, y_ref = refs[-2:]
    index = index_of(index_ref)
    place = index.place
    outer = jnp.where(place == 0, 1, jnp.where(place == 1, 0, 2))
    middle = jnp.where(place == 1, 2, 1)
    own_rows(index, outer, tokens_ref, x_ref)
    own_rows(index, middle, tokens_ref, y_ref)

    @pl.when((place == 1) & (index.owner(0) != 1))
    def _():
        x_ref[...] = b_ref[...]

    @pl.when(((place == 1) | (place == 2)) & (index.owner(middle) != place))
    def _():
        y_ref[...] = a_ref[...]


def settle_kernel(index_of, index_ref, tokens_ref, x_ref, y_ref, *refs):
    out_refs = refs[-len(CHUNK_ROWS) :]
    index = index_of(index_ref)
    place = index.place
    owner = index.owner(place)
    mine = owner == place
    edge = (place == 0) | ((place == 1) & (owner == 0)) | ((place == 2) & (owner == 3))
    start = 0
    for out_ref in out_refs:
        rows = slice(start, start + out_ref.shape[0])
        own_rows(index, place, tokens_ref, out_ref, start)

        @pl.when(jnp.logical_not(mine) & edge)
        def _(out_ref=out_ref, rows=rows):
            out_ref[...] = x_ref[rows]

        @pl.when(jnp.logical_not(mine | edge))
        def _(out_ref=out_ref, rows=rows):
            out_ref[...] = y_ref[rows]

        start += out_ref.shape[0]


def collect_kernel(index_of, count, index_ref, home_ref, outer_ref, *refs):
    inner_refs, outer_refs, out_ref = refs[:2], refs[2:4], refs[-1]
    index = index_of(index_ref)
    place = index.place

    def put(block, ref):
        at = pl.multiple_of(index.position(block) * count, 16)
        out_ref[pl.ds(at, count)] = ref[...]

    put(place, home_ref)
    put(place ^ 1, outer_ref)
    middle = (place == 1) | (place == 2)

    @pl.when(middle)
    def _():
        put(3 - place, inner_refs[0])
        put(place ^ 2, inner_refs[1])

    @pl.when(jnp.logical_not(middle))
    def _():
        put(place ^ 2, outer_refs[0])
        put(3 - place, outer_refs[1])


def after(values, far=()):
    specs = [
        pl.BlockSpec((1,) * (v.ndim - 2) + (16, 128), lambda *_, n=v.ndim: (0,) * n) for v in values
    ] + [pl.BlockSpec(memory_space=pl.ANY)] * len(far)
    return specs, [*values, *(in_hbm(v) for v in far)]


def hop_call(kernel, index, tokens, heights, received, waits, name):
    specs, extra = after(waits)
    width = tokens.shape[1]
    return pl.pallas_call(
        kernel,
        grid_spec=pltpu.PrefetchScalarGridSpec(
            num_scalar_prefetch=1,
            grid=(1,),
            in_specs=[held()] * (1 + len(received)) + specs,
            out_specs=[held()] * len(heights),
        ),
        out_shape=[pltpu.VMEM((height, width), tokens.dtype) for height in heights],
        compiler_params=SMALL,
        cost_estimate=BRIEF,
        name=name,
    )(index, tokens, *[in_vmem(r) for r in received], *extra)


class Relay:
    def __init__(self, index_of, index, tokens):
        self.index_of, self.index, self.tokens = index_of, index, tokens

    def call(self, kernel, heights, received, waits, name):
        kernel = functools.partial(kernel, self.index_of)
        return hop_call(kernel, self.index, self.tokens, heights, received, waits, name)

    def first(self, waits=()):
        inward, left = self.call(first_hop_kernel, (BLK, BLK), (), waits, "first_hop")
        self.received = (
            lax.ppermute(inward, "dp", [(3, 2), (0, 1)]),
            lax.ppermute(left, "dp", [(2, 1)]),
        )
        return inward

    def second(self, waits=()):
        outer, middle = self.call(
            second_hop_kernel, (BLK, BLK), self.received, waits, "second_hop"
        )
        self.received = (
            lax.ppermute(outer, "dp", [(1, 0), (0, 1), (3, 2)]),
            lax.ppermute(middle, "dp", [(2, 1), (1, 2)]),
        )
        return outer

    def settle(self, waits=()):
        homes = self.call(settle_kernel, CHUNK_ROWS, self.received, waits, "settle")
        self.arrived = [self.spread(home) for home in homes]
        return homes[0]

    def spread(self, home):
        outer = lax.ppermute(home, "dp", [(0, 1), (1, 0), (2, 3), (3, 2)])
        inner = lax.ppermute(home, "dp", [(1, 2), (2, 1)])
        outer_2 = lax.ppermute(inner, "dp", [(1, 0), (2, 3)])
        inner_2 = lax.ppermute(outer, "dp", [(1, 2), (2, 1)])
        outer_3 = lax.ppermute(inner_2, "dp", [(1, 0), (2, 3)])
        return home, outer, inner, inner_2, outer_2, outer_3

    def rows(self, chunk, waits=()):
        arrived = self.arrived[chunk]
        count, width = arrived[0].shape
        specs, extra = after(waits)
        return pl.pallas_call(
            functools.partial(collect_kernel, self.index_of, count),
            grid_spec=pltpu.PrefetchScalarGridSpec(
                num_scalar_prefetch=1,
                grid=(1,),
                in_specs=[held()] * len(arrived) + specs,
                out_specs=held(),
            ),
            out_shape=pltpu.VMEM((4 * count, width), self.tokens.dtype),
            compiler_params=SMALL,
            cost_estimate=BRIEF,
            name="collect",
        )(self.index, *[in_vmem(a) for a in arrived], *extra)


def load_weight_kernel(w_ref, *refs):
    out_ref, sems = refs[-2:]
    streams = sems.shape[0]
    depth = w_ref.shape[0] // streams
    copies = [
        pltpu.make_async_copy(
            w_ref.at[pl.ds(i * depth, depth)], out_ref.at[pl.ds(i * depth, depth)], sems.at[i]
        )
        for i in range(streams)
    ]
    for copy in copies:
        copy.start()
    for copy in copies:
        copy.wait()


def load_weight(weight, waits):
    specs, extra = after(waits)
    return pl.pallas_call(
        load_weight_kernel,
        grid=(1,),
        in_specs=[pl.BlockSpec(memory_space=pl.ANY)] + specs,
        out_specs=pl.BlockSpec(memory_space=pl.ANY),
        out_shape=pltpu.VMEM(weight.shape, weight.dtype),
        scratch_shapes=[pltpu.SemaphoreType.DMA((4,))],
        compiler_params=SMALL,
        cost_estimate=BRIEF,
        name="load_weight",
    )(in_hbm(weight), *extra)


def split_product_kernel(each, half, first, tile, rows_ref, w_ref, *refs):
    send_ref, other_ref, own_ref = refs[-3:]
    for n in range(own_ref.shape[1] // tile):
        total = jnp.dot(
            rows_ref[...],
            w_ref[:, first + n * tile : first + (n + 1) * tile],
            preferred_element_type=jnp.float32,
        )
        columns = slice(n * tile, (n + 1) * tile)
        send_ref[:, columns] = total[:half].astype(send_ref.dtype)
        own_ref[:, columns] = total[half : half + each]
        other_ref[:, columns] = total[half + each :]


def split_product(shape, rows, weight, part, part_count, waits):
    half = rows.shape[0] // 2
    each = half // shape.chips
    width = weight.shape[1] // part_count
    specs, extra = after(waits)
    return pl.pallas_call(
        functools.partial(split_product_kernel, each, half, part * width, min(512, width)),
        grid=(1,),
        in_specs=[held(), held()] + specs,
        out_specs=[held()] * 3,
        out_shape=[
            pltpu.VMEM((half, width), jnp.bfloat16),
            pltpu.VMEM((half - each, width), jnp.float32),
            pltpu.VMEM((each, width), jnp.float32),
        ],
        compiler_params=SMALL,
        cost_estimate=BRIEF,
        name="split_product",
    )(in_vmem(rows), in_vmem(weight), *extra)


def narrow_kernel(index_of, index_ref, tokens_ref, down_ref, cot_ref, up_ref, *refs):
    send_ref, keep_ref, back_ref, low = refs[-4:]
    index = index_of(index_ref)
    for m in range(CAP):
        low[m] = lax.dot_general(
            down_ref[0],
            tokens_ref[m * BLK : (m + 1) * BLK],
            LAST,
            preferred_element_type=jnp.float32,
        )
    for core_bit, out_ref in ((1, send_ref), (0, keep_ref)):
        for chip_bits in range(index.chips):
            for i in range(index.per_part):
                block = index.block(core_bit, chip_bits, i)
                mine = index.owner(block) == index.place
                out_ref[chip_bits, i] = jnp.where(mine, low[index.slot(block)], 0.0)
    for i in range(index.per_part):
        adapter = index.owner(index.block(0, 0, i))
        back_ref[i] = lax.dot_general(
            up_ref[adapter],
            cot_ref[i * BLK : (i + 1) * BLK],
            LAST,
            preferred_element_type=jnp.float32,
        )


def narrow(index_of, index, shape, tokens, down, cotangent, up, waits):
    rank = up.shape[1]
    one = (shape.per_part, rank, BLK)
    outs = [(shape.chips,) + one, (shape.chips,) + one, one]
    operands = (tokens, down, cotangent, up)
    specs, extra = after(waits)
    return pl.pallas_call(
        functools.partial(narrow_kernel, index_of),
        grid_spec=pltpu.PrefetchScalarGridSpec(
            num_scalar_prefetch=1,
            grid=(1,),
            in_specs=[held()] + [whole(o.shape) for o in operands[1:]] + specs,
            out_specs=[whole(o) for o in outs],
            scratch_shapes=[pltpu.VMEM((CAP, rank, BLK), jnp.float32)],
        ),
        out_shape=[shape_of(o, jnp.float32) for o in outs],
        compiler_params=SMALL,
        cost_estimate=BRIEF,
        name="narrow",
    )(index, *operands, *extra)


def merge_kernel(keep_ref, arrived_ref, back_ref, *refs):
    out_ref = refs[-1]
    total = keep_ref[0] + arrived_ref[0]
    for ref in refs[:-1][: keep_ref.shape[0] - 1]:
        total = total + ref[...]
    out_ref[0] = total
    out_ref[1] = back_ref[...]


def merge(keep, arrived, back, others, waits):
    specs, extra = after(waits)
    operands = (keep, arrived, back, *others)
    out = (2,) + back.shape
    return pl.pallas_call(
        merge_kernel,
        grid=(1,),
        in_specs=[whole(o.shape) for o in operands] + specs,
        out_specs=whole(out),
        out_shape=shape_of(out, jnp.float32),
        compiler_params=SMALL,
        cost_estimate=BRIEF,
        name="merge",
    )(*operands, *extra)


def pieces_kernel(index_of, index_ref, sum_ref, more_ref, cot_ref, low_ref, back_ref, piece_ref):
    index = index_of(index_ref)
    for i in range(index.per_part):
        live = index.live_rows(index.block(0, 0, i))
        keep = lax.broadcasted_iota(jnp.int32, low_ref.shape[1:], 1) < live
        lowered = jnp.where(keep, sum_ref[0, i] + more_ref[0, i], 0.0).astype(low_ref.dtype)
        back = jnp.where(keep, sum_ref[1, i] + more_ref[1, i], 0.0)
        low_ref[i] = lowered
        back_ref[i] = back.astype(back_ref.dtype)
        piece_ref[i] = jnp.dot(
            lowered, cot_ref[i * BLK : (i + 1) * BLK], preferred_element_type=jnp.float32
        ).astype(piece_ref.dtype)


def make_pieces(index_of, index, shape, total, more, cotangent):
    _, per_part, rank, _ = total.shape
    width = cotangent.shape[1]
    outs = [(per_part, rank, BLK), (per_part, rank, BLK), (per_part, rank, width)]
    operands = (total, more, cotangent)
    return pl.pallas_call(
        functools.partial(pieces_kernel, index_of),
        grid_spec=pltpu.PrefetchScalarGridSpec(
            num_scalar_prefetch=1,
            grid=(1,),
            in_specs=[whole(o.shape) for o in operands],
            out_specs=[whole(o) for o in outs],
        ),
        out_shape=[shape_of(o, jnp.bfloat16) for o in outs],
        compiler_params=SMALL,
        cost_estimate=BRIEF,
        name="pieces",
    )(index, *operands)


def down_gradient_kernel(index_of, index_ref, tokens_ref, *refs):
    back_refs, out_ref = refs[:-1], refs[-1]
    index = index_of(index_ref)
    out_ref[...] = jnp.zeros_like(out_ref)
    for core_bit in range(CORES):
        for chip_bits in range(index.chips):
            for i in range(index.per_part):
                block = index.block(core_bit, chip_bits, i)
                back_ref = back_refs[core_bit * index.chips + chip_bits]

                @pl.when(index.owner(block) == index.place)
                def _(block=block, back_ref=back_ref, i=i):
                    at = pl.multiple_of(index.slot(block) * BLK, BLK)
                    out_ref[0] += adapter_scale * jnp.dot(
                        back_ref[i],
                        tokens_ref[pl.ds(at, BLK)],
                        preferred_element_type=jnp.float32,
                    )


def down_gradient(index_of, index, tokens, backs):
    out = (1, backs[0].shape[1], tokens.shape[1])
    operands = (tokens, *backs)
    return pl.pallas_call(
        functools.partial(down_gradient_kernel, index_of),
        grid_spec=pltpu.PrefetchScalarGridSpec(
            num_scalar_prefetch=1,
            grid=(1,),
            in_specs=[held()] + [whole(o.shape) for o in backs],
            out_specs=whole(out),
        ),
        out_shape=shape_of(out, jnp.float32),
        compiler_params=SMALL,
        cost_estimate=BRIEF,
        name="down_gradient",
    )(index, *operands)


def up_gradient_kernel(index_of, index_ref, *refs):
    piece_refs, out_ref = refs[:-1], refs[-1]
    index = index_of(index_ref)

    def of_device(core_bit, chip_bits, adapter):
        total = None
        for i in range(index.per_part):
            mine = index.owner(index.block(core_bit, chip_bits, i)) == adapter
            piece = piece_refs[core_bit * index.chips + chip_bits][i].astype(jnp.float32)
            term = jnp.where(mine, piece, 0.0)
            total = term if total is None else total + term
        return total

    for adapter in range(index.adapters):
        level = [
            of_device(0, j, adapter) + of_device(1, j, adapter) for j in range(index.chips)
        ]
        while len(level) > 1:
            level = [level[j] + level[j + 1] for j in range(0, len(level), 2)]
        out_ref[adapter] = adapter_scale * level[0]


def up_gradient(index_of, index, adapter_count, pieces):
    per_part, rank, width = pieces[0].shape
    tile = 1024
    out = (adapter_count, rank, width)
    return pl.pallas_call(
        functools.partial(up_gradient_kernel, index_of),
        grid_spec=pltpu.PrefetchScalarGridSpec(
            num_scalar_prefetch=1,
            grid=(width // tile,),
            in_specs=[pl.BlockSpec((per_part, rank, tile), lambda n, _: (0, 0, n))] * len(pieces),
            out_specs=pl.BlockSpec((adapter_count, rank, tile), lambda n, _: (0, 0, n)),
        ),
        out_shape=shape_of(out, jnp.float32),
        compiler_params=SMALL,
        cost_estimate=BRIEF,
        name="up_gradient",
    )(index, *pieces)


def finish_kernel(index_of, layout, tiles, terms, index_ref, low_ref, *refs):
    index = index_of(index_ref)
    up_refs, sum_refs, out_ref = refs[: index.per_part], refs[index.per_part : -1], refs[-1]
    step = pl.program_id(0)
    for i in range(index.per_part):
        block = index.block(0, 0, i)
        live = index.live_rows(block)
        side = lax.dot_general(
            low_ref[i],
            up_refs[i][0],
            (((0,), (0,)), ((), ())),
            preferred_element_type=jnp.float32,
        )
        start, at_ref = 0, 0
        for count, spans in layout:
            for p in range(tiles // spans):
                parts = sum_refs[at_ref : at_ref + terms]
                at_ref += terms

                @pl.when(step // spans == p)
                def _(parts=parts, start=start, count=count):
                    total = adapter_scale * side[start : start + count]
                    for ref in parts:
                        total = total + ref[i * count : (i + 1) * count].astype(jnp.float32)
                    keep = start + lax.broadcasted_iota(jnp.int32, total.shape, 0) < live
                    at = i * BLK + start
                    out_ref[at : at + count] = jnp.where(keep, total, 0.0).astype(out_ref.dtype)

            start += count


def finish(index_of, index, lowered, up, sums, part, part_count, projected, far):
    per_part = lowered.shape[0]
    _, rank, width = up.shape
    tile = width // max(PARTS)
    tiles = width // part_count // tile
    first = part * tiles
    out = (per_part * BLK, width)

    def factor(i):
        def at(n, index_ref):
            index = index_of(index_ref)
            return (index.owner(index.block(0, 0, i)), 0, first + n)

        return pl.BlockSpec((1, rank, tile), at)

    specs, flat, layout = [], [], []
    for chunk, count in zip(sums, CHUNK_ROWS):
        each = max(1, len(chunk) // part_count)
        begin = part * len(chunk) // part_count
        spans = tiles // each
        layout.append((count, spans))
        for p in range(each):
            offset = first - begin * (width // len(chunk) // tile) - p * spans
            limit = width // len(chunk) // tile - 1
            for value in chunk[begin + p]:
                specs.append(
                    pl.BlockSpec(
                        (per_part * count, tile),
                        lambda n, _, o=offset, m=limit: (0, jnp.clip(o + n, 0, m)),
                    )
                )
                flat.append(value)
    terms = len(sums[0][0])
    operands = [index, lowered, *[up] * per_part, *flat]
    aliases = {}
    if projected is not None:
        aliases = {len(operands): 0}
        far = [projected]
    more, extra = after((), far)
    if projected is not None:
        extra = [projected]

    def kernel(*refs):
        finish_kernel(index_of, layout, tiles, terms, *refs[: len(operands)], refs[-1])

    return pl.pallas_call(
        kernel,
        grid_spec=pltpu.PrefetchScalarGridSpec(
            num_scalar_prefetch=1,
            grid=(tiles,),
            in_specs=[whole(lowered.shape)] + [factor(i) for i in range(per_part)] + specs + more,
            out_specs=pl.BlockSpec((out[0], tile), lambda n, _: (0, first + n)),
        ),
        out_shape=shape_of(out, jnp.bfloat16),
        input_output_aliases=aliases,
        compiler_params=SMALL,
        cost_estimate=BRIEF,
        name="finish",
    )(*operands, *extra)


def per_device(
    tokens,
    cotangent,
    frozen_up_weight,
    adapter_down_factor,
    adapter_up_factor,
    tokens_per_adapter,
    adapter_of_block,
    slot_of_block,
):
    owners = lax.axis_size("dp")
    parts = lax.axis_size("tensor")
    chips = parts // CORES
    block_count = adapter_of_block.shape[0]
    adapter_count = adapter_up_factor.shape[0]
    width_dev = tokens.shape[1]
    index_of = functools.partial(
        Index, block_count=block_count, adapter_count=adapter_count, parts=parts
    )
    shape = index_of(None)
    index = Index.pack(adapter_of_block, slot_of_block, tokens_per_adapter)

    def to_other_core(value):
        return lax.ppermute(value, "tensor", [(i, i ^ 1) for i in range(parts)])

    def to_chip(value, k):
        return lax.ppermute(value, "tensor", [(i, i ^ (k * CORES)) for i in range(parts)])

    def across_dp(value, k):
        return lax.ppermute(value, "dp", [(i, i ^ k) for i in range(owners)])

    def same_core(value):
        return [value] + [to_chip(value, k) for k in range(1, chips)]

    def with_other_core(values):
        return values + [to_other_core(v) for v in values]

    rows_here = in_vmem(tokens)

    def small_products(waits):
        return narrow(
            index_of,
            index,
            shape,
            rows_here,
            jnp.swapaxes(adapter_down_factor, 1, 2),
            cotangent,
            adapter_up_factor,
            waits,
        )

    def over_parts(send, keep):
        arrived = to_other_core(send)
        return arrived, [to_chip(keep[k] + arrived[k], k) for k in range(1, chips)]

    def halfway_over_dp(total):
        k = 1
        while 2 * k < owners:
            total = total + across_dp(total, k)
            k *= 2
        return total

    def over_dp(total):
        return make_pieces(
            index_of, index, shape, total, across_dp(total, owners // 2), cotangent
        )

    if owners == 4 and block_count == 4:
        relay = Relay(index_of, index, rows_here)
        sent = relay.first()
        send, keep, back = small_products([sent])
        arrived, others = over_parts(send, keep)
        sent = relay.second(others)
        weight = load_weight(frozen_up_weight, [sent])
        total = halfway_over_dp(merge(keep, arrived, back, others, [sent]))
        relay.settle([weight, total])
        lowered, back_rows, pieces = over_dp(total)
        pieces_same_core = same_core(pieces)
        ahead = [v for chunk in relay.arrived[1:] for v in chunk[3:5]]
        chunks = [relay.rows(0, [lowered, *pieces_same_core[1:], *ahead])]
        chunks += [relay.rows(c) for c in range(1, len(CHUNK_ROWS))]
    else:
        weight = load_weight(frozen_up_weight, [])
        send, keep, back = small_products([])
        arrived, others = over_parts(send, keep)
        total = halfway_over_dp(merge(keep, arrived, back, others, []))
        lowered, back_rows, pieces = over_dp(total)
        pieces_same_core = same_core(pieces)
        every_slot = lax.all_gather(
            tokens.reshape(CAP, BLK, width_dev), "dp", axis=0, tiled=True
        )
        part = lax.axis_index("tensor")
        devices = jnp.arange(parts, dtype=jnp.int32)
        order = (devices // chips ^ 1) + (devices % chips) * CORES ^ part
        blocks = (order[:, None] * shape.per_part + jnp.arange(shape.per_part)).reshape(-1)
        picked = every_slot[adapter_of_block[blocks] * CAP + slot_of_block[blocks]]
        starts = [sum(CHUNK_ROWS[:c]) for c in range(len(CHUNK_ROWS))]
        chunks = [
            picked[:, s : s + count].reshape(-1, width_dev)
            for s, count in zip(starts, CHUNK_ROWS)
        ]
    def summed(rows, part, part_count, waits):
        each = rows.shape[0] // parts
        send, other, own = split_product(shape, rows, weight, part, part_count, waits)
        arrived = to_other_core(send)
        outgoing = (other + arrived[each:].astype(jnp.float32)).astype(jnp.bfloat16)
        return [own, arrived] + [
            to_chip(outgoing[(k - 1) * each : k * each], k) for k in range(1, chips)
        ]

    sums, waits = [], []
    for rows, part_count in zip(chunks, PARTS):
        sums.append([])
        for part in range(part_count):
            sums[-1].append(summed(rows, part, part_count, waits))
            waits = []
        waits = [v for terms in sums[-1] for v in terms[2:]]
    up_grad = up_gradient(index_of, index, adapter_count, with_other_core(pieces_same_core))
    down_grad = down_gradient(index_of, index, rows_here, with_other_core(same_core(back_rows)))
    projected = None
    for part in range(PARTS[-1]):
        projected = finish(
            index_of,
            index,
            lowered,
            adapter_up_factor,
            sums,
            part,
            PARTS[-1],
            projected,
            [up_grad, down_grad],
        )
    return (projected, jnp.swapaxes(down_grad, 1, 2), up_grad)


def solution(mesh):
    return jax.shard_map(
        per_device,
        mesh=mesh,
        in_specs=(
            P(("groups", "dp"), "tensor"),
            P(("groups", "tensor"), "dp"),
            P("tensor", "dp"),
            P(("groups", "dp"), "tensor", None),
            P("groups", None, "dp"),
            P("groups"),
            P("groups"),
            P("groups"),
        ),
        out_specs=(
            P(("groups", "tensor"), "dp"),
            P(("groups", "dp"), "tensor", None),
            P("groups", None, "dp"),
        ),
        check_vma=False,
    )
```

```python
import functools

import jax
import jax.numpy as jnp
from jax import lax
from jax.experimental import pallas as pl
from jax.experimental.pallas import tpu as pltpu
from jax.sharding import PartitionSpec as P

BLK = 128
CAP = 3
CORES = 2
CHUNK_ROWS = (64, 64)
PARTS = 2
SMALL = pltpu.CompilerParams(vmem_limit_bytes=12 * 2**20)

adapter_scale = 0.5

LAST = (((1,), (1,)), ((), ()))


class Index:
    def __init__(self, ref, block_count, adapter_count, parts):
        self.ref = ref
        self.blocks, self.adapters, self.parts = block_count, adapter_count, parts
        self.chips = parts // CORES
        self.per_part = block_count // parts

    @staticmethod
    def pack(adapter_of_block, slot_of_block, tokens_per_adapter):
        place = jnp.stack([lax.axis_index("dp"), lax.axis_index("tensor")]).astype(jnp.int32)
        return jnp.concatenate([adapter_of_block, slot_of_block, tokens_per_adapter, place])

    def owner(self, block):
        return self.ref[block]

    def slot(self, block):
        return self.ref[self.blocks + block]

    def tokens(self, adapter):
        return self.ref[2 * self.blocks + adapter]

    @property
    def place(self):
        return self.ref[2 * self.blocks + self.adapters]

    @property
    def part(self):
        return self.ref[2 * self.blocks + self.adapters + 1]

    def block(self, core_bit, chip_bits, i):
        return (self.part ^ (chip_bits * CORES + core_bit)) * self.per_part + i

    def position(self, block):
        bits = (block // self.per_part) ^ self.part
        half = (1 - bits % CORES) * self.chips + bits // CORES
        return half * self.per_part + block % self.per_part

    def live_rows(self, block):
        adapter = self.owner(block)
        first = jnp.int32(0)
        for a in range(self.adapters):
            count = (self.tokens(a) + BLK - 1) // BLK
            first = first + jnp.where(a < adapter, count, 0)
        return self.tokens(adapter) - (block - first) * BLK


def in_vmem(value):
    return pltpu.with_memory_space_constraint(value, pltpu.VMEM)


def in_hbm(value):
    return pltpu.with_memory_space_constraint(value, pltpu.HBM)


def held():
    return pl.BlockSpec(memory_space=pltpu.VMEM)


def whole(shape):
    return pl.BlockSpec(shape, lambda *_: (0,) * len(shape))


def shape_of(shape, dtype):
    return jax.ShapeDtypeStruct(shape, dtype)


BRIEF = pl.CostEstimate(flops=1, bytes_accessed=1, transcendentals=0)


def own_rows(index, block, tokens_ref, out_ref, start=0):
    at = pl.multiple_of(index.slot(block) * BLK + start, 16)
    out_ref[...] = tokens_ref[pl.ds(at, out_ref.shape[0])]


def first_hop_kernel(index_of, index_ref, tokens_ref, *refs):
    a_ref, b_ref, sems = refs[-3:]
    index = index_of(index_ref)
    copies = [
        pltpu.make_async_copy(
            tokens_ref.at[pl.ds(pl.multiple_of(index.slot(block) * BLK, BLK), BLK)],
            out_ref,
            sems.at[i],
        )
        for i, (block, out_ref) in enumerate(
            ((jnp.where(index.place == 0, 2, 1), a_ref), (0, b_ref))
        )
    ]
    for copy in copies:
        copy.start()
    for copy in copies:
        copy.wait()


def second_hop_kernel(index_of, index_ref, tokens_ref, a_ref, b_ref, *refs):
    x_ref, y_ref = refs[-2:]
    index = index_of(index_ref)
    place = index.place
    outer = jnp.where(place == 0, 1, jnp.where(place == 1, 0, 2))
    middle = jnp.where(place == 1, 2, 1)
    own_rows(index, outer, tokens_ref, x_ref)
    own_rows(index, middle, tokens_ref, y_ref)

    @pl.when((place == 1) & (index.owner(0) != 1))
    def _():
        x_ref[...] = b_ref[...]

    @pl.when(((place == 1) | (place == 2)) & (index.owner(middle) != place))
    def _():
        y_ref[...] = a_ref[...]


def settle_kernel(index_of, index_ref, tokens_ref, x_ref, y_ref, *refs):
    out_refs = refs[-len(CHUNK_ROWS) :]
    index = index_of(index_ref)
    place = index.place
    owner = index.owner(place)
    mine = owner == place
    edge = (place == 0) | ((place == 1) & (owner == 0)) | ((place == 2) & (owner == 3))
    start = 0
    for out_ref in out_refs:
        rows = slice(start, start + out_ref.shape[0])
        own_rows(index, place, tokens_ref, out_ref, start)

        @pl.when(jnp.logical_not(mine) & edge)
        def _(out_ref=out_ref, rows=rows):
            out_ref[...] = x_ref[rows]

        @pl.when(jnp.logical_not(mine | edge))
        def _(out_ref=out_ref, rows=rows):
            out_ref[...] = y_ref[rows]

        start += out_ref.shape[0]


def collect_kernel(index_of, count, index_ref, home_ref, outer_ref, *refs):
    inner_refs, outer_refs, out_ref = refs[:2], refs[2:4], refs[-1]
    index = index_of(index_ref)
    place = index.place

    def put(block, ref):
        at = pl.multiple_of(index.position(block) * count, 16)
        out_ref[pl.ds(at, count)] = ref[...]

    put(place, home_ref)
    put(place ^ 1, outer_ref)
    middle = (place == 1) | (place == 2)

    @pl.when(middle)
    def _():
        put(3 - place, inner_refs[0])
        put(place ^ 2, inner_refs[1])

    @pl.when(jnp.logical_not(middle))
    def _():
        put(place ^ 2, outer_refs[0])
        put(3 - place, outer_refs[1])


def after(values, far=()):
    specs = [
        pl.BlockSpec((1,) * (v.ndim - 2) + (16, 128), lambda *_, n=v.ndim: (0,) * n) for v in values
    ] + [pl.BlockSpec(memory_space=pl.ANY)] * len(far)
    return specs, [*values, *(in_hbm(v) for v in far)]


def hop_call(kernel, index, tokens, heights, received, waits, name):
    specs, extra = after(waits)
    width = tokens.shape[1]
    first = not received
    return pl.pallas_call(
        kernel,
        grid_spec=pltpu.PrefetchScalarGridSpec(
            num_scalar_prefetch=1,
            grid=(1,),
            in_specs=[pl.BlockSpec(memory_space=pl.ANY) if first else held()]
            + [held()] * len(received)
            + specs,
            out_specs=[held()] * len(heights),
            scratch_shapes=[pltpu.SemaphoreType.DMA((len(heights),))] * first,
        ),
        out_shape=[pltpu.VMEM((height, width), tokens.dtype) for height in heights],
        compiler_params=SMALL,
        cost_estimate=BRIEF,
        name=name,
    )(index, (in_hbm if first else in_vmem)(tokens), *[in_vmem(r) for r in received], *extra)


class Relay:
    def __init__(self, index_of, index, tokens):
        self.index_of, self.index, self.tokens = index_of, index, tokens

    def call(self, kernel, heights, received, waits, name):
        kernel = functools.partial(kernel, self.index_of)
        return hop_call(kernel, self.index, self.tokens, heights, received, waits, name)

    def first(self, waits=()):
        inward, left = self.call(first_hop_kernel, (BLK, BLK), (), waits, "first_hop")
        self.received = (
            lax.ppermute(inward, "dp", [(3, 2), (0, 1)]),
            lax.ppermute(left, "dp", [(2, 1)]),
        )
        return inward

    def second(self, waits=()):
        outer, middle = self.call(
            second_hop_kernel, (BLK, BLK), self.received, waits, "second_hop"
        )
        self.received = (
            lax.ppermute(outer, "dp", [(1, 0), (0, 1), (3, 2)]),
            lax.ppermute(middle, "dp", [(2, 1), (1, 2)]),
        )
        return outer

    def settle(self, waits=()):
        homes = self.call(settle_kernel, CHUNK_ROWS, self.received, waits, "settle")
        self.arrived = [self.spread(home) for home in homes]

    def spread(self, home):
        outer = lax.ppermute(home, "dp", [(0, 1), (1, 0), (2, 3), (3, 2)])
        inner = lax.ppermute(home, "dp", [(1, 2), (2, 1)])
        outer_2 = lax.ppermute(inner, "dp", [(1, 0), (2, 3)])
        inner_2 = lax.ppermute(outer, "dp", [(1, 2), (2, 1)])
        outer_3 = lax.ppermute(inner_2, "dp", [(1, 0), (2, 3)])
        return home, outer, inner, inner_2, outer_2, outer_3

    def rows(self, chunk, waits=(), far=()):
        arrived = self.arrived[chunk]
        count, width = arrived[0].shape
        specs, extra = after(waits, far)
        return pl.pallas_call(
            functools.partial(collect_kernel, self.index_of, count),
            grid_spec=pltpu.PrefetchScalarGridSpec(
                num_scalar_prefetch=1,
                grid=(1,),
                in_specs=[held()] * len(arrived) + specs,
                out_specs=held(),
            ),
            out_shape=pltpu.VMEM((4 * count, width), self.tokens.dtype),
            compiler_params=SMALL,
            cost_estimate=BRIEF,
            name="collect",
        )(self.index, *[in_vmem(a) for a in arrived], *extra)


def load_weight_kernel(w_ref, *refs):
    out_ref, sems = refs[-2:]
    streams = sems.shape[0]
    depth = w_ref.shape[0] // streams
    copies = [
        pltpu.make_async_copy(
            w_ref.at[pl.ds(i * depth, depth)], out_ref.at[pl.ds(i * depth, depth)], sems.at[i]
        )
        for i in range(streams)
    ]
    for copy in copies:
        copy.start()
    for copy in copies:
        copy.wait()


def load_weight(weight, waits):
    specs, extra = after(waits)
    return pl.pallas_call(
        load_weight_kernel,
        grid=(1,),
        in_specs=[pl.BlockSpec(memory_space=pl.ANY)] + specs,
        out_specs=pl.BlockSpec(memory_space=pl.ANY),
        out_shape=pltpu.VMEM(weight.shape, weight.dtype),
        scratch_shapes=[pltpu.SemaphoreType.DMA((4,))],
        compiler_params=SMALL,
        cost_estimate=BRIEF,
        name="load_weight",
    )(in_hbm(weight), *extra)


def split_product_kernel(each, half, first, tile, rows_ref, w_ref, *refs):
    send_ref, other_ref, own_ref = refs[-3:]
    for n in range(own_ref.shape[1] // tile):
        total = jnp.dot(
            rows_ref[...],
            w_ref[:, first + n * tile : first + (n + 1) * tile],
            preferred_element_type=jnp.float32,
        )
        columns = slice(n * tile, (n + 1) * tile)
        send_ref[:, columns] = total[:half].astype(send_ref.dtype)
        own_ref[:, columns] = total[half : half + each]
        other_ref[:, columns] = total[half + each :]


def split_product(shape, rows, weight, part, part_count, waits):
    half = rows.shape[0] // 2
    each = half // shape.chips
    width = weight.shape[1] // part_count
    specs, extra = after(waits)
    return pl.pallas_call(
        functools.partial(split_product_kernel, each, half, part * width, min(512, width)),
        grid=(1,),
        in_specs=[held(), held()] + specs,
        out_specs=[held()] * 3,
        out_shape=[
            pltpu.VMEM((half, width), jnp.bfloat16),
            pltpu.VMEM((half - each, width), jnp.float32),
            pltpu.VMEM((each, width), jnp.float32),
        ],
        compiler_params=SMALL,
        cost_estimate=BRIEF,
        name="split_product",
    )(in_vmem(rows), in_vmem(weight), *extra)


def narrow_kernel(index_of, index_ref, tokens_ref, down_ref, cot_ref, up_ref, *refs):
    send_ref, keep_ref, back_ref, low = refs[-4:]
    index = index_of(index_ref)
    for m in range(CAP):
        low[m] = lax.dot_general(
            down_ref[0],
            tokens_ref[m * BLK : (m + 1) * BLK],
            LAST,
            preferred_element_type=jnp.float32,
        )
    for core_bit, out_ref in ((1, send_ref), (0, keep_ref)):
        for chip_bits in range(index.chips):
            for i in range(index.per_part):
                block = index.block(core_bit, chip_bits, i)
                mine = index.owner(block) == index.place
                out_ref[chip_bits, i] = jnp.where(mine, low[index.slot(block)], 0.0)
    for i in range(index.per_part):
        adapter = index.owner(index.block(0, 0, i))
        back_ref[i] = lax.dot_general(
            up_ref[adapter],
            cot_ref[i * BLK : (i + 1) * BLK],
            LAST,
            preferred_element_type=jnp.float32,
        )


def narrow(index_of, index, shape, tokens, down, cotangent, up, waits):
    rank = up.shape[1]
    one = (shape.per_part, rank, BLK)
    outs = [(shape.chips,) + one, (shape.chips,) + one, one]
    operands = (in_vmem(tokens), down, cotangent, up)
    specs, extra = after(waits)
    return pl.pallas_call(
        functools.partial(narrow_kernel, index_of),
        grid_spec=pltpu.PrefetchScalarGridSpec(
            num_scalar_prefetch=1,
            grid=(1,),
            in_specs=[held()] + [whole(o.shape) for o in operands[1:]] + specs,
            out_specs=[whole(o) for o in outs],
            scratch_shapes=[pltpu.VMEM((CAP, rank, BLK), jnp.float32)],
        ),
        out_shape=[shape_of(o, jnp.float32) for o in outs],
        compiler_params=SMALL,
        cost_estimate=BRIEF,
        name="narrow",
    )(index, *operands, *extra)


def merge_kernel(keep_ref, arrived_ref, back_ref, *refs):
    out_ref = refs[-1]
    total = keep_ref[0] + arrived_ref[0]
    for ref in refs[:-1][: keep_ref.shape[0] - 1]:
        total = total + ref[...]
    out_ref[0] = total
    out_ref[1] = back_ref[...]


def merge(keep, arrived, back, others, waits):
    specs, extra = after(waits)
    operands = (keep, arrived, back, *others)
    out = (2,) + back.shape
    return pl.pallas_call(
        merge_kernel,
        grid=(1,),
        in_specs=[whole(o.shape) for o in operands] + specs,
        out_specs=whole(out),
        out_shape=shape_of(out, jnp.float32),
        compiler_params=SMALL,
        cost_estimate=BRIEF,
        name="merge",
    )(*operands, *extra)


def pieces_kernel(index_of, count, index_ref, cot_ref, sum_ref, *refs):
    more_refs, (low_ref, back_ref, piece_ref) = refs[:count], refs[-3:]
    index = index_of(index_ref)
    level = [sum_ref[...]] + [ref[...] for ref in more_refs]
    while len(level) > 1:
        level = [level[j] + level[j + 1] for j in range(0, len(level), 2)]
    for i in range(index.per_part):
        live = index.live_rows(index.block(0, 0, i))
        keep = lax.broadcasted_iota(jnp.int32, low_ref.shape[1:], 1) < live
        lowered = jnp.where(keep, level[0][0, i], 0.0).astype(low_ref.dtype)
        low_ref[i] = lowered
        back_ref[i] = jnp.where(keep, level[0][1, i], 0.0).astype(back_ref.dtype)
        piece_ref[i] = jnp.dot(
            lowered, cot_ref[i * BLK : (i + 1) * BLK], preferred_element_type=jnp.float32
        ).astype(piece_ref.dtype)


def make_pieces(index_of, index, shape, total, more, cotangent, waits):
    _, per_part, rank, _ = total.shape
    width = cotangent.shape[1]
    outs = [(per_part, rank, BLK), (per_part, rank, BLK), (per_part, rank, width)]
    operands = (cotangent, total, *more)
    specs, extra = after(waits)
    return pl.pallas_call(
        functools.partial(pieces_kernel, index_of, len(more)),
        grid_spec=pltpu.PrefetchScalarGridSpec(
            num_scalar_prefetch=1,
            grid=(1,),
            in_specs=[whole(o.shape) for o in operands] + specs,
            out_specs=[whole(o) for o in outs],
        ),
        out_shape=[shape_of(o, jnp.bfloat16) for o in outs],
        compiler_params=SMALL,
        cost_estimate=BRIEF,
        name="pieces",
    )(index, *operands, *extra)


def down_gradient_kernel(index_of, index_ref, tokens_ref, *refs):
    back_refs, out_ref = refs[:-1], refs[-1]
    index = index_of(index_ref)
    out_ref[...] = jnp.zeros_like(out_ref)
    for core_bit in range(CORES):
        for chip_bits in range(index.chips):
            for i in range(index.per_part):
                block = index.block(core_bit, chip_bits, i)
                back_ref = back_refs[core_bit * index.chips + chip_bits]

                @pl.when(index.owner(block) == index.place)
                def _(block=block, back_ref=back_ref, i=i):
                    at = pl.multiple_of(index.slot(block) * BLK, BLK)
                    out_ref[0] += adapter_scale * jnp.dot(
                        back_ref[i],
                        tokens_ref[pl.ds(at, BLK)],
                        preferred_element_type=jnp.float32,
                    )


def down_gradient(index_of, index, tokens, backs):
    out = (1, backs[0].shape[1], tokens.shape[1])
    operands = (in_vmem(tokens), *backs)
    return pl.pallas_call(
        functools.partial(down_gradient_kernel, index_of),
        grid_spec=pltpu.PrefetchScalarGridSpec(
            num_scalar_prefetch=1,
            grid=(1,),
            in_specs=[held()] + [whole(o.shape) for o in backs],
            out_specs=whole(out),
        ),
        out_shape=shape_of(out, jnp.float32),
        compiler_params=SMALL,
        cost_estimate=BRIEF,
        name="down_gradient",
    )(index, *operands)


def up_gradient_kernel(index_of, index_ref, *refs):
    piece_refs, out_ref = refs[:-1], refs[-1]
    index = index_of(index_ref)

    def of_device(core_bit, chip_bits, adapter):
        total = None
        for i in range(index.per_part):
            mine = index.owner(index.block(core_bit, chip_bits, i)) == adapter
            piece = piece_refs[core_bit * index.chips + chip_bits][i].astype(jnp.float32)
            term = jnp.where(mine, piece, 0.0)
            total = term if total is None else total + term
        return total

    for adapter in range(index.adapters):
        level = [
            of_device(0, j, adapter) + of_device(1, j, adapter) for j in range(index.chips)
        ]
        while len(level) > 1:
            level = [level[j] + level[j + 1] for j in range(0, len(level), 2)]
        out_ref[adapter] = adapter_scale * level[0]


def up_gradient(index_of, index, adapter_count, pieces):
    per_part, rank, width = pieces[0].shape
    tile = 1024
    out = (adapter_count, rank, width)
    return pl.pallas_call(
        functools.partial(up_gradient_kernel, index_of),
        grid_spec=pltpu.PrefetchScalarGridSpec(
            num_scalar_prefetch=1,
            grid=(width // tile,),
            in_specs=[pl.BlockSpec((per_part, rank, tile), lambda n, _: (0, 0, n))] * len(pieces),
            out_specs=pl.BlockSpec((adapter_count, rank, tile), lambda n, _: (0, 0, n)),
        ),
        out_shape=shape_of(out, jnp.float32),
        compiler_params=SMALL,
        cost_estimate=BRIEF,
        name="up_gradient",
    )(index, *pieces)


def finish_kernel(index_of, index_ref, low_ref, *refs):
    index = index_of(index_ref)
    up_refs, sum_refs, out_ref = refs[: index.per_part], refs[index.per_part : -1], refs[-1]
    per_chunk = len(sum_refs) // len(CHUNK_ROWS)
    for i in range(index.per_part):
        block = index.block(0, 0, i)
        live = index.live_rows(block)
        side = lax.dot_general(
            low_ref[i],
            up_refs[i][0],
            (((0,), (0,)), ((), ())),
            preferred_element_type=jnp.float32,
        )
        start = 0
        for c, count in enumerate(CHUNK_ROWS):
            total = adapter_scale * side[start : start + count]
            for ref in sum_refs[c * per_chunk : (c + 1) * per_chunk]:
                total = total + ref[i * count : (i + 1) * count].astype(jnp.float32)
            keep = start + lax.broadcasted_iota(jnp.int32, total.shape, 0) < live
            at = i * BLK + start
            out_ref[at : at + count] = jnp.where(keep, total, 0.0).astype(out_ref.dtype)
            start += count


def finish(index_of, index, lowered, up, sums, part, projected):
    per_part = lowered.shape[0]
    _, rank, width = up.shape
    tile = min(1024, width // PARTS)
    tiles = width // PARTS // tile
    first = part * tiles
    out = (per_part * BLK, width)

    def factor(i):
        def at(n, index_ref):
            index = index_of(index_ref)
            return (index.owner(index.block(0, 0, i)), 0, first + n)

        return pl.BlockSpec((1, rank, tile), at)

    flat = [term for chunk in sums for term in chunk]
    specs = [
        pl.BlockSpec((per_part * count, tile), lambda n, _: (0, n))
        for chunk, count in zip(sums, CHUNK_ROWS)
        for _ in chunk
    ]
    operands = [index, lowered, *[up] * per_part, *flat]
    aliases, more, extra = {}, [], []
    if projected is not None:
        aliases = {len(operands): 0}
        more, extra = [pl.BlockSpec(memory_space=pl.ANY)], [projected]

    def kernel(*refs):
        finish_kernel(index_of, *refs[: len(operands)], refs[-1])

    return pl.pallas_call(
        kernel,
        grid_spec=pltpu.PrefetchScalarGridSpec(
            num_scalar_prefetch=1,
            grid=(tiles,),
            in_specs=[whole(lowered.shape)] + [factor(i) for i in range(per_part)] + specs + more,
            out_specs=pl.BlockSpec((out[0], tile), lambda n, _: (0, first + n)),
        ),
        out_shape=shape_of(out, jnp.bfloat16),
        input_output_aliases=aliases,
        compiler_params=SMALL,
        cost_estimate=BRIEF,
        name="finish",
    )(*operands, *extra)


def per_device(
    tokens,
    cotangent,
    frozen_up_weight,
    adapter_down_factor,
    adapter_up_factor,
    tokens_per_adapter,
    adapter_of_block,
    slot_of_block,
):
    owners = lax.axis_size("dp")
    parts = lax.axis_size("tensor")
    chips = parts // CORES
    block_count = adapter_of_block.shape[0]
    adapter_count = adapter_up_factor.shape[0]
    width_dev = tokens.shape[1]
    index_of = functools.partial(
        Index, block_count=block_count, adapter_count=adapter_count, parts=parts
    )
    shape = index_of(None)
    index = Index.pack(adapter_of_block, slot_of_block, tokens_per_adapter)

    def to_other_core(value):
        return lax.ppermute(value, "tensor", [(i, i ^ 1) for i in range(parts)])

    def to_chip(value, k):
        return lax.ppermute(value, "tensor", [(i, i ^ (k * CORES)) for i in range(parts)])

    def across_dp(value, k):
        return lax.ppermute(value, "dp", [(i, i ^ k) for i in range(owners)])

    def same_core(value):
        return [value] + [to_chip(value, k) for k in range(1, chips)]

    def with_other_core(values):
        return values + [to_other_core(v) for v in values]

    def small_products(waits):
        return narrow(
            index_of,
            index,
            shape,
            tokens,
            jnp.swapaxes(adapter_down_factor, 1, 2),
            cotangent,
            adapter_up_factor,
            waits,
        )

    def over_parts(send, keep):
        arrived = to_other_core(send)
        return arrived, [to_chip(keep[k] + arrived[k], k) for k in range(1, chips)]

    def over_dp(total):
        k = 1
        while True:
            more = [across_dp(total, j * k) for j in range(1, min(4, owners // k))]
            if k * 4 >= owners:
                return total, more
            total = (total + more[0]) + (more[1] + more[2])
            k *= 4

    def gradients(total, more, waits):
        lowered, back_rows, pieces = make_pieces(
            index_of, index, shape, total, more, cotangent, waits
        )
        pieces, back_rows = same_core(pieces), same_core(back_rows)
        return (
            lowered,
            up_gradient(index_of, index, adapter_count, with_other_core(pieces)),
            down_gradient(index_of, index, tokens, with_other_core(back_rows)),
        )

    if owners == 4 and block_count == 4:
        relay = Relay(index_of, index, tokens)
        sent = relay.first()
        send, keep, back = small_products([sent])
        arrived, others = over_parts(send, keep)
        sent = relay.second(others)
        weight = load_weight(frozen_up_weight, [sent])
        total, more = over_dp(merge(keep, arrived, back, others, [sent]))
        relay.settle([weight, *more])
        lowered, up_grad, down_grad = gradients(total, more, relay.arrived[0][1:3])
        ahead = [v for chunk in relay.arrived[1:] for v in chunk[3:5]]
        chunks = [lambda waits: relay.rows(0, ahead, [up_grad, down_grad])]
        chunks += [functools.partial(relay.rows, c) for c in range(1, len(CHUNK_ROWS))]
    else:
        weight = load_weight(frozen_up_weight, [])
        send, keep, back = small_products([])
        arrived, others = over_parts(send, keep)
        total, more = over_dp(merge(keep, arrived, back, others, []))
        lowered, up_grad, down_grad = gradients(total, more, [])
        every_slot = lax.all_gather(
            tokens.reshape(CAP, BLK, width_dev), "dp", axis=0, tiled=True
        )
        part = lax.axis_index("tensor")
        devices = jnp.arange(parts, dtype=jnp.int32)
        order = (devices // chips ^ 1) + (devices % chips) * CORES ^ part
        blocks = (order[:, None] * shape.per_part + jnp.arange(shape.per_part)).reshape(-1)
        picked = every_slot[adapter_of_block[blocks] * CAP + slot_of_block[blocks]]
        starts = [sum(CHUNK_ROWS[:c]) for c in range(len(CHUNK_ROWS))]
        chunks = [
            lambda waits, s=s, count=count: picked[:, s : s + count].reshape(-1, width_dev)
            for s, count in zip(starts, CHUNK_ROWS)
        ]
    def summed(rows, part, waits):
        each = rows.shape[0] // parts
        send, other, own = split_product(shape, rows, weight, part, PARTS, waits)
        arrived = to_other_core(send)
        outgoing = (other + arrived[each:].astype(jnp.float32)).astype(jnp.bfloat16)
        across = [to_chip(outgoing[(k - 1) * each : k * each], k) for k in range(1, chips)]
        return [own, arrived] + across, outgoing

    sums, rows, waits = [], [], []
    for chunk in chunks:
        rows.append(chunk(waits))
        sums.append([summed(rows[-1], 0, ())])
        waits = [sums[-1][0][1]]
    for part in range(1, PARTS):
        for chunk_rows, done in zip(rows, sums):
            done.append(summed(chunk_rows, part, rows[-1:]))
    projected = None
    for part in range(PARTS):
        projected = finish(
            index_of,
            index,
            lowered,
            adapter_up_factor,
            [done[part][0] for done in sums],
            part,
            projected,
        )
    return (projected, jnp.swapaxes(down_grad, 1, 2), up_grad)


def solution(mesh):
    return jax.shard_map(
        per_device,
        mesh=mesh,
        in_specs=(
            P(("groups", "dp"), "tensor"),
            P(("groups", "tensor"), "dp"),
            P("tensor", "dp"),
            P(("groups", "dp"), "tensor", None),
            P("groups", None, "dp"),
            P("groups"),
            P("groups"),
            P("groups"),
        ),
        out_specs=(
            P(("groups", "tensor"), "dp"),
            P(("groups", "dp"), "tensor", None),
            P("groups", None, "dp"),
        ),
        check_vma=False,
    )
```

```python
import functools

import jax
import jax.numpy as jnp
from jax import lax
from jax.experimental import pallas as pl
from jax.experimental.pallas import tpu as pltpu
from jax.sharding import PartitionSpec as P

BLK = 128
CAP = 3
CORES = 2
CHUNK_ROWS = (64, 64)
PARTS = 2
SMALL = pltpu.CompilerParams(vmem_limit_bytes=12 * 2**20)

adapter_scale = 0.5

LAST = (((1,), (1,)), ((), ()))


class Index:
    def __init__(self, ref, block_count, adapter_count, parts):
        self.ref = ref
        self.blocks, self.adapters, self.parts = block_count, adapter_count, parts
        self.chips = parts // CORES
        self.per_part = block_count // parts

    @staticmethod
    def pack(adapter_of_block, slot_of_block, tokens_per_adapter):
        place = jnp.stack([lax.axis_index("dp"), lax.axis_index("tensor")]).astype(jnp.int32)
        return jnp.concatenate([adapter_of_block, slot_of_block, tokens_per_adapter, place])

    def owner(self, block):
        return self.ref[block]

    def slot(self, block):
        return self.ref[self.blocks + block]

    def tokens(self, adapter):
        return self.ref[2 * self.blocks + adapter]

    @property
    def place(self):
        return self.ref[2 * self.blocks + self.adapters]

    @property
    def part(self):
        return self.ref[2 * self.blocks + self.adapters + 1]

    def block(self, core_bit, chip_bits, i):
        return (self.part ^ (chip_bits * CORES + core_bit)) * self.per_part + i

    def position(self, block):
        bits = (block // self.per_part) ^ self.part
        half = (1 - bits % CORES) * self.chips + bits // CORES
        return half * self.per_part + block % self.per_part

    def live_rows(self, block):
        adapter = self.owner(block)
        first = jnp.int32(0)
        for a in range(self.adapters):
            count = (self.tokens(a) + BLK - 1) // BLK
            first = first + jnp.where(a < adapter, count, 0)
        return self.tokens(adapter) - (block - first) * BLK


def in_vmem(value):
    return pltpu.with_memory_space_constraint(value, pltpu.VMEM)


def in_hbm(value):
    return pltpu.with_memory_space_constraint(value, pltpu.HBM)


def held():
    return pl.BlockSpec(memory_space=pltpu.VMEM)


def whole(shape):
    return pl.BlockSpec(shape, lambda *_: (0,) * len(shape))


def shape_of(shape, dtype):
    return jax.ShapeDtypeStruct(shape, dtype)


BRIEF = pl.CostEstimate(flops=1, bytes_accessed=1, transcendentals=0)


def own_rows(index, block, tokens_ref, out_ref, start=0):
    at = pl.multiple_of(index.slot(block) * BLK + start, 16)
    out_ref[...] = tokens_ref[pl.ds(at, out_ref.shape[0])]


def first_hop_kernel(index_of, index_ref, tokens_ref, *refs):
    a_ref, b_ref, sems = refs[-3:]
    index = index_of(index_ref)
    copies = [
        pltpu.make_async_copy(
            tokens_ref.at[pl.ds(pl.multiple_of(index.slot(block) * BLK, BLK), BLK)],
            out_ref,
            sems.at[i],
        )
        for i, (block, out_ref) in enumerate(
            ((jnp.where(index.place == 0, 2, 1), a_ref), (0, b_ref))
        )
    ]
    for copy in copies:
        copy.start()
    for copy in copies:
        copy.wait()


def second_hop_kernel(index_of, index_ref, tokens_ref, a_ref, b_ref, *refs):
    x_ref, y_ref = refs[-2:]
    index = index_of(index_ref)
    place = index.place
    outer = jnp.where(place == 0, 1, jnp.where(place == 1, 0, 2))
    middle = jnp.where(place == 1, 2, 1)
    own_rows(index, outer, tokens_ref, x_ref)
    own_rows(index, middle, tokens_ref, y_ref)

    @pl.when((place == 1) & (index.owner(0) != 1))
    def _():
        x_ref[...] = b_ref[...]

    @pl.when(((place == 1) | (place == 2)) & (index.owner(middle) != place))
    def _():
        y_ref[...] = a_ref[...]


def settle_kernel(index_of, index_ref, tokens_ref, x_ref, y_ref, *refs):
    out_refs = refs[-len(CHUNK_ROWS) :]
    index = index_of(index_ref)
    place = index.place
    owner = index.owner(place)
    mine = owner == place
    edge = (place == 0) | ((place == 1) & (owner == 0)) | ((place == 2) & (owner == 3))
    start = 0
    for out_ref in out_refs:
        rows = slice(start, start + out_ref.shape[0])
        own_rows(index, place, tokens_ref, out_ref, start)

        @pl.when(jnp.logical_not(mine) & edge)
        def _(out_ref=out_ref, rows=rows):
            out_ref[...] = x_ref[rows]

        @pl.when(jnp.logical_not(mine | edge))
        def _(out_ref=out_ref, rows=rows):
            out_ref[...] = y_ref[rows]

        start += out_ref.shape[0]


def collect_kernel(index_of, count, index_ref, home_ref, outer_ref, *refs):
    inner_refs, outer_refs, out_ref = refs[:2], refs[2:4], refs[-1]
    index = index_of(index_ref)
    place = index.place

    def put(block, ref):
        at = pl.multiple_of(index.position(block) * count, 16)
        out_ref[pl.ds(at, count)] = ref[...]

    put(place, home_ref)
    put(place ^ 1, outer_ref)
    middle = (place == 1) | (place == 2)

    @pl.when(middle)
    def _():
        put(3 - place, inner_refs[0])
        put(place ^ 2, inner_refs[1])

    @pl.when(jnp.logical_not(middle))
    def _():
        put(place ^ 2, outer_refs[0])
        put(3 - place, outer_refs[1])


def after(values, far=()):
    specs = [
        pl.BlockSpec((1,) * (v.ndim - 2) + (16, 128), lambda *_, n=v.ndim: (0,) * n) for v in values
    ] + [pl.BlockSpec(memory_space=pl.ANY)] * len(far)
    return specs, [*values, *(in_hbm(v) for v in far)]


def hop_call(kernel, index, tokens, heights, received, waits, name):
    specs, extra = after(waits)
    width = tokens.shape[1]
    first = not received
    return pl.pallas_call(
        kernel,
        grid_spec=pltpu.PrefetchScalarGridSpec(
            num_scalar_prefetch=1,
            grid=(1,),
            in_specs=[pl.BlockSpec(memory_space=pl.ANY) if first else held()]
            + [held()] * len(received)
            + specs,
            out_specs=[held()] * len(heights),
            scratch_shapes=[pltpu.SemaphoreType.DMA((len(heights),))] * first,
        ),
        out_shape=[pltpu.VMEM((height, width), tokens.dtype) for height in heights],
        compiler_params=SMALL,
        cost_estimate=BRIEF,
        name=name,
    )(index, (in_hbm if first else in_vmem)(tokens), *[in_vmem(r) for r in received], *extra)


class Relay:
    def __init__(self, index_of, index, tokens):
        self.index_of, self.index, self.tokens = index_of, index, tokens

    def call(self, kernel, heights, received, waits, name):
        kernel = functools.partial(kernel, self.index_of)
        return hop_call(kernel, self.index, self.tokens, heights, received, waits, name)

    def first(self, waits=()):
        inward, left = self.call(first_hop_kernel, (BLK, BLK), (), waits, "first_hop")
        self.received = (
            lax.ppermute(inward, "dp", [(3, 2), (0, 1)]),
            lax.ppermute(left, "dp", [(2, 1)]),
        )
        return inward

    def second(self, waits=()):
        outer, middle = self.call(
            second_hop_kernel, (BLK, BLK), self.received, waits, "second_hop"
        )
        self.received = (
            lax.ppermute(outer, "dp", [(1, 0), (0, 1), (3, 2)]),
            lax.ppermute(middle, "dp", [(2, 1), (1, 2)]),
        )
        return outer

    def settle(self, waits=()):
        homes = self.call(settle_kernel, CHUNK_ROWS, self.received, waits, "settle")
        self.arrived = [self.spread(home) for home in homes]

    def spread(self, home):
        outer = lax.ppermute(home, "dp", [(0, 1), (1, 0), (2, 3), (3, 2)])
        inner = lax.ppermute(home, "dp", [(1, 2), (2, 1)])
        outer_2 = lax.ppermute(inner, "dp", [(1, 0), (2, 3)])
        inner_2 = lax.ppermute(outer, "dp", [(1, 2), (2, 1)])
        outer_3 = lax.ppermute(inner_2, "dp", [(1, 0), (2, 3)])
        return home, outer, inner, inner_2, outer_2, outer_3

    def rows(self, chunk, waits=(), far=()):
        arrived = self.arrived[chunk]
        count, width = arrived[0].shape
        specs, extra = after(waits, far)
        return pl.pallas_call(
            functools.partial(collect_kernel, self.index_of, count),
            grid_spec=pltpu.PrefetchScalarGridSpec(
                num_scalar_prefetch=1,
                grid=(1,),
                in_specs=[held()] * len(arrived) + specs,
                out_specs=held(),
            ),
            out_shape=pltpu.VMEM((4 * count, width), self.tokens.dtype),
            compiler_params=SMALL,
            cost_estimate=BRIEF,
            name="collect",
        )(self.index, *[in_vmem(a) for a in arrived], *extra)


def load_weight_kernel(w_ref, *refs):
    out_ref, sems = refs[-2:]
    streams = sems.shape[0]
    depth = w_ref.shape[0] // streams
    copies = [
        pltpu.make_async_copy(
            w_ref.at[pl.ds(i * depth, depth)], out_ref.at[pl.ds(i * depth, depth)], sems.at[i]
        )
        for i in range(streams)
    ]
    for copy in copies:
        copy.start()
    for copy in copies:
        copy.wait()


def load_weight(weight, waits):
    specs, extra = after(waits)
    return pl.pallas_call(
        load_weight_kernel,
        grid=(1,),
        in_specs=[pl.BlockSpec(memory_space=pl.ANY)] + specs,
        out_specs=pl.BlockSpec(memory_space=pl.ANY),
        out_shape=pltpu.VMEM(weight.shape, weight.dtype),
        scratch_shapes=[pltpu.SemaphoreType.DMA((4,))],
        compiler_params=SMALL,
        cost_estimate=BRIEF,
        name="load_weight",
    )(in_hbm(weight), *extra)


def split_product_kernel(each, half, first, tile, rows_ref, w_ref, *refs):
    send_own_ref, send_ref, own_ref, other_ref = refs[-4:]
    for n in range(own_ref.shape[1] // tile):
        total = jnp.dot(
            rows_ref[...],
            w_ref[:, first + n * tile : first + (n + 1) * tile],
            preferred_element_type=jnp.float32,
        )
        columns = slice(n * tile, (n + 1) * tile)
        send_own_ref[:, columns] = total[:each].astype(send_own_ref.dtype)
        send_ref[:, columns] = total[each:half].astype(send_ref.dtype)
        own_ref[:, columns] = total[half : half + each]
        other_ref[:, columns] = total[half + each :]


def split_product(shape, rows, weight, part, part_count, waits):
    half = rows.shape[0] // 2
    each = half // shape.chips
    width = weight.shape[1] // part_count
    specs, extra = after(waits)
    return pl.pallas_call(
        functools.partial(split_product_kernel, each, half, part * width, min(512, width)),
        grid=(1,),
        in_specs=[held(), held()] + specs,
        out_specs=[held()] * 4,
        out_shape=[
            pltpu.VMEM((each, width), jnp.bfloat16),
            pltpu.VMEM((half - each, width), jnp.bfloat16),
            pltpu.VMEM((each, width), jnp.float32),
            pltpu.VMEM((half - each, width), jnp.float32),
        ],
        compiler_params=SMALL,
        cost_estimate=BRIEF,
        name="split_product",
    )(in_vmem(rows), in_vmem(weight), *extra)


def narrow_kernel(index_of, index_ref, tokens_ref, down_ref, cot_ref, up_ref, *refs):
    send_ref, keep_ref, back_ref, low, tokens, down, cot, up, sems = refs[-9:]
    index = index_of(index_ref)
    pairs = [(tokens_ref, tokens), (down_ref, down), (cot_ref, cot)]
    for i in range(index.per_part):
        adapter = index.owner(index.block(0, 0, i))
        pairs.append((up_ref.at[adapter], up.at[i]))
    copies = [
        pltpu.make_async_copy(source, target, sems.at[j])
        for j, (source, target) in enumerate(pairs)
    ]
    for copy in copies:
        copy.start()
    for copy in copies[:2]:
        copy.wait()
    for m in range(CAP):
        low[m] = lax.dot_general(
            down[0],
            tokens[m * BLK : (m + 1) * BLK],
            LAST,
            preferred_element_type=jnp.float32,
        )
    for core_bit, out_ref in ((1, send_ref), (0, keep_ref)):
        for chip_bits in range(index.chips):
            for i in range(index.per_part):
                block = index.block(core_bit, chip_bits, i)
                mine = index.owner(block) == index.place
                out_ref[chip_bits, i] = jnp.where(mine, low[index.slot(block)], 0.0)
    for copy in copies[2:]:
        copy.wait()
    for i in range(index.per_part):
        back_ref[i] = lax.dot_general(
            up[i], cot[i * BLK : (i + 1) * BLK], LAST, preferred_element_type=jnp.float32
        )


def narrow(index_of, index, shape, tokens, down, cotangent, up, waits):
    rank = up.shape[1]
    one = (shape.per_part, rank, BLK)
    outs = [(shape.chips,) + one, (shape.chips,) + one, one]
    operands = (tokens, down, cotangent, up)
    specs, extra = after(waits)
    return pl.pallas_call(
        functools.partial(narrow_kernel, index_of),
        grid_spec=pltpu.PrefetchScalarGridSpec(
            num_scalar_prefetch=1,
            grid=(1,),
            in_specs=[pl.BlockSpec(memory_space=pl.ANY)] * len(operands) + specs,
            out_specs=[held()] * len(outs),
            scratch_shapes=[
                pltpu.VMEM((CAP, rank, BLK), jnp.float32),
                pltpu.VMEM(tokens.shape, tokens.dtype),
                pltpu.VMEM(down.shape, down.dtype),
                pltpu.VMEM(cotangent.shape, cotangent.dtype),
                pltpu.VMEM((shape.per_part,) + up.shape[1:], up.dtype),
                pltpu.SemaphoreType.DMA((3 + shape.per_part,)),
            ],
        ),
        out_shape=[pltpu.VMEM(o, jnp.float32) for o in outs],
        compiler_params=SMALL,
        cost_estimate=BRIEF,
        name="narrow",
    )(index, *[in_hbm(o) for o in operands], *extra)


def merge_kernel(keep_ref, arrived_ref, back_ref, *refs):
    out_ref = refs[-1]
    total = keep_ref[0] + arrived_ref[0]
    for ref in refs[:-1][: keep_ref.shape[0] - 1]:
        total = total + ref[...]
    out_ref[0] = total
    out_ref[1] = back_ref[...]


def merge(keep, arrived, back, others, waits):
    specs, extra = after(waits)
    operands = (keep, arrived, back, *others)
    out = (2,) + back.shape
    return pl.pallas_call(
        merge_kernel,
        grid=(1,),
        in_specs=[whole(o.shape) for o in operands] + specs,
        out_specs=whole(out),
        out_shape=shape_of(out, jnp.float32),
        compiler_params=SMALL,
        cost_estimate=BRIEF,
        name="merge",
    )(*operands, *extra)


def pieces_kernel(index_of, count, index_ref, cot_ref, sum_ref, *refs):
    more_refs, (low_ref, back_ref, piece_ref) = refs[:count], refs[-3:]
    index = index_of(index_ref)
    level = [sum_ref[...]] + [ref[...] for ref in more_refs]
    while len(level) > 1:
        level = [level[j] + level[j + 1] for j in range(0, len(level), 2)]
    for i in range(index.per_part):
        live = index.live_rows(index.block(0, 0, i))
        keep = lax.broadcasted_iota(jnp.int32, low_ref.shape[1:], 1) < live
        lowered = jnp.where(keep, level[0][0, i], 0.0).astype(low_ref.dtype)
        low_ref[i] = lowered
        back_ref[i] = jnp.where(keep, level[0][1, i], 0.0).astype(back_ref.dtype)
        piece_ref[i] = jnp.dot(
            lowered, cot_ref[i * BLK : (i + 1) * BLK], preferred_element_type=jnp.float32
        ).astype(piece_ref.dtype)


def make_pieces(index_of, index, shape, total, more, cotangent, waits):
    _, per_part, rank, _ = total.shape
    width = cotangent.shape[1]
    outs = [(per_part, rank, BLK), (per_part, rank, BLK), (per_part, rank, width)]
    operands = (cotangent, total, *more)
    specs, extra = after(waits)
    return pl.pallas_call(
        functools.partial(pieces_kernel, index_of, len(more)),
        grid_spec=pltpu.PrefetchScalarGridSpec(
            num_scalar_prefetch=1,
            grid=(1,),
            in_specs=[whole(o.shape) for o in operands] + specs,
            out_specs=[whole(o) for o in outs],
        ),
        out_shape=[shape_of(o, jnp.bfloat16) for o in outs],
        compiler_params=SMALL,
        cost_estimate=BRIEF,
        name="pieces",
    )(index, *operands, *extra)


def down_gradient_kernel(index_of, index_ref, tokens_ref, *refs):
    back_refs, out_ref = refs[:-1], refs[-1]
    index = index_of(index_ref)
    out_ref[...] = jnp.zeros_like(out_ref)
    for core_bit in range(CORES):
        for chip_bits in range(index.chips):
            for i in range(index.per_part):
                block = index.block(core_bit, chip_bits, i)
                back_ref = back_refs[core_bit * index.chips + chip_bits]

                @pl.when(index.owner(block) == index.place)
                def _(block=block, back_ref=back_ref, i=i):
                    at = pl.multiple_of(index.slot(block) * BLK, BLK)
                    out_ref[0] += adapter_scale * jnp.dot(
                        back_ref[i],
                        tokens_ref[pl.ds(at, BLK)],
                        preferred_element_type=jnp.float32,
                    )


def down_gradient(index_of, index, tokens, backs):
    out = (1, backs[0].shape[1], tokens.shape[1])
    operands = (in_vmem(tokens), *backs)
    return pl.pallas_call(
        functools.partial(down_gradient_kernel, index_of),
        grid_spec=pltpu.PrefetchScalarGridSpec(
            num_scalar_prefetch=1,
            grid=(1,),
            in_specs=[held()] + [whole(o.shape) for o in backs],
            out_specs=whole(out),
        ),
        out_shape=shape_of(out, jnp.float32),
        compiler_params=SMALL,
        cost_estimate=BRIEF,
        name="down_gradient",
    )(index, *operands)


def up_gradient_kernel(index_of, index_ref, *refs):
    piece_refs, out_ref = refs[:-1], refs[-1]
    index = index_of(index_ref)

    def of_device(core_bit, chip_bits, adapter):
        total = None
        for i in range(index.per_part):
            mine = index.owner(index.block(core_bit, chip_bits, i)) == adapter
            piece = piece_refs[core_bit * index.chips + chip_bits][i].astype(jnp.float32)
            term = jnp.where(mine, piece, 0.0)
            total = term if total is None else total + term
        return total

    for adapter in range(index.adapters):
        level = [
            of_device(0, j, adapter) + of_device(1, j, adapter) for j in range(index.chips)
        ]
        while len(level) > 1:
            level = [level[j] + level[j + 1] for j in range(0, len(level), 2)]
        out_ref[adapter] = adapter_scale * level[0]


def up_gradient(index_of, index, adapter_count, pieces):
    per_part, rank, width = pieces[0].shape
    tile = 1024
    out = (adapter_count, rank, width)
    return pl.pallas_call(
        functools.partial(up_gradient_kernel, index_of),
        grid_spec=pltpu.PrefetchScalarGridSpec(
            num_scalar_prefetch=1,
            grid=(width // tile,),
            in_specs=[pl.BlockSpec((per_part, rank, tile), lambda n, _: (0, 0, n))] * len(pieces),
            out_specs=pl.BlockSpec((adapter_count, rank, tile), lambda n, _: (0, 0, n)),
        ),
        out_shape=shape_of(out, jnp.float32),
        compiler_params=SMALL,
        cost_estimate=BRIEF,
        name="up_gradient",
    )(index, *pieces)


def finish_kernel(index_of, index_ref, low_ref, *refs):
    index = index_of(index_ref)
    up_refs, sum_refs, out_ref = refs[: index.per_part], refs[index.per_part : -1], refs[-1]
    per_chunk = len(sum_refs) // len(CHUNK_ROWS)
    for i in range(index.per_part):
        block = index.block(0, 0, i)
        live = index.live_rows(block)
        side = lax.dot_general(
            low_ref[i],
            up_refs[i][0],
            (((0,), (0,)), ((), ())),
            preferred_element_type=jnp.float32,
        )
        start = 0
        for c, count in enumerate(CHUNK_ROWS):
            total = adapter_scale * side[start : start + count]
            for ref in sum_refs[c * per_chunk : (c + 1) * per_chunk]:
                total = total + ref[i * count : (i + 1) * count].astype(jnp.float32)
            keep = start + lax.broadcasted_iota(jnp.int32, total.shape, 0) < live
            at = i * BLK + start
            out_ref[at : at + count] = jnp.where(keep, total, 0.0).astype(out_ref.dtype)
            start += count


def finish(index_of, index, lowered, up, sums, part, projected):
    per_part = lowered.shape[0]
    _, rank, width = up.shape
    tile = min(1024, width // PARTS)
    tiles = width // PARTS // tile
    first = part * tiles
    out = (per_part * BLK, width)

    def factor(i):
        def at(n, index_ref):
            index = index_of(index_ref)
            return (index.owner(index.block(0, 0, i)), 0, first + n)

        return pl.BlockSpec((1, rank, tile), at)

    flat = [term for chunk in sums for term in chunk]
    specs = [
        pl.BlockSpec((per_part * count, tile), lambda n, _: (0, n))
        for chunk, count in zip(sums, CHUNK_ROWS)
        for _ in chunk
    ]
    operands = [index, lowered, *[up] * per_part, *flat]
    aliases, more, extra = {}, [], []
    if projected is not None:
        aliases = {len(operands): 0}
        more, extra = [pl.BlockSpec(memory_space=pl.ANY)], [projected]

    def kernel(*refs):
        finish_kernel(index_of, *refs[: len(operands)], refs[-1])

    return pl.pallas_call(
        kernel,
        grid_spec=pltpu.PrefetchScalarGridSpec(
            num_scalar_prefetch=1,
            grid=(tiles,),
            in_specs=[whole(lowered.shape)] + [factor(i) for i in range(per_part)] + specs + more,
            out_specs=pl.BlockSpec((out[0], tile), lambda n, _: (0, first + n)),
        ),
        out_shape=shape_of(out, jnp.bfloat16),
        input_output_aliases=aliases,
        compiler_params=SMALL,
        cost_estimate=BRIEF,
        name="finish",
    )(*operands, *extra)


def per_device(
    tokens,
    cotangent,
    frozen_up_weight,
    adapter_down_factor,
    adapter_up_factor,
    tokens_per_adapter,
    adapter_of_block,
    slot_of_block,
):
    owners = lax.axis_size("dp")
    parts = lax.axis_size("tensor")
    chips = parts // CORES
    block_count = adapter_of_block.shape[0]
    adapter_count = adapter_up_factor.shape[0]
    width_dev = tokens.shape[1]
    index_of = functools.partial(
        Index, block_count=block_count, adapter_count=adapter_count, parts=parts
    )
    shape = index_of(None)
    index = Index.pack(adapter_of_block, slot_of_block, tokens_per_adapter)

    def to_other_core(value):
        return lax.ppermute(value, "tensor", [(i, i ^ 1) for i in range(parts)])

    def to_chip(value, k):
        return lax.ppermute(value, "tensor", [(i, i ^ (k * CORES)) for i in range(parts)])

    def across_dp(value, k):
        return lax.ppermute(value, "dp", [(i, i ^ k) for i in range(owners)])

    def same_core(value):
        return [value] + [to_chip(value, k) for k in range(1, chips)]

    def with_other_core(values):
        return values + [to_other_core(v) for v in values]

    def small_products(waits):
        return narrow(
            index_of,
            index,
            shape,
            tokens,
            jnp.swapaxes(adapter_down_factor, 1, 2),
            cotangent,
            adapter_up_factor,
            waits,
        )

    def over_parts(send, keep):
        arrived = to_other_core(send)
        return arrived, [to_chip(keep[k] + arrived[k], k) for k in range(1, chips)]

    def over_dp(total):
        k = 1
        while True:
            more = [across_dp(total, j * k) for j in range(1, min(4, owners // k))]
            if k * 4 >= owners:
                return total, more
            total = (total + more[0]) + (more[1] + more[2])
            k *= 4

    def gradients(pieces, back_rows):
        return (
            up_gradient(index_of, index, adapter_count, with_other_core(pieces)),
            down_gradient(index_of, index, tokens, with_other_core(back_rows)),
        )

    if owners == 4 and block_count == 4:
        relay = Relay(index_of, index, tokens)
        sent = relay.first()
        send, keep, back = small_products([sent])
        arrived, others = over_parts(send, keep)
        total, more = over_dp(merge(keep, arrived, back, others, []))
        lowered, back_rows, pieces = make_pieces(
            index_of, index, shape, total, more, cotangent, []
        )
        sent = relay.second([lowered])
        pieces, back_rows = same_core(pieces), same_core(back_rows)
        weight = load_weight(frozen_up_weight, [sent])
        relay.settle([weight, *pieces[1:], *back_rows[1:]])
        up_grad, down_grad = gradients(pieces, back_rows)
        ahead = [v for chunk in relay.arrived[1:] for v in chunk[3:5]]
        chunks = [lambda waits: relay.rows(0, ahead, [up_grad, down_grad])]
        chunks += [functools.partial(relay.rows, c) for c in range(1, len(CHUNK_ROWS))]
    else:
        weight = load_weight(frozen_up_weight, [])
        send, keep, back = small_products([])
        arrived, others = over_parts(send, keep)
        total, more = over_dp(merge(keep, arrived, back, others, []))
        lowered, back_rows, pieces = make_pieces(
            index_of, index, shape, total, more, cotangent, []
        )
        up_grad, down_grad = gradients(same_core(pieces), same_core(back_rows))
        every_slot = lax.all_gather(
            tokens.reshape(CAP, BLK, width_dev), "dp", axis=0, tiled=True
        )
        part = lax.axis_index("tensor")
        devices = jnp.arange(parts, dtype=jnp.int32)
        order = (devices // chips ^ 1) + (devices % chips) * CORES ^ part
        blocks = (order[:, None] * shape.per_part + jnp.arange(shape.per_part)).reshape(-1)
        picked = every_slot[adapter_of_block[blocks] * CAP + slot_of_block[blocks]]
        starts = [sum(CHUNK_ROWS[:c]) for c in range(len(CHUNK_ROWS))]
        chunks = [
            lambda waits, s=s, count=count: picked[:, s : s + count].reshape(-1, width_dev)
            for s, count in zip(starts, CHUNK_ROWS)
        ]
    def summed(rows, part, waits):
        each = rows.shape[0] // parts
        send_own, send, own, other = split_product(shape, rows, weight, part, PARTS, waits)
        outgoing = (other + to_other_core(send).astype(jnp.float32)).astype(jnp.bfloat16)
        across = [to_chip(outgoing[(k - 1) * each : k * each], k) for k in range(1, chips)]
        return [own, to_other_core(send_own)] + across, outgoing

    sums, rows, waits = [], [], []
    for chunk in chunks:
        rows.append(chunk(waits))
        sums.append([summed(rows[-1], 0, ())])
        waits = [sums[-1][0][1]]
    for part in range(1, PARTS):
        waits = rows[-1:]
        for chunk_rows, done in zip(rows, sums):
            done.append(summed(chunk_rows, part, waits))
            waits = [*sums[0][part - 1][0][2:], sums[-1][part - 1][1]]
    projected = None
    for part in range(PARTS):
        projected = finish(
            index_of,
            index,
            lowered,
            adapter_up_factor,
            [done[part][0] for done in sums],
            part,
            projected,
        )
    return (projected, jnp.swapaxes(down_grad, 1, 2), up_grad)


def solution(mesh):
    return jax.shard_map(
        per_device,
        mesh=mesh,
        in_specs=(
            P(("groups", "dp"), "tensor"),
            P(("groups", "tensor"), "dp"),
            P("tensor", "dp"),
            P(("groups", "dp"), "tensor", None),
            P("groups", None, "dp"),
            P("groups"),
            P("groups"),
            P("groups"),
        ),
        out_specs=(
            P(("groups", "tensor"), "dp"),
            P(("groups", "dp"), "tensor", None),
            P("groups", None, "dp"),
        ),
        check_vma=False,
    )
```

```python
import functools

import jax
import jax.numpy as jnp
from jax import lax
from jax.experimental import pallas as pl
from jax.experimental.pallas import tpu as pltpu
from jax.sharding import PartitionSpec as P

BLK = 128
CAP = 3
CORES = 2
STREAM_ROWS = (64, 64)
PARTS = 4
WRITES = 2
SMALL = pltpu.CompilerParams(vmem_limit_bytes=12 * 2**20)

adapter_scale = 0.5

LAST = (((1,), (1,)), ((), ()))


class Index:
    def __init__(self, ref, block_count, adapter_count, parts):
        self.ref = ref
        self.blocks, self.adapters, self.parts = block_count, adapter_count, parts
        self.chips = parts // CORES
        self.per_part = block_count // parts

    @staticmethod
    def pack(adapter_of_block, slot_of_block, tokens_per_adapter):
        place = jnp.stack([lax.axis_index("dp"), lax.axis_index("tensor")]).astype(jnp.int32)
        return jnp.concatenate([adapter_of_block, slot_of_block, tokens_per_adapter, place])

    def owner(self, block):
        return self.ref[block]

    def slot(self, block):
        return self.ref[self.blocks + block]

    def tokens(self, adapter):
        return self.ref[2 * self.blocks + adapter]

    @property
    def place(self):
        return self.ref[2 * self.blocks + self.adapters]

    @property
    def part(self):
        return self.ref[2 * self.blocks + self.adapters + 1]

    def block(self, core_bit, chip_bits, i):
        return (self.part ^ (chip_bits * CORES + core_bit)) * self.per_part + i

    def position(self, block):
        bits = (block // self.per_part) ^ self.part
        half = (1 - bits % CORES) * self.chips + bits // CORES
        return half * self.per_part + block % self.per_part

    def live_rows(self, block):
        adapter = self.owner(block)
        first = jnp.int32(0)
        for a in range(self.adapters):
            count = (self.tokens(a) + BLK - 1) // BLK
            first = first + jnp.where(a < adapter, count, 0)
        return self.tokens(adapter) - (block - first) * BLK


def in_vmem(value):
    return pltpu.with_memory_space_constraint(value, pltpu.VMEM)


def in_hbm(value):
    return pltpu.with_memory_space_constraint(value, pltpu.HBM)


def held():
    return pl.BlockSpec(memory_space=pltpu.VMEM)


def whole(shape):
    return pl.BlockSpec(shape, lambda *_: (0,) * len(shape))


def shape_of(shape, dtype):
    return jax.ShapeDtypeStruct(shape, dtype)


BRIEF = pl.CostEstimate(flops=1, bytes_accessed=1, transcendentals=0)


def own_rows(index, block, tokens_ref, out_ref, start=0):
    at = pl.multiple_of(index.slot(block) * BLK + start, 16)
    out_ref[...] = tokens_ref[pl.ds(at, out_ref.shape[0])]


def first_hop_kernel(index_of, index_ref, tokens_ref, *refs):
    a_ref, b_ref, sems = refs[-3:]
    index = index_of(index_ref)
    copies = [
        pltpu.make_async_copy(
            tokens_ref.at[pl.ds(pl.multiple_of(index.slot(block) * BLK, BLK), BLK)],
            out_ref,
            sems.at[i],
        )
        for i, (block, out_ref) in enumerate(
            ((jnp.where(index.place == 0, 2, 1), a_ref), (0, b_ref))
        )
    ]
    for copy in copies:
        copy.start()
    for copy in copies:
        copy.wait()


def second_hop_kernel(index_of, index_ref, tokens_ref, a_ref, b_ref, *refs):
    x_ref, y_ref = refs[-2:]
    index = index_of(index_ref)
    place = index.place
    outer = jnp.where(place == 0, 1, jnp.where(place == 1, 0, 2))
    middle = jnp.where(place == 1, 2, 1)
    own_rows(index, outer, tokens_ref, x_ref)
    own_rows(index, middle, tokens_ref, y_ref)

    @pl.when((place == 1) & (index.owner(0) != 1))
    def _():
        x_ref[...] = b_ref[...]

    @pl.when(((place == 1) | (place == 2)) & (index.owner(middle) != place))
    def _():
        y_ref[...] = a_ref[...]


def settle_kernel(index_of, index_ref, tokens_ref, x_ref, y_ref, *refs):
    out_refs = refs[-len(STREAM_ROWS) :]
    index = index_of(index_ref)
    place = index.place
    owner = index.owner(place)
    mine = owner == place
    edge = (place == 0) | ((place == 1) & (owner == 0)) | ((place == 2) & (owner == 3))
    start = 0
    for out_ref in out_refs:
        rows = slice(start, start + out_ref.shape[0])
        own_rows(index, place, tokens_ref, out_ref, start)

        @pl.when(jnp.logical_not(mine) & edge)
        def _(out_ref=out_ref, rows=rows):
            out_ref[...] = x_ref[rows]

        @pl.when(jnp.logical_not(mine | edge))
        def _(out_ref=out_ref, rows=rows):
            out_ref[...] = y_ref[rows]

        start += out_ref.shape[0]


def collect_kernel(index_of, index_ref, *refs):
    out_ref = refs[-1]
    index = index_of(index_ref)
    place = index.place
    middle = (place == 1) | (place == 2)
    start = 0
    for stream, count in enumerate(STREAM_ROWS):
        home, outer, inner, inner_2, outer_2, outer_3 = refs[6 * stream : 6 * stream + 6]

        def put(block, ref, start=start, count=count):
            at = pl.multiple_of(index.position(block) * BLK + start, 16)
            out_ref[pl.ds(at, count)] = ref[...]

        put(place, home)
        put(place ^ 1, outer)

        @pl.when(middle)
        def _(put=put, inner=inner, inner_2=inner_2):
            put(3 - place, inner)
            put(place ^ 2, inner_2)

        @pl.when(jnp.logical_not(middle))
        def _(put=put, outer_2=outer_2, outer_3=outer_3):
            put(place ^ 2, outer_2)
            put(3 - place, outer_3)

        start += count


def after(values, far=()):
    specs = [
        pl.BlockSpec((1,) * (v.ndim - 2) + (16, 128), lambda *_, n=v.ndim: (0,) * n) for v in values
    ] + [pl.BlockSpec(memory_space=pl.ANY)] * len(far)
    return specs, [*values, *(in_hbm(v) for v in far)]


def hop_call(kernel, index, tokens, heights, received, waits, name):
    specs, extra = after(waits)
    width = tokens.shape[1]
    first = not received
    return pl.pallas_call(
        kernel,
        grid_spec=pltpu.PrefetchScalarGridSpec(
            num_scalar_prefetch=1,
            grid=(1,),
            in_specs=[pl.BlockSpec(memory_space=pl.ANY) if first else held()]
            + [held()] * len(received)
            + specs,
            out_specs=[held()] * len(heights),
            scratch_shapes=[pltpu.SemaphoreType.DMA((len(heights),))] * first,
        ),
        out_shape=[pltpu.VMEM((height, width), tokens.dtype) for height in heights],
        compiler_params=SMALL,
        cost_estimate=BRIEF,
        name=name,
    )(index, (in_hbm if first else in_vmem)(tokens), *[in_vmem(r) for r in received], *extra)


class Relay:
    def __init__(self, index_of, index, tokens):
        self.index_of, self.index, self.tokens = index_of, index, tokens

    def call(self, kernel, heights, received, waits, name):
        kernel = functools.partial(kernel, self.index_of)
        return hop_call(kernel, self.index, self.tokens, heights, received, waits, name)

    def first(self, waits=()):
        inward, left = self.call(first_hop_kernel, (BLK, BLK), (), waits, "first_hop")
        self.received = (
            lax.ppermute(inward, "dp", [(3, 2), (0, 1)]),
            lax.ppermute(left, "dp", [(2, 1)]),
        )
        return inward

    def second(self, waits=()):
        outer, middle = self.call(
            second_hop_kernel, (BLK, BLK), self.received, waits, "second_hop"
        )
        self.received = (
            lax.ppermute(outer, "dp", [(1, 0), (0, 1), (3, 2)]),
            lax.ppermute(middle, "dp", [(2, 1), (1, 2)]),
        )
        return outer

    def settle(self, waits=()):
        homes = self.call(settle_kernel, STREAM_ROWS, self.received, waits, "settle")
        self.arrived = [self.spread(home) for home in homes]

    def spread(self, home):
        outer = lax.ppermute(home, "dp", [(0, 1), (1, 0), (2, 3), (3, 2)])
        inner = lax.ppermute(home, "dp", [(1, 2), (2, 1)])
        outer_2 = lax.ppermute(inner, "dp", [(1, 0), (2, 3)])
        inner_2 = lax.ppermute(outer, "dp", [(1, 2), (2, 1)])
        outer_3 = lax.ppermute(inner_2, "dp", [(1, 0), (2, 3)])
        return home, outer, inner, inner_2, outer_2, outer_3

    def rows(self, waits):
        arrived = [in_vmem(a) for stream in self.arrived for a in stream]
        specs, extra = after(waits)
        return pl.pallas_call(
            functools.partial(collect_kernel, self.index_of),
            grid_spec=pltpu.PrefetchScalarGridSpec(
                num_scalar_prefetch=1,
                grid=(1,),
                in_specs=[held()] * len(arrived) + specs,
                out_specs=held(),
            ),
            out_shape=pltpu.VMEM((4 * BLK, self.tokens.shape[1]), self.tokens.dtype),
            compiler_params=SMALL,
            cost_estimate=BRIEF,
            name="collect",
        )(self.index, *arrived, *extra)


def load_weight_kernel(w_ref, *refs):
    out_ref, sems = refs[-2:]
    streams = sems.shape[0]
    depth = w_ref.shape[0] // streams
    copies = [
        pltpu.make_async_copy(
            w_ref.at[pl.ds(i * depth, depth)], out_ref.at[pl.ds(i * depth, depth)], sems.at[i]
        )
        for i in range(streams)
    ]
    for copy in copies:
        copy.start()
    for copy in copies:
        copy.wait()


def load_weight(weight, waits):
    specs, extra = after(waits)
    return pl.pallas_call(
        load_weight_kernel,
        grid=(1,),
        in_specs=[pl.BlockSpec(memory_space=pl.ANY)] + specs,
        out_specs=pl.BlockSpec(memory_space=pl.ANY),
        out_shape=pltpu.VMEM(weight.shape, weight.dtype),
        scratch_shapes=[pltpu.SemaphoreType.DMA((4,))],
        compiler_params=SMALL,
        cost_estimate=BRIEF,
        name="load_weight",
    )(in_hbm(weight), *extra)


def split_product_kernel(each, half, first, tile, rows_ref, w_ref, *refs):
    send_own_ref, send_ref, own_ref, other_ref = refs[-4:]
    for n in range(own_ref.shape[1] // tile):
        total = jnp.dot(
            rows_ref[...],
            w_ref[:, first + n * tile : first + (n + 1) * tile],
            preferred_element_type=jnp.float32,
        )
        columns = slice(n * tile, (n + 1) * tile)
        send_own_ref[:, columns] = total[:each].astype(send_own_ref.dtype)
        send_ref[:, columns] = total[each:half].astype(send_ref.dtype)
        own_ref[:, columns] = total[half : half + each]
        other_ref[:, columns] = total[half + each :]


def split_product(shape, rows, weight, part, part_count, waits):
    half = rows.shape[0] // 2
    each = half // shape.chips
    width = weight.shape[1] // part_count
    specs, extra = after(waits)
    return pl.pallas_call(
        functools.partial(split_product_kernel, each, half, part * width, min(512, width)),
        grid=(1,),
        in_specs=[held(), held()] + specs,
        out_specs=[held()] * 4,
        out_shape=[
            pltpu.VMEM((each, width), jnp.bfloat16),
            pltpu.VMEM((half - each, width), jnp.bfloat16),
            pltpu.VMEM((each, width), jnp.float32),
            pltpu.VMEM((half - each, width), jnp.float32),
        ],
        compiler_params=SMALL,
        cost_estimate=BRIEF,
        name="split_product",
    )(in_vmem(rows), in_vmem(weight), *extra)


def narrow_kernel(index_of, index_ref, tokens_ref, down_ref, cot_ref, up_ref, *refs):
    send_ref, keep_ref, back_ref, low, tokens, down, cot, up, sems = refs[-9:]
    index = index_of(index_ref)
    pairs = [(tokens_ref, tokens), (down_ref, down), (cot_ref, cot)]
    for i in range(index.per_part):
        adapter = index.owner(index.block(0, 0, i))
        pairs.append((up_ref.at[adapter], up.at[i]))
    copies = [
        pltpu.make_async_copy(source, target, sems.at[j])
        for j, (source, target) in enumerate(pairs)
    ]
    for copy in copies:
        copy.start()
    for copy in copies[:2]:
        copy.wait()
    for m in range(CAP):
        low[m] = lax.dot_general(
            down[0],
            tokens[m * BLK : (m + 1) * BLK],
            LAST,
            preferred_element_type=jnp.float32,
        )
    for core_bit, out_ref in ((1, send_ref), (0, keep_ref)):
        for chip_bits in range(index.chips):
            for i in range(index.per_part):
                block = index.block(core_bit, chip_bits, i)
                mine = index.owner(block) == index.place
                out_ref[chip_bits, i] = jnp.where(mine, low[index.slot(block)], 0.0)
    for copy in copies[2:]:
        copy.wait()
    for i in range(index.per_part):
        back_ref[i] = lax.dot_general(
            up[i], cot[i * BLK : (i + 1) * BLK], LAST, preferred_element_type=jnp.float32
        )


def narrow(index_of, index, shape, tokens, down, cotangent, up, waits):
    rank = up.shape[1]
    one = (shape.per_part, rank, BLK)
    outs = [(shape.chips,) + one, (shape.chips,) + one, one]
    operands = (tokens, down, cotangent, up)
    specs, extra = after(waits)
    return pl.pallas_call(
        functools.partial(narrow_kernel, index_of),
        grid_spec=pltpu.PrefetchScalarGridSpec(
            num_scalar_prefetch=1,
            grid=(1,),
            in_specs=[pl.BlockSpec(memory_space=pl.ANY)] * len(operands) + specs,
            out_specs=[held()] * len(outs),
            scratch_shapes=[
                pltpu.VMEM((CAP, rank, BLK), jnp.float32),
                pltpu.VMEM(tokens.shape, tokens.dtype),
                pltpu.VMEM(down.shape, down.dtype),
                pltpu.VMEM(cotangent.shape, cotangent.dtype),
                pltpu.VMEM((shape.per_part,) + up.shape[1:], up.dtype),
                pltpu.SemaphoreType.DMA((3 + shape.per_part,)),
            ],
        ),
        out_shape=[pltpu.VMEM(o, jnp.float32) for o in outs],
        compiler_params=SMALL,
        cost_estimate=BRIEF,
        name="narrow",
    )(index, *[in_hbm(o) for o in operands], *extra)


def merge_kernel(keep_ref, arrived_ref, back_ref, *refs):
    out_ref = refs[-1]
    total = keep_ref[0] + arrived_ref[0]
    for ref in refs[:-1][: keep_ref.shape[0] - 1]:
        total = total + ref[...]
    out_ref[0] = total
    out_ref[1] = back_ref[...]


def merge(keep, arrived, back, others, waits):
    specs, extra = after(waits)
    operands = (keep, arrived, back, *others)
    out = (2,) + back.shape
    return pl.pallas_call(
        merge_kernel,
        grid=(1,),
        in_specs=[whole(o.shape) for o in operands] + specs,
        out_specs=whole(out),
        out_shape=shape_of(out, jnp.float32),
        compiler_params=SMALL,
        cost_estimate=BRIEF,
        name="merge",
    )(*operands, *extra)


def pieces_kernel(index_of, count, index_ref, cot_ref, sum_ref, *refs):
    more_refs, (low_ref, back_ref, piece_ref) = refs[:count], refs[-3:]
    index = index_of(index_ref)
    level = [sum_ref[...]] + [ref[...] for ref in more_refs]
    while len(level) > 1:
        level = [level[j] + level[j + 1] for j in range(0, len(level), 2)]
    for i in range(index.per_part):
        live = index.live_rows(index.block(0, 0, i))
        keep = lax.broadcasted_iota(jnp.int32, low_ref.shape[1:], 1) < live
        lowered = jnp.where(keep, level[0][0, i], 0.0).astype(low_ref.dtype)
        low_ref[i] = lowered
        back_ref[i] = jnp.where(keep, level[0][1, i], 0.0).astype(back_ref.dtype)
        piece_ref[i] = jnp.dot(
            lowered, cot_ref[i * BLK : (i + 1) * BLK], preferred_element_type=jnp.float32
        ).astype(piece_ref.dtype)


def make_pieces(index_of, index, shape, total, more, cotangent, waits):
    _, per_part, rank, _ = total.shape
    width = cotangent.shape[1]
    outs = [(per_part, rank, BLK), (per_part, rank, BLK), (per_part, rank, width)]
    operands = (cotangent, total, *more)
    specs, extra = after(waits)
    return pl.pallas_call(
        functools.partial(pieces_kernel, index_of, len(more)),
        grid_spec=pltpu.PrefetchScalarGridSpec(
            num_scalar_prefetch=1,
            grid=(1,),
            in_specs=[whole(o.shape) for o in operands] + specs,
            out_specs=[whole(o) for o in outs],
        ),
        out_shape=[shape_of(o, jnp.bfloat16) for o in outs],
        compiler_params=SMALL,
        cost_estimate=BRIEF,
        name="pieces",
    )(index, *operands, *extra)


def down_gradient_kernel(index_of, index_ref, tokens_ref, *refs):
    back_refs, out_ref = refs[:-1], refs[-1]
    index = index_of(index_ref)
    out_ref[...] = jnp.zeros_like(out_ref)
    for core_bit in range(CORES):
        for chip_bits in range(index.chips):
            for i in range(index.per_part):
                block = index.block(core_bit, chip_bits, i)
                back_ref = back_refs[core_bit * index.chips + chip_bits]

                @pl.when(index.owner(block) == index.place)
                def _(block=block, back_ref=back_ref, i=i):
                    at = pl.multiple_of(index.slot(block) * BLK, BLK)
                    out_ref[0] += adapter_scale * jnp.dot(
                        back_ref[i],
                        tokens_ref[pl.ds(at, BLK)],
                        preferred_element_type=jnp.float32,
                    )


def down_gradient(index_of, index, tokens, backs):
    out = (1, backs[0].shape[1], tokens.shape[1])
    operands = (in_vmem(tokens), *backs)
    return pl.pallas_call(
        functools.partial(down_gradient_kernel, index_of),
        grid_spec=pltpu.PrefetchScalarGridSpec(
            num_scalar_prefetch=1,
            grid=(1,),
            in_specs=[held()] + [whole(o.shape) for o in backs],
            out_specs=whole(out),
        ),
        out_shape=shape_of(out, jnp.float32),
        compiler_params=SMALL,
        cost_estimate=BRIEF,
        name="down_gradient",
    )(index, *operands)


def up_gradient_kernel(index_of, index_ref, *refs):
    piece_refs, out_ref = refs[:-1], refs[-1]
    index = index_of(index_ref)

    def of_device(core_bit, chip_bits, adapter):
        total = None
        for i in range(index.per_part):
            mine = index.owner(index.block(core_bit, chip_bits, i)) == adapter
            piece = piece_refs[core_bit * index.chips + chip_bits][i].astype(jnp.float32)
            term = jnp.where(mine, piece, 0.0)
            total = term if total is None else total + term
        return total

    for adapter in range(index.adapters):
        level = [
            of_device(0, j, adapter) + of_device(1, j, adapter) for j in range(index.chips)
        ]
        while len(level) > 1:
            level = [level[j] + level[j + 1] for j in range(0, len(level), 2)]
        out_ref[adapter] = adapter_scale * level[0]


def up_gradient(index_of, index, adapter_count, pieces):
    per_part, rank, width = pieces[0].shape
    tile = 1024
    out = (adapter_count, rank, width)
    return pl.pallas_call(
        functools.partial(up_gradient_kernel, index_of),
        grid_spec=pltpu.PrefetchScalarGridSpec(
            num_scalar_prefetch=1,
            grid=(width // tile,),
            in_specs=[pl.BlockSpec((per_part, rank, tile), lambda n, _: (0, 0, n))] * len(pieces),
            out_specs=pl.BlockSpec((adapter_count, rank, tile), lambda n, _: (0, 0, n)),
        ),
        out_shape=shape_of(out, jnp.float32),
        compiler_params=SMALL,
        cost_estimate=BRIEF,
        name="up_gradient",
    )(index, *pieces)


def finish_kernel(index_of, tiles, index_ref, low_ref, *refs):
    index = index_of(index_ref)
    up_refs, sum_refs, out_ref = refs[: index.per_part], refs[index.per_part : -1], refs[-1]
    terms = len(sum_refs) // tiles
    for i in range(index.per_part):
        block = index.block(0, 0, i)
        live = index.live_rows(block)
        side = lax.dot_general(
            low_ref[i],
            up_refs[i][0],
            (((0,), (0,)), ((), ())),
            preferred_element_type=jnp.float32,
        )
        keep = lax.broadcasted_iota(jnp.int32, side.shape, 0) < live
        rows = slice(i * BLK, (i + 1) * BLK)
        for n in range(tiles):

            @pl.when(pl.program_id(0) == n)
            def _(n=n):
                total = adapter_scale * side
                for ref in sum_refs[n * terms : (n + 1) * terms]:
                    total = total + ref[rows].astype(jnp.float32)
                out_ref[rows] = jnp.where(keep, total, 0.0).astype(out_ref.dtype)


def finish(index_of, index, lowered, up, sums, part, projected, far):
    per_part = lowered.shape[0]
    _, rank, width = up.shape
    tiles = len(sums)
    tile = width // WRITES // tiles
    first = part * tiles
    out = (per_part * BLK, width)

    def factor(i):
        def at(n, index_ref):
            index = index_of(index_ref)
            return (index.owner(index.block(0, 0, i)), 0, first + n)

        return pl.BlockSpec((1, rank, tile), at)

    flat = [term for terms in sums for term in terms]
    operands = [index, lowered, *[up] * per_part, *flat]
    more, extra = after((), far)
    aliases = {}
    if projected is not None:
        aliases = {len(operands): 0}
        more, extra = [pl.BlockSpec(memory_space=pl.ANY)] + more, [projected] + extra

    def kernel(*refs):
        finish_kernel(index_of, tiles, *refs[: len(operands)], refs[-1])

    return pl.pallas_call(
        kernel,
        grid_spec=pltpu.PrefetchScalarGridSpec(
            num_scalar_prefetch=1,
            grid=(tiles,),
            in_specs=[whole(lowered.shape)]
            + [factor(i) for i in range(per_part)]
            + [whole((per_part * BLK, tile))] * len(flat)
            + more,
            out_specs=pl.BlockSpec((out[0], tile), lambda n, _: (0, first + n)),
        ),
        out_shape=shape_of(out, jnp.bfloat16),
        input_output_aliases=aliases,
        compiler_params=SMALL,
        cost_estimate=BRIEF,
        name="finish",
    )(*operands, *extra)


def per_device(
    tokens,
    cotangent,
    frozen_up_weight,
    adapter_down_factor,
    adapter_up_factor,
    tokens_per_adapter,
    adapter_of_block,
    slot_of_block,
):
    owners = lax.axis_size("dp")
    parts = lax.axis_size("tensor")
    chips = parts // CORES
    block_count = adapter_of_block.shape[0]
    adapter_count = adapter_up_factor.shape[0]
    width_dev = tokens.shape[1]
    index_of = functools.partial(
        Index, block_count=block_count, adapter_count=adapter_count, parts=parts
    )
    shape = index_of(None)
    index = Index.pack(adapter_of_block, slot_of_block, tokens_per_adapter)

    def to_other_core(value):
        return lax.ppermute(value, "tensor", [(i, i ^ 1) for i in range(parts)])

    def to_chip(value, k):
        return lax.ppermute(value, "tensor", [(i, i ^ (k * CORES)) for i in range(parts)])

    def across_dp(value, k):
        return lax.ppermute(value, "dp", [(i, i ^ k) for i in range(owners)])

    def same_core(value):
        return [value] + [to_chip(value, k) for k in range(1, chips)]

    def with_other_core(values):
        return values + [to_other_core(v) for v in values]

    def small_products(waits):
        return narrow(
            index_of,
            index,
            shape,
            tokens,
            jnp.swapaxes(adapter_down_factor, 1, 2),
            cotangent,
            adapter_up_factor,
            waits,
        )

    def over_parts(send, keep):
        arrived = to_other_core(send)
        return arrived, [to_chip(keep[k] + arrived[k], k) for k in range(1, chips)]

    def over_dp(total):
        k = 1
        while True:
            more = [across_dp(total, j * k) for j in range(1, min(4, owners // k))]
            if k * 4 >= owners:
                return total, more
            total = (total + more[0]) + (more[1] + more[2])
            k *= 4

    if owners == 4 and block_count == 4:
        relay = Relay(index_of, index, tokens)
        sent = relay.first()
        send, keep, back = small_products([sent])
        arrived, others = over_parts(send, keep)
        sent = relay.second(others)
        weight = load_weight(frozen_up_weight, [sent])
        relay.settle([weight])
        first_round = [v for stream in relay.arrived for v in stream[1:3]]
        total, more = over_dp(merge(keep, arrived, back, others, first_round))
        lowered, back_rows, pieces = make_pieces(
            index_of, index, shape, total, more, cotangent, []
        )
        pieces, back_rows = same_core(pieces), same_core(back_rows)
        rows = relay.rows([])
    else:
        weight = load_weight(frozen_up_weight, [])
        send, keep, back = small_products([])
        arrived, others = over_parts(send, keep)
        total, more = over_dp(merge(keep, arrived, back, others, []))
        lowered, back_rows, pieces = make_pieces(
            index_of, index, shape, total, more, cotangent, []
        )
        pieces, back_rows = same_core(pieces), same_core(back_rows)
        every_slot = lax.all_gather(
            tokens.reshape(CAP, BLK, width_dev), "dp", axis=0, tiled=True
        )
        part = lax.axis_index("tensor")
        devices = jnp.arange(parts, dtype=jnp.int32)
        order = (devices // chips ^ 1) + (devices % chips) * CORES ^ part
        blocks = (order[:, None] * shape.per_part + jnp.arange(shape.per_part)).reshape(-1)
        picked = every_slot[adapter_of_block[blocks] * CAP + slot_of_block[blocks]]
        rows = picked.reshape(-1, width_dev)

    pieces, back_rows = with_other_core(pieces), with_other_core(back_rows)
    up_grad = up_gradient(index_of, index, adapter_count, pieces)
    down_grad = down_gradient(index_of, index, tokens, back_rows)

    def summed(part, waits):
        each = rows.shape[0] // parts
        send_own, send, own, other = split_product(shape, rows, weight, part, PARTS, waits)
        outgoing = (other + to_other_core(send).astype(jnp.float32)).astype(jnp.bfloat16)
        across = [to_chip(outgoing[(k - 1) * each : k * each], k) for k in range(1, chips)]
        return [own, to_other_core(send_own)] + across, outgoing

    sums, outgoing = [], []
    for part in range(PARTS):
        waits = []
        if part == 1:
            waits.extend([*pieces[1:chips], *back_rows[1:chips]])
        if part == 2:
            waits.extend([*pieces[chips:], *back_rows[chips:]])
        if part >= 2:
            waits.append(outgoing[part - 2])
        if part >= 3:
            waits.extend([sums[part - 1][0], *sums[part - 3][2:]])
        terms, sent = summed(part, waits)
        sums.append(terms)
        outgoing.append(sent)
    projected = None
    for part in range(WRITES):
        each = PARTS // WRITES
        projected = finish(
            index_of,
            index,
            lowered,
            adapter_up_factor,
            sums[part * each : (part + 1) * each],
            part,
            projected,
            [] if projected is not None else [up_grad, down_grad],
        )
    return (projected, jnp.swapaxes(down_grad, 1, 2), up_grad)


def solution(mesh):
    return jax.shard_map(
        per_device,
        mesh=mesh,
        in_specs=(
            P(("groups", "dp"), "tensor"),
            P(("groups", "tensor"), "dp"),
            P("tensor", "dp"),
            P(("groups", "dp"), "tensor", None),
            P("groups", None, "dp"),
            P("groups"),
            P("groups"),
            P("groups"),
        ),
        out_specs=(
            P(("groups", "tensor"), "dp"),
            P(("groups", "dp"), "tensor", None),
            P("groups", None, "dp"),
        ),
        check_vma=False,
    )
```

```python
import functools

import jax
import jax.numpy as jnp
from jax import lax
from jax.experimental import pallas as pl
from jax.experimental.pallas import tpu as pltpu
from jax.sharding import PartitionSpec as P

BLK = 128
CAP = 3
CORES = 2
CHUNK_ROWS = (64, 64)
PARTS = 2
SMALL = pltpu.CompilerParams(vmem_limit_bytes=12 * 2**20)

adapter_scale = 0.5

LAST = (((1,), (1,)), ((), ()))


class Index:
    def __init__(self, ref, block_count, adapter_count, parts):
        self.ref = ref
        self.blocks, self.adapters, self.parts = block_count, adapter_count, parts
        self.chips = parts // CORES
        self.per_part = block_count // parts

    @staticmethod
    def pack(adapter_of_block, slot_of_block, tokens_per_adapter):
        place = jnp.stack([lax.axis_index("dp"), lax.axis_index("tensor")]).astype(jnp.int32)
        return jnp.concatenate([adapter_of_block, slot_of_block, tokens_per_adapter, place])

    def owner(self, block):
        return self.ref[block]

    def slot(self, block):
        return self.ref[self.blocks + block]

    def tokens(self, adapter):
        return self.ref[2 * self.blocks + adapter]

    @property
    def place(self):
        return self.ref[2 * self.blocks + self.adapters]

    @property
    def part(self):
        return self.ref[2 * self.blocks + self.adapters + 1]

    def block(self, core_bit, chip_bits, i):
        return (self.part ^ (chip_bits * CORES + core_bit)) * self.per_part + i

    def position(self, block):
        bits = (block // self.per_part) ^ self.part
        half = (1 - bits % CORES) * self.chips + bits // CORES
        return half * self.per_part + block % self.per_part

    def live_rows(self, block):
        adapter = self.owner(block)
        first = jnp.int32(0)
        for a in range(self.adapters):
            count = (self.tokens(a) + BLK - 1) // BLK
            first = first + jnp.where(a < adapter, count, 0)
        return self.tokens(adapter) - (block - first) * BLK


def in_vmem(value):
    return pltpu.with_memory_space_constraint(value, pltpu.VMEM)


def in_hbm(value):
    return pltpu.with_memory_space_constraint(value, pltpu.HBM)


def held():
    return pl.BlockSpec(memory_space=pltpu.VMEM)


def whole(shape):
    return pl.BlockSpec(shape, lambda *_: (0,) * len(shape))


def shape_of(shape, dtype):
    return jax.ShapeDtypeStruct(shape, dtype)


BRIEF = pl.CostEstimate(flops=1, bytes_accessed=1, transcendentals=0)


def own_rows(index, block, tokens_ref, out_ref, start=0):
    at = pl.multiple_of(index.slot(block) * BLK + start, 16)
    out_ref[...] = tokens_ref[pl.ds(at, out_ref.shape[0])]


def first_hop_kernel(index_of, index_ref, tokens_ref, *refs):
    a_ref, b_ref, sems = refs[-3:]
    index = index_of(index_ref)
    copies = [
        pltpu.make_async_copy(
            tokens_ref.at[pl.ds(pl.multiple_of(index.slot(block) * BLK, BLK), BLK)],
            out_ref,
            sems.at[i],
        )
        for i, (block, out_ref) in enumerate(
            ((jnp.where(index.place == 0, 2, 1), a_ref), (0, b_ref))
        )
    ]
    for copy in copies:
        copy.start()
    for copy in copies:
        copy.wait()


def second_hop_kernel(index_of, index_ref, tokens_ref, a_ref, b_ref, *refs):
    x_ref, y_ref = refs[-2:]
    index = index_of(index_ref)
    place = index.place
    outer = jnp.where(place == 0, 1, jnp.where(place == 1, 0, 2))
    middle = jnp.where(place == 1, 2, 1)
    own_rows(index, outer, tokens_ref, x_ref)
    own_rows(index, middle, tokens_ref, y_ref)

    @pl.when((place == 1) & (index.owner(0) != 1))
    def _():
        x_ref[...] = b_ref[...]

    @pl.when(((place == 1) | (place == 2)) & (index.owner(middle) != place))
    def _():
        y_ref[...] = a_ref[...]


def settle_kernel(index_of, index_ref, tokens_ref, x_ref, y_ref, *refs):
    out_refs = refs[-len(CHUNK_ROWS) :]
    index = index_of(index_ref)
    place = index.place
    owner = index.owner(place)
    mine = owner == place
    edge = (place == 0) | ((place == 1) & (owner == 0)) | ((place == 2) & (owner == 3))
    start = 0
    for out_ref in out_refs:
        rows = slice(start, start + out_ref.shape[0])
        own_rows(index, place, tokens_ref, out_ref, start)

        @pl.when(jnp.logical_not(mine) & edge)
        def _(out_ref=out_ref, rows=rows):
            out_ref[...] = x_ref[rows]

        @pl.when(jnp.logical_not(mine | edge))
        def _(out_ref=out_ref, rows=rows):
            out_ref[...] = y_ref[rows]

        start += out_ref.shape[0]


def collect_kernel(index_of, count, index_ref, home_ref, outer_ref, *refs):
    inner_refs, outer_refs, out_ref = refs[:2], refs[2:4], refs[-1]
    index = index_of(index_ref)
    place = index.place

    def put(block, ref):
        at = pl.multiple_of(index.position(block) * count, 16)
        out_ref[pl.ds(at, count)] = ref[...]

    put(place, home_ref)
    put(place ^ 1, outer_ref)
    middle = (place == 1) | (place == 2)

    @pl.when(middle)
    def _():
        put(3 - place, inner_refs[0])
        put(place ^ 2, inner_refs[1])

    @pl.when(jnp.logical_not(middle))
    def _():
        put(place ^ 2, outer_refs[0])
        put(3 - place, outer_refs[1])


def after(values, far=()):
    specs = [
        pl.BlockSpec((1,) * (v.ndim - 2) + (16, 128), lambda *_, n=v.ndim: (0,) * n) for v in values
    ] + [pl.BlockSpec(memory_space=pl.ANY)] * len(far)
    return specs, [*values, *(in_hbm(v) for v in far)]


def hop_call(kernel, index, tokens, heights, received, waits, name):
    specs, extra = after(waits)
    width = tokens.shape[1]
    first = not received
    return pl.pallas_call(
        kernel,
        grid_spec=pltpu.PrefetchScalarGridSpec(
            num_scalar_prefetch=1,
            grid=(1,),
            in_specs=[pl.BlockSpec(memory_space=pl.ANY) if first else held()]
            + [held()] * len(received)
            + specs,
            out_specs=[held()] * len(heights),
            scratch_shapes=[pltpu.SemaphoreType.DMA((len(heights),))] * first,
        ),
        out_shape=[pltpu.VMEM((height, width), tokens.dtype) for height in heights],
        compiler_params=SMALL,
        cost_estimate=BRIEF,
        name=name,
    )(index, (in_hbm if first else in_vmem)(tokens), *[in_vmem(r) for r in received], *extra)


class Relay:
    def __init__(self, index_of, index, tokens):
        self.index_of, self.index, self.tokens = index_of, index, tokens

    def call(self, kernel, heights, received, waits, name):
        kernel = functools.partial(kernel, self.index_of)
        return hop_call(kernel, self.index, self.tokens, heights, received, waits, name)

    def first(self, waits=()):
        inward, left = self.call(first_hop_kernel, (BLK, BLK), (), waits, "first_hop")
        self.received = (
            lax.ppermute(inward, "dp", [(3, 2), (0, 1)]),
            lax.ppermute(left, "dp", [(2, 1)]),
        )
        return inward

    def second(self, waits=()):
        outer, middle = self.call(
            second_hop_kernel, (BLK, BLK), self.received, waits, "second_hop"
        )
        self.received = (
            lax.ppermute(outer, "dp", [(1, 0), (0, 1), (3, 2)]),
            lax.ppermute(middle, "dp", [(2, 1), (1, 2)]),
        )
        return outer

    def settle(self, waits=()):
        homes = self.call(settle_kernel, CHUNK_ROWS, self.received, waits, "settle")
        self.arrived = [self.spread(home) for home in homes]

    def spread(self, home):
        outer = lax.ppermute(home, "dp", [(0, 1), (1, 0), (2, 3), (3, 2)])
        inner = lax.ppermute(home, "dp", [(1, 2), (2, 1)])
        outer_2 = lax.ppermute(inner, "dp", [(1, 0), (2, 3)])
        inner_2 = lax.ppermute(outer, "dp", [(1, 2), (2, 1)])
        outer_3 = lax.ppermute(inner_2, "dp", [(1, 0), (2, 3)])
        return home, outer, inner, inner_2, outer_2, outer_3

    def rows(self, chunk, waits=(), far=()):
        arrived = self.arrived[chunk]
        count, width = arrived[0].shape
        specs, extra = after(waits, far)
        return pl.pallas_call(
            functools.partial(collect_kernel, self.index_of, count),
            grid_spec=pltpu.PrefetchScalarGridSpec(
                num_scalar_prefetch=1,
                grid=(1,),
                in_specs=[held()] * len(arrived) + specs,
                out_specs=held(),
            ),
            out_shape=pltpu.VMEM((4 * count, width), self.tokens.dtype),
            compiler_params=SMALL,
            cost_estimate=BRIEF,
            name="collect",
        )(self.index, *[in_vmem(a) for a in arrived], *extra)


def load_weight_kernel(w_ref, *refs):
    out_ref, sems = refs[-2:]
    streams = sems.shape[0]
    depth = w_ref.shape[0] // streams
    copies = [
        pltpu.make_async_copy(
            w_ref.at[pl.ds(i * depth, depth)], out_ref.at[pl.ds(i * depth, depth)], sems.at[i]
        )
        for i in range(streams)
    ]
    for copy in copies:
        copy.start()
    for copy in copies:
        copy.wait()


def load_weight(weight, waits):
    specs, extra = after(waits)
    return pl.pallas_call(
        load_weight_kernel,
        grid=(1,),
        in_specs=[pl.BlockSpec(memory_space=pl.ANY)] + specs,
        out_specs=pl.BlockSpec(memory_space=pl.ANY),
        out_shape=pltpu.VMEM(weight.shape, weight.dtype),
        scratch_shapes=[pltpu.SemaphoreType.DMA((4,))],
        compiler_params=SMALL,
        cost_estimate=BRIEF,
        name="load_weight",
    )(in_hbm(weight), *extra)


def split_product_kernel(each, half, first, tile, rows_ref, w_ref, *refs):
    send_own_ref, send_ref, own_ref, other_ref = refs[-4:]
    for n in range(own_ref.shape[1] // tile):
        total = jnp.dot(
            rows_ref[...],
            w_ref[:, first + n * tile : first + (n + 1) * tile],
            preferred_element_type=jnp.float32,
        )
        columns = slice(n * tile, (n + 1) * tile)
        send_own_ref[:, columns] = total[:each].astype(send_own_ref.dtype)
        send_ref[:, columns] = total[each:half].astype(send_ref.dtype)
        own_ref[:, columns] = total[half : half + each]
        other_ref[:, columns] = total[half + each :]


def split_product(shape, rows, weight, part, part_count, waits):
    half = rows.shape[0] // 2
    each = half // shape.chips
    width = weight.shape[1] // part_count
    specs, extra = after(waits)
    return pl.pallas_call(
        functools.partial(split_product_kernel, each, half, part * width, min(512, width)),
        grid=(1,),
        in_specs=[held(), held()] + specs,
        out_specs=[held()] * 4,
        out_shape=[
            pltpu.VMEM((each, width), jnp.bfloat16),
            pltpu.VMEM((half - each, width), jnp.bfloat16),
            pltpu.VMEM((each, width), jnp.float32),
            pltpu.VMEM((half - each, width), jnp.float32),
        ],
        compiler_params=SMALL,
        cost_estimate=BRIEF,
        name="split_product",
    )(in_vmem(rows), in_vmem(weight), *extra)


def narrow_kernel(index_of, index_ref, tokens_ref, down_ref, cot_ref, up_ref, *refs):
    send_ref, keep_ref, back_ref, low, tokens, down, cot, up, sems = refs[-9:]
    index = index_of(index_ref)
    pairs = [(tokens_ref, tokens), (down_ref, down), (cot_ref, cot)]
    for i in range(index.per_part):
        adapter = index.owner(index.block(0, 0, i))
        pairs.append((up_ref.at[adapter], up.at[i]))
    copies = [
        pltpu.make_async_copy(source, target, sems.at[j])
        for j, (source, target) in enumerate(pairs)
    ]
    for copy in copies:
        copy.start()
    for copy in copies[:2]:
        copy.wait()
    for m in range(CAP):
        low[m] = lax.dot_general(
            down[0],
            tokens[m * BLK : (m + 1) * BLK],
            LAST,
            preferred_element_type=jnp.float32,
        )
    for core_bit, out_ref in ((1, send_ref), (0, keep_ref)):
        for chip_bits in range(index.chips):
            for i in range(index.per_part):
                block = index.block(core_bit, chip_bits, i)
                mine = index.owner(block) == index.place
                out_ref[chip_bits, i] = jnp.where(mine, low[index.slot(block)], 0.0)
    for copy in copies[2:]:
        copy.wait()
    for i in range(index.per_part):
        back_ref[i] = lax.dot_general(
            up[i], cot[i * BLK : (i + 1) * BLK], LAST, preferred_element_type=jnp.float32
        )


def narrow(index_of, index, shape, tokens, down, cotangent, up, waits):
    rank = up.shape[1]
    one = (shape.per_part, rank, BLK)
    outs = [(shape.chips,) + one, (shape.chips,) + one, one]
    operands = (tokens, down, cotangent, up)
    specs, extra = after(waits)
    return pl.pallas_call(
        functools.partial(narrow_kernel, index_of),
        grid_spec=pltpu.PrefetchScalarGridSpec(
            num_scalar_prefetch=1,
            grid=(1,),
            in_specs=[pl.BlockSpec(memory_space=pl.ANY)] * len(operands) + specs,
            out_specs=[held()] * len(outs),
            scratch_shapes=[
                pltpu.VMEM((CAP, rank, BLK), jnp.float32),
                pltpu.VMEM(tokens.shape, tokens.dtype),
                pltpu.VMEM(down.shape, down.dtype),
                pltpu.VMEM(cotangent.shape, cotangent.dtype),
                pltpu.VMEM((shape.per_part,) + up.shape[1:], up.dtype),
                pltpu.SemaphoreType.DMA((3 + shape.per_part,)),
            ],
        ),
        out_shape=[pltpu.VMEM(o, jnp.float32) for o in outs],
        compiler_params=SMALL,
        cost_estimate=BRIEF,
        name="narrow",
    )(index, *[in_hbm(o) for o in operands], *extra)


def merge_kernel(keep_ref, arrived_ref, back_ref, *refs):
    out_ref = refs[-1]
    total = keep_ref[0] + arrived_ref[0]
    for ref in refs[:-1][: keep_ref.shape[0] - 1]:
        total = total + ref[...]
    out_ref[0] = total
    out_ref[1] = back_ref[...]


def merge(keep, arrived, back, others, waits):
    specs, extra = after(waits)
    operands = (keep, arrived, back, *others)
    out = (2,) + back.shape
    return pl.pallas_call(
        merge_kernel,
        grid=(1,),
        in_specs=[whole(o.shape) for o in operands] + specs,
        out_specs=whole(out),
        out_shape=shape_of(out, jnp.float32),
        compiler_params=SMALL,
        cost_estimate=BRIEF,
        name="merge",
    )(*operands, *extra)


def pieces_kernel(index_of, count, index_ref, cot_ref, sum_ref, *refs):
    more_refs, (low_ref, back_ref, piece_ref) = refs[:count], refs[-3:]
    index = index_of(index_ref)
    level = [sum_ref[...]] + [ref[...] for ref in more_refs]
    while len(level) > 1:
        level = [level[j] + level[j + 1] for j in range(0, len(level), 2)]
    for i in range(index.per_part):
        live = index.live_rows(index.block(0, 0, i))
        keep = lax.broadcasted_iota(jnp.int32, low_ref.shape[1:], 1) < live
        lowered = jnp.where(keep, level[0][0, i], 0.0).astype(low_ref.dtype)
        low_ref[i] = lowered
        back_ref[i] = jnp.where(keep, level[0][1, i], 0.0).astype(back_ref.dtype)
        piece_ref[i] = jnp.dot(
            lowered, cot_ref[i * BLK : (i + 1) * BLK], preferred_element_type=jnp.float32
        ).astype(piece_ref.dtype)


def make_pieces(index_of, index, shape, total, more, cotangent, waits):
    _, per_part, rank, _ = total.shape
    width = cotangent.shape[1]
    outs = [(per_part, rank, BLK), (per_part, rank, BLK), (per_part, rank, width)]
    operands = (cotangent, total, *more)
    specs, extra = after(waits)
    return pl.pallas_call(
        functools.partial(pieces_kernel, index_of, len(more)),
        grid_spec=pltpu.PrefetchScalarGridSpec(
            num_scalar_prefetch=1,
            grid=(1,),
            in_specs=[whole(o.shape) for o in operands] + specs,
            out_specs=[whole(o) for o in outs],
        ),
        out_shape=[shape_of(o, jnp.bfloat16) for o in outs],
        compiler_params=SMALL,
        cost_estimate=BRIEF,
        name="pieces",
    )(index, *operands, *extra)


def down_gradient_kernel(index_of, index_ref, tokens_ref, *refs):
    back_refs, out_ref = refs[:-1], refs[-1]
    index = index_of(index_ref)
    out_ref[...] = jnp.zeros_like(out_ref)
    for core_bit in range(CORES):
        for chip_bits in range(index.chips):
            for i in range(index.per_part):
                block = index.block(core_bit, chip_bits, i)
                back_ref = back_refs[core_bit * index.chips + chip_bits]

                @pl.when(index.owner(block) == index.place)
                def _(block=block, back_ref=back_ref, i=i):
                    at = pl.multiple_of(index.slot(block) * BLK, BLK)
                    out_ref[0] += adapter_scale * jnp.dot(
                        back_ref[i],
                        tokens_ref[pl.ds(at, BLK)],
                        preferred_element_type=jnp.float32,
                    )


def down_gradient(index_of, index, tokens, backs):
    out = (1, backs[0].shape[1], tokens.shape[1])
    operands = (in_vmem(tokens), *backs)
    return pl.pallas_call(
        functools.partial(down_gradient_kernel, index_of),
        grid_spec=pltpu.PrefetchScalarGridSpec(
            num_scalar_prefetch=1,
            grid=(1,),
            in_specs=[held()] + [whole(o.shape) for o in backs],
            out_specs=whole(out),
        ),
        out_shape=shape_of(out, jnp.float32),
        compiler_params=SMALL,
        cost_estimate=BRIEF,
        name="down_gradient",
    )(index, *operands)


def up_gradient_kernel(index_of, index_ref, *refs):
    piece_refs, out_ref = refs[:-1], refs[-1]
    index = index_of(index_ref)

    def of_device(core_bit, chip_bits, adapter):
        total = None
        for i in range(index.per_part):
            mine = index.owner(index.block(core_bit, chip_bits, i)) == adapter
            piece = piece_refs[core_bit * index.chips + chip_bits][i].astype(jnp.float32)
            term = jnp.where(mine, piece, 0.0)
            total = term if total is None else total + term
        return total

    for adapter in range(index.adapters):
        level = [
            of_device(0, j, adapter) + of_device(1, j, adapter) for j in range(index.chips)
        ]
        while len(level) > 1:
            level = [level[j] + level[j + 1] for j in range(0, len(level), 2)]
        out_ref[adapter] = adapter_scale * level[0]


def up_gradient(index_of, index, adapter_count, pieces):
    per_part, rank, width = pieces[0].shape
    tile = 1024
    out = (adapter_count, rank, width)
    return pl.pallas_call(
        functools.partial(up_gradient_kernel, index_of),
        grid_spec=pltpu.PrefetchScalarGridSpec(
            num_scalar_prefetch=1,
            grid=(width // tile,),
            in_specs=[pl.BlockSpec((per_part, rank, tile), lambda n, _: (0, 0, n))] * len(pieces),
            out_specs=pl.BlockSpec((adapter_count, rank, tile), lambda n, _: (0, 0, n)),
        ),
        out_shape=shape_of(out, jnp.float32),
        compiler_params=SMALL,
        cost_estimate=BRIEF,
        name="up_gradient",
    )(index, *pieces)


def finish_kernel(index_of, index_ref, low_ref, *refs):
    index = index_of(index_ref)
    up_refs, sum_refs, out_ref = refs[: index.per_part], refs[index.per_part : -1], refs[-1]
    per_chunk = len(sum_refs) // len(CHUNK_ROWS)
    for i in range(index.per_part):
        block = index.block(0, 0, i)
        live = index.live_rows(block)
        side = lax.dot_general(
            low_ref[i],
            up_refs[i][0],
            (((0,), (0,)), ((), ())),
            preferred_element_type=jnp.float32,
        )
        start = 0
        for c, count in enumerate(CHUNK_ROWS):
            total = adapter_scale * side[start : start + count]
            for ref in sum_refs[c * per_chunk : (c + 1) * per_chunk]:
                total = total + ref[i * count : (i + 1) * count].astype(jnp.float32)
            keep = start + lax.broadcasted_iota(jnp.int32, total.shape, 0) < live
            at = i * BLK + start
            out_ref[at : at + count] = jnp.where(keep, total, 0.0).astype(out_ref.dtype)
            start += count


def finish(index_of, index, lowered, up, sums, part, projected, far):
    per_part = lowered.shape[0]
    _, rank, width = up.shape
    tile = min(1024, width // PARTS)
    tiles = width // PARTS // tile
    first = part * tiles
    out = (per_part * BLK, width)

    def factor(i):
        def at(n, index_ref):
            index = index_of(index_ref)
            return (index.owner(index.block(0, 0, i)), 0, first + n)

        return pl.BlockSpec((1, rank, tile), at)

    flat = [term for chunk in sums for term in chunk]
    specs = [
        pl.BlockSpec((per_part * count, tile), lambda n, _: (0, n))
        for chunk, count in zip(sums, CHUNK_ROWS)
        for _ in chunk
    ]
    operands = [index, lowered, *[up] * per_part, *flat]
    more, extra = after((), far)
    aliases = {}
    if projected is not None:
        aliases = {len(operands): 0}
        more, extra = [pl.BlockSpec(memory_space=pl.ANY)] + more, [projected] + extra

    def kernel(*refs):
        finish_kernel(index_of, *refs[: len(operands)], refs[-1])

    return pl.pallas_call(
        kernel,
        grid_spec=pltpu.PrefetchScalarGridSpec(
            num_scalar_prefetch=1,
            grid=(tiles,),
            in_specs=[whole(lowered.shape)] + [factor(i) for i in range(per_part)] + specs + more,
            out_specs=pl.BlockSpec((out[0], tile), lambda n, _: (0, first + n)),
        ),
        out_shape=shape_of(out, jnp.bfloat16),
        input_output_aliases=aliases,
        compiler_params=SMALL,
        cost_estimate=BRIEF,
        name="finish",
    )(*operands, *extra)


def per_device(
    tokens,
    cotangent,
    frozen_up_weight,
    adapter_down_factor,
    adapter_up_factor,
    tokens_per_adapter,
    adapter_of_block,
    slot_of_block,
):
    owners = lax.axis_size("dp")
    parts = lax.axis_size("tensor")
    chips = parts // CORES
    block_count = adapter_of_block.shape[0]
    adapter_count = adapter_up_factor.shape[0]
    width_dev = tokens.shape[1]
    index_of = functools.partial(
        Index, block_count=block_count, adapter_count=adapter_count, parts=parts
    )
    shape = index_of(None)
    index = Index.pack(adapter_of_block, slot_of_block, tokens_per_adapter)

    def to_other_core(value):
        return lax.ppermute(value, "tensor", [(i, i ^ 1) for i in range(parts)])

    def to_chip(value, k):
        return lax.ppermute(value, "tensor", [(i, i ^ (k * CORES)) for i in range(parts)])

    def across_dp(value, k):
        return lax.ppermute(value, "dp", [(i, i ^ k) for i in range(owners)])

    def same_core(value):
        return [value] + [to_chip(value, k) for k in range(1, chips)]

    def with_other_core(values):
        return values + [to_other_core(v) for v in values]

    def small_products(waits):
        return narrow(
            index_of,
            index,
            shape,
            tokens,
            jnp.swapaxes(adapter_down_factor, 1, 2),
            cotangent,
            adapter_up_factor,
            waits,
        )

    def over_parts(send, keep):
        arrived = to_other_core(send)
        return arrived, [to_chip(keep[k] + arrived[k], k) for k in range(1, chips)]

    def over_dp(total):
        k = 1
        while 2 * k < owners:
            total = total + across_dp(total, k)
            k *= 2
        return total, [across_dp(total, k)]

    if owners == 4 and block_count == 4:
        relay = Relay(index_of, index, tokens)
        sent = relay.first()
        send, keep, back = small_products([sent])
        arrived, others = over_parts(send, keep)
        sent = relay.second(others)
        total, more = over_dp(merge(keep, arrived, back, others, []))
        lowered, back_rows, pieces = make_pieces(
            index_of, index, shape, total, more, cotangent, []
        )
        relay.settle([lowered])
        weight = load_weight(frozen_up_weight, relay.arrived[-1][1:3])
        pieces = with_other_core(same_core(pieces))
        back_rows = with_other_core(same_core(back_rows))
        ahead = [v for chunk in relay.arrived[1:] for v in chunk[3:5]]
        ahead += [weight, *pieces[chips:]]
        chunks = [lambda waits: relay.rows(0, ahead)]
        chunks += [functools.partial(relay.rows, c) for c in range(1, len(CHUNK_ROWS))]
    else:
        weight = load_weight(frozen_up_weight, [])
        send, keep, back = small_products([])
        arrived, others = over_parts(send, keep)
        total, more = over_dp(merge(keep, arrived, back, others, []))
        lowered, back_rows, pieces = make_pieces(
            index_of, index, shape, total, more, cotangent, []
        )
        pieces = with_other_core(same_core(pieces))
        back_rows = with_other_core(same_core(back_rows))
        every_slot = lax.all_gather(
            tokens.reshape(CAP, BLK, width_dev), "dp", axis=0, tiled=True
        )
        part = lax.axis_index("tensor")
        devices = jnp.arange(parts, dtype=jnp.int32)
        order = (devices // chips ^ 1) + (devices % chips) * CORES ^ part
        blocks = (order[:, None] * shape.per_part + jnp.arange(shape.per_part)).reshape(-1)
        picked = every_slot[adapter_of_block[blocks] * CAP + slot_of_block[blocks]]
        starts = [sum(CHUNK_ROWS[:c]) for c in range(len(CHUNK_ROWS))]
        chunks = [
            lambda waits, s=s, count=count: picked[:, s : s + count].reshape(-1, width_dev)
            for s, count in zip(starts, CHUNK_ROWS)
        ]
    def summed(rows, part, waits):
        each = rows.shape[0] // parts
        send_own, send, own, other = split_product(shape, rows, weight, part, PARTS, waits)
        outgoing = (other + to_other_core(send).astype(jnp.float32)).astype(jnp.bfloat16)
        across = [to_chip(outgoing[(k - 1) * each : k * each], k) for k in range(1, chips)]
        return [own, to_other_core(send_own)] + across, outgoing

    sums, waits, ready = [], [()] * PARTS, ()
    for chunk in chunks:
        rows = chunk(ready)
        done = [summed(rows, part, waits[part]) for part in range(PARTS)]
        sums.append([terms for terms, _ in done])
        ready = [done[0][1]]
        waits = [[*sums[-1][0][2:], *back_rows[1:chips]], [*sums[-1][1][2:], *back_rows[chips:]]]
    up_grad = up_gradient(index_of, index, adapter_count, pieces)
    down_grad = down_gradient(index_of, index, tokens, back_rows)
    projected = None
    for part in range(PARTS):
        projected = finish(
            index_of,
            index,
            lowered,
            adapter_up_factor,
            [done[part] for done in sums],
            part,
            projected,
            [] if projected is not None else [up_grad, down_grad],
        )
    return (projected, jnp.swapaxes(down_grad, 1, 2), up_grad)


def solution(mesh):
    return jax.shard_map(
        per_device,
        mesh=mesh,
        in_specs=(
            P(("groups", "dp"), "tensor"),
            P(("groups", "tensor"), "dp"),
            P("tensor", "dp"),
            P(("groups", "dp"), "tensor", None),
            P("groups", None, "dp"),
            P("groups"),
            P("groups"),
            P("groups"),
        ),
        out_specs=(
            P(("groups", "tensor"), "dp"),
            P(("groups", "dp"), "tensor", None),
            P("groups", None, "dp"),
        ),
        check_vma=False,
    )
```

```python
import functools

import jax
import jax.numpy as jnp
from jax import lax
from jax.experimental import pallas as pl
from jax.experimental.pallas import tpu as pltpu
from jax.sharding import PartitionSpec as P

BLK = 128
CAP = 3
CORES = 2
CHUNK_ROWS = (64, 64)
PARTS = 2
SMALL = pltpu.CompilerParams(vmem_limit_bytes=12 * 2**20)

adapter_scale = 0.5

LAST = (((1,), (1,)), ((), ()))


class Index:
    def __init__(self, ref, block_count, adapter_count, parts):
        self.ref = ref
        self.blocks, self.adapters, self.parts = block_count, adapter_count, parts
        self.chips = parts // CORES
        self.per_part = block_count // parts

    @staticmethod
    def pack(adapter_of_block, slot_of_block, tokens_per_adapter):
        place = jnp.stack([lax.axis_index("dp"), lax.axis_index("tensor")]).astype(jnp.int32)
        return jnp.concatenate([adapter_of_block, slot_of_block, tokens_per_adapter, place])

    def owner(self, block):
        return self.ref[block]

    def slot(self, block):
        return self.ref[self.blocks + block]

    def tokens(self, adapter):
        return self.ref[2 * self.blocks + adapter]

    @property
    def place(self):
        return self.ref[2 * self.blocks + self.adapters]

    @property
    def part(self):
        return self.ref[2 * self.blocks + self.adapters + 1]

    def block(self, core_bit, chip_bits, i):
        return (self.part ^ (chip_bits * CORES + core_bit)) * self.per_part + i

    def position(self, block):
        bits = (block // self.per_part) ^ self.part
        half = (1 - bits % CORES) * self.chips + bits // CORES
        return half * self.per_part + block % self.per_part

    def live_rows(self, block):
        adapter = self.owner(block)
        first = jnp.int32(0)
        for a in range(self.adapters):
            count = (self.tokens(a) + BLK - 1) // BLK
            first = first + jnp.where(a < adapter, count, 0)
        return self.tokens(adapter) - (block - first) * BLK


def in_vmem(value):
    return pltpu.with_memory_space_constraint(value, pltpu.VMEM)


def in_hbm(value):
    return pltpu.with_memory_space_constraint(value, pltpu.HBM)


def held():
    return pl.BlockSpec(memory_space=pltpu.VMEM)


def whole(shape):
    return pl.BlockSpec(shape, lambda *_: (0,) * len(shape))


def shape_of(shape, dtype):
    return jax.ShapeDtypeStruct(shape, dtype)


BRIEF = pl.CostEstimate(flops=1, bytes_accessed=1, transcendentals=0)


def own_rows(index, block, tokens_ref, out_ref, start=0):
    at = pl.multiple_of(index.slot(block) * BLK + start, 16)
    out_ref[...] = tokens_ref[pl.ds(at, out_ref.shape[0])]


def first_hop_kernel(index_of, index_ref, tokens_ref, *refs):
    a_ref, b_ref, sems = refs[-3:]
    index = index_of(index_ref)
    copies = [
        pltpu.make_async_copy(
            tokens_ref.at[pl.ds(pl.multiple_of(index.slot(block) * BLK, BLK), BLK)],
            out_ref,
            sems.at[i],
        )
        for i, (block, out_ref) in enumerate(
            ((jnp.where(index.place == 0, 2, 1), a_ref), (0, b_ref))
        )
    ]
    for copy in copies:
        copy.start()
    for copy in copies:
        copy.wait()


def second_hop_kernel(index_of, index_ref, tokens_ref, a_ref, b_ref, *refs):
    x_ref, y_ref = refs[-2:]
    index = index_of(index_ref)
    place = index.place
    outer = jnp.where(place == 0, 1, jnp.where(place == 1, 0, 2))
    middle = jnp.where(place == 1, 2, 1)
    own_rows(index, outer, tokens_ref, x_ref)
    own_rows(index, middle, tokens_ref, y_ref)

    @pl.when((place == 1) & (index.owner(0) != 1))
    def _():
        x_ref[...] = b_ref[...]

    @pl.when(((place == 1) | (place == 2)) & (index.owner(middle) != place))
    def _():
        y_ref[...] = a_ref[...]


def settle_kernel(index_of, index_ref, tokens_ref, x_ref, y_ref, *refs):
    out_refs = refs[-len(CHUNK_ROWS) :]
    index = index_of(index_ref)
    place = index.place
    owner = index.owner(place)
    mine = owner == place
    edge = (place == 0) | ((place == 1) & (owner == 0)) | ((place == 2) & (owner == 3))
    start = 0
    for out_ref in out_refs:
        rows = slice(start, start + out_ref.shape[0])
        own_rows(index, place, tokens_ref, out_ref, start)

        @pl.when(jnp.logical_not(mine) & edge)
        def _(out_ref=out_ref, rows=rows):
            out_ref[...] = x_ref[rows]

        @pl.when(jnp.logical_not(mine | edge))
        def _(out_ref=out_ref, rows=rows):
            out_ref[...] = y_ref[rows]

        start += out_ref.shape[0]


def collect_kernel(index_of, count, index_ref, home_ref, outer_ref, *refs):
    inner_refs, outer_refs, out_ref = refs[:2], refs[2:4], refs[-1]
    index = index_of(index_ref)
    place = index.place

    def put(block, ref):
        at = pl.multiple_of(index.position(block) * count, 16)
        out_ref[pl.ds(at, count)] = ref[...]

    put(place, home_ref)
    put(place ^ 1, outer_ref)
    middle = (place == 1) | (place == 2)

    @pl.when(middle)
    def _():
        put(3 - place, inner_refs[0])
        put(place ^ 2, inner_refs[1])

    @pl.when(jnp.logical_not(middle))
    def _():
        put(place ^ 2, outer_refs[0])
        put(3 - place, outer_refs[1])


def after(values, far=()):
    specs = [
        pl.BlockSpec((1,) * (v.ndim - 2) + (16, 128), lambda *_, n=v.ndim: (0,) * n) for v in values
    ] + [pl.BlockSpec(memory_space=pl.ANY)] * len(far)
    return specs, [*values, *(in_hbm(v) for v in far)]


def hop_call(kernel, index, tokens, heights, received, waits, name):
    specs, extra = after(waits)
    width = tokens.shape[1]
    first = not received
    return pl.pallas_call(
        kernel,
        grid_spec=pltpu.PrefetchScalarGridSpec(
            num_scalar_prefetch=1,
            grid=(1,),
            in_specs=[pl.BlockSpec(memory_space=pl.ANY) if first else held()]
            + [held()] * len(received)
            + specs,
            out_specs=[held()] * len(heights),
            scratch_shapes=[pltpu.SemaphoreType.DMA((len(heights),))] * first,
        ),
        out_shape=[pltpu.VMEM((height, width), tokens.dtype) for height in heights],
        compiler_params=SMALL,
        cost_estimate=BRIEF,
        name=name,
    )(index, (in_hbm if first else in_vmem)(tokens), *[in_vmem(r) for r in received], *extra)


class Relay:
    def __init__(self, index_of, index, tokens):
        self.index_of, self.index, self.tokens = index_of, index, tokens

    def call(self, kernel, heights, received, waits, name):
        kernel = functools.partial(kernel, self.index_of)
        return hop_call(kernel, self.index, self.tokens, heights, received, waits, name)

    def first(self, waits=()):
        inward, left = self.call(first_hop_kernel, (BLK, BLK), (), waits, "first_hop")
        self.received = (
            lax.ppermute(inward, "dp", [(3, 2), (0, 1)]),
            lax.ppermute(left, "dp", [(2, 1)]),
        )
        return inward

    def second(self, waits=()):
        outer, middle = self.call(
            second_hop_kernel, (BLK, BLK), self.received, waits, "second_hop"
        )
        self.received = (
            lax.ppermute(outer, "dp", [(1, 0), (0, 1), (3, 2)]),
            lax.ppermute(middle, "dp", [(2, 1), (1, 2)]),
        )
        return outer

    def settle(self, waits=()):
        homes = self.call(settle_kernel, CHUNK_ROWS, self.received, waits, "settle")
        self.arrived = [self.spread(home) for home in homes]

    def spread(self, home):
        outer = lax.ppermute(home, "dp", [(0, 1), (1, 0), (2, 3), (3, 2)])
        inner = lax.ppermute(home, "dp", [(1, 2), (2, 1)])
        outer_2 = lax.ppermute(inner, "dp", [(1, 0), (2, 3)])
        inner_2 = lax.ppermute(outer, "dp", [(1, 2), (2, 1)])
        outer_3 = lax.ppermute(inner_2, "dp", [(1, 0), (2, 3)])
        return home, outer, inner, inner_2, outer_2, outer_3

    def rows(self, chunk, waits=(), far=()):
        arrived = self.arrived[chunk]
        count, width = arrived[0].shape
        specs, extra = after(waits, far)
        return pl.pallas_call(
            functools.partial(collect_kernel, self.index_of, count),
            grid_spec=pltpu.PrefetchScalarGridSpec(
                num_scalar_prefetch=1,
                grid=(1,),
                in_specs=[held()] * len(arrived) + specs,
                out_specs=held(),
            ),
            out_shape=pltpu.VMEM((4 * count, width), self.tokens.dtype),
            compiler_params=SMALL,
            cost_estimate=BRIEF,
            name="collect",
        )(self.index, *[in_vmem(a) for a in arrived], *extra)


def load_weight_kernel(w_ref, *refs):
    out_ref, sems = refs[-2:]
    streams = sems.shape[0]
    depth = w_ref.shape[0] // streams
    copies = [
        pltpu.make_async_copy(
            w_ref.at[pl.ds(i * depth, depth)], out_ref.at[pl.ds(i * depth, depth)], sems.at[i]
        )
        for i in range(streams)
    ]
    for copy in copies:
        copy.start()
    for copy in copies:
        copy.wait()


def load_weight(weight, waits):
    specs, extra = after(waits)
    return pl.pallas_call(
        load_weight_kernel,
        grid=(1,),
        in_specs=[pl.BlockSpec(memory_space=pl.ANY)] + specs,
        out_specs=pl.BlockSpec(memory_space=pl.ANY),
        out_shape=pltpu.VMEM(weight.shape, weight.dtype),
        scratch_shapes=[pltpu.SemaphoreType.DMA((4,))],
        compiler_params=SMALL,
        cost_estimate=BRIEF,
        name="load_weight",
    )(in_hbm(weight), *extra)


def split_product_kernel(each, half, first, tile, rows_ref, w_ref, *refs):
    send_own_ref, send_ref, own_ref, other_ref = refs[-4:]
    for n in range(own_ref.shape[1] // tile):
        total = jnp.dot(
            rows_ref[...],
            w_ref[:, first + n * tile : first + (n + 1) * tile],
            preferred_element_type=jnp.float32,
        )
        columns = slice(n * tile, (n + 1) * tile)
        send_own_ref[:, columns] = total[:each].astype(send_own_ref.dtype)
        send_ref[:, columns] = total[each:half].astype(send_ref.dtype)
        own_ref[:, columns] = total[half : half + each]
        other_ref[:, columns] = total[half + each :]


def split_product(shape, rows, weight, part, part_count, waits):
    half = rows.shape[0] // 2
    each = half // shape.chips
    width = weight.shape[1] // part_count
    specs, extra = after(waits)
    return pl.pallas_call(
        functools.partial(split_product_kernel, each, half, part * width, min(512, width)),
        grid=(1,),
        in_specs=[held(), held()] + specs,
        out_specs=[held()] * 4,
        out_shape=[
            pltpu.VMEM((each, width), jnp.bfloat16),
            pltpu.VMEM((half - each, width), jnp.bfloat16),
            pltpu.VMEM((each, width), jnp.float32),
            pltpu.VMEM((half - each, width), jnp.float32),
        ],
        compiler_params=SMALL,
        cost_estimate=BRIEF,
        name="split_product",
    )(in_vmem(rows), in_vmem(weight), *extra)


def narrow_kernel(index_of, index_ref, tokens_ref, down_ref, cot_ref, up_ref, *refs):
    send_ref, keep_ref, back_ref, low, tokens, down, cot, up, sems = refs[-9:]
    index = index_of(index_ref)
    pairs = [(tokens_ref, tokens), (down_ref, down), (cot_ref, cot)]
    for i in range(index.per_part):
        adapter = index.owner(index.block(0, 0, i))
        pairs.append((up_ref.at[adapter], up.at[i]))
    copies = [
        pltpu.make_async_copy(source, target, sems.at[j])
        for j, (source, target) in enumerate(pairs)
    ]
    for copy in copies:
        copy.start()
    for copy in copies[:2]:
        copy.wait()
    for m in range(CAP):
        low[m] = lax.dot_general(
            down[0],
            tokens[m * BLK : (m + 1) * BLK],
            LAST,
            preferred_element_type=jnp.float32,
        )
    for core_bit, out_ref in ((1, send_ref), (0, keep_ref)):
        for chip_bits in range(index.chips):
            for i in range(index.per_part):
                block = index.block(core_bit, chip_bits, i)
                mine = index.owner(block) == index.place
                out_ref[chip_bits, i] = jnp.where(mine, low[index.slot(block)], 0.0)
    for copy in copies[2:]:
        copy.wait()
    for i in range(index.per_part):
        back_ref[i] = lax.dot_general(
            up[i], cot[i * BLK : (i + 1) * BLK], LAST, preferred_element_type=jnp.float32
        )


def narrow(index_of, index, shape, tokens, down, cotangent, up, waits):
    rank = up.shape[1]
    one = (shape.per_part, rank, BLK)
    outs = [(shape.chips,) + one, (shape.chips,) + one, one]
    operands = (tokens, down, cotangent, up)
    specs, extra = after(waits)
    return pl.pallas_call(
        functools.partial(narrow_kernel, index_of),
        grid_spec=pltpu.PrefetchScalarGridSpec(
            num_scalar_prefetch=1,
            grid=(1,),
            in_specs=[pl.BlockSpec(memory_space=pl.ANY)] * len(operands) + specs,
            out_specs=[held()] * len(outs),
            scratch_shapes=[
                pltpu.VMEM((CAP, rank, BLK), jnp.float32),
                pltpu.VMEM(tokens.shape, tokens.dtype),
                pltpu.VMEM(down.shape, down.dtype),
                pltpu.VMEM(cotangent.shape, cotangent.dtype),
                pltpu.VMEM((shape.per_part,) + up.shape[1:], up.dtype),
                pltpu.SemaphoreType.DMA((3 + shape.per_part,)),
            ],
        ),
        out_shape=[pltpu.VMEM(o, jnp.float32) for o in outs],
        compiler_params=SMALL,
        cost_estimate=BRIEF,
        name="narrow",
    )(index, *[in_hbm(o) for o in operands], *extra)


def merge_kernel(keep_ref, arrived_ref, back_ref, *refs):
    out_ref = refs[-1]
    total = keep_ref[0] + arrived_ref[0]
    for ref in refs[:-1][: keep_ref.shape[0] - 1]:
        total = total + ref[...]
    out_ref[0] = total
    out_ref[1] = back_ref[...]


def merge(keep, arrived, back, others, waits):
    specs, extra = after(waits)
    operands = (keep, arrived, back, *others)
    out = (2,) + back.shape
    return pl.pallas_call(
        merge_kernel,
        grid=(1,),
        in_specs=[whole(o.shape) for o in operands] + specs,
        out_specs=whole(out),
        out_shape=shape_of(out, jnp.float32),
        compiler_params=SMALL,
        cost_estimate=BRIEF,
        name="merge",
    )(*operands, *extra)


def pieces_kernel(index_of, count, index_ref, cot_ref, sum_ref, *refs):
    more_refs, (low_ref, back_ref, piece_ref) = refs[:count], refs[-3:]
    index = index_of(index_ref)
    level = [sum_ref[...]] + [ref[...] for ref in more_refs]
    while len(level) > 1:
        level = [level[j] + level[j + 1] for j in range(0, len(level), 2)]
    for i in range(index.per_part):
        live = index.live_rows(index.block(0, 0, i))
        keep = lax.broadcasted_iota(jnp.int32, low_ref.shape[1:], 1) < live
        lowered = jnp.where(keep, level[0][0, i], 0.0).astype(low_ref.dtype)
        low_ref[i] = lowered
        back_ref[i] = jnp.where(keep, level[0][1, i], 0.0).astype(back_ref.dtype)
        piece_ref[i] = jnp.dot(
            lowered, cot_ref[i * BLK : (i + 1) * BLK], preferred_element_type=jnp.float32
        ).astype(piece_ref.dtype)


def make_pieces(index_of, index, shape, total, more, cotangent, waits):
    _, per_part, rank, _ = total.shape
    width = cotangent.shape[1]
    outs = [(per_part, rank, BLK), (per_part, rank, BLK), (per_part, rank, width)]
    operands = (cotangent, total, *more)
    specs, extra = after(waits)
    return pl.pallas_call(
        functools.partial(pieces_kernel, index_of, len(more)),
        grid_spec=pltpu.PrefetchScalarGridSpec(
            num_scalar_prefetch=1,
            grid=(1,),
            in_specs=[whole(o.shape) for o in operands] + specs,
            out_specs=[whole(o) for o in outs],
        ),
        out_shape=[shape_of(o, jnp.bfloat16) for o in outs],
        compiler_params=SMALL,
        cost_estimate=BRIEF,
        name="pieces",
    )(index, *operands, *extra)


def down_gradient_kernel(index_of, index_ref, tokens_ref, *refs):
    back_refs, out_ref = refs[:-1], refs[-1]
    index = index_of(index_ref)
    out_ref[...] = jnp.zeros_like(out_ref)
    for core_bit in range(CORES):
        for chip_bits in range(index.chips):
            for i in range(index.per_part):
                block = index.block(core_bit, chip_bits, i)
                back_ref = back_refs[core_bit * index.chips + chip_bits]

                @pl.when(index.owner(block) == index.place)
                def _(block=block, back_ref=back_ref, i=i):
                    at = pl.multiple_of(index.slot(block) * BLK, BLK)
                    out_ref[0] += adapter_scale * jnp.dot(
                        back_ref[i],
                        tokens_ref[pl.ds(at, BLK)],
                        preferred_element_type=jnp.float32,
                    )


def down_gradient(index_of, index, tokens, backs):
    out = (1, backs[0].shape[1], tokens.shape[1])
    operands = (in_vmem(tokens), *backs)
    return pl.pallas_call(
        functools.partial(down_gradient_kernel, index_of),
        grid_spec=pltpu.PrefetchScalarGridSpec(
            num_scalar_prefetch=1,
            grid=(1,),
            in_specs=[held()] + [whole(o.shape) for o in backs],
            out_specs=whole(out),
        ),
        out_shape=shape_of(out, jnp.float32),
        compiler_params=SMALL,
        cost_estimate=BRIEF,
        name="down_gradient",
    )(index, *operands)


def up_gradient_kernel(index_of, index_ref, *refs):
    piece_refs, out_ref = refs[:-1], refs[-1]
    index = index_of(index_ref)

    def of_device(core_bit, chip_bits, adapter):
        total = None
        for i in range(index.per_part):
            mine = index.owner(index.block(core_bit, chip_bits, i)) == adapter
            piece = piece_refs[core_bit * index.chips + chip_bits][i].astype(jnp.float32)
            term = jnp.where(mine, piece, 0.0)
            total = term if total is None else total + term
        return total

    for adapter in range(index.adapters):
        level = [
            of_device(0, j, adapter) + of_device(1, j, adapter) for j in range(index.chips)
        ]
        while len(level) > 1:
            level = [level[j] + level[j + 1] for j in range(0, len(level), 2)]
        out_ref[adapter] = adapter_scale * level[0]


def up_gradient(index_of, index, adapter_count, pieces):
    per_part, rank, width = pieces[0].shape
    tile = 1024
    out = (adapter_count, rank, width)
    return pl.pallas_call(
        functools.partial(up_gradient_kernel, index_of),
        grid_spec=pltpu.PrefetchScalarGridSpec(
            num_scalar_prefetch=1,
            grid=(width // tile,),
            in_specs=[pl.BlockSpec((per_part, rank, tile), lambda n, _: (0, 0, n))] * len(pieces),
            out_specs=pl.BlockSpec((adapter_count, rank, tile), lambda n, _: (0, 0, n)),
        ),
        out_shape=shape_of(out, jnp.float32),
        compiler_params=SMALL,
        cost_estimate=BRIEF,
        name="up_gradient",
    )(index, *pieces)


def finish_kernel(index_of, index_ref, low_ref, *refs):
    index = index_of(index_ref)
    up_refs, sum_refs, out_ref = refs[: index.per_part], refs[index.per_part : -1], refs[-1]
    per_chunk = len(sum_refs) // len(CHUNK_ROWS)
    for i in range(index.per_part):
        block = index.block(0, 0, i)
        live = index.live_rows(block)
        side = lax.dot_general(
            low_ref[i],
            up_refs[i][0],
            (((0,), (0,)), ((), ())),
            preferred_element_type=jnp.float32,
        )
        start = 0
        for c, count in enumerate(CHUNK_ROWS):
            total = adapter_scale * side[start : start + count]
            for ref in sum_refs[c * per_chunk : (c + 1) * per_chunk]:
                total = total + ref[i * count : (i + 1) * count].astype(jnp.float32)
            keep = start + lax.broadcasted_iota(jnp.int32, total.shape, 0) < live
            at = i * BLK + start
            out_ref[at : at + count] = jnp.where(keep, total, 0.0).astype(out_ref.dtype)
            start += count


def finish(index_of, index, lowered, up, sums, part, projected, far):
    per_part = lowered.shape[0]
    _, rank, width = up.shape
    tile = min(1024, width // PARTS)
    tiles = width // PARTS // tile
    first = part * tiles
    out = (per_part * BLK, width)

    def factor(i):
        def at(n, index_ref):
            index = index_of(index_ref)
            return (index.owner(index.block(0, 0, i)), 0, first + n)

        return pl.BlockSpec((1, rank, tile), at)

    flat = [term for chunk in sums for term in chunk]
    specs = [
        pl.BlockSpec((per_part * count, tile), lambda n, _: (0, n))
        for chunk, count in zip(sums, CHUNK_ROWS)
        for _ in chunk
    ]
    operands = [index, lowered, *[up] * per_part, *flat]
    more, extra = after((), far)
    aliases = {}
    if projected is not None:
        aliases = {len(operands): 0}
        more, extra = [pl.BlockSpec(memory_space=pl.ANY)] + more, [projected] + extra

    def kernel(*refs):
        finish_kernel(index_of, *refs[: len(operands)], refs[-1])

    return pl.pallas_call(
        kernel,
        grid_spec=pltpu.PrefetchScalarGridSpec(
            num_scalar_prefetch=1,
            grid=(tiles,),
            in_specs=[whole(lowered.shape)] + [factor(i) for i in range(per_part)] + specs + more,
            out_specs=pl.BlockSpec((out[0], tile), lambda n, _: (0, first + n)),
        ),
        out_shape=shape_of(out, jnp.bfloat16),
        input_output_aliases=aliases,
        compiler_params=SMALL,
        cost_estimate=BRIEF,
        name="finish",
    )(*operands, *extra)


def per_device(
    tokens,
    cotangent,
    frozen_up_weight,
    adapter_down_factor,
    adapter_up_factor,
    tokens_per_adapter,
    adapter_of_block,
    slot_of_block,
):
    owners = lax.axis_size("dp")
    parts = lax.axis_size("tensor")
    chips = parts // CORES
    block_count = adapter_of_block.shape[0]
    adapter_count = adapter_up_factor.shape[0]
    width_dev = tokens.shape[1]
    index_of = functools.partial(
        Index, block_count=block_count, adapter_count=adapter_count, parts=parts
    )
    shape = index_of(None)
    index = Index.pack(adapter_of_block, slot_of_block, tokens_per_adapter)

    def to_other_core(value):
        return lax.ppermute(value, "tensor", [(i, i ^ 1) for i in range(parts)])

    def to_chip(value, k):
        return lax.ppermute(value, "tensor", [(i, i ^ (k * CORES)) for i in range(parts)])

    def across_dp(value, k):
        return lax.ppermute(value, "dp", [(i, i ^ k) for i in range(owners)])

    def same_core(value):
        return [value] + [to_chip(value, k) for k in range(1, chips)]

    def with_other_core(values):
        return values + [to_other_core(v) for v in values]

    def small_products(waits):
        return narrow(
            index_of,
            index,
            shape,
            tokens,
            jnp.swapaxes(adapter_down_factor, 1, 2),
            cotangent,
            adapter_up_factor,
            waits,
        )

    def over_parts(send, keep):
        arrived = to_other_core(send)
        return arrived, [to_chip(keep[k] + arrived[k], k) for k in range(1, chips)]

    def over_dp(total):
        k = 1
        while 2 * k < owners:
            total = total + across_dp(total, k)
            k *= 2
        return total, [across_dp(total, k)]

    if owners == 4 and block_count == 4:
        relay = Relay(index_of, index, tokens)
        sent = relay.first()
        send, keep, back = small_products([sent])
        arrived, others = over_parts(send, keep)
        total, more = over_dp(merge(keep, arrived, back, others, []))
        relay.second([total])
        lowered, back_rows, pieces = make_pieces(
            index_of, index, shape, total, more, cotangent, []
        )
        relay.settle([lowered])
        weight = load_weight(frozen_up_weight, relay.arrived[-1][1:3])
        pieces = with_other_core(same_core(pieces))
        back_rows = with_other_core(same_core(back_rows))
        ahead = [v for chunk in relay.arrived[1:] for v in chunk[3:5]]
        ahead.append(weight)
        chunks = [lambda waits: relay.rows(0, ahead)]
        chunks += [functools.partial(relay.rows, c) for c in range(1, len(CHUNK_ROWS))]
    else:
        weight = load_weight(frozen_up_weight, [])
        send, keep, back = small_products([])
        arrived, others = over_parts(send, keep)
        total, more = over_dp(merge(keep, arrived, back, others, []))
        lowered, back_rows, pieces = make_pieces(
            index_of, index, shape, total, more, cotangent, []
        )
        pieces = with_other_core(same_core(pieces))
        back_rows = with_other_core(same_core(back_rows))
        every_slot = lax.all_gather(
            tokens.reshape(CAP, BLK, width_dev), "dp", axis=0, tiled=True
        )
        part = lax.axis_index("tensor")
        devices = jnp.arange(parts, dtype=jnp.int32)
        order = (devices // chips ^ 1) + (devices % chips) * CORES ^ part
        blocks = (order[:, None] * shape.per_part + jnp.arange(shape.per_part)).reshape(-1)
        picked = every_slot[adapter_of_block[blocks] * CAP + slot_of_block[blocks]]
        starts = [sum(CHUNK_ROWS[:c]) for c in range(len(CHUNK_ROWS))]
        chunks = [
            lambda waits, s=s, count=count: picked[:, s : s + count].reshape(-1, width_dev)
            for s, count in zip(starts, CHUNK_ROWS)
        ]
    def summed(rows, part, waits):
        each = rows.shape[0] // parts
        send_own, send, own, other = split_product(shape, rows, weight, part, PARTS, waits)
        outgoing = (other + to_other_core(send).astype(jnp.float32)).astype(jnp.bfloat16)
        across = [to_chip(outgoing[(k - 1) * each : k * each], k) for k in range(1, chips)]
        return [own, to_other_core(send_own)] + across, outgoing

    sums, ready = [], ()
    waits = [pieces[1:chips], ()]
    for chunk in chunks:
        rows = chunk(ready)
        done = [summed(rows, part, waits[part]) for part in range(PARTS)]
        sums.append([terms for terms, _ in done])
        ready = [done[0][1]]
        waits = [
            [*sums[-1][0][2:], *back_rows[1:chips]],
            [*sums[-1][1][2:], *back_rows[chips:], *pieces[chips:]],
        ]
    up_grad = up_gradient(index_of, index, adapter_count, pieces)
    down_grad = down_gradient(index_of, index, tokens, back_rows)
    projected = None
    for part in range(PARTS):
        projected = finish(
            index_of,
            index,
            lowered,
            adapter_up_factor,
            [done[part] for done in sums],
            part,
            projected,
            [] if projected is not None else [up_grad, down_grad],
        )
    return (projected, jnp.swapaxes(down_grad, 1, 2), up_grad)


def solution(mesh):
    return jax.shard_map(
        per_device,
        mesh=mesh,
        in_specs=(
            P(("groups", "dp"), "tensor"),
            P(("groups", "tensor"), "dp"),
            P("tensor", "dp"),
            P(("groups", "dp"), "tensor", None),
            P("groups", None, "dp"),
            P("groups"),
            P("groups"),
            P("groups"),
        ),
        out_specs=(
            P(("groups", "tensor"), "dp"),
            P(("groups", "dp"), "tensor", None),
            P("groups", None, "dp"),
        ),
        check_vma=False,
    )
```

```python
import functools

import jax
import jax.numpy as jnp
from jax import lax
from jax.experimental import pallas as pl
from jax.experimental.pallas import tpu as pltpu
from jax.sharding import PartitionSpec as P

BLK = 128
CAP = 3
CORES = 2
CHUNK_ROWS = (64, 64)
PARTS = 2
SMALL = pltpu.CompilerParams(vmem_limit_bytes=12 * 2**20)

adapter_scale = 0.5

LAST = (((1,), (1,)), ((), ()))


class Index:
    def __init__(self, ref, block_count, adapter_count, parts):
        self.ref = ref
        self.blocks, self.adapters, self.parts = block_count, adapter_count, parts
        self.chips = parts // CORES
        self.per_part = block_count // parts

    @staticmethod
    def pack(adapter_of_block, slot_of_block, tokens_per_adapter):
        place = jnp.stack([lax.axis_index("dp"), lax.axis_index("tensor")]).astype(jnp.int32)
        return jnp.concatenate([adapter_of_block, slot_of_block, tokens_per_adapter, place])

    def owner(self, block):
        return self.ref[block]

    def slot(self, block):
        return self.ref[self.blocks + block]

    def tokens(self, adapter):
        return self.ref[2 * self.blocks + adapter]

    @property
    def place(self):
        return self.ref[2 * self.blocks + self.adapters]

    @property
    def part(self):
        return self.ref[2 * self.blocks + self.adapters + 1]

    def block(self, core_bit, chip_bits, i):
        return (self.part ^ (chip_bits * CORES + core_bit)) * self.per_part + i

    def position(self, block):
        bits = (block // self.per_part) ^ self.part
        half = (1 - bits % CORES) * self.chips + bits // CORES
        return half * self.per_part + block % self.per_part

    def live_rows(self, block):
        adapter = self.owner(block)
        first = jnp.int32(0)
        for a in range(self.adapters):
            count = (self.tokens(a) + BLK - 1) // BLK
            first = first + jnp.where(a < adapter, count, 0)
        return self.tokens(adapter) - (block - first) * BLK


def in_vmem(value):
    return pltpu.with_memory_space_constraint(value, pltpu.VMEM)


def in_hbm(value):
    return pltpu.with_memory_space_constraint(value, pltpu.HBM)


def held():
    return pl.BlockSpec(memory_space=pltpu.VMEM)


def whole(shape):
    return pl.BlockSpec(shape, lambda *_: (0,) * len(shape))


def shape_of(shape, dtype):
    return jax.ShapeDtypeStruct(shape, dtype)


BRIEF = pl.CostEstimate(flops=1, bytes_accessed=1, transcendentals=0)


def own_rows(index, block, tokens_ref, out_ref, start=0):
    at = pl.multiple_of(index.slot(block) * BLK + start, 16)
    out_ref[...] = tokens_ref[pl.ds(at, out_ref.shape[0])]


def first_hop_kernel(index_of, index_ref, tokens_ref, *refs):
    a_ref, b_ref, sems = refs[-3:]
    index = index_of(index_ref)
    copies = [
        pltpu.make_async_copy(
            tokens_ref.at[pl.ds(pl.multiple_of(index.slot(block) * BLK, BLK), BLK)],
            out_ref,
            sems.at[i],
        )
        for i, (block, out_ref) in enumerate(
            ((jnp.where(index.place == 0, 2, 1), a_ref), (0, b_ref))
        )
    ]
    for copy in copies:
        copy.start()
    for copy in copies:
        copy.wait()


def second_hop_kernel(index_of, index_ref, tokens_ref, a_ref, b_ref, *refs):
    x_ref, y_ref = refs[-2:]
    index = index_of(index_ref)
    place = index.place
    outer = jnp.where(place == 0, 1, jnp.where(place == 1, 0, 2))
    middle = jnp.where(place == 1, 2, 1)
    own_rows(index, outer, tokens_ref, x_ref)
    own_rows(index, middle, tokens_ref, y_ref)

    @pl.when((place == 1) & (index.owner(0) != 1))
    def _():
        x_ref[...] = b_ref[...]

    @pl.when(((place == 1) | (place == 2)) & (index.owner(middle) != place))
    def _():
        y_ref[...] = a_ref[...]


def settle_kernel(index_of, index_ref, tokens_ref, x_ref, y_ref, *refs):
    out_refs = refs[-len(CHUNK_ROWS) :]
    index = index_of(index_ref)
    place = index.place
    owner = index.owner(place)
    mine = owner == place
    edge = (place == 0) | ((place == 1) & (owner == 0)) | ((place == 2) & (owner == 3))
    start = 0
    for out_ref in out_refs:
        rows = slice(start, start + out_ref.shape[0])
        own_rows(index, place, tokens_ref, out_ref, start)

        @pl.when(jnp.logical_not(mine) & edge)
        def _(out_ref=out_ref, rows=rows):
            out_ref[...] = x_ref[rows]

        @pl.when(jnp.logical_not(mine | edge))
        def _(out_ref=out_ref, rows=rows):
            out_ref[...] = y_ref[rows]

        start += out_ref.shape[0]


def collect_kernel(index_of, count, index_ref, home_ref, outer_ref, *refs):
    inner_refs, outer_refs, out_ref = refs[:2], refs[2:4], refs[-1]
    index = index_of(index_ref)
    place = index.place

    def put(block, ref):
        at = pl.multiple_of(index.position(block) * count, 16)
        out_ref[pl.ds(at, count)] = ref[...]

    put(place, home_ref)
    put(place ^ 1, outer_ref)
    middle = (place == 1) | (place == 2)

    @pl.when(middle)
    def _():
        put(3 - place, inner_refs[0])
        put(place ^ 2, inner_refs[1])

    @pl.when(jnp.logical_not(middle))
    def _():
        put(place ^ 2, outer_refs[0])
        put(3 - place, outer_refs[1])


def after(values, far=()):
    specs = [
        pl.BlockSpec((1,) * (v.ndim - 2) + (16, 128), lambda *_, n=v.ndim: (0,) * n) for v in values
    ] + [pl.BlockSpec(memory_space=pl.ANY)] * len(far)
    return specs, [*values, *(in_hbm(v) for v in far)]


def hop_call(kernel, index, tokens, heights, received, waits, name):
    specs, extra = after(waits)
    width = tokens.shape[1]
    first = not received
    return pl.pallas_call(
        kernel,
        grid_spec=pltpu.PrefetchScalarGridSpec(
            num_scalar_prefetch=1,
            grid=(1,),
            in_specs=[pl.BlockSpec(memory_space=pl.ANY) if first else held()]
            + [held()] * len(received)
            + specs,
            out_specs=[held()] * len(heights),
            scratch_shapes=[pltpu.SemaphoreType.DMA((len(heights),))] * first,
        ),
        out_shape=[pltpu.VMEM((height, width), tokens.dtype) for height in heights],
        compiler_params=SMALL,
        cost_estimate=BRIEF,
        name=name,
    )(index, (in_hbm if first else in_vmem)(tokens), *[in_vmem(r) for r in received], *extra)


class Relay:
    def __init__(self, index_of, index, tokens):
        self.index_of, self.index, self.tokens = index_of, index, tokens

    def call(self, kernel, heights, received, waits, name):
        kernel = functools.partial(kernel, self.index_of)
        return hop_call(kernel, self.index, self.tokens, heights, received, waits, name)

    def first(self, waits=()):
        inward, left = self.call(first_hop_kernel, (BLK, BLK), (), waits, "first_hop")
        self.received = (
            lax.ppermute(inward, "dp", [(3, 2), (0, 1)]),
            lax.ppermute(left, "dp", [(2, 1)]),
        )
        return inward

    def second(self, waits=()):
        outer, middle = self.call(
            second_hop_kernel, (BLK, BLK), self.received, waits, "second_hop"
        )
        self.received = (
            lax.ppermute(outer, "dp", [(1, 0), (0, 1), (3, 2)]),
            lax.ppermute(middle, "dp", [(2, 1), (1, 2)]),
        )
        return outer

    def settle(self, waits=()):
        homes = self.call(settle_kernel, CHUNK_ROWS, self.received, waits, "settle")
        self.arrived = [self.spread(home) for home in homes]

    def spread(self, home):
        outer = lax.ppermute(home, "dp", [(0, 1), (1, 0), (2, 3), (3, 2)])
        inner = lax.ppermute(home, "dp", [(1, 2), (2, 1)])
        outer_2 = lax.ppermute(inner, "dp", [(1, 0), (2, 3)])
        inner_2 = lax.ppermute(outer, "dp", [(1, 2), (2, 1)])
        outer_3 = lax.ppermute(inner_2, "dp", [(1, 0), (2, 3)])
        return home, outer, inner, inner_2, outer_2, outer_3

    def rows(self, chunk, waits=(), far=()):
        arrived = self.arrived[chunk]
        count, width = arrived[0].shape
        specs, extra = after(waits, far)
        return pl.pallas_call(
            functools.partial(collect_kernel, self.index_of, count),
            grid_spec=pltpu.PrefetchScalarGridSpec(
                num_scalar_prefetch=1,
                grid=(1,),
                in_specs=[held()] * len(arrived) + specs,
                out_specs=held(),
            ),
            out_shape=pltpu.VMEM((4 * count, width), self.tokens.dtype),
            compiler_params=SMALL,
            cost_estimate=BRIEF,
            name="collect",
        )(self.index, *[in_vmem(a) for a in arrived], *extra)


def load_weight_kernel(w_ref, *refs):
    out_ref, sems = refs[-2:]
    streams = sems.shape[0]
    depth = w_ref.shape[0] // streams
    copies = [
        pltpu.make_async_copy(
            w_ref.at[pl.ds(i * depth, depth)], out_ref.at[pl.ds(i * depth, depth)], sems.at[i]
        )
        for i in range(streams)
    ]
    for copy in copies:
        copy.start()
    for copy in copies:
        copy.wait()


def load_weight(weight, waits):
    specs, extra = after(waits)
    return pl.pallas_call(
        load_weight_kernel,
        grid=(1,),
        in_specs=[pl.BlockSpec(memory_space=pl.ANY)] + specs,
        out_specs=pl.BlockSpec(memory_space=pl.ANY),
        out_shape=pltpu.VMEM(weight.shape, weight.dtype),
        scratch_shapes=[pltpu.SemaphoreType.DMA((4,))],
        compiler_params=SMALL,
        cost_estimate=BRIEF,
        name="load_weight",
    )(in_hbm(weight), *extra)


def split_product_kernel(each, half, first, tile, rows_ref, w_ref, *refs):
    send_ref, own_ref, other_ref = refs[-3:]
    for n in range(own_ref.shape[1] // tile):
        total = jnp.dot(
            rows_ref[...],
            w_ref[:, first + n * tile : first + (n + 1) * tile],
            preferred_element_type=jnp.float32,
        )
        columns = slice(n * tile, (n + 1) * tile)
        send_ref[:, columns] = total[:half].astype(send_ref.dtype)
        own_ref[:, columns] = total[half : half + each]
        other_ref[:, columns] = total[half + each :]


def split_product(shape, rows, weight, part, part_count, waits):
    half = rows.shape[0] // 2
    each = half // shape.chips
    width = weight.shape[1] // part_count
    specs, extra = after(waits)
    return pl.pallas_call(
        functools.partial(split_product_kernel, each, half, part * width, min(512, width)),
        grid=(1,),
        in_specs=[held(), held()] + specs,
        out_specs=[held()] * 3,
        out_shape=[
            pltpu.VMEM((half, width), jnp.bfloat16),
            pltpu.VMEM((each, width), jnp.float32),
            pltpu.VMEM((half - each, width), jnp.float32),
        ],
        compiler_params=SMALL,
        cost_estimate=BRIEF,
        name="split_product",
    )(in_vmem(rows), in_vmem(weight), *extra)


def narrow_kernel(index_of, index_ref, tokens_ref, down_ref, cot_ref, up_ref, *refs):
    send_ref, keep_ref, back_ref, low, tokens, down, cot, up, sems = refs[-9:]
    index = index_of(index_ref)
    pairs = [(tokens_ref, tokens), (down_ref, down), (cot_ref, cot)]
    for i in range(index.per_part):
        adapter = index.owner(index.block(0, 0, i))
        pairs.append((up_ref.at[adapter], up.at[i]))
    copies = [
        pltpu.make_async_copy(source, target, sems.at[j])
        for j, (source, target) in enumerate(pairs)
    ]
    for copy in copies:
        copy.start()
    for copy in copies[:2]:
        copy.wait()
    for m in range(CAP):
        low[m] = lax.dot_general(
            down[0],
            tokens[m * BLK : (m + 1) * BLK],
            LAST,
            preferred_element_type=jnp.float32,
        )
    for core_bit, out_ref in ((1, send_ref), (0, keep_ref)):
        for chip_bits in range(index.chips):
            for i in range(index.per_part):
                block = index.block(core_bit, chip_bits, i)
                mine = index.owner(block) == index.place
                out_ref[chip_bits, i] = jnp.where(mine, low[index.slot(block)], 0.0)
    for copy in copies[2:]:
        copy.wait()
    for i in range(index.per_part):
        back_ref[i] = lax.dot_general(
            up[i], cot[i * BLK : (i + 1) * BLK], LAST, preferred_element_type=jnp.float32
        )


def narrow(index_of, index, shape, tokens, down, cotangent, up, waits):
    rank = up.shape[1]
    one = (shape.per_part, rank, BLK)
    outs = [(shape.chips,) + one, (shape.chips,) + one, one]
    operands = (tokens, down, cotangent, up)
    specs, extra = after(waits)
    return pl.pallas_call(
        functools.partial(narrow_kernel, index_of),
        grid_spec=pltpu.PrefetchScalarGridSpec(
            num_scalar_prefetch=1,
            grid=(1,),
            in_specs=[pl.BlockSpec(memory_space=pl.ANY)] * len(operands) + specs,
            out_specs=[held()] * len(outs),
            scratch_shapes=[
                pltpu.VMEM((CAP, rank, BLK), jnp.float32),
                pltpu.VMEM(tokens.shape, tokens.dtype),
                pltpu.VMEM(down.shape, down.dtype),
                pltpu.VMEM(cotangent.shape, cotangent.dtype),
                pltpu.VMEM((shape.per_part,) + up.shape[1:], up.dtype),
                pltpu.SemaphoreType.DMA((3 + shape.per_part,)),
            ],
        ),
        out_shape=[pltpu.VMEM(o, jnp.float32) for o in outs],
        compiler_params=SMALL,
        cost_estimate=BRIEF,
        name="narrow",
    )(index, *[in_hbm(o) for o in operands], *extra)


def merge_kernel(keep_ref, arrived_ref, back_ref, *refs):
    out_ref = refs[-1]
    total = keep_ref[0] + arrived_ref[0]
    for ref in refs[:-1][: keep_ref.shape[0] - 1]:
        total = total + ref[...]
    out_ref[0] = total
    out_ref[1] = back_ref[...]


def merge(keep, arrived, back, others, waits):
    specs, extra = after(waits)
    operands = (keep, arrived, back, *others)
    out = (2,) + back.shape
    return pl.pallas_call(
        merge_kernel,
        grid=(1,),
        in_specs=[whole(o.shape) for o in operands] + specs,
        out_specs=whole(out),
        out_shape=shape_of(out, jnp.float32),
        compiler_params=SMALL,
        cost_estimate=BRIEF,
        name="merge",
    )(*operands, *extra)


def pieces_kernel(index_of, count, index_ref, cot_ref, sum_ref, *refs):
    more_refs, (low_ref, back_ref, piece_ref) = refs[:count], refs[-3:]
    index = index_of(index_ref)
    level = [sum_ref[...]] + [ref[...] for ref in more_refs]
    while len(level) > 1:
        level = [level[j] + level[j + 1] for j in range(0, len(level), 2)]
    for i in range(index.per_part):
        live = index.live_rows(index.block(0, 0, i))
        keep = lax.broadcasted_iota(jnp.int32, low_ref.shape[1:], 1) < live
        lowered = jnp.where(keep, level[0][0, i], 0.0).astype(low_ref.dtype)
        low_ref[i] = lowered
        back_ref[i] = jnp.where(keep, level[0][1, i], 0.0).astype(back_ref.dtype)
        piece_ref[i] = jnp.dot(
            lowered, cot_ref[i * BLK : (i + 1) * BLK], preferred_element_type=jnp.float32
        ).astype(piece_ref.dtype)


def make_pieces(index_of, index, shape, total, more, cotangent, waits):
    _, per_part, rank, _ = total.shape
    width = cotangent.shape[1]
    outs = [(per_part, rank, BLK), (per_part, rank, BLK), (per_part, rank, width)]
    operands = (cotangent, total, *more)
    specs, extra = after(waits)
    return pl.pallas_call(
        functools.partial(pieces_kernel, index_of, len(more)),
        grid_spec=pltpu.PrefetchScalarGridSpec(
            num_scalar_prefetch=1,
            grid=(1,),
            in_specs=[whole(o.shape) for o in operands] + specs,
            out_specs=[whole(o) for o in outs],
        ),
        out_shape=[shape_of(o, jnp.bfloat16) for o in outs],
        compiler_params=SMALL,
        cost_estimate=BRIEF,
        name="pieces",
    )(index, *operands, *extra)


def down_gradient_kernel(index_of, index_ref, tokens_ref, *refs):
    back_refs, out_ref = refs[:-1], refs[-1]
    index = index_of(index_ref)
    out_ref[...] = jnp.zeros_like(out_ref)
    for core_bit in range(CORES):
        for chip_bits in range(index.chips):
            for i in range(index.per_part):
                block = index.block(core_bit, chip_bits, i)
                back_ref = back_refs[core_bit * index.chips + chip_bits]

                @pl.when(index.owner(block) == index.place)
                def _(block=block, back_ref=back_ref, i=i):
                    at = pl.multiple_of(index.slot(block) * BLK, BLK)
                    out_ref[0] += adapter_scale * jnp.dot(
                        back_ref[i],
                        tokens_ref[pl.ds(at, BLK)],
                        preferred_element_type=jnp.float32,
                    )


def down_gradient(index_of, index, tokens, backs):
    out = (1, backs[0].shape[1], tokens.shape[1])
    operands = (in_vmem(tokens), *backs)
    return pl.pallas_call(
        functools.partial(down_gradient_kernel, index_of),
        grid_spec=pltpu.PrefetchScalarGridSpec(
            num_scalar_prefetch=1,
            grid=(1,),
            in_specs=[held()] + [whole(o.shape) for o in backs],
            out_specs=whole(out),
        ),
        out_shape=shape_of(out, jnp.float32),
        compiler_params=SMALL,
        cost_estimate=BRIEF,
        name="down_gradient",
    )(index, *operands)


def up_gradient_kernel(index_of, index_ref, *refs):
    piece_refs, out_ref = refs[:-1], refs[-1]
    index = index_of(index_ref)

    def of_device(core_bit, chip_bits, adapter):
        total = None
        for i in range(index.per_part):
            mine = index.owner(index.block(core_bit, chip_bits, i)) == adapter
            piece = piece_refs[core_bit * index.chips + chip_bits][i].astype(jnp.float32)
            term = jnp.where(mine, piece, 0.0)
            total = term if total is None else total + term
        return total

    for adapter in range(index.adapters):
        level = [
            of_device(0, j, adapter) + of_device(1, j, adapter) for j in range(index.chips)
        ]
        while len(level) > 1:
            level = [level[j] + level[j + 1] for j in range(0, len(level), 2)]
        out_ref[adapter] = adapter_scale * level[0]


def up_gradient(index_of, index, adapter_count, pieces):
    per_part, rank, width = pieces[0].shape
    tile = 1024
    out = (adapter_count, rank, width)
    return pl.pallas_call(
        functools.partial(up_gradient_kernel, index_of),
        grid_spec=pltpu.PrefetchScalarGridSpec(
            num_scalar_prefetch=1,
            grid=(width // tile,),
            in_specs=[pl.BlockSpec((per_part, rank, tile), lambda n, _: (0, 0, n))] * len(pieces),
            out_specs=pl.BlockSpec((adapter_count, rank, tile), lambda n, _: (0, 0, n)),
        ),
        out_shape=shape_of(out, jnp.float32),
        compiler_params=SMALL,
        cost_estimate=BRIEF,
        name="up_gradient",
    )(index, *pieces)


def finish_kernel(index_of, index_ref, low_ref, *refs):
    index = index_of(index_ref)
    up_refs, sum_refs, out_ref = refs[: index.per_part], refs[index.per_part : -1], refs[-1]
    per_chunk = len(sum_refs) // len(CHUNK_ROWS)
    for i in range(index.per_part):
        block = index.block(0, 0, i)
        live = index.live_rows(block)
        side = lax.dot_general(
            low_ref[i],
            up_refs[i][0],
            (((0,), (0,)), ((), ())),
            preferred_element_type=jnp.float32,
        )
        start = 0
        for c, count in enumerate(CHUNK_ROWS):
            total = adapter_scale * side[start : start + count]
            for ref in sum_refs[c * per_chunk : (c + 1) * per_chunk]:
                total = total + ref[i * count : (i + 1) * count].astype(jnp.float32)
            keep = start + lax.broadcasted_iota(jnp.int32, total.shape, 0) < live
            at = i * BLK + start
            out_ref[at : at + count] = jnp.where(keep, total, 0.0).astype(out_ref.dtype)
            start += count


def finish(index_of, index, lowered, up, sums, part, projected, far):
    per_part = lowered.shape[0]
    _, rank, width = up.shape
    tile = min(1024, width // PARTS)
    tiles = width // PARTS // tile
    first = part * tiles
    out = (per_part * BLK, width)

    def factor(i):
        def at(n, index_ref):
            index = index_of(index_ref)
            return (index.owner(index.block(0, 0, i)), 0, first + n)

        return pl.BlockSpec((1, rank, tile), at)

    flat = [term for chunk in sums for term in chunk]
    specs = [
        pl.BlockSpec((per_part * count, tile), lambda n, _: (0, n))
        for chunk, count in zip(sums, CHUNK_ROWS)
        for _ in chunk
    ]
    operands = [index, lowered, *[up] * per_part, *flat]
    more, extra = after((), far)
    aliases = {}
    if projected is not None:
        aliases = {len(operands): 0}
        more, extra = [pl.BlockSpec(memory_space=pl.ANY)] + more, [projected] + extra

    def kernel(*refs):
        finish_kernel(index_of, *refs[: len(operands)], refs[-1])

    return pl.pallas_call(
        kernel,
        grid_spec=pltpu.PrefetchScalarGridSpec(
            num_scalar_prefetch=1,
            grid=(tiles,),
            in_specs=[whole(lowered.shape)] + [factor(i) for i in range(per_part)] + specs + more,
            out_specs=pl.BlockSpec((out[0], tile), lambda n, _: (0, first + n)),
        ),
        out_shape=shape_of(out, jnp.bfloat16),
        input_output_aliases=aliases,
        compiler_params=SMALL,
        cost_estimate=BRIEF,
        name="finish",
    )(*operands, *extra)


def per_device(
    tokens,
    cotangent,
    frozen_up_weight,
    adapter_down_factor,
    adapter_up_factor,
    tokens_per_adapter,
    adapter_of_block,
    slot_of_block,
):
    owners = lax.axis_size("dp")
    parts = lax.axis_size("tensor")
    chips = parts // CORES
    block_count = adapter_of_block.shape[0]
    adapter_count = adapter_up_factor.shape[0]
    width_dev = tokens.shape[1]
    index_of = functools.partial(
        Index, block_count=block_count, adapter_count=adapter_count, parts=parts
    )
    shape = index_of(None)
    index = Index.pack(adapter_of_block, slot_of_block, tokens_per_adapter)

    def to_other_core(value):
        return lax.ppermute(value, "tensor", [(i, i ^ 1) for i in range(parts)])

    def to_chip(value, k):
        return lax.ppermute(value, "tensor", [(i, i ^ (k * CORES)) for i in range(parts)])

    def across_dp(value, k):
        return lax.ppermute(value, "dp", [(i, i ^ k) for i in range(owners)])

    def same_core(value):
        return [value] + [to_chip(value, k) for k in range(1, chips)]

    def with_other_core(values):
        return values + [to_other_core(v) for v in values]

    def small_products(waits):
        return narrow(
            index_of,
            index,
            shape,
            tokens,
            jnp.swapaxes(adapter_down_factor, 1, 2),
            cotangent,
            adapter_up_factor,
            waits,
        )

    def over_parts(send, keep):
        arrived = to_other_core(send)
        return arrived, [to_chip(keep[k] + arrived[k], k) for k in range(1, chips)]

    def over_dp(total):
        k = 1
        while 2 * k < owners:
            total = total + across_dp(total, k)
            k *= 2
        return total, [across_dp(total, k)]

    if owners == 4 and block_count == 4:
        relay = Relay(index_of, index, tokens)
        sent = relay.first()
        send, keep, back = small_products([sent])
        arrived, others = over_parts(send, keep)
        total, more = over_dp(merge(keep, arrived, back, others, []))
        relay.second([total])
        lowered, back_rows, pieces = make_pieces(
            index_of, index, shape, total, more, cotangent, []
        )
        relay.settle([lowered])
        weight = load_weight(frozen_up_weight, relay.arrived[-1][1:3])
        pieces = with_other_core(same_core(pieces))
        back_rows = with_other_core(same_core(back_rows))
        ahead = [v for chunk in relay.arrived[1:] for v in chunk[3:5]]
        ahead.append(weight)
        chunks = [lambda waits: relay.rows(0, ahead)]
        chunks += [functools.partial(relay.rows, c) for c in range(1, len(CHUNK_ROWS))]
    else:
        weight = load_weight(frozen_up_weight, [])
        send, keep, back = small_products([])
        arrived, others = over_parts(send, keep)
        total, more = over_dp(merge(keep, arrived, back, others, []))
        lowered, back_rows, pieces = make_pieces(
            index_of, index, shape, total, more, cotangent, []
        )
        pieces = with_other_core(same_core(pieces))
        back_rows = with_other_core(same_core(back_rows))
        every_slot = lax.all_gather(
            tokens.reshape(CAP, BLK, width_dev), "dp", axis=0, tiled=True
        )
        part = lax.axis_index("tensor")
        devices = jnp.arange(parts, dtype=jnp.int32)
        order = (devices // chips ^ 1) + (devices % chips) * CORES ^ part
        blocks = (order[:, None] * shape.per_part + jnp.arange(shape.per_part)).reshape(-1)
        picked = every_slot[adapter_of_block[blocks] * CAP + slot_of_block[blocks]]
        starts = [sum(CHUNK_ROWS[:c]) for c in range(len(CHUNK_ROWS))]
        chunks = [
            lambda waits, s=s, count=count: picked[:, s : s + count].reshape(-1, width_dev)
            for s, count in zip(starts, CHUNK_ROWS)
        ]
    def summed(rows, part, waits):
        each = rows.shape[0] // parts
        send, own, other = split_product(shape, rows, weight, part, PARTS, waits)
        arrived = to_other_core(send)
        outgoing = (other + arrived[each:].astype(jnp.float32)).astype(jnp.bfloat16)
        across = [to_chip(outgoing[(k - 1) * each : k * each], k) for k in range(1, chips)]
        return [own, arrived] + across, outgoing

    first = chunks[0](())
    first_0 = summed(first, 0, pieces[1:chips])
    first_1 = summed(first, 1, ())
    second = chunks[1]([first_0[1], first_1[1]])
    second_0 = summed(second, 0, first_0[0][2:])
    second_1 = summed(second, 1, first_1[0][2:])
    sums = [[first_0[0], first_1[0]], [second_0[0], second_1[0]]]
    up_grad = up_gradient(index_of, index, adapter_count, pieces)
    down_grad = down_gradient(index_of, index, tokens, back_rows)
    projected = None
    for part in range(PARTS):
        projected = finish(
            index_of,
            index,
            lowered,
            adapter_up_factor,
            [done[part] for done in sums],
            part,
            projected,
            [] if projected is not None else [up_grad, down_grad],
        )
    return (projected, jnp.swapaxes(down_grad, 1, 2), up_grad)


def solution(mesh):
    return jax.shard_map(
        per_device,
        mesh=mesh,
        in_specs=(
            P(("groups", "dp"), "tensor"),
            P(("groups", "tensor"), "dp"),
            P("tensor", "dp"),
            P(("groups", "dp"), "tensor", None),
            P("groups", None, "dp"),
            P("groups"),
            P("groups"),
            P("groups"),
        ),
        out_specs=(
            P(("groups", "tensor"), "dp"),
            P(("groups", "dp"), "tensor", None),
            P("groups", None, "dp"),
        ),
        check_vma=False,
    )
```

```python
import functools

import jax
import jax.numpy as jnp
from jax import lax
from jax.experimental import pallas as pl
from jax.experimental.pallas import tpu as pltpu
from jax.sharding import PartitionSpec as P

BLK = 128
CAP = 3
CORES = 2
CHUNK_ROWS = (64, 64)
PARTS = 2
SMALL = pltpu.CompilerParams(vmem_limit_bytes=12 * 2**20)

adapter_scale = 0.5

LAST = (((1,), (1,)), ((), ()))


class Index:
    def __init__(self, ref, block_count, adapter_count, parts):
        self.ref = ref
        self.blocks, self.adapters, self.parts = block_count, adapter_count, parts
        self.chips = parts // CORES
        self.per_part = block_count // parts

    @staticmethod
    def pack(adapter_of_block, slot_of_block, tokens_per_adapter):
        place = jnp.stack([lax.axis_index("dp"), lax.axis_index("tensor")]).astype(jnp.int32)
        return jnp.concatenate([adapter_of_block, slot_of_block, tokens_per_adapter, place])

    def owner(self, block):
        return self.ref[block]

    def slot(self, block):
        return self.ref[self.blocks + block]

    def tokens(self, adapter):
        return self.ref[2 * self.blocks + adapter]

    @property
    def place(self):
        return self.ref[2 * self.blocks + self.adapters]

    @property
    def part(self):
        return self.ref[2 * self.blocks + self.adapters + 1]

    def block(self, core_bit, chip_bits, i):
        return (self.part ^ (chip_bits * CORES + core_bit)) * self.per_part + i

    def position(self, block):
        bits = (block // self.per_part) ^ self.part
        half = (1 - bits % CORES) * self.chips + bits // CORES
        return half * self.per_part + block % self.per_part

    def live_rows(self, block):
        adapter = self.owner(block)
        first = jnp.int32(0)
        for a in range(self.adapters):
            count = (self.tokens(a) + BLK - 1) // BLK
            first = first + jnp.where(a < adapter, count, 0)
        return self.tokens(adapter) - (block - first) * BLK


def in_vmem(value):
    return pltpu.with_memory_space_constraint(value, pltpu.VMEM)


def in_hbm(value):
    return pltpu.with_memory_space_constraint(value, pltpu.HBM)


def held():
    return pl.BlockSpec(memory_space=pltpu.VMEM)


def whole(shape):
    return pl.BlockSpec(shape, lambda *_: (0,) * len(shape))


def shape_of(shape, dtype):
    return jax.ShapeDtypeStruct(shape, dtype)


BRIEF = pl.CostEstimate(flops=1, bytes_accessed=1, transcendentals=0)


def own_rows(index, block, tokens_ref, out_ref, start=0):
    at = pl.multiple_of(index.slot(block) * BLK + start, 16)
    out_ref[...] = tokens_ref[pl.ds(at, out_ref.shape[0])]


def first_hop_kernel(index_of, index_ref, tokens_ref, *refs):
    a_ref, b_ref, sems = refs[-3:]
    index = index_of(index_ref)
    copies = [
        pltpu.make_async_copy(
            tokens_ref.at[pl.ds(pl.multiple_of(index.slot(block) * BLK, BLK), BLK)],
            out_ref,
            sems.at[i],
        )
        for i, (block, out_ref) in enumerate(
            ((jnp.where(index.place == 0, 2, 1), a_ref), (0, b_ref))
        )
    ]
    for copy in copies:
        copy.start()
    for copy in copies:
        copy.wait()


def second_hop_kernel(index_of, index_ref, tokens_ref, a_ref, b_ref, *refs):
    x_ref, y_ref = refs[-2:]
    index = index_of(index_ref)
    place = index.place
    outer = jnp.where(place == 0, 1, jnp.where(place == 1, 0, 2))
    middle = jnp.where(place == 1, 2, 1)
    own_rows(index, outer, tokens_ref, x_ref)
    own_rows(index, middle, tokens_ref, y_ref)

    @pl.when((place == 1) & (index.owner(0) != 1))
    def _():
        x_ref[...] = b_ref[...]

    @pl.when(((place == 1) | (place == 2)) & (index.owner(middle) != place))
    def _():
        y_ref[...] = a_ref[...]


def settle_kernel(index_of, index_ref, tokens_ref, x_ref, y_ref, *refs):
    out_refs = refs[-len(CHUNK_ROWS) :]
    index = index_of(index_ref)
    place = index.place
    owner = index.owner(place)
    mine = owner == place
    edge = (place == 0) | ((place == 1) & (owner == 0)) | ((place == 2) & (owner == 3))
    start = 0
    for out_ref in out_refs:
        rows = slice(start, start + out_ref.shape[0])
        own_rows(index, place, tokens_ref, out_ref, start)

        @pl.when(jnp.logical_not(mine) & edge)
        def _(out_ref=out_ref, rows=rows):
            out_ref[...] = x_ref[rows]

        @pl.when(jnp.logical_not(mine | edge))
        def _(out_ref=out_ref, rows=rows):
            out_ref[...] = y_ref[rows]

        start += out_ref.shape[0]


def collect_kernel(index_of, count, index_ref, home_ref, outer_ref, *refs):
    inner_refs, outer_refs, out_ref = refs[:2], refs[2:4], refs[-1]
    index = index_of(index_ref)
    place = index.place

    def put(block, ref):
        at = pl.multiple_of(index.position(block) * count, 16)
        out_ref[pl.ds(at, count)] = ref[...]

    put(place, home_ref)
    put(place ^ 1, outer_ref)
    middle = (place == 1) | (place == 2)

    @pl.when(middle)
    def _():
        put(3 - place, inner_refs[0])
        put(place ^ 2, inner_refs[1])

    @pl.when(jnp.logical_not(middle))
    def _():
        put(place ^ 2, outer_refs[0])
        put(3 - place, outer_refs[1])


def after(values, far=()):
    specs = [
        pl.BlockSpec((1,) * (v.ndim - 2) + (16, 128), lambda *_, n=v.ndim: (0,) * n) for v in values
    ] + [pl.BlockSpec(memory_space=pl.ANY)] * len(far)
    return specs, [*values, *(in_hbm(v) for v in far)]


def hop_call(kernel, index, tokens, heights, received, waits, name):
    specs, extra = after(waits)
    width = tokens.shape[1]
    first = not received
    return pl.pallas_call(
        kernel,
        grid_spec=pltpu.PrefetchScalarGridSpec(
            num_scalar_prefetch=1,
            grid=(1,),
            in_specs=[pl.BlockSpec(memory_space=pl.ANY) if first else held()]
            + [held()] * len(received)
            + specs,
            out_specs=[held()] * len(heights),
            scratch_shapes=[pltpu.SemaphoreType.DMA((len(heights),))] * first,
        ),
        out_shape=[pltpu.VMEM((height, width), tokens.dtype) for height in heights],
        compiler_params=SMALL,
        cost_estimate=BRIEF,
        name=name,
    )(index, (in_hbm if first else in_vmem)(tokens), *[in_vmem(r) for r in received], *extra)


class Relay:
    def __init__(self, index_of, index, tokens):
        self.index_of, self.index, self.tokens = index_of, index, tokens

    def call(self, kernel, heights, received, waits, name):
        kernel = functools.partial(kernel, self.index_of)
        return hop_call(kernel, self.index, self.tokens, heights, received, waits, name)

    def first(self, waits=()):
        inward, left = self.call(first_hop_kernel, (BLK, BLK), (), waits, "first_hop")
        self.received = (
            lax.ppermute(inward, "dp", [(3, 2), (0, 1)]),
            lax.ppermute(left, "dp", [(2, 1)]),
        )
        return inward

    def second(self, waits=()):
        outer, middle = self.call(
            second_hop_kernel, (BLK, BLK), self.received, waits, "second_hop"
        )
        self.received = (
            lax.ppermute(outer, "dp", [(1, 0), (0, 1), (3, 2)]),
            lax.ppermute(middle, "dp", [(2, 1), (1, 2)]),
        )
        return outer

    def settle(self, waits=()):
        homes = self.call(settle_kernel, CHUNK_ROWS, self.received, waits, "settle")
        self.arrived = [self.spread(home) for home in homes]

    def spread(self, home):
        outer = lax.ppermute(home, "dp", [(0, 1), (1, 0), (2, 3), (3, 2)])
        inner = lax.ppermute(home, "dp", [(1, 2), (2, 1)])
        outer_2 = lax.ppermute(inner, "dp", [(1, 0), (2, 3)])
        inner_2 = lax.ppermute(outer, "dp", [(1, 2), (2, 1)])
        outer_3 = lax.ppermute(inner_2, "dp", [(1, 0), (2, 3)])
        return home, outer, inner, inner_2, outer_2, outer_3

    def rows(self, chunk, waits=(), far=()):
        arrived = self.arrived[chunk]
        count, width = arrived[0].shape
        specs, extra = after(waits, far)
        return pl.pallas_call(
            functools.partial(collect_kernel, self.index_of, count),
            grid_spec=pltpu.PrefetchScalarGridSpec(
                num_scalar_prefetch=1,
                grid=(1,),
                in_specs=[held()] * len(arrived) + specs,
                out_specs=held(),
            ),
            out_shape=pltpu.VMEM((4 * count, width), self.tokens.dtype),
            compiler_params=SMALL,
            cost_estimate=BRIEF,
            name="collect",
        )(self.index, *[in_vmem(a) for a in arrived], *extra)


def load_weight_kernel(w_ref, *refs):
    out_ref, sems = refs[-2:]
    streams = sems.shape[0]
    depth = w_ref.shape[0] // streams
    copies = [
        pltpu.make_async_copy(
            w_ref.at[pl.ds(i * depth, depth)], out_ref.at[pl.ds(i * depth, depth)], sems.at[i]
        )
        for i in range(streams)
    ]
    for copy in copies:
        copy.start()
    for copy in copies:
        copy.wait()


def load_weight(weight, waits):
    specs, extra = after(waits)
    return pl.pallas_call(
        load_weight_kernel,
        grid=(1,),
        in_specs=[pl.BlockSpec(memory_space=pl.ANY)] + specs,
        out_specs=pl.BlockSpec(memory_space=pl.ANY),
        out_shape=pltpu.VMEM(weight.shape, weight.dtype),
        scratch_shapes=[pltpu.SemaphoreType.DMA((4,))],
        compiler_params=SMALL,
        cost_estimate=BRIEF,
        name="load_weight",
    )(in_hbm(weight), *extra)


def split_product_kernel(each, half, first, tile, rows_ref, w_ref, *refs):
    send_own_ref, send_ref, own_ref, other_ref = refs[-4:]
    for n in range(own_ref.shape[1] // tile):
        total = jnp.dot(
            rows_ref[...],
            w_ref[:, first + n * tile : first + (n + 1) * tile],
            preferred_element_type=jnp.float32,
        )
        columns = slice(n * tile, (n + 1) * tile)
        send_own_ref[:, columns] = total[:each].astype(send_own_ref.dtype)
        send_ref[:, columns] = total[each:half].astype(send_ref.dtype)
        own_ref[:, columns] = total[half : half + each]
        other_ref[:, columns] = total[half + each :]


def split_product(shape, rows, weight, part, part_count, waits):
    half = rows.shape[0] // 2
    each = half // shape.chips
    width = weight.shape[1] // part_count
    specs, extra = after(waits)
    return pl.pallas_call(
        functools.partial(split_product_kernel, each, half, part * width, min(512, width)),
        grid=(1,),
        in_specs=[held(), held()] + specs,
        out_specs=[held()] * 4,
        out_shape=[
            pltpu.VMEM((each, width), jnp.bfloat16),
            pltpu.VMEM((half - each, width), jnp.bfloat16),
            pltpu.VMEM((each, width), jnp.float32),
            pltpu.VMEM((half - each, width), jnp.float32),
        ],
        compiler_params=SMALL,
        cost_estimate=BRIEF,
        name="split_product",
    )(in_vmem(rows), in_vmem(weight), *extra)


def narrow_kernel(index_of, index_ref, tokens_ref, down_ref, cot_ref, up_ref, *refs):
    send_ref, keep_ref, back_ref, low, tokens, down, cot, up, sems = refs[-9:]
    index = index_of(index_ref)
    pairs = [(tokens_ref, tokens), (down_ref, down), (cot_ref, cot)]
    for i in range(index.per_part):
        adapter = index.owner(index.block(0, 0, i))
        pairs.append((up_ref.at[adapter], up.at[i]))
    copies = [
        pltpu.make_async_copy(source, target, sems.at[j])
        for j, (source, target) in enumerate(pairs)
    ]
    for copy in copies:
        copy.start()
    for copy in copies[:2]:
        copy.wait()
    for m in range(CAP):
        low[m] = lax.dot_general(
            down[0],
            tokens[m * BLK : (m + 1) * BLK],
            LAST,
            preferred_element_type=jnp.float32,
        )
    for core_bit, out_ref in ((1, send_ref), (0, keep_ref)):
        for chip_bits in range(index.chips):
            for i in range(index.per_part):
                block = index.block(core_bit, chip_bits, i)
                mine = index.owner(block) == index.place
                out_ref[chip_bits, i] = jnp.where(mine, low[index.slot(block)], 0.0)
    for copy in copies[2:]:
        copy.wait()
    for i in range(index.per_part):
        back_ref[i] = lax.dot_general(
            up[i], cot[i * BLK : (i + 1) * BLK], LAST, preferred_element_type=jnp.float32
        )


def narrow(index_of, index, shape, tokens, down, cotangent, up, waits):
    rank = up.shape[1]
    one = (shape.per_part, rank, BLK)
    outs = [(shape.chips,) + one, (shape.chips,) + one, one]
    operands = (tokens, down, cotangent, up)
    specs, extra = after(waits)
    return pl.pallas_call(
        functools.partial(narrow_kernel, index_of),
        grid_spec=pltpu.PrefetchScalarGridSpec(
            num_scalar_prefetch=1,
            grid=(1,),
            in_specs=[pl.BlockSpec(memory_space=pl.ANY)] * len(operands) + specs,
            out_specs=[held()] * len(outs),
            scratch_shapes=[
                pltpu.VMEM((CAP, rank, BLK), jnp.float32),
                pltpu.VMEM(tokens.shape, tokens.dtype),
                pltpu.VMEM(down.shape, down.dtype),
                pltpu.VMEM(cotangent.shape, cotangent.dtype),
                pltpu.VMEM((shape.per_part,) + up.shape[1:], up.dtype),
                pltpu.SemaphoreType.DMA((3 + shape.per_part,)),
            ],
        ),
        out_shape=[pltpu.VMEM(o, jnp.float32) for o in outs],
        compiler_params=SMALL,
        cost_estimate=BRIEF,
        name="narrow",
    )(index, *[in_hbm(o) for o in operands], *extra)


def merge_kernel(keep_ref, arrived_ref, back_ref, *refs):
    out_ref = refs[-1]
    total = keep_ref[0] + arrived_ref[0]
    for ref in refs[:-1][: keep_ref.shape[0] - 1]:
        total = total + ref[...]
    out_ref[0] = total
    out_ref[1] = back_ref[...]


def merge(keep, arrived, back, others, waits):
    specs, extra = after(waits)
    operands = (keep, arrived, back, *others)
    out = (2,) + back.shape
    return pl.pallas_call(
        merge_kernel,
        grid=(1,),
        in_specs=[whole(o.shape) for o in operands] + specs,
        out_specs=whole(out),
        out_shape=shape_of(out, jnp.float32),
        compiler_params=SMALL,
        cost_estimate=BRIEF,
        name="merge",
    )(*operands, *extra)


def pieces_kernel(index_of, count, index_ref, cot_ref, sum_ref, *refs):
    more_refs, (low_ref, back_ref, piece_ref) = refs[:count], refs[-3:]
    index = index_of(index_ref)
    level = [sum_ref[...]] + [ref[...] for ref in more_refs]
    while len(level) > 1:
        level = [level[j] + level[j + 1] for j in range(0, len(level), 2)]
    for i in range(index.per_part):
        live = index.live_rows(index.block(0, 0, i))
        keep = lax.broadcasted_iota(jnp.int32, low_ref.shape[1:], 1) < live
        lowered = jnp.where(keep, level[0][0, i], 0.0).astype(low_ref.dtype)
        low_ref[i] = lowered
        back_ref[i] = jnp.where(keep, level[0][1, i], 0.0).astype(back_ref.dtype)
        piece_ref[i] = jnp.dot(
            lowered, cot_ref[i * BLK : (i + 1) * BLK], preferred_element_type=jnp.float32
        ).astype(piece_ref.dtype)


def make_pieces(index_of, index, shape, total, more, cotangent, waits):
    _, per_part, rank, _ = total.shape
    width = cotangent.shape[1]
    outs = [(per_part, rank, BLK), (per_part, rank, BLK), (per_part, rank, width)]
    operands = (cotangent, total, *more)
    specs, extra = after(waits)
    return pl.pallas_call(
        functools.partial(pieces_kernel, index_of, len(more)),
        grid_spec=pltpu.PrefetchScalarGridSpec(
            num_scalar_prefetch=1,
            grid=(1,),
            in_specs=[whole(o.shape) for o in operands] + specs,
            out_specs=[whole(o) for o in outs],
        ),
        out_shape=[shape_of(o, jnp.bfloat16) for o in outs],
        compiler_params=SMALL,
        cost_estimate=BRIEF,
        name="pieces",
    )(index, *operands, *extra)


def down_gradient_kernel(index_of, index_ref, tokens_ref, *refs):
    back_refs, out_ref = refs[:-1], refs[-1]
    index = index_of(index_ref)
    out_ref[...] = jnp.zeros_like(out_ref)
    for core_bit in range(CORES):
        for chip_bits in range(index.chips):
            for i in range(index.per_part):
                block = index.block(core_bit, chip_bits, i)
                back_ref = back_refs[core_bit * index.chips + chip_bits]

                @pl.when(index.owner(block) == index.place)
                def _(block=block, back_ref=back_ref, i=i):
                    at = pl.multiple_of(index.slot(block) * BLK, BLK)
                    out_ref[0] += adapter_scale * jnp.dot(
                        back_ref[i],
                        tokens_ref[pl.ds(at, BLK)],
                        preferred_element_type=jnp.float32,
                    )


def down_gradient(index_of, index, tokens, backs):
    out = (1, backs[0].shape[1], tokens.shape[1])
    operands = (in_vmem(tokens), *backs)
    return pl.pallas_call(
        functools.partial(down_gradient_kernel, index_of),
        grid_spec=pltpu.PrefetchScalarGridSpec(
            num_scalar_prefetch=1,
            grid=(1,),
            in_specs=[held()] + [whole(o.shape) for o in backs],
            out_specs=whole(out),
        ),
        out_shape=shape_of(out, jnp.float32),
        compiler_params=SMALL,
        cost_estimate=BRIEF,
        name="down_gradient",
    )(index, *operands)


def up_gradient_kernel(index_of, index_ref, *refs):
    piece_refs, out_ref = refs[:-1], refs[-1]
    index = index_of(index_ref)

    def of_device(core_bit, chip_bits, adapter):
        total = None
        for i in range(index.per_part):
            mine = index.owner(index.block(core_bit, chip_bits, i)) == adapter
            piece = piece_refs[core_bit * index.chips + chip_bits][i].astype(jnp.float32)
            term = jnp.where(mine, piece, 0.0)
            total = term if total is None else total + term
        return total

    for adapter in range(index.adapters):
        level = [
            of_device(0, j, adapter) + of_device(1, j, adapter) for j in range(index.chips)
        ]
        while len(level) > 1:
            level = [level[j] + level[j + 1] for j in range(0, len(level), 2)]
        out_ref[adapter] = adapter_scale * level[0]


def up_gradient(index_of, index, adapter_count, pieces):
    per_part, rank, width = pieces[0].shape
    tile = 1024
    out = (adapter_count, rank, width)
    return pl.pallas_call(
        functools.partial(up_gradient_kernel, index_of),
        grid_spec=pltpu.PrefetchScalarGridSpec(
            num_scalar_prefetch=1,
            grid=(width // tile,),
            in_specs=[pl.BlockSpec((per_part, rank, tile), lambda n, _: (0, 0, n))] * len(pieces),
            out_specs=pl.BlockSpec((adapter_count, rank, tile), lambda n, _: (0, 0, n)),
        ),
        out_shape=shape_of(out, jnp.float32),
        compiler_params=SMALL,
        cost_estimate=BRIEF,
        name="up_gradient",
    )(index, *pieces)


def finish_kernel(index_of, index_ref, low_ref, *refs):
    index = index_of(index_ref)
    up_refs, sum_refs, out_ref = refs[: index.per_part], refs[index.per_part : -1], refs[-1]
    per_chunk = len(sum_refs) // len(CHUNK_ROWS)
    for i in range(index.per_part):
        block = index.block(0, 0, i)
        live = index.live_rows(block)
        side = lax.dot_general(
            low_ref[i],
            up_refs[i][0],
            (((0,), (0,)), ((), ())),
            preferred_element_type=jnp.float32,
        )
        start = 0
        for c, count in enumerate(CHUNK_ROWS):
            total = adapter_scale * side[start : start + count]
            for ref in sum_refs[c * per_chunk : (c + 1) * per_chunk]:
                total = total + ref[i * count : (i + 1) * count].astype(jnp.float32)
            keep = start + lax.broadcasted_iota(jnp.int32, total.shape, 0) < live
            at = i * BLK + start
            out_ref[at : at + count] = jnp.where(keep, total, 0.0).astype(out_ref.dtype)
            start += count


def finish(index_of, index, lowered, up, sums, part, projected, far):
    per_part = lowered.shape[0]
    _, rank, width = up.shape
    tile = min(1024, width // PARTS)
    tiles = width // PARTS // tile
    first = part * tiles
    out = (per_part * BLK, width)

    def factor(i):
        def at(n, index_ref):
            index = index_of(index_ref)
            return (index.owner(index.block(0, 0, i)), 0, first + n)

        return pl.BlockSpec((1, rank, tile), at)

    flat = [term for chunk in sums for term in chunk]
    specs = [
        pl.BlockSpec((per_part * count, tile), lambda n, _: (0, n))
        for chunk, count in zip(sums, CHUNK_ROWS)
        for _ in chunk
    ]
    operands = [index, lowered, *[up] * per_part, *flat]
    more, extra = after((), far)
    aliases = {}
    if projected is not None:
        aliases = {len(operands): 0}
        more, extra = [pl.BlockSpec(memory_space=pl.ANY)] + more, [projected] + extra

    def kernel(*refs):
        finish_kernel(index_of, *refs[: len(operands)], refs[-1])

    return pl.pallas_call(
        kernel,
        grid_spec=pltpu.PrefetchScalarGridSpec(
            num_scalar_prefetch=1,
            grid=(tiles,),
            in_specs=[whole(lowered.shape)] + [factor(i) for i in range(per_part)] + specs + more,
            out_specs=pl.BlockSpec((out[0], tile), lambda n, _: (0, first + n)),
        ),
        out_shape=shape_of(out, jnp.bfloat16),
        input_output_aliases=aliases,
        compiler_params=SMALL,
        cost_estimate=BRIEF,
        name="finish",
    )(*operands, *extra)


def per_device(
    tokens,
    cotangent,
    frozen_up_weight,
    adapter_down_factor,
    adapter_up_factor,
    tokens_per_adapter,
    adapter_of_block,
    slot_of_block,
):
    owners = lax.axis_size("dp")
    parts = lax.axis_size("tensor")
    chips = parts // CORES
    block_count = adapter_of_block.shape[0]
    adapter_count = adapter_up_factor.shape[0]
    width_dev = tokens.shape[1]
    index_of = functools.partial(
        Index, block_count=block_count, adapter_count=adapter_count, parts=parts
    )
    shape = index_of(None)
    index = Index.pack(adapter_of_block, slot_of_block, tokens_per_adapter)

    def to_other_core(value):
        return lax.ppermute(value, "tensor", [(i, i ^ 1) for i in range(parts)])

    def to_chip(value, k):
        return lax.ppermute(value, "tensor", [(i, i ^ (k * CORES)) for i in range(parts)])

    def across_dp(value, k):
        return lax.ppermute(value, "dp", [(i, i ^ k) for i in range(owners)])

    def same_core(value):
        return [value] + [to_chip(value, k) for k in range(1, chips)]

    def with_other_core(values):
        return values + [to_other_core(v) for v in values]

    def small_products(waits):
        return narrow(
            index_of,
            index,
            shape,
            tokens,
            jnp.swapaxes(adapter_down_factor, 1, 2),
            cotangent,
            adapter_up_factor,
            waits,
        )

    def over_parts(send, keep):
        arrived = to_other_core(send)
        return arrived, [to_chip(keep[k] + arrived[k], k) for k in range(1, chips)]

    def over_dp(total):
        k = 1
        while 2 * k < owners:
            total = total + across_dp(total, k)
            k *= 2
        return total, [across_dp(total, k)]

    if owners == 4 and block_count == 4:
        relay = Relay(index_of, index, tokens)
        sent = relay.first()
        send, keep, back = small_products([sent])
        arrived, others = over_parts(send, keep)
        total, more = over_dp(merge(keep, arrived, back, others, []))
        relay.second([total])
        lowered, back_rows, pieces = make_pieces(
            index_of, index, shape, total, more, cotangent, []
        )
        relay.settle([lowered])
        weight = load_weight(frozen_up_weight, relay.arrived[-1][1:3])
        pieces = with_other_core(same_core(pieces))
        back_rows = with_other_core(same_core(back_rows))
        ahead = [v for chunk in relay.arrived[1:] for v in chunk[3:5]]
        ahead.append(weight)
        chunks = [lambda waits: relay.rows(0, ahead)]
        chunks += [functools.partial(relay.rows, c) for c in range(1, len(CHUNK_ROWS))]
    else:
        weight = load_weight(frozen_up_weight, [])
        send, keep, back = small_products([])
        arrived, others = over_parts(send, keep)
        total, more = over_dp(merge(keep, arrived, back, others, []))
        lowered, back_rows, pieces = make_pieces(
            index_of, index, shape, total, more, cotangent, []
        )
        pieces = with_other_core(same_core(pieces))
        back_rows = with_other_core(same_core(back_rows))
        every_slot = lax.all_gather(
            tokens.reshape(CAP, BLK, width_dev), "dp", axis=0, tiled=True
        )
        part = lax.axis_index("tensor")
        devices = jnp.arange(parts, dtype=jnp.int32)
        order = (devices // chips ^ 1) + (devices % chips) * CORES ^ part
        blocks = (order[:, None] * shape.per_part + jnp.arange(shape.per_part)).reshape(-1)
        picked = every_slot[adapter_of_block[blocks] * CAP + slot_of_block[blocks]]
        starts = [sum(CHUNK_ROWS[:c]) for c in range(len(CHUNK_ROWS))]
        chunks = [
            lambda waits, s=s, count=count: picked[:, s : s + count].reshape(-1, width_dev)
            for s, count in zip(starts, CHUNK_ROWS)
        ]
    def summed(rows, part, waits):
        each = rows.shape[0] // parts
        send_own, send, own, other = split_product(shape, rows, weight, part, PARTS, waits)
        outgoing = (other + to_other_core(send).astype(jnp.float32)).astype(jnp.bfloat16)
        across = [to_chip(outgoing[(k - 1) * each : k * each], k) for k in range(1, chips)]
        return [own, to_other_core(send_own)] + across, outgoing

    sums, ready = [], ()
    waits = [pieces[1:chips], ()]
    for chunk in chunks:
        rows = chunk(ready)
        done = [summed(rows, part, waits[part]) for part in range(PARTS)]
        sums.append([terms for terms, _ in done])
        ready = [done[0][1]]
        waits = [
            [*sums[-1][0][2:], *back_rows[1:chips]],
            [*back_rows[chips:], *pieces[chips:]],
        ]
    up_grad = up_gradient(index_of, index, adapter_count, pieces)
    down_grad = down_gradient(index_of, index, tokens, back_rows)
    projected = None
    for part in range(PARTS):
        projected = finish(
            index_of,
            index,
            lowered,
            adapter_up_factor,
            [done[part] for done in sums],
            part,
            projected,
            [] if projected is not None else [up_grad, down_grad],
        )
    return (projected, jnp.swapaxes(down_grad, 1, 2), up_grad)


def solution(mesh):
    return jax.shard_map(
        per_device,
        mesh=mesh,
        in_specs=(
            P(("groups", "dp"), "tensor"),
            P(("groups", "tensor"), "dp"),
            P("tensor", "dp"),
            P(("groups", "dp"), "tensor", None),
            P("groups", None, "dp"),
            P("groups"),
            P("groups"),
            P("groups"),
        ),
        out_specs=(
            P(("groups", "tensor"), "dp"),
            P(("groups", "dp"), "tensor", None),
            P("groups", None, "dp"),
        ),
        check_vma=False,
    )
```

```python
import functools

import jax
import jax.numpy as jnp
from jax import lax
from jax.experimental import pallas as pl
from jax.experimental.pallas import tpu as pltpu
from jax.sharding import PartitionSpec as P

BLK = 128
CAP = 3
CORES = 2
CHUNK_ROWS = (64, 64)
PARTS = 2
SMALL = pltpu.CompilerParams(vmem_limit_bytes=12 * 2**20)

adapter_scale = 0.5

LAST = (((1,), (1,)), ((), ()))


class Index:
    def __init__(self, ref, block_count, adapter_count, parts):
        self.ref = ref
        self.blocks, self.adapters, self.parts = block_count, adapter_count, parts
        self.chips = parts // CORES
        self.per_part = block_count // parts

    @staticmethod
    def pack(adapter_of_block, slot_of_block, tokens_per_adapter):
        place = jnp.stack([lax.axis_index("dp"), lax.axis_index("tensor")]).astype(jnp.int32)
        return jnp.concatenate([adapter_of_block, slot_of_block, tokens_per_adapter, place])

    def owner(self, block):
        return self.ref[block]

    def slot(self, block):
        return self.ref[self.blocks + block]

    def tokens(self, adapter):
        return self.ref[2 * self.blocks + adapter]

    @property
    def place(self):
        return self.ref[2 * self.blocks + self.adapters]

    @property
    def part(self):
        return self.ref[2 * self.blocks + self.adapters + 1]

    def block(self, core_bit, chip_bits, i):
        return (self.part ^ (chip_bits * CORES + core_bit)) * self.per_part + i

    def position(self, block):
        bits = (block // self.per_part) ^ self.part
        half = (1 - bits % CORES) * self.chips + bits // CORES
        return half * self.per_part + block % self.per_part

    def live_rows(self, block):
        adapter = self.owner(block)
        first = jnp.int32(0)
        for a in range(self.adapters):
            count = (self.tokens(a) + BLK - 1) // BLK
            first = first + jnp.where(a < adapter, count, 0)
        return self.tokens(adapter) - (block - first) * BLK


def in_vmem(value):
    return pltpu.with_memory_space_constraint(value, pltpu.VMEM)


def in_hbm(value):
    return pltpu.with_memory_space_constraint(value, pltpu.HBM)


def held():
    return pl.BlockSpec(memory_space=pltpu.VMEM)


def whole(shape):
    return pl.BlockSpec(shape, lambda *_: (0,) * len(shape))


def shape_of(shape, dtype):
    return jax.ShapeDtypeStruct(shape, dtype)


BRIEF = pl.CostEstimate(flops=1, bytes_accessed=1, transcendentals=0)


def own_rows(index, block, tokens_ref, out_ref, start=0):
    at = pl.multiple_of(index.slot(block) * BLK + start, 16)
    out_ref[...] = tokens_ref[pl.ds(at, out_ref.shape[0])]


def first_hop_kernel(index_of, index_ref, tokens_ref, *refs):
    a_ref, b_ref, sems = refs[-3:]
    index = index_of(index_ref)
    copies = [
        pltpu.make_async_copy(
            tokens_ref.at[pl.ds(pl.multiple_of(index.slot(block) * BLK, BLK), BLK)],
            out_ref,
            sems.at[i],
        )
        for i, (block, out_ref) in enumerate(
            ((jnp.where(index.place == 0, 2, 1), a_ref), (0, b_ref))
        )
    ]
    for copy in copies:
        copy.start()
    for copy in copies:
        copy.wait()


def second_hop_kernel(index_of, index_ref, tokens_ref, a_ref, b_ref, *refs):
    x_ref, y_ref = refs[-2:]
    index = index_of(index_ref)
    place = index.place
    outer = jnp.where(place == 0, 1, jnp.where(place == 1, 0, 2))
    middle = jnp.where(place == 1, 2, 1)
    own_rows(index, outer, tokens_ref, x_ref)
    own_rows(index, middle, tokens_ref, y_ref)

    @pl.when((place == 1) & (index.owner(0) != 1))
    def _():
        x_ref[...] = b_ref[...]

    @pl.when(((place == 1) | (place == 2)) & (index.owner(middle) != place))
    def _():
        y_ref[...] = a_ref[...]


def settle_kernel(index_of, index_ref, tokens_ref, x_ref, y_ref, *refs):
    out_refs = refs[-len(CHUNK_ROWS) :]
    index = index_of(index_ref)
    place = index.place
    owner = index.owner(place)
    mine = owner == place
    edge = (place == 0) | ((place == 1) & (owner == 0)) | ((place == 2) & (owner == 3))
    start = 0
    for out_ref in out_refs:
        rows = slice(start, start + out_ref.shape[0])
        own_rows(index, place, tokens_ref, out_ref, start)

        @pl.when(jnp.logical_not(mine) & edge)
        def _(out_ref=out_ref, rows=rows):
            out_ref[...] = x_ref[rows]

        @pl.when(jnp.logical_not(mine | edge))
        def _(out_ref=out_ref, rows=rows):
            out_ref[...] = y_ref[rows]

        start += out_ref.shape[0]


def collect_kernel(index_of, count, index_ref, home_ref, outer_ref, *refs):
    inner_refs, outer_refs, out_ref = refs[:2], refs[2:4], refs[-1]
    index = index_of(index_ref)
    place = index.place

    def put(block, ref):
        at = pl.multiple_of(index.position(block) * count, 16)
        out_ref[pl.ds(at, count)] = ref[...]

    put(place, home_ref)
    put(place ^ 1, outer_ref)
    middle = (place == 1) | (place == 2)

    @pl.when(middle)
    def _():
        put(3 - place, inner_refs[0])
        put(place ^ 2, inner_refs[1])

    @pl.when(jnp.logical_not(middle))
    def _():
        put(place ^ 2, outer_refs[0])
        put(3 - place, outer_refs[1])


def after(values, far=()):
    specs = [
        pl.BlockSpec((1,) * (v.ndim - 2) + (16, 128), lambda *_, n=v.ndim: (0,) * n) for v in values
    ] + [pl.BlockSpec(memory_space=pl.ANY)] * len(far)
    return specs, [*values, *(in_hbm(v) for v in far)]


def hop_call(kernel, index, tokens, heights, received, waits, name):
    specs, extra = after(waits)
    width = tokens.shape[1]
    first = not received
    return pl.pallas_call(
        kernel,
        grid_spec=pltpu.PrefetchScalarGridSpec(
            num_scalar_prefetch=1,
            grid=(1,),
            in_specs=[pl.BlockSpec(memory_space=pl.ANY) if first else held()]
            + [held()] * len(received)
            + specs,
            out_specs=[held()] * len(heights),
            scratch_shapes=[pltpu.SemaphoreType.DMA((len(heights),))] * first,
        ),
        out_shape=[pltpu.VMEM((height, width), tokens.dtype) for height in heights],
        compiler_params=SMALL,
        cost_estimate=BRIEF,
        name=name,
    )(index, (in_hbm if first else in_vmem)(tokens), *[in_vmem(r) for r in received], *extra)


class Relay:
    def __init__(self, index_of, index, tokens):
        self.index_of, self.index, self.tokens = index_of, index, tokens

    def call(self, kernel, heights, received, waits, name):
        kernel = functools.partial(kernel, self.index_of)
        return hop_call(kernel, self.index, self.tokens, heights, received, waits, name)

    def first(self, waits=()):
        inward, left = self.call(first_hop_kernel, (BLK, BLK), (), waits, "first_hop")
        self.received = (
            lax.ppermute(inward, "dp", [(3, 2), (0, 1)]),
            lax.ppermute(left, "dp", [(2, 1)]),
        )
        return inward

    def second(self, waits=()):
        outer, middle = self.call(
            second_hop_kernel, (BLK, BLK), self.received, waits, "second_hop"
        )
        self.received = (
            lax.ppermute(outer, "dp", [(1, 0), (0, 1), (3, 2)]),
            lax.ppermute(middle, "dp", [(2, 1), (1, 2)]),
        )
        return outer

    def settle(self, waits=()):
        homes = self.call(settle_kernel, CHUNK_ROWS, self.received, waits, "settle")
        self.arrived = [self.spread(home) for home in homes]

    def spread(self, home):
        outer = lax.ppermute(home, "dp", [(0, 1), (1, 0), (2, 3), (3, 2)])
        inner = lax.ppermute(home, "dp", [(1, 2), (2, 1)])
        outer_2 = lax.ppermute(inner, "dp", [(1, 0), (2, 3)])
        inner_2 = lax.ppermute(outer, "dp", [(1, 2), (2, 1)])
        outer_3 = lax.ppermute(inner_2, "dp", [(1, 0), (2, 3)])
        return home, outer, inner, inner_2, outer_2, outer_3

    def rows(self, chunk, waits=(), far=()):
        arrived = self.arrived[chunk]
        count, width = arrived[0].shape
        specs, extra = after(waits, far)
        return pl.pallas_call(
            functools.partial(collect_kernel, self.index_of, count),
            grid_spec=pltpu.PrefetchScalarGridSpec(
                num_scalar_prefetch=1,
                grid=(1,),
                in_specs=[held()] * len(arrived) + specs,
                out_specs=held(),
            ),
            out_shape=pltpu.VMEM((4 * count, width), self.tokens.dtype),
            compiler_params=SMALL,
            cost_estimate=BRIEF,
            name="collect",
        )(self.index, *[in_vmem(a) for a in arrived], *extra)


def load_weight_kernel(w_ref, *refs):
    out_ref, sems = refs[-2:]
    streams = sems.shape[0]
    depth = w_ref.shape[0] // streams
    copies = [
        pltpu.make_async_copy(
            w_ref.at[pl.ds(i * depth, depth)], out_ref.at[pl.ds(i * depth, depth)], sems.at[i]
        )
        for i in range(streams)
    ]
    for copy in copies:
        copy.start()
    for copy in copies:
        copy.wait()


def load_weight(weight, waits):
    specs, extra = after(waits)
    return pl.pallas_call(
        load_weight_kernel,
        grid=(1,),
        in_specs=[pl.BlockSpec(memory_space=pl.ANY)] + specs,
        out_specs=pl.BlockSpec(memory_space=pl.ANY),
        out_shape=pltpu.VMEM(weight.shape, weight.dtype),
        scratch_shapes=[pltpu.SemaphoreType.DMA((4,))],
        compiler_params=SMALL,
        cost_estimate=BRIEF,
        name="load_weight",
    )(in_hbm(weight), *extra)


def split_product_kernel(each, half, first, tile, rows_ref, w_ref, *refs):
    send_own_ref, send_ref, own_ref, other_ref = refs[-4:]
    for n in range(own_ref.shape[1] // tile):
        total = jnp.dot(
            rows_ref[...],
            w_ref[:, first + n * tile : first + (n + 1) * tile],
            preferred_element_type=jnp.float32,
        )
        columns = slice(n * tile, (n + 1) * tile)
        send_own_ref[:, columns] = total[:each].astype(send_own_ref.dtype)
        send_ref[:, columns] = total[each:half].astype(send_ref.dtype)
        own_ref[:, columns] = total[half : half + each]
        other_ref[:, columns] = total[half + each :]


def split_product(shape, rows, weight, part, part_count, waits):
    half = rows.shape[0] // 2
    each = half // shape.chips
    width = weight.shape[1] // part_count
    specs, extra = after(waits)
    return pl.pallas_call(
        functools.partial(split_product_kernel, each, half, part * width, min(512, width)),
        grid=(1,),
        in_specs=[held(), held()] + specs,
        out_specs=[held()] * 4,
        out_shape=[
            pltpu.VMEM((each, width), jnp.bfloat16),
            pltpu.VMEM((half - each, width), jnp.bfloat16),
            pltpu.VMEM((each, width), jnp.float32),
            pltpu.VMEM((half - each, width), jnp.float32),
        ],
        compiler_params=SMALL,
        cost_estimate=BRIEF,
        name="split_product",
    )(in_vmem(rows), in_vmem(weight), *extra)


def narrow_kernel(index_of, index_ref, tokens_ref, down_ref, cot_ref, up_ref, *refs):
    send_ref, keep_ref, back_ref, low, tokens, down, cot, up, sems = refs[-9:]
    index = index_of(index_ref)
    pairs = [(tokens_ref, tokens), (down_ref, down), (cot_ref, cot)]
    for i in range(index.per_part):
        adapter = index.owner(index.block(0, 0, i))
        pairs.append((up_ref.at[adapter], up.at[i]))
    copies = [
        pltpu.make_async_copy(source, target, sems.at[j])
        for j, (source, target) in enumerate(pairs)
    ]
    for copy in copies:
        copy.start()
    for copy in copies[:2]:
        copy.wait()
    for m in range(CAP):
        low[m] = lax.dot_general(
            down[0],
            tokens[m * BLK : (m + 1) * BLK],
            LAST,
            preferred_element_type=jnp.float32,
        )
    for core_bit, out_ref in ((1, send_ref), (0, keep_ref)):
        for chip_bits in range(index.chips):
            for i in range(index.per_part):
                block = index.block(core_bit, chip_bits, i)
                mine = index.owner(block) == index.place
                out_ref[chip_bits, i] = jnp.where(mine, low[index.slot(block)], 0.0)
    for copy in copies[2:]:
        copy.wait()
    for i in range(index.per_part):
        back_ref[i] = lax.dot_general(
            up[i], cot[i * BLK : (i + 1) * BLK], LAST, preferred_element_type=jnp.float32
        )


def narrow(index_of, index, shape, tokens, down, cotangent, up, waits):
    rank = up.shape[1]
    one = (shape.per_part, rank, BLK)
    outs = [(shape.chips,) + one, (shape.chips,) + one, one]
    operands = (tokens, down, cotangent, up)
    specs, extra = after(waits)
    return pl.pallas_call(
        functools.partial(narrow_kernel, index_of),
        grid_spec=pltpu.PrefetchScalarGridSpec(
            num_scalar_prefetch=1,
            grid=(1,),
            in_specs=[pl.BlockSpec(memory_space=pl.ANY)] * len(operands) + specs,
            out_specs=[held()] * len(outs),
            scratch_shapes=[
                pltpu.VMEM((CAP, rank, BLK), jnp.float32),
                pltpu.VMEM(tokens.shape, tokens.dtype),
                pltpu.VMEM(down.shape, down.dtype),
                pltpu.VMEM(cotangent.shape, cotangent.dtype),
                pltpu.VMEM((shape.per_part,) + up.shape[1:], up.dtype),
                pltpu.SemaphoreType.DMA((3 + shape.per_part,)),
            ],
        ),
        out_shape=[pltpu.VMEM(o, jnp.float32) for o in outs],
        compiler_params=SMALL,
        cost_estimate=BRIEF,
        name="narrow",
    )(index, *[in_hbm(o) for o in operands], *extra)


def merge_kernel(keep_ref, arrived_ref, back_ref, *refs):
    out_ref = refs[-1]
    total = keep_ref[0] + arrived_ref[0]
    for ref in refs[:-1][: keep_ref.shape[0] - 1]:
        total = total + ref[...]
    out_ref[0] = total
    out_ref[1] = back_ref[...]


def merge(keep, arrived, back, others, waits):
    specs, extra = after(waits)
    operands = (keep, arrived, back, *others)
    out = (2,) + back.shape
    return pl.pallas_call(
        merge_kernel,
        grid=(1,),
        in_specs=[whole(o.shape) for o in operands] + specs,
        out_specs=whole(out),
        out_shape=shape_of(out, jnp.float32),
        compiler_params=SMALL,
        cost_estimate=BRIEF,
        name="merge",
    )(*operands, *extra)


def pieces_kernel(index_of, count, index_ref, cot_ref, sum_ref, *refs):
    more_refs, (low_ref, back_ref, piece_ref) = refs[:count], refs[-3:]
    index = index_of(index_ref)
    level = [sum_ref[...]] + [ref[...] for ref in more_refs]
    while len(level) > 1:
        level = [level[j] + level[j + 1] for j in range(0, len(level), 2)]
    for i in range(index.per_part):
        live = index.live_rows(index.block(0, 0, i))
        keep = lax.broadcasted_iota(jnp.int32, low_ref.shape[1:], 1) < live
        lowered = jnp.where(keep, level[0][0, i], 0.0).astype(low_ref.dtype)
        low_ref[i] = lowered
        back_ref[i] = jnp.where(keep, level[0][1, i], 0.0).astype(back_ref.dtype)
        piece_ref[i] = jnp.dot(
            lowered, cot_ref[i * BLK : (i + 1) * BLK], preferred_element_type=jnp.float32
        ).astype(piece_ref.dtype)


def make_pieces(index_of, index, shape, total, more, cotangent, waits):
    _, per_part, rank, _ = total.shape
    width = cotangent.shape[1]
    outs = [(per_part, rank, BLK), (per_part, rank, BLK), (per_part, rank, width)]
    operands = (cotangent, total, *more)
    specs, extra = after(waits)
    return pl.pallas_call(
        functools.partial(pieces_kernel, index_of, len(more)),
        grid_spec=pltpu.PrefetchScalarGridSpec(
            num_scalar_prefetch=1,
            grid=(1,),
            in_specs=[whole(o.shape) for o in operands] + specs,
            out_specs=[whole(o) for o in outs],
        ),
        out_shape=[shape_of(o, jnp.bfloat16) for o in outs],
        compiler_params=SMALL,
        cost_estimate=BRIEF,
        name="pieces",
    )(index, *operands, *extra)


def hand_on_kernel(count, *refs):
    for source, target in zip(refs[:count], refs[-count:]):
        target[...] = source[...]


def hand_on(values, waits):
    specs, extra = after(waits)
    return pl.pallas_call(
        functools.partial(hand_on_kernel, len(values)),
        grid=(1,),
        in_specs=[held()] * len(values) + specs,
        out_specs=[held()] * len(values),
        out_shape=[pltpu.VMEM(v.shape, v.dtype) for v in values],
        compiler_params=SMALL,
        cost_estimate=BRIEF,
        name="hand_on",
    )(*[in_vmem(v) for v in values], *extra)


def down_gradient_kernel(index_of, index_ref, tokens_ref, *refs):
    back_refs, out_ref = refs[:-1], refs[-1]
    index = index_of(index_ref)
    out_ref[...] = jnp.zeros_like(out_ref)
    for core_bit in range(CORES):
        for chip_bits in range(index.chips):
            for i in range(index.per_part):
                block = index.block(core_bit, chip_bits, i)
                back_ref = back_refs[core_bit * index.chips + chip_bits]

                @pl.when(index.owner(block) == index.place)
                def _(block=block, back_ref=back_ref, i=i):
                    at = pl.multiple_of(index.slot(block) * BLK, BLK)
                    out_ref[0] += adapter_scale * jnp.dot(
                        back_ref[i],
                        tokens_ref[pl.ds(at, BLK)],
                        preferred_element_type=jnp.float32,
                    )


def down_gradient(index_of, index, tokens, backs):
    out = (1, backs[0].shape[1], tokens.shape[1])
    operands = (in_vmem(tokens), *backs)
    return pl.pallas_call(
        functools.partial(down_gradient_kernel, index_of),
        grid_spec=pltpu.PrefetchScalarGridSpec(
            num_scalar_prefetch=1,
            grid=(1,),
            in_specs=[held()] + [whole(o.shape) for o in backs],
            out_specs=whole(out),
        ),
        out_shape=shape_of(out, jnp.float32),
        compiler_params=SMALL,
        cost_estimate=BRIEF,
        name="down_gradient",
    )(index, *operands)


def up_gradient_kernel(index_of, index_ref, *refs):
    piece_refs, out_ref = refs[:-1], refs[-1]
    index = index_of(index_ref)

    def of_device(core_bit, chip_bits, adapter):
        total = None
        for i in range(index.per_part):
            mine = index.owner(index.block(core_bit, chip_bits, i)) == adapter
            piece = piece_refs[core_bit * index.chips + chip_bits][i].astype(jnp.float32)
            term = jnp.where(mine, piece, 0.0)
            total = term if total is None else total + term
        return total

    for adapter in range(index.adapters):
        level = [
            of_device(0, j, adapter) + of_device(1, j, adapter) for j in range(index.chips)
        ]
        while len(level) > 1:
            level = [level[j] + level[j + 1] for j in range(0, len(level), 2)]
        out_ref[adapter] = adapter_scale * level[0]


def up_gradient(index_of, index, adapter_count, pieces):
    per_part, rank, width = pieces[0].shape
    tile = 1024
    out = (adapter_count, rank, width)
    return pl.pallas_call(
        functools.partial(up_gradient_kernel, index_of),
        grid_spec=pltpu.PrefetchScalarGridSpec(
            num_scalar_prefetch=1,
            grid=(width // tile,),
            in_specs=[pl.BlockSpec((per_part, rank, tile), lambda n, _: (0, 0, n))] * len(pieces),
            out_specs=pl.BlockSpec((adapter_count, rank, tile), lambda n, _: (0, 0, n)),
        ),
        out_shape=shape_of(out, jnp.float32),
        compiler_params=SMALL,
        cost_estimate=BRIEF,
        name="up_gradient",
    )(index, *pieces)


def finish_kernel(index_of, index_ref, low_ref, *refs):
    index = index_of(index_ref)
    up_refs, sum_refs, out_ref = refs[: index.per_part], refs[index.per_part : -1], refs[-1]
    per_chunk = len(sum_refs) // len(CHUNK_ROWS)
    for i in range(index.per_part):
        block = index.block(0, 0, i)
        live = index.live_rows(block)
        side = lax.dot_general(
            low_ref[i],
            up_refs[i][0],
            (((0,), (0,)), ((), ())),
            preferred_element_type=jnp.float32,
        )
        start = 0
        for c, count in enumerate(CHUNK_ROWS):
            total = adapter_scale * side[start : start + count]
            for ref in sum_refs[c * per_chunk : (c + 1) * per_chunk]:
                total = total + ref[i * count : (i + 1) * count].astype(jnp.float32)
            keep = start + lax.broadcasted_iota(jnp.int32, total.shape, 0) < live
            at = i * BLK + start
            out_ref[at : at + count] = jnp.where(keep, total, 0.0).astype(out_ref.dtype)
            start += count


def finish(index_of, index, lowered, up, sums, part, projected, far):
    per_part = lowered.shape[0]
    _, rank, width = up.shape
    tile = min(1024, width // PARTS)
    tiles = width // PARTS // tile
    first = part * tiles
    out = (per_part * BLK, width)

    def factor(i):
        def at(n, index_ref):
            index = index_of(index_ref)
            return (index.owner(index.block(0, 0, i)), 0, first + n)

        return pl.BlockSpec((1, rank, tile), at)

    flat = [term for chunk in sums for term in chunk]
    specs = [
        pl.BlockSpec((per_part * count, tile), lambda n, _: (0, n))
        for chunk, count in zip(sums, CHUNK_ROWS)
        for _ in chunk
    ]
    operands = [index, lowered, *[up] * per_part, *flat]
    more, extra = after((), far)
    aliases = {}
    if projected is not None:
        aliases = {len(operands): 0}
        more, extra = [pl.BlockSpec(memory_space=pl.ANY)] + more, [projected] + extra

    def kernel(*refs):
        finish_kernel(index_of, *refs[: len(operands)], refs[-1])

    return pl.pallas_call(
        kernel,
        grid_spec=pltpu.PrefetchScalarGridSpec(
            num_scalar_prefetch=1,
            grid=(tiles,),
            in_specs=[whole(lowered.shape)] + [factor(i) for i in range(per_part)] + specs + more,
            out_specs=pl.BlockSpec((out[0], tile), lambda n, _: (0, first + n)),
        ),
        out_shape=shape_of(out, jnp.bfloat16),
        input_output_aliases=aliases,
        compiler_params=SMALL,
        cost_estimate=BRIEF,
        name="finish",
    )(*operands, *extra)


def per_device(
    tokens,
    cotangent,
    frozen_up_weight,
    adapter_down_factor,
    adapter_up_factor,
    tokens_per_adapter,
    adapter_of_block,
    slot_of_block,
):
    owners = lax.axis_size("dp")
    parts = lax.axis_size("tensor")
    chips = parts // CORES
    block_count = adapter_of_block.shape[0]
    adapter_count = adapter_up_factor.shape[0]
    width_dev = tokens.shape[1]
    index_of = functools.partial(
        Index, block_count=block_count, adapter_count=adapter_count, parts=parts
    )
    shape = index_of(None)
    index = Index.pack(adapter_of_block, slot_of_block, tokens_per_adapter)

    def to_other_core(value):
        return lax.ppermute(value, "tensor", [(i, i ^ 1) for i in range(parts)])

    def to_chip(value, k):
        return lax.ppermute(value, "tensor", [(i, i ^ (k * CORES)) for i in range(parts)])

    def across_dp(value, k):
        return lax.ppermute(value, "dp", [(i, i ^ k) for i in range(owners)])

    def same_core(value):
        return [value] + [to_chip(value, k) for k in range(1, chips)]

    def with_other_core(values):
        return values + [to_other_core(v) for v in values]

    def small_products(waits):
        return narrow(
            index_of,
            index,
            shape,
            tokens,
            jnp.swapaxes(adapter_down_factor, 1, 2),
            cotangent,
            adapter_up_factor,
            waits,
        )

    def over_parts(send, keep):
        arrived = to_other_core(send)
        return arrived, [to_chip(keep[k] + arrived[k], k) for k in range(1, chips)]

    def over_dp(total):
        k = 1
        while 2 * k < owners:
            total = total + across_dp(total, k)
            k *= 2
        return total, [across_dp(total, k)]

    if owners == 4 and block_count == 4:
        relay = Relay(index_of, index, tokens)
        sent = relay.first()
        send, keep, back = small_products([sent])
        arrived, others = over_parts(send, keep)
        total, more = over_dp(merge(keep, arrived, back, others, []))
        relay.second([total])
        lowered, back_rows, pieces = make_pieces(
            index_of, index, shape, total, more, cotangent, []
        )
        relay.settle([lowered])
        weight = load_weight(frozen_up_weight, relay.arrived[-1][1:3])
        pieces = with_other_core(same_core(pieces))
        back_rows = same_core(back_rows)
        ahead = [v for chunk in relay.arrived[1:] for v in chunk[3:5]]
        ahead.append(weight)
        chunks = [lambda waits: relay.rows(0, ahead)]
        chunks += [functools.partial(relay.rows, c) for c in range(1, len(CHUNK_ROWS))]
    else:
        weight = load_weight(frozen_up_weight, [])
        send, keep, back = small_products([])
        arrived, others = over_parts(send, keep)
        total, more = over_dp(merge(keep, arrived, back, others, []))
        lowered, back_rows, pieces = make_pieces(
            index_of, index, shape, total, more, cotangent, []
        )
        pieces = with_other_core(same_core(pieces))
        back_rows = same_core(back_rows)
        every_slot = lax.all_gather(
            tokens.reshape(CAP, BLK, width_dev), "dp", axis=0, tiled=True
        )
        part = lax.axis_index("tensor")
        devices = jnp.arange(parts, dtype=jnp.int32)
        order = (devices // chips ^ 1) + (devices % chips) * CORES ^ part
        blocks = (order[:, None] * shape.per_part + jnp.arange(shape.per_part)).reshape(-1)
        picked = every_slot[adapter_of_block[blocks] * CAP + slot_of_block[blocks]]
        starts = [sum(CHUNK_ROWS[:c]) for c in range(len(CHUNK_ROWS))]
        chunks = [
            lambda waits, s=s, count=count: picked[:, s : s + count].reshape(-1, width_dev)
            for s, count in zip(starts, CHUNK_ROWS)
        ]
    def summed(rows, part, waits):
        each = rows.shape[0] // parts
        send_own, send, own, other = split_product(shape, rows, weight, part, PARTS, waits)
        outgoing = (other + to_other_core(send).astype(jnp.float32)).astype(jnp.bfloat16)
        across = [to_chip(outgoing[(k - 1) * each : k * each], k) for k in range(1, chips)]
        return [own, to_other_core(send_own)] + across, outgoing

    first = chunks[0](())
    first_0 = summed(first, 0, pieces[1:chips])
    first_1 = summed(first, 1, ())
    back_rows = with_other_core(list(hand_on(back_rows, first_1[0][2:])))
    second = chunks[1]([first_0[1]])
    second_0 = summed(second, 0, back_rows[1:chips])
    second_1 = summed(second, 1, [*first_0[0][2:], *back_rows[chips:]])
    sums = [[first_0[0], first_1[0]], [second_0[0], second_1[0]]]
    up_grad = up_gradient(index_of, index, adapter_count, pieces)
    down_grad = down_gradient(index_of, index, tokens, back_rows)
    projected = None
    for part in range(PARTS):
        projected = finish(
            index_of,
            index,
            lowered,
            adapter_up_factor,
            [done[part] for done in sums],
            part,
            projected,
            [] if projected is not None else [up_grad, down_grad],
        )
    return (projected, jnp.swapaxes(down_grad, 1, 2), up_grad)


def solution(mesh):
    return jax.shard_map(
        per_device,
        mesh=mesh,
        in_specs=(
            P(("groups", "dp"), "tensor"),
            P(("groups", "tensor"), "dp"),
            P("tensor", "dp"),
            P(("groups", "dp"), "tensor", None),
            P("groups", None, "dp"),
            P("groups"),
            P("groups"),
            P("groups"),
        ),
        out_specs=(
            P(("groups", "tensor"), "dp"),
            P(("groups", "dp"), "tensor", None),
            P("groups", None, "dp"),
        ),
        check_vma=False,
    )
```

```python
import functools

import jax
import jax.numpy as jnp
from jax import lax
from jax.experimental import pallas as pl
from jax.experimental.pallas import tpu as pltpu
from jax.sharding import PartitionSpec as P

BLK = 128
CAP = 3
CORES = 2
CHUNK_ROWS = (64, 64)
PARTS = 2
SMALL = pltpu.CompilerParams(vmem_limit_bytes=12 * 2**20)

adapter_scale = 0.5

LAST = (((1,), (1,)), ((), ()))


class Index:
    def __init__(self, ref, block_count, adapter_count, parts):
        self.ref = ref
        self.blocks, self.adapters, self.parts = block_count, adapter_count, parts
        self.chips = parts // CORES
        self.per_part = block_count // parts

    @staticmethod
    def pack(adapter_of_block, slot_of_block, tokens_per_adapter):
        place = jnp.stack([lax.axis_index("dp"), lax.axis_index("tensor")]).astype(jnp.int32)
        return jnp.concatenate([adapter_of_block, slot_of_block, tokens_per_adapter, place])

    def owner(self, block):
        return self.ref[block]

    def slot(self, block):
        return self.ref[self.blocks + block]

    def tokens(self, adapter):
        return self.ref[2 * self.blocks + adapter]

    @property
    def place(self):
        return self.ref[2 * self.blocks + self.adapters]

    @property
    def part(self):
        return self.ref[2 * self.blocks + self.adapters + 1]

    def block(self, core_bit, chip_bits, i):
        return (self.part ^ (chip_bits * CORES + core_bit)) * self.per_part + i

    def position(self, block):
        bits = (block // self.per_part) ^ self.part
        half = (1 - bits % CORES) * self.chips + bits // CORES
        return half * self.per_part + block % self.per_part

    def live_rows(self, block):
        adapter = self.owner(block)
        first = jnp.int32(0)
        for a in range(self.adapters):
            count = (self.tokens(a) + BLK - 1) // BLK
            first = first + jnp.where(a < adapter, count, 0)
        return self.tokens(adapter) - (block - first) * BLK


def in_vmem(value):
    return pltpu.with_memory_space_constraint(value, pltpu.VMEM)


def in_hbm(value):
    return pltpu.with_memory_space_constraint(value, pltpu.HBM)


def held():
    return pl.BlockSpec(memory_space=pltpu.VMEM)


def whole(shape):
    return pl.BlockSpec(shape, lambda *_: (0,) * len(shape))


def shape_of(shape, dtype):
    return jax.ShapeDtypeStruct(shape, dtype)


BRIEF = pl.CostEstimate(flops=1, bytes_accessed=1, transcendentals=0)


def own_rows(index, block, tokens_ref, out_ref, start=0):
    at = pl.multiple_of(index.slot(block) * BLK + start, 16)
    out_ref[...] = tokens_ref[pl.ds(at, out_ref.shape[0])]


def first_hop_kernel(index_of, index_ref, tokens_ref, *refs):
    a_ref, b_ref, sems = refs[-3:]
    index = index_of(index_ref)
    copies = [
        pltpu.make_async_copy(
            tokens_ref.at[pl.ds(pl.multiple_of(index.slot(block) * BLK, BLK), BLK)],
            out_ref,
            sems.at[i],
        )
        for i, (block, out_ref) in enumerate(
            ((jnp.where(index.place == 0, 2, 1), a_ref), (0, b_ref))
        )
    ]
    for copy in copies:
        copy.start()
    for copy in copies:
        copy.wait()


def second_hop_kernel(index_of, index_ref, tokens_ref, a_ref, b_ref, *refs):
    x_ref, y_ref = refs[-2:]
    index = index_of(index_ref)
    place = index.place
    outer = jnp.where(place == 0, 1, jnp.where(place == 1, 0, 2))
    middle = jnp.where(place == 1, 2, 1)
    own_rows(index, outer, tokens_ref, x_ref)
    own_rows(index, middle, tokens_ref, y_ref)

    @pl.when((place == 1) & (index.owner(0) != 1))
    def _():
        x_ref[...] = b_ref[...]

    @pl.when(((place == 1) | (place == 2)) & (index.owner(middle) != place))
    def _():
        y_ref[...] = a_ref[...]


def settle_kernel(index_of, index_ref, tokens_ref, x_ref, y_ref, *refs):
    out_refs = refs[-len(CHUNK_ROWS) :]
    index = index_of(index_ref)
    place = index.place
    owner = index.owner(place)
    mine = owner == place
    edge = (place == 0) | ((place == 1) & (owner == 0)) | ((place == 2) & (owner == 3))
    start = 0
    for out_ref in out_refs:
        rows = slice(start, start + out_ref.shape[0])
        own_rows(index, place, tokens_ref, out_ref, start)

        @pl.when(jnp.logical_not(mine) & edge)
        def _(out_ref=out_ref, rows=rows):
            out_ref[...] = x_ref[rows]

        @pl.when(jnp.logical_not(mine | edge))
        def _(out_ref=out_ref, rows=rows):
            out_ref[...] = y_ref[rows]

        start += out_ref.shape[0]


def collect_kernel(index_of, count, index_ref, home_ref, outer_ref, *refs):
    inner_refs, outer_refs, out_ref = refs[:2], refs[2:4], refs[-1]
    index = index_of(index_ref)
    place = index.place

    def put(block, ref):
        at = pl.multiple_of(index.position(block) * count, 16)
        out_ref[pl.ds(at, count)] = ref[...]

    put(place, home_ref)
    put(place ^ 1, outer_ref)
    middle = (place == 1) | (place == 2)

    @pl.when(middle)
    def _():
        put(3 - place, inner_refs[0])
        put(place ^ 2, inner_refs[1])

    @pl.when(jnp.logical_not(middle))
    def _():
        put(place ^ 2, outer_refs[0])
        put(3 - place, outer_refs[1])


def after(values, far=()):
    specs = [
        pl.BlockSpec((1,) * (v.ndim - 2) + (16, 128), lambda *_, n=v.ndim: (0,) * n) for v in values
    ] + [pl.BlockSpec(memory_space=pl.ANY)] * len(far)
    return specs, [*values, *(in_hbm(v) for v in far)]


def hop_call(kernel, index, tokens, heights, received, waits, name):
    specs, extra = after(waits)
    width = tokens.shape[1]
    first = not received
    return pl.pallas_call(
        kernel,
        grid_spec=pltpu.PrefetchScalarGridSpec(
            num_scalar_prefetch=1,
            grid=(1,),
            in_specs=[pl.BlockSpec(memory_space=pl.ANY) if first else held()]
            + [held()] * len(received)
            + specs,
            out_specs=[held()] * len(heights),
            scratch_shapes=[pltpu.SemaphoreType.DMA((len(heights),))] * first,
        ),
        out_shape=[pltpu.VMEM((height, width), tokens.dtype) for height in heights],
        compiler_params=SMALL,
        cost_estimate=BRIEF,
        name=name,
    )(index, (in_hbm if first else in_vmem)(tokens), *[in_vmem(r) for r in received], *extra)


class Relay:
    def __init__(self, index_of, index, tokens):
        self.index_of, self.index, self.tokens = index_of, index, tokens

    def call(self, kernel, heights, received, waits, name):
        kernel = functools.partial(kernel, self.index_of)
        return hop_call(kernel, self.index, self.tokens, heights, received, waits, name)

    def first(self, waits=()):
        inward, left = self.call(first_hop_kernel, (BLK, BLK), (), waits, "first_hop")
        self.received = (
            lax.ppermute(inward, "dp", [(3, 2), (0, 1)]),
            lax.ppermute(left, "dp", [(2, 1)]),
        )
        return inward

    def second(self, waits=()):
        outer, middle = self.call(
            second_hop_kernel, (BLK, BLK), self.received, waits, "second_hop"
        )
        self.received = (
            lax.ppermute(outer, "dp", [(1, 0), (0, 1), (3, 2)]),
            lax.ppermute(middle, "dp", [(2, 1), (1, 2)]),
        )
        return outer

    def settle(self, waits=()):
        homes = self.call(settle_kernel, CHUNK_ROWS, self.received, waits, "settle")
        self.arrived = [self.spread(home) for home in homes]

    def spread(self, home):
        outer = lax.ppermute(home, "dp", [(0, 1), (1, 0), (2, 3), (3, 2)])
        inner = lax.ppermute(home, "dp", [(1, 2), (2, 1)])
        outer_2 = lax.ppermute(inner, "dp", [(1, 0), (2, 3)])
        inner_2 = lax.ppermute(outer, "dp", [(1, 2), (2, 1)])
        outer_3 = lax.ppermute(inner_2, "dp", [(1, 0), (2, 3)])
        return home, outer, inner, inner_2, outer_2, outer_3

    def rows(self, chunk, waits=(), far=()):
        arrived = self.arrived[chunk]
        count, width = arrived[0].shape
        specs, extra = after(waits, far)
        return pl.pallas_call(
            functools.partial(collect_kernel, self.index_of, count),
            grid_spec=pltpu.PrefetchScalarGridSpec(
                num_scalar_prefetch=1,
                grid=(1,),
                in_specs=[held()] * len(arrived) + specs,
                out_specs=held(),
            ),
            out_shape=pltpu.VMEM((4 * count, width), self.tokens.dtype),
            compiler_params=SMALL,
            cost_estimate=BRIEF,
            name="collect",
        )(self.index, *[in_vmem(a) for a in arrived], *extra)


def load_weight_kernel(w_ref, *refs):
    out_ref, sems = refs[-2:]
    streams = sems.shape[0]
    depth = w_ref.shape[0] // streams
    copies = [
        pltpu.make_async_copy(
            w_ref.at[pl.ds(i * depth, depth)], out_ref.at[pl.ds(i * depth, depth)], sems.at[i]
        )
        for i in range(streams)
    ]
    for copy in copies:
        copy.start()
    for copy in copies:
        copy.wait()


def load_weight(weight, waits):
    specs, extra = after(waits)
    return pl.pallas_call(
        load_weight_kernel,
        grid=(1,),
        in_specs=[pl.BlockSpec(memory_space=pl.ANY)] + specs,
        out_specs=pl.BlockSpec(memory_space=pl.ANY),
        out_shape=pltpu.VMEM(weight.shape, weight.dtype),
        scratch_shapes=[pltpu.SemaphoreType.DMA((4,))],
        compiler_params=SMALL,
        cost_estimate=BRIEF,
        name="load_weight",
    )(in_hbm(weight), *extra)


def split_product_kernel(each, half, first, tile, rows_ref, w_ref, *refs):
    send_own_ref, send_ref, own_ref, other_ref = refs[-4:]
    for n in range(own_ref.shape[1] // tile):
        total = jnp.dot(
            rows_ref[...],
            w_ref[:, first + n * tile : first + (n + 1) * tile],
            preferred_element_type=jnp.float32,
        )
        columns = slice(n * tile, (n + 1) * tile)
        send_own_ref[:, columns] = total[:each].astype(send_own_ref.dtype)
        send_ref[:, columns] = total[each:half].astype(send_ref.dtype)
        own_ref[:, columns] = total[half : half + each]
        other_ref[:, columns] = total[half + each :]


def split_product(shape, rows, weight, part, part_count, waits):
    half = rows.shape[0] // 2
    each = half // shape.chips
    width = weight.shape[1] // part_count
    specs, extra = after(waits)
    return pl.pallas_call(
        functools.partial(split_product_kernel, each, half, part * width, min(512, width)),
        grid=(1,),
        in_specs=[held(), held()] + specs,
        out_specs=[held()] * 4,
        out_shape=[
            pltpu.VMEM((each, width), jnp.bfloat16),
            pltpu.VMEM((half - each, width), jnp.bfloat16),
            pltpu.VMEM((each, width), jnp.float32),
            pltpu.VMEM((half - each, width), jnp.float32),
        ],
        compiler_params=SMALL,
        cost_estimate=BRIEF,
        name="split_product",
    )(in_vmem(rows), in_vmem(weight), *extra)


def narrow_kernel(index_of, index_ref, tokens_ref, down_ref, cot_ref, up_ref, *refs):
    send_ref, keep_ref, back_ref, low, tokens, down, cot, up, sems = refs[-9:]
    index = index_of(index_ref)
    pairs = [(tokens_ref, tokens), (down_ref, down), (cot_ref, cot)]
    for i in range(index.per_part):
        adapter = index.owner(index.block(0, 0, i))
        pairs.append((up_ref.at[adapter], up.at[i]))
    copies = [
        pltpu.make_async_copy(source, target, sems.at[j])
        for j, (source, target) in enumerate(pairs)
    ]
    for copy in copies:
        copy.start()
    for copy in copies[:2]:
        copy.wait()
    for m in range(CAP):
        low[m] = lax.dot_general(
            down[0],
            tokens[m * BLK : (m + 1) * BLK],
            LAST,
            preferred_element_type=jnp.float32,
        )
    for core_bit, out_ref in ((1, send_ref), (0, keep_ref)):
        for chip_bits in range(index.chips):
            for i in range(index.per_part):
                block = index.block(core_bit, chip_bits, i)
                mine = index.owner(block) == index.place
                out_ref[chip_bits, i] = jnp.where(mine, low[index.slot(block)], 0.0)
    for copy in copies[2:]:
        copy.wait()
    for i in range(index.per_part):
        back_ref[i] = lax.dot_general(
            up[i], cot[i * BLK : (i + 1) * BLK], LAST, preferred_element_type=jnp.float32
        )


def narrow(index_of, index, shape, tokens, down, cotangent, up, waits):
    rank = up.shape[1]
    one = (shape.per_part, rank, BLK)
    outs = [(shape.chips,) + one, (shape.chips,) + one, one]
    operands = (tokens, down, cotangent, up)
    specs, extra = after(waits)
    return pl.pallas_call(
        functools.partial(narrow_kernel, index_of),
        grid_spec=pltpu.PrefetchScalarGridSpec(
            num_scalar_prefetch=1,
            grid=(1,),
            in_specs=[pl.BlockSpec(memory_space=pl.ANY)] * len(operands) + specs,
            out_specs=[held()] * len(outs),
            scratch_shapes=[
                pltpu.VMEM((CAP, rank, BLK), jnp.float32),
                pltpu.VMEM(tokens.shape, tokens.dtype),
                pltpu.VMEM(down.shape, down.dtype),
                pltpu.VMEM(cotangent.shape, cotangent.dtype),
                pltpu.VMEM((shape.per_part,) + up.shape[1:], up.dtype),
                pltpu.SemaphoreType.DMA((3 + shape.per_part,)),
            ],
        ),
        out_shape=[pltpu.VMEM(o, jnp.float32) for o in outs],
        compiler_params=SMALL,
        cost_estimate=BRIEF,
        name="narrow",
    )(index, *[in_hbm(o) for o in operands], *extra)


def merge_kernel(keep_ref, arrived_ref, back_ref, *refs):
    out_ref = refs[-1]
    total = keep_ref[0] + arrived_ref[0]
    for ref in refs[:-1][: keep_ref.shape[0] - 1]:
        total = total + ref[...]
    out_ref[0] = total
    out_ref[1] = back_ref[...]


def merge(keep, arrived, back, others, waits):
    specs, extra = after(waits)
    operands = (keep, arrived, back, *others)
    out = (2,) + back.shape
    return pl.pallas_call(
        merge_kernel,
        grid=(1,),
        in_specs=[whole(o.shape) for o in operands] + specs,
        out_specs=whole(out),
        out_shape=shape_of(out, jnp.float32),
        compiler_params=SMALL,
        cost_estimate=BRIEF,
        name="merge",
    )(*operands, *extra)


def pieces_kernel(index_of, count, index_ref, cot_ref, sum_ref, *refs):
    more_refs, (low_ref, back_ref, piece_ref) = refs[:count], refs[-3:]
    index = index_of(index_ref)
    level = [sum_ref[...]] + [ref[...] for ref in more_refs]
    while len(level) > 1:
        level = [level[j] + level[j + 1] for j in range(0, len(level), 2)]
    for i in range(index.per_part):
        live = index.live_rows(index.block(0, 0, i))
        keep = lax.broadcasted_iota(jnp.int32, low_ref.shape[1:], 1) < live
        lowered = jnp.where(keep, level[0][0, i], 0.0).astype(low_ref.dtype)
        low_ref[i] = lowered
        back_ref[i] = jnp.where(keep, level[0][1, i], 0.0).astype(back_ref.dtype)
        piece_ref[i] = jnp.dot(
            lowered, cot_ref[i * BLK : (i + 1) * BLK], preferred_element_type=jnp.float32
        ).astype(piece_ref.dtype)


def make_pieces(index_of, index, shape, total, more, cotangent, waits):
    _, per_part, rank, _ = total.shape
    width = cotangent.shape[1]
    outs = [(per_part, rank, BLK), (per_part, rank, BLK), (per_part, rank, width)]
    operands = (cotangent, total, *more)
    specs, extra = after(waits)
    return pl.pallas_call(
        functools.partial(pieces_kernel, index_of, len(more)),
        grid_spec=pltpu.PrefetchScalarGridSpec(
            num_scalar_prefetch=1,
            grid=(1,),
            in_specs=[whole(o.shape) for o in operands] + specs,
            out_specs=[whole(o) for o in outs],
        ),
        out_shape=[shape_of(o, jnp.bfloat16) for o in outs],
        compiler_params=SMALL,
        cost_estimate=BRIEF,
        name="pieces",
    )(index, *operands, *extra)


def down_gradient_kernel(index_of, index_ref, tokens_ref, *refs):
    back_refs, out_ref = refs[:-1], refs[-1]
    index = index_of(index_ref)
    out_ref[...] = jnp.zeros_like(out_ref)
    for core_bit in range(CORES):
        for chip_bits in range(index.chips):
            for i in range(index.per_part):
                block = index.block(core_bit, chip_bits, i)
                back_ref = back_refs[core_bit * index.chips + chip_bits]

                @pl.when(index.owner(block) == index.place)
                def _(block=block, back_ref=back_ref, i=i):
                    at = pl.multiple_of(index.slot(block) * BLK, BLK)
                    out_ref[0] += adapter_scale * jnp.dot(
                        back_ref[i],
                        tokens_ref[pl.ds(at, BLK)],
                        preferred_element_type=jnp.float32,
                    )


def down_gradient(index_of, index, tokens, backs):
    out = (1, backs[0].shape[1], tokens.shape[1])
    operands = (in_vmem(tokens), *backs)
    return pl.pallas_call(
        functools.partial(down_gradient_kernel, index_of),
        grid_spec=pltpu.PrefetchScalarGridSpec(
            num_scalar_prefetch=1,
            grid=(1,),
            in_specs=[held()] + [whole(o.shape) for o in backs],
            out_specs=whole(out),
        ),
        out_shape=shape_of(out, jnp.float32),
        compiler_params=SMALL,
        cost_estimate=BRIEF,
        name="down_gradient",
    )(index, *operands)


def up_gradient_kernel(index_of, index_ref, *refs):
    piece_refs, out_ref = refs[:-1], refs[-1]
    index = index_of(index_ref)

    def of_device(core_bit, chip_bits, adapter):
        total = None
        for i in range(index.per_part):
            mine = index.owner(index.block(core_bit, chip_bits, i)) == adapter
            piece = piece_refs[core_bit * index.chips + chip_bits][i].astype(jnp.float32)
            term = jnp.where(mine, piece, 0.0)
            total = term if total is None else total + term
        return total

    for adapter in range(index.adapters):
        level = [
            of_device(0, j, adapter) + of_device(1, j, adapter) for j in range(index.chips)
        ]
        while len(level) > 1:
            level = [level[j] + level[j + 1] for j in range(0, len(level), 2)]
        out_ref[adapter] = adapter_scale * level[0]


def up_gradient(index_of, index, adapter_count, pieces):
    per_part, rank, width = pieces[0].shape
    tile = 1024
    out = (adapter_count, rank, width)
    return pl.pallas_call(
        functools.partial(up_gradient_kernel, index_of),
        grid_spec=pltpu.PrefetchScalarGridSpec(
            num_scalar_prefetch=1,
            grid=(width // tile,),
            in_specs=[pl.BlockSpec((per_part, rank, tile), lambda n, _: (0, 0, n))] * len(pieces),
            out_specs=pl.BlockSpec((adapter_count, rank, tile), lambda n, _: (0, 0, n)),
        ),
        out_shape=shape_of(out, jnp.float32),
        compiler_params=SMALL,
        cost_estimate=BRIEF,
        name="up_gradient",
    )(index, *pieces)


def finish_kernel(index_of, index_ref, low_ref, *refs):
    index = index_of(index_ref)
    up_refs, sum_refs, out_ref = refs[: index.per_part], refs[index.per_part : -1], refs[-1]
    per_chunk = len(sum_refs) // len(CHUNK_ROWS)
    for i in range(index.per_part):
        block = index.block(0, 0, i)
        live = index.live_rows(block)
        side = lax.dot_general(
            low_ref[i],
            up_refs[i][0],
            (((0,), (0,)), ((), ())),
            preferred_element_type=jnp.float32,
        )
        start = 0
        for c, count in enumerate(CHUNK_ROWS):
            total = adapter_scale * side[start : start + count]
            for ref in sum_refs[c * per_chunk : (c + 1) * per_chunk]:
                total = total + ref[i * count : (i + 1) * count].astype(jnp.float32)
            keep = start + lax.broadcasted_iota(jnp.int32, total.shape, 0) < live
            at = i * BLK + start
            out_ref[at : at + count] = jnp.where(keep, total, 0.0).astype(out_ref.dtype)
            start += count


def finish(index_of, index, lowered, up, sums, part, projected, far):
    per_part = lowered.shape[0]
    _, rank, width = up.shape
    tile = min(1024, width // PARTS)
    tiles = width // PARTS // tile
    first = part * tiles
    out = (per_part * BLK, width)

    def factor(i):
        def at(n, index_ref):
            index = index_of(index_ref)
            return (index.owner(index.block(0, 0, i)), 0, first + n)

        return pl.BlockSpec((1, rank, tile), at)

    flat = [term for chunk in sums for term in chunk]
    specs = [
        pl.BlockSpec((per_part * count, tile), lambda n, _: (0, n))
        for chunk, count in zip(sums, CHUNK_ROWS)
        for _ in chunk
    ]
    operands = [index, lowered, *[up] * per_part, *flat]
    more, extra = after((), far)
    aliases = {}
    if projected is not None:
        aliases = {len(operands): 0}
        more, extra = [pl.BlockSpec(memory_space=pl.ANY)] + more, [projected] + extra

    def kernel(*refs):
        finish_kernel(index_of, *refs[: len(operands)], refs[-1])

    return pl.pallas_call(
        kernel,
        grid_spec=pltpu.PrefetchScalarGridSpec(
            num_scalar_prefetch=1,
            grid=(tiles,),
            in_specs=[whole(lowered.shape)] + [factor(i) for i in range(per_part)] + specs + more,
            out_specs=pl.BlockSpec((out[0], tile), lambda n, _: (0, first + n)),
        ),
        out_shape=shape_of(out, jnp.bfloat16),
        input_output_aliases=aliases,
        compiler_params=SMALL,
        cost_estimate=BRIEF,
        name="finish",
    )(*operands, *extra)


def per_device(
    tokens,
    cotangent,
    frozen_up_weight,
    adapter_down_factor,
    adapter_up_factor,
    tokens_per_adapter,
    adapter_of_block,
    slot_of_block,
):
    owners = lax.axis_size("dp")
    parts = lax.axis_size("tensor")
    chips = parts // CORES
    block_count = adapter_of_block.shape[0]
    adapter_count = adapter_up_factor.shape[0]
    width_dev = tokens.shape[1]
    index_of = functools.partial(
        Index, block_count=block_count, adapter_count=adapter_count, parts=parts
    )
    shape = index_of(None)
    index = Index.pack(adapter_of_block, slot_of_block, tokens_per_adapter)

    def to_other_core(value):
        return lax.ppermute(value, "tensor", [(i, i ^ 1) for i in range(parts)])

    def to_chip(value, k):
        return lax.ppermute(value, "tensor", [(i, i ^ (k * CORES)) for i in range(parts)])

    def across_dp(value, k):
        return lax.ppermute(value, "dp", [(i, i ^ k) for i in range(owners)])

    def same_core(value):
        return [value] + [to_chip(value, k) for k in range(1, chips)]

    def with_other_core(values):
        return values + [to_other_core(v) for v in values]

    def small_products(waits):
        return narrow(
            index_of,
            index,
            shape,
            tokens,
            jnp.swapaxes(adapter_down_factor, 1, 2),
            cotangent,
            adapter_up_factor,
            waits,
        )

    def over_parts(send, keep):
        arrived = to_other_core(send)
        return arrived, [to_chip(keep[k] + arrived[k], k) for k in range(1, chips)]

    def over_dp(total):
        k = owners // 2
        while k > 1:
            total = total + across_dp(total, k)
            k //= 2
        return total, [across_dp(total, 1)]

    if owners == 4 and block_count == 4:
        relay = Relay(index_of, index, tokens)
        sent = relay.first()
        send, keep, back = small_products([sent])
        arrived, others = over_parts(send, keep)
        total, more = over_dp(merge(keep, arrived, back, others, []))
        relay.second([total])
        lowered, back_rows, pieces = make_pieces(
            index_of, index, shape, total, more, cotangent, []
        )
        relay.settle(more)
        weight = load_weight(frozen_up_weight, relay.arrived[-1][1:3])
        pieces = with_other_core(same_core(pieces))
        back_rows = with_other_core(same_core(back_rows))
        ahead = [v for chunk in relay.arrived[1:] for v in chunk[3:5]]
        ahead.append(weight)
        chunks = [lambda waits: relay.rows(0, ahead)]
        chunks += [functools.partial(relay.rows, c) for c in range(1, len(CHUNK_ROWS))]
    else:
        weight = load_weight(frozen_up_weight, [])
        send, keep, back = small_products([])
        arrived, others = over_parts(send, keep)
        total, more = over_dp(merge(keep, arrived, back, others, []))
        lowered, back_rows, pieces = make_pieces(
            index_of, index, shape, total, more, cotangent, []
        )
        pieces = with_other_core(same_core(pieces))
        back_rows = with_other_core(same_core(back_rows))
        every_slot = lax.all_gather(
            tokens.reshape(CAP, BLK, width_dev), "dp", axis=0, tiled=True
        )
        part = lax.axis_index("tensor")
        devices = jnp.arange(parts, dtype=jnp.int32)
        order = (devices // chips ^ 1) + (devices % chips) * CORES ^ part
        blocks = (order[:, None] * shape.per_part + jnp.arange(shape.per_part)).reshape(-1)
        picked = every_slot[adapter_of_block[blocks] * CAP + slot_of_block[blocks]]
        starts = [sum(CHUNK_ROWS[:c]) for c in range(len(CHUNK_ROWS))]
        chunks = [
            lambda waits, s=s, count=count: picked[:, s : s + count].reshape(-1, width_dev)
            for s, count in zip(starts, CHUNK_ROWS)
        ]
    def summed(rows, part, waits):
        each = rows.shape[0] // parts
        send_own, send, own, other = split_product(shape, rows, weight, part, PARTS, waits)
        outgoing = (other + to_other_core(send).astype(jnp.float32)).astype(jnp.bfloat16)
        across = [to_chip(outgoing[(k - 1) * each : k * each], k) for k in range(1, chips)]
        return [own, to_other_core(send_own)] + across, outgoing

    sums, ready = [], ()
    waits = [pieces[1:chips], ()]
    for chunk in chunks:
        rows = chunk(ready)
        done = [summed(rows, part, waits[part]) for part in range(PARTS)]
        sums.append([terms for terms, _ in done])
        ready = [done[0][1]]
        waits = [
            [*sums[-1][0][2:], *back_rows[1:chips]],
            [*back_rows[chips:], *pieces[chips:]],
        ]
    up_grad = up_gradient(index_of, index, adapter_count, pieces)
    down_grad = down_gradient(index_of, index, tokens, back_rows)
    projected = None
    for part in range(PARTS):
        projected = finish(
            index_of,
            index,
            lowered,
            adapter_up_factor,
            [done[part] for done in sums],
            part,
            projected,
            [] if projected is not None else [up_grad, down_grad],
        )
    return (projected, jnp.swapaxes(down_grad, 1, 2), up_grad)


def solution(mesh):
    return jax.shard_map(
        per_device,
        mesh=mesh,
        in_specs=(
            P(("groups", "dp"), "tensor"),
            P(("groups", "tensor"), "dp"),
            P("tensor", "dp"),
            P(("groups", "dp"), "tensor", None),
            P("groups", None, "dp"),
            P("groups"),
            P("groups"),
            P("groups"),
        ),
        out_specs=(
            P(("groups", "tensor"), "dp"),
            P(("groups", "dp"), "tensor", None),
            P("groups", None, "dp"),
        ),
        check_vma=False,
    )
```

```python
import functools

import jax
import jax.numpy as jnp
from jax import lax
from jax.experimental import pallas as pl
from jax.experimental.pallas import tpu as pltpu
from jax.sharding import PartitionSpec as P

BLK = 128
CAP = 3
CORES = 2
CHUNK_ROWS = (64, 64)
PARTS = 2
SMALL = pltpu.CompilerParams(vmem_limit_bytes=12 * 2**20)

adapter_scale = 0.5

LAST = (((1,), (1,)), ((), ()))


class Index:
    def __init__(self, ref, block_count, adapter_count, parts):
        self.ref = ref
        self.blocks, self.adapters, self.parts = block_count, adapter_count, parts
        self.chips = parts // CORES
        self.per_part = block_count // parts

    @staticmethod
    def pack(adapter_of_block, slot_of_block, tokens_per_adapter):
        place = jnp.stack([lax.axis_index("dp"), lax.axis_index("tensor")]).astype(jnp.int32)
        return jnp.concatenate([adapter_of_block, slot_of_block, tokens_per_adapter, place])

    def owner(self, block):
        return self.ref[block]

    def slot(self, block):
        return self.ref[self.blocks + block]

    def tokens(self, adapter):
        return self.ref[2 * self.blocks + adapter]

    @property
    def place(self):
        return self.ref[2 * self.blocks + self.adapters]

    @property
    def part(self):
        return self.ref[2 * self.blocks + self.adapters + 1]

    def block(self, core_bit, chip_bits, i):
        return (self.part ^ (chip_bits * CORES + core_bit)) * self.per_part + i

    def position(self, block):
        bits = (block // self.per_part) ^ self.part
        half = (1 - bits % CORES) * self.chips + bits // CORES
        return half * self.per_part + block % self.per_part

    def live_rows(self, block):
        adapter = self.owner(block)
        first = jnp.int32(0)
        for a in range(self.adapters):
            count = (self.tokens(a) + BLK - 1) // BLK
            first = first + jnp.where(a < adapter, count, 0)
        return self.tokens(adapter) - (block - first) * BLK


def in_vmem(value):
    return pltpu.with_memory_space_constraint(value, pltpu.VMEM)


def in_hbm(value):
    return pltpu.with_memory_space_constraint(value, pltpu.HBM)


def held():
    return pl.BlockSpec(memory_space=pltpu.VMEM)


def whole(shape):
    return pl.BlockSpec(shape, lambda *_: (0,) * len(shape))


def shape_of(shape, dtype):
    return jax.ShapeDtypeStruct(shape, dtype)


BRIEF = pl.CostEstimate(flops=1, bytes_accessed=1, transcendentals=0)


def own_rows(index, block, tokens_ref, out_ref, start=0):
    at = pl.multiple_of(index.slot(block) * BLK + start, 16)
    out_ref[...] = tokens_ref[pl.ds(at, out_ref.shape[0])]


def first_hop_kernel(index_of, index_ref, tokens_ref, *refs):
    a_ref, b_ref, sems = refs[-3:]
    index = index_of(index_ref)
    copies = [
        pltpu.make_async_copy(
            tokens_ref.at[pl.ds(pl.multiple_of(index.slot(block) * BLK, BLK), BLK)],
            out_ref,
            sems.at[i],
        )
        for i, (block, out_ref) in enumerate(
            ((jnp.where(index.place == 0, 2, 1), a_ref), (0, b_ref))
        )
    ]
    for copy in copies:
        copy.start()
    for copy in copies:
        copy.wait()


def second_hop_kernel(index_of, index_ref, tokens_ref, a_ref, b_ref, *refs):
    x_ref, y_ref = refs[-2:]
    index = index_of(index_ref)
    place = index.place
    outer = jnp.where(place == 0, 1, jnp.where(place == 1, 0, 2))
    middle = jnp.where(place == 1, 2, 1)
    own_rows(index, outer, tokens_ref, x_ref)
    own_rows(index, middle, tokens_ref, y_ref)

    @pl.when((place == 1) & (index.owner(0) != 1))
    def _():
        x_ref[...] = b_ref[...]

    @pl.when(((place == 1) | (place == 2)) & (index.owner(middle) != place))
    def _():
        y_ref[...] = a_ref[...]


def settle_kernel(index_of, index_ref, tokens_ref, x_ref, y_ref, *refs):
    out_refs = refs[-len(CHUNK_ROWS) :]
    index = index_of(index_ref)
    place = index.place
    owner = index.owner(place)
    mine = owner == place
    edge = (place == 0) | ((place == 1) & (owner == 0)) | ((place == 2) & (owner == 3))
    start = 0
    for out_ref in out_refs:
        rows = slice(start, start + out_ref.shape[0])
        own_rows(index, place, tokens_ref, out_ref, start)

        @pl.when(jnp.logical_not(mine) & edge)
        def _(out_ref=out_ref, rows=rows):
            out_ref[...] = x_ref[rows]

        @pl.when(jnp.logical_not(mine | edge))
        def _(out_ref=out_ref, rows=rows):
            out_ref[...] = y_ref[rows]

        start += out_ref.shape[0]


def collect_kernel(index_of, count, index_ref, home_ref, outer_ref, *refs):
    inner_refs, outer_refs, out_ref = refs[:2], refs[2:4], refs[-1]
    index = index_of(index_ref)
    place = index.place

    def put(block, ref):
        at = pl.multiple_of(index.position(block) * count, 16)
        out_ref[pl.ds(at, count)] = ref[...]

    put(place, home_ref)
    put(place ^ 1, outer_ref)
    middle = (place == 1) | (place == 2)

    @pl.when(middle)
    def _():
        put(3 - place, inner_refs[0])
        put(place ^ 2, inner_refs[1])

    @pl.when(jnp.logical_not(middle))
    def _():
        put(place ^ 2, outer_refs[0])
        put(3 - place, outer_refs[1])


def after(values, far=()):
    specs = [
        pl.BlockSpec((1,) * (v.ndim - 2) + (16, 128), lambda *_, n=v.ndim: (0,) * n) for v in values
    ] + [pl.BlockSpec(memory_space=pl.ANY)] * len(far)
    return specs, [*values, *(in_hbm(v) for v in far)]


def hop_call(kernel, index, tokens, heights, received, waits, name):
    specs, extra = after(waits)
    width = tokens.shape[1]
    first = not received
    return pl.pallas_call(
        kernel,
        grid_spec=pltpu.PrefetchScalarGridSpec(
            num_scalar_prefetch=1,
            grid=(1,),
            in_specs=[pl.BlockSpec(memory_space=pl.ANY) if first else held()]
            + [held()] * len(received)
            + specs,
            out_specs=[held()] * len(heights),
            scratch_shapes=[pltpu.SemaphoreType.DMA((len(heights),))] * first,
        ),
        out_shape=[pltpu.VMEM((height, width), tokens.dtype) for height in heights],
        compiler_params=SMALL,
        cost_estimate=BRIEF,
        name=name,
    )(index, (in_hbm if first else in_vmem)(tokens), *[in_vmem(r) for r in received], *extra)


class Relay:
    def __init__(self, index_of, index, tokens):
        self.index_of, self.index, self.tokens = index_of, index, tokens

    def call(self, kernel, heights, received, waits, name):
        kernel = functools.partial(kernel, self.index_of)
        return hop_call(kernel, self.index, self.tokens, heights, received, waits, name)

    def first(self, waits=()):
        inward, left = self.call(first_hop_kernel, (BLK, BLK), (), waits, "first_hop")
        self.received = (
            lax.ppermute(inward, "dp", [(3, 2), (0, 1)]),
            lax.ppermute(left, "dp", [(2, 1)]),
        )
        return inward

    def second(self, waits=()):
        outer, middle = self.call(
            second_hop_kernel, (BLK, BLK), self.received, waits, "second_hop"
        )
        self.received = (
            lax.ppermute(outer, "dp", [(1, 0), (0, 1), (3, 2)]),
            lax.ppermute(middle, "dp", [(2, 1), (1, 2)]),
        )
        return outer

    def settle(self, waits=()):
        homes = self.call(settle_kernel, CHUNK_ROWS, self.received, waits, "settle")
        self.arrived = [self.spread(home) for home in homes]

    def spread(self, home):
        outer = lax.ppermute(home, "dp", [(0, 1), (1, 0), (2, 3), (3, 2)])
        inner = lax.ppermute(home, "dp", [(1, 2), (2, 1)])
        outer_2 = lax.ppermute(inner, "dp", [(1, 0), (2, 3)])
        inner_2 = lax.ppermute(outer, "dp", [(1, 2), (2, 1)])
        outer_3 = lax.ppermute(inner_2, "dp", [(1, 0), (2, 3)])
        return home, outer, inner, inner_2, outer_2, outer_3

    def rows(self, chunk, waits=(), far=()):
        arrived = self.arrived[chunk]
        count, width = arrived[0].shape
        specs, extra = after(waits, far)
        return pl.pallas_call(
            functools.partial(collect_kernel, self.index_of, count),
            grid_spec=pltpu.PrefetchScalarGridSpec(
                num_scalar_prefetch=1,
                grid=(1,),
                in_specs=[held()] * len(arrived) + specs,
                out_specs=held(),
            ),
            out_shape=pltpu.VMEM((4 * count, width), self.tokens.dtype),
            compiler_params=SMALL,
            cost_estimate=BRIEF,
            name="collect",
        )(self.index, *[in_vmem(a) for a in arrived], *extra)


def load_weight_kernel(w_ref, *refs):
    out_ref, sems = refs[-2:]
    streams = sems.shape[0]
    depth = w_ref.shape[0] // streams
    copies = [
        pltpu.make_async_copy(
            w_ref.at[pl.ds(i * depth, depth)], out_ref.at[pl.ds(i * depth, depth)], sems.at[i]
        )
        for i in range(streams)
    ]
    for copy in copies:
        copy.start()
    for copy in copies:
        copy.wait()


def load_weight(weight, waits):
    specs, extra = after(waits)
    return pl.pallas_call(
        load_weight_kernel,
        grid=(1,),
        in_specs=[pl.BlockSpec(memory_space=pl.ANY)] + specs,
        out_specs=pl.BlockSpec(memory_space=pl.ANY),
        out_shape=pltpu.VMEM(weight.shape, weight.dtype),
        scratch_shapes=[pltpu.SemaphoreType.DMA((4,))],
        compiler_params=SMALL,
        cost_estimate=BRIEF,
        name="load_weight",
    )(in_hbm(weight), *extra)


def split_product_kernel(each, half, first, tile, rows_ref, w_ref, *refs):
    send_own_ref, send_ref, own_ref, other_ref = refs[-4:]
    for n in range(own_ref.shape[1] // tile):
        total = jnp.dot(
            rows_ref[...],
            w_ref[:, first + n * tile : first + (n + 1) * tile],
            preferred_element_type=jnp.float32,
        )
        columns = slice(n * tile, (n + 1) * tile)
        send_own_ref[:, columns] = total[:each].astype(send_own_ref.dtype)
        send_ref[:, columns] = total[each:half].astype(send_ref.dtype)
        own_ref[:, columns] = total[half : half + each]
        other_ref[:, columns] = total[half + each :]


def split_product(shape, rows, weight, part, part_count, waits):
    half = rows.shape[0] // 2
    each = half // shape.chips
    width = weight.shape[1] // part_count
    specs, extra = after(waits)
    return pl.pallas_call(
        functools.partial(split_product_kernel, each, half, part * width, min(512, width)),
        grid=(1,),
        in_specs=[held(), held()] + specs,
        out_specs=[held()] * 4,
        out_shape=[
            pltpu.VMEM((each, width), jnp.bfloat16),
            pltpu.VMEM((half - each, width), jnp.bfloat16),
            pltpu.VMEM((each, width), jnp.float32),
            pltpu.VMEM((half - each, width), jnp.float32),
        ],
        compiler_params=SMALL,
        cost_estimate=BRIEF,
        name="split_product",
    )(in_vmem(rows), in_vmem(weight), *extra)


def narrow_kernel(index_of, index_ref, tokens_ref, down_ref, cot_ref, up_ref, *refs):
    send_ref, keep_ref, back_ref, low, tokens, down, cot, up, sems = refs[-9:]
    index = index_of(index_ref)
    pairs = [(tokens_ref, tokens), (down_ref, down), (cot_ref, cot)]
    for i in range(index.per_part):
        adapter = index.owner(index.block(0, 0, i))
        pairs.append((up_ref.at[adapter], up.at[i]))
    copies = [
        pltpu.make_async_copy(source, target, sems.at[j])
        for j, (source, target) in enumerate(pairs)
    ]
    for copy in copies:
        copy.start()
    for copy in copies[:2]:
        copy.wait()
    for m in range(CAP):
        low[m] = lax.dot_general(
            down[0],
            tokens[m * BLK : (m + 1) * BLK],
            LAST,
            preferred_element_type=jnp.float32,
        )
    for core_bit, out_ref in ((1, send_ref), (0, keep_ref)):
        for chip_bits in range(index.chips):
            for i in range(index.per_part):
                block = index.block(core_bit, chip_bits, i)
                mine = index.owner(block) == index.place
                out_ref[chip_bits, i] = jnp.where(mine, low[index.slot(block)], 0.0)
    for copy in copies[2:]:
        copy.wait()
    for i in range(index.per_part):
        back_ref[i] = lax.dot_general(
            up[i], cot[i * BLK : (i + 1) * BLK], LAST, preferred_element_type=jnp.float32
        )


def narrow(index_of, index, shape, tokens, down, cotangent, up, waits):
    rank = up.shape[1]
    one = (shape.per_part, rank, BLK)
    outs = [(shape.chips,) + one, (shape.chips,) + one, one]
    operands = (tokens, down, cotangent, up)
    specs, extra = after(waits)
    return pl.pallas_call(
        functools.partial(narrow_kernel, index_of),
        grid_spec=pltpu.PrefetchScalarGridSpec(
            num_scalar_prefetch=1,
            grid=(1,),
            in_specs=[pl.BlockSpec(memory_space=pl.ANY)] * len(operands) + specs,
            out_specs=[held()] * len(outs),
            scratch_shapes=[
                pltpu.VMEM((CAP, rank, BLK), jnp.float32),
                pltpu.VMEM(tokens.shape, tokens.dtype),
                pltpu.VMEM(down.shape, down.dtype),
                pltpu.VMEM(cotangent.shape, cotangent.dtype),
                pltpu.VMEM((shape.per_part,) + up.shape[1:], up.dtype),
                pltpu.SemaphoreType.DMA((3 + shape.per_part,)),
            ],
        ),
        out_shape=[pltpu.VMEM(o, jnp.float32) for o in outs],
        compiler_params=SMALL,
        cost_estimate=BRIEF,
        name="narrow",
    )(index, *[in_hbm(o) for o in operands], *extra)


def merge_kernel(keep_ref, arrived_ref, back_ref, *refs):
    out_ref = refs[-1]
    total = keep_ref[0] + arrived_ref[0]
    for ref in refs[:-1][: keep_ref.shape[0] - 1]:
        total = total + ref[...]
    out_ref[0] = total
    out_ref[1] = back_ref[...]


def merge(keep, arrived, back, others, waits):
    specs, extra = after(waits)
    operands = (keep, arrived, back, *others)
    out = (2,) + back.shape
    return pl.pallas_call(
        merge_kernel,
        grid=(1,),
        in_specs=[whole(o.shape) for o in operands] + specs,
        out_specs=whole(out),
        out_shape=shape_of(out, jnp.float32),
        compiler_params=SMALL,
        cost_estimate=BRIEF,
        name="merge",
    )(*operands, *extra)


def pieces_kernel(index_of, count, index_ref, cot_ref, sum_ref, *refs):
    more_refs, (low_ref, back_ref, piece_ref) = refs[:count], refs[-3:]
    index = index_of(index_ref)
    level = [sum_ref[...]] + [ref[...] for ref in more_refs]
    while len(level) > 1:
        level = [level[j] + level[j + 1] for j in range(0, len(level), 2)]
    for i in range(index.per_part):
        live = index.live_rows(index.block(0, 0, i))
        keep = lax.broadcasted_iota(jnp.int32, low_ref.shape[1:], 1) < live
        lowered = jnp.where(keep, level[0][0, i], 0.0).astype(low_ref.dtype)
        low_ref[i] = lowered
        back_ref[i] = jnp.where(keep, level[0][1, i], 0.0).astype(back_ref.dtype)
        piece_ref[i] = jnp.dot(
            lowered, cot_ref[i * BLK : (i + 1) * BLK], preferred_element_type=jnp.float32
        ).astype(piece_ref.dtype)


def make_pieces(index_of, index, shape, total, more, cotangent, waits):
    _, per_part, rank, _ = total.shape
    width = cotangent.shape[1]
    outs = [(per_part, rank, BLK), (per_part, rank, BLK), (per_part, rank, width)]
    operands = (cotangent, total, *more)
    specs, extra = after(waits)
    return pl.pallas_call(
        functools.partial(pieces_kernel, index_of, len(more)),
        grid_spec=pltpu.PrefetchScalarGridSpec(
            num_scalar_prefetch=1,
            grid=(1,),
            in_specs=[whole(o.shape) for o in operands] + specs,
            out_specs=[whole(o) for o in outs],
        ),
        out_shape=[shape_of(o, jnp.bfloat16) for o in outs],
        compiler_params=SMALL,
        cost_estimate=BRIEF,
        name="pieces",
    )(index, *operands, *extra)


def down_gradient_kernel(index_of, index_ref, tokens_ref, *refs):
    back_refs, out_ref = refs[:-1], refs[-1]
    index = index_of(index_ref)
    out_ref[...] = jnp.zeros_like(out_ref)
    for core_bit in range(CORES):
        for chip_bits in range(index.chips):
            for i in range(index.per_part):
                block = index.block(core_bit, chip_bits, i)
                back_ref = back_refs[core_bit * index.chips + chip_bits]

                @pl.when(index.owner(block) == index.place)
                def _(block=block, back_ref=back_ref, i=i):
                    at = pl.multiple_of(index.slot(block) * BLK, BLK)
                    out_ref[0] += adapter_scale * jnp.dot(
                        back_ref[i],
                        tokens_ref[pl.ds(at, BLK)],
                        preferred_element_type=jnp.float32,
                    )


def down_gradient(index_of, index, tokens, backs):
    out = (1, backs[0].shape[1], tokens.shape[1])
    operands = (in_vmem(tokens), *backs)
    return pl.pallas_call(
        functools.partial(down_gradient_kernel, index_of),
        grid_spec=pltpu.PrefetchScalarGridSpec(
            num_scalar_prefetch=1,
            grid=(1,),
            in_specs=[held()] + [whole(o.shape) for o in backs],
            out_specs=whole(out),
        ),
        out_shape=shape_of(out, jnp.float32),
        compiler_params=SMALL,
        cost_estimate=BRIEF,
        name="down_gradient",
    )(index, *operands)


def up_gradient_kernel(index_of, index_ref, *refs):
    piece_refs, out_ref = refs[:-1], refs[-1]
    index = index_of(index_ref)

    def of_device(core_bit, chip_bits, adapter):
        total = None
        for i in range(index.per_part):
            mine = index.owner(index.block(core_bit, chip_bits, i)) == adapter
            piece = piece_refs[core_bit * index.chips + chip_bits][i].astype(jnp.float32)
            term = jnp.where(mine, piece, 0.0)
            total = term if total is None else total + term
        return total

    for adapter in range(index.adapters):
        level = [
            of_device(0, j, adapter) + of_device(1, j, adapter) for j in range(index.chips)
        ]
        while len(level) > 1:
            level = [level[j] + level[j + 1] for j in range(0, len(level), 2)]
        out_ref[adapter] = adapter_scale * level[0]


def up_gradient(index_of, index, adapter_count, pieces):
    per_part, rank, width = pieces[0].shape
    tile = 1024
    out = (adapter_count, rank, width)
    return pl.pallas_call(
        functools.partial(up_gradient_kernel, index_of),
        grid_spec=pltpu.PrefetchScalarGridSpec(
            num_scalar_prefetch=1,
            grid=(width // tile,),
            in_specs=[pl.BlockSpec((per_part, rank, tile), lambda n, _: (0, 0, n))] * len(pieces),
            out_specs=pl.BlockSpec((adapter_count, rank, tile), lambda n, _: (0, 0, n)),
        ),
        out_shape=shape_of(out, jnp.float32),
        compiler_params=SMALL,
        cost_estimate=BRIEF,
        name="up_gradient",
    )(index, *pieces)


def finish_kernel(index_of, index_ref, low_ref, *refs):
    index = index_of(index_ref)
    up_refs, sum_refs, out_ref = refs[: index.per_part], refs[index.per_part : -1], refs[-1]
    per_chunk = len(sum_refs) // len(CHUNK_ROWS)
    for i in range(index.per_part):
        block = index.block(0, 0, i)
        live = index.live_rows(block)
        side = lax.dot_general(
            low_ref[i],
            up_refs[i][0],
            (((0,), (0,)), ((), ())),
            preferred_element_type=jnp.float32,
        )
        start = 0
        for c, count in enumerate(CHUNK_ROWS):
            total = adapter_scale * side[start : start + count]
            for ref in sum_refs[c * per_chunk : (c + 1) * per_chunk]:
                total = total + ref[i * count : (i + 1) * count].astype(jnp.float32)
            keep = start + lax.broadcasted_iota(jnp.int32, total.shape, 0) < live
            at = i * BLK + start
            out_ref[at : at + count] = jnp.where(keep, total, 0.0).astype(out_ref.dtype)
            start += count


def finish(index_of, index, lowered, up, sums, part, projected, far):
    per_part = lowered.shape[0]
    _, rank, width = up.shape
    tile = min(1024, width // PARTS)
    tiles = width // PARTS // tile
    first = part * tiles
    out = (per_part * BLK, width)

    def factor(i):
        def at(n, index_ref):
            index = index_of(index_ref)
            return (index.owner(index.block(0, 0, i)), 0, first + n)

        return pl.BlockSpec((1, rank, tile), at)

    flat = [term for chunk in sums for term in chunk]
    specs = [
        pl.BlockSpec((per_part * count, tile), lambda n, _: (0, n))
        for chunk, count in zip(sums, CHUNK_ROWS)
        for _ in chunk
    ]
    operands = [index, lowered, *[up] * per_part, *flat]
    more, extra = after((), far)
    aliases = {}
    if projected is not None:
        aliases = {len(operands): 0}
        more, extra = [pl.BlockSpec(memory_space=pl.ANY)] + more, [projected] + extra

    def kernel(*refs):
        finish_kernel(index_of, *refs[: len(operands)], refs[-1])

    return pl.pallas_call(
        kernel,
        grid_spec=pltpu.PrefetchScalarGridSpec(
            num_scalar_prefetch=1,
            grid=(tiles,),
            in_specs=[whole(lowered.shape)] + [factor(i) for i in range(per_part)] + specs + more,
            out_specs=pl.BlockSpec((out[0], tile), lambda n, _: (0, first + n)),
        ),
        out_shape=shape_of(out, jnp.bfloat16),
        input_output_aliases=aliases,
        compiler_params=SMALL,
        cost_estimate=BRIEF,
        name="finish",
    )(*operands, *extra)


def per_device(
    tokens,
    cotangent,
    frozen_up_weight,
    adapter_down_factor,
    adapter_up_factor,
    tokens_per_adapter,
    adapter_of_block,
    slot_of_block,
):
    owners = lax.axis_size("dp")
    parts = lax.axis_size("tensor")
    chips = parts // CORES
    block_count = adapter_of_block.shape[0]
    adapter_count = adapter_up_factor.shape[0]
    width_dev = tokens.shape[1]
    index_of = functools.partial(
        Index, block_count=block_count, adapter_count=adapter_count, parts=parts
    )
    shape = index_of(None)
    index = Index.pack(adapter_of_block, slot_of_block, tokens_per_adapter)

    def to_other_core(value):
        return lax.ppermute(value, "tensor", [(i, i ^ 1) for i in range(parts)])

    def to_chip(value, k):
        return lax.ppermute(value, "tensor", [(i, i ^ (k * CORES)) for i in range(parts)])

    def across_dp(value, k):
        return lax.ppermute(value, "dp", [(i, i ^ k) for i in range(owners)])

    def same_core(value):
        return [value] + [to_chip(value, k) for k in range(1, chips)]

    def with_other_core(values):
        return values + [to_other_core(v) for v in values]

    def small_products(waits):
        return narrow(
            index_of,
            index,
            shape,
            tokens,
            jnp.swapaxes(adapter_down_factor, 1, 2),
            cotangent,
            adapter_up_factor,
            waits,
        )

    def over_parts(send, keep):
        arrived = to_other_core(send)
        return arrived, [to_chip(keep[k] + arrived[k], k) for k in range(1, chips)]

    def over_dp(total):
        k = owners // 2
        while k > 1:
            total = total + across_dp(total, k)
            k //= 2
        return total, [across_dp(total, 1)]

    if owners == 4 and block_count == 4:
        relay = Relay(index_of, index, tokens)
        sent = relay.first()
        send, keep, back = small_products([sent])
        arrived, others = over_parts(send, keep)
        total, more = over_dp(merge(keep, arrived, back, others, []))
        relay.second([total])
        lowered, back_rows, pieces = make_pieces(
            index_of, index, shape, total, more, cotangent, []
        )
        relay.settle(more)
        weight = load_weight(frozen_up_weight, relay.arrived[-1][1:3])
        pieces = with_other_core(same_core(pieces))
        back_rows = with_other_core(same_core(back_rows))
        ahead = [v for chunk in relay.arrived[1:] for v in chunk[3:5]]
        ahead.append(weight)
        chunks = [lambda waits: relay.rows(0, ahead)]
        chunks += [functools.partial(relay.rows, c) for c in range(1, len(CHUNK_ROWS))]
    else:
        weight = load_weight(frozen_up_weight, [])
        send, keep, back = small_products([])
        arrived, others = over_parts(send, keep)
        total, more = over_dp(merge(keep, arrived, back, others, []))
        lowered, back_rows, pieces = make_pieces(
            index_of, index, shape, total, more, cotangent, []
        )
        pieces = with_other_core(same_core(pieces))
        back_rows = with_other_core(same_core(back_rows))
        every_slot = lax.all_gather(
            tokens.reshape(CAP, BLK, width_dev), "dp", axis=0, tiled=True
        )
        part = lax.axis_index("tensor")
        devices = jnp.arange(parts, dtype=jnp.int32)
        order = (devices // chips ^ 1) + (devices % chips) * CORES ^ part
        blocks = (order[:, None] * shape.per_part + jnp.arange(shape.per_part)).reshape(-1)
        picked = every_slot[adapter_of_block[blocks] * CAP + slot_of_block[blocks]]
        starts = [sum(CHUNK_ROWS[:c]) for c in range(len(CHUNK_ROWS))]
        chunks = [
            lambda waits, s=s, count=count: picked[:, s : s + count].reshape(-1, width_dev)
            for s, count in zip(starts, CHUNK_ROWS)
        ]
    def summed(rows, part, waits):
        each = rows.shape[0] // parts
        send_own, send, own, other = split_product(shape, rows, weight, part, PARTS, waits)
        outgoing = (other + to_other_core(send).astype(jnp.float32)).astype(jnp.bfloat16)
        across = [to_chip(outgoing[(k - 1) * each : k * each], k) for k in range(1, chips)]
        return [own, to_other_core(send_own)] + across, outgoing

    first = chunks[0](())
    first_0 = summed(first, 0, pieces[1:chips])
    second = chunks[1](())
    first_1 = summed(first, 1, [second])
    second_0 = summed(second, 0, [*first_0[0][2:], *back_rows[1:chips]])
    second_1 = summed(second, 1, [*first_1[0][2:], *back_rows[chips:], *pieces[chips:]])
    sums = [[first_0[0], first_1[0]], [second_0[0], second_1[0]]]
    up_grad = up_gradient(index_of, index, adapter_count, pieces)
    down_grad = down_gradient(index_of, index, tokens, back_rows)
    projected = None
    for part in range(PARTS):
        projected = finish(
            index_of,
            index,
            lowered,
            adapter_up_factor,
            [done[part] for done in sums],
            part,
            projected,
            [] if projected is not None else [up_grad, down_grad],
        )
    return (projected, jnp.swapaxes(down_grad, 1, 2), up_grad)


def solution(mesh):
    return jax.shard_map(
        per_device,
        mesh=mesh,
        in_specs=(
            P(("groups", "dp"), "tensor"),
            P(("groups", "tensor"), "dp"),
            P("tensor", "dp"),
            P(("groups", "dp"), "tensor", None),
            P("groups", None, "dp"),
            P("groups"),
            P("groups"),
            P("groups"),
        ),
        out_specs=(
            P(("groups", "tensor"), "dp"),
            P(("groups", "dp"), "tensor", None),
            P("groups", None, "dp"),
        ),
        check_vma=False,
    )
```

```python
import functools

import jax
import jax.numpy as jnp
from jax import lax
from jax.experimental import pallas as pl
from jax.experimental.pallas import tpu as pltpu
from jax.sharding import PartitionSpec as P

BLK = 128
CAP = 3
CORES = 2
CHUNK_ROWS = (64, 64)
PARTS = 2
SMALL = pltpu.CompilerParams(vmem_limit_bytes=12 * 2**20)

adapter_scale = 0.5

LAST = (((1,), (1,)), ((), ()))


class Index:
    def __init__(self, ref, block_count, adapter_count, parts):
        self.ref = ref
        self.blocks, self.adapters, self.parts = block_count, adapter_count, parts
        self.chips = parts // CORES
        self.per_part = block_count // parts

    @staticmethod
    def pack(adapter_of_block, slot_of_block, tokens_per_adapter):
        place = jnp.stack([lax.axis_index("dp"), lax.axis_index("tensor")]).astype(jnp.int32)
        return jnp.concatenate([adapter_of_block, slot_of_block, tokens_per_adapter, place])

    def owner(self, block):
        return self.ref[block]

    def slot(self, block):
        return self.ref[self.blocks + block]

    def tokens(self, adapter):
        return self.ref[2 * self.blocks + adapter]

    @property
    def place(self):
        return self.ref[2 * self.blocks + self.adapters]

    @property
    def part(self):
        return self.ref[2 * self.blocks + self.adapters + 1]

    def block(self, core_bit, chip_bits, i):
        return (self.part ^ (chip_bits * CORES + core_bit)) * self.per_part + i

    def position(self, block):
        bits = (block // self.per_part) ^ self.part
        half = (1 - bits % CORES) * self.chips + bits // CORES
        return half * self.per_part + block % self.per_part

    def live_rows(self, block):
        adapter = self.owner(block)
        first = jnp.int32(0)
        for a in range(self.adapters):
            count = (self.tokens(a) + BLK - 1) // BLK
            first = first + jnp.where(a < adapter, count, 0)
        return self.tokens(adapter) - (block - first) * BLK


def in_vmem(value):
    return pltpu.with_memory_space_constraint(value, pltpu.VMEM)


def in_hbm(value):
    return pltpu.with_memory_space_constraint(value, pltpu.HBM)


def held():
    return pl.BlockSpec(memory_space=pltpu.VMEM)


def whole(shape):
    return pl.BlockSpec(shape, lambda *_: (0,) * len(shape))


def shape_of(shape, dtype):
    return jax.ShapeDtypeStruct(shape, dtype)


BRIEF = pl.CostEstimate(flops=1, bytes_accessed=1, transcendentals=0)


def own_rows(index, block, tokens_ref, out_ref, start=0):
    at = pl.multiple_of(index.slot(block) * BLK + start, 16)
    out_ref[...] = tokens_ref[pl.ds(at, out_ref.shape[0])]


def first_hop_kernel(index_of, index_ref, tokens_ref, *refs):
    a_ref, b_ref, sems = refs[-3:]
    index = index_of(index_ref)
    copies = [
        pltpu.make_async_copy(
            tokens_ref.at[pl.ds(pl.multiple_of(index.slot(block) * BLK, BLK), BLK)],
            out_ref,
            sems.at[i],
        )
        for i, (block, out_ref) in enumerate(
            ((jnp.where(index.place == 0, 2, 1), a_ref), (0, b_ref))
        )
    ]
    for copy in copies:
        copy.start()
    for copy in copies:
        copy.wait()


def second_hop_kernel(index_of, index_ref, tokens_ref, a_ref, b_ref, *refs):
    x_ref, y_ref = refs[-2:]
    index = index_of(index_ref)
    place = index.place
    outer = jnp.where(place == 0, 1, jnp.where(place == 1, 0, 2))
    middle = jnp.where(place == 1, 2, 1)
    own_rows(index, outer, tokens_ref, x_ref)
    own_rows(index, middle, tokens_ref, y_ref)

    @pl.when((place == 1) & (index.owner(0) != 1))
    def _():
        x_ref[...] = b_ref[...]

    @pl.when(((place == 1) | (place == 2)) & (index.owner(middle) != place))
    def _():
        y_ref[...] = a_ref[...]


def settle_kernel(index_of, index_ref, tokens_ref, x_ref, y_ref, *refs):
    out_refs = refs[-len(CHUNK_ROWS) :]
    index = index_of(index_ref)
    place = index.place
    owner = index.owner(place)
    mine = owner == place
    edge = (place == 0) | ((place == 1) & (owner == 0)) | ((place == 2) & (owner == 3))
    start = 0
    for out_ref in out_refs:
        rows = slice(start, start + out_ref.shape[0])
        own_rows(index, place, tokens_ref, out_ref, start)

        @pl.when(jnp.logical_not(mine) & edge)
        def _(out_ref=out_ref, rows=rows):
            out_ref[...] = x_ref[rows]

        @pl.when(jnp.logical_not(mine | edge))
        def _(out_ref=out_ref, rows=rows):
            out_ref[...] = y_ref[rows]

        start += out_ref.shape[0]


def collect_kernel(index_of, count, index_ref, home_ref, outer_ref, *refs):
    inner_refs, outer_refs, out_ref = refs[:2], refs[2:4], refs[-1]
    index = index_of(index_ref)
    place = index.place

    def put(block, ref):
        at = pl.multiple_of(index.position(block) * count, 16)
        out_ref[pl.ds(at, count)] = ref[...]

    put(place, home_ref)
    put(place ^ 1, outer_ref)
    middle = (place == 1) | (place == 2)

    @pl.when(middle)
    def _():
        put(3 - place, inner_refs[0])
        put(place ^ 2, inner_refs[1])

    @pl.when(jnp.logical_not(middle))
    def _():
        put(place ^ 2, outer_refs[0])
        put(3 - place, outer_refs[1])


def after(values, far=()):
    specs = [
        pl.BlockSpec((1,) * (v.ndim - 2) + (16, 128), lambda *_, n=v.ndim: (0,) * n) for v in values
    ] + [pl.BlockSpec(memory_space=pl.ANY)] * len(far)
    return specs, [*values, *(in_hbm(v) for v in far)]


def hop_call(kernel, index, tokens, heights, received, waits, name):
    specs, extra = after(waits)
    width = tokens.shape[1]
    first = not received
    return pl.pallas_call(
        kernel,
        grid_spec=pltpu.PrefetchScalarGridSpec(
            num_scalar_prefetch=1,
            grid=(1,),
            in_specs=[pl.BlockSpec(memory_space=pl.ANY) if first else held()]
            + [held()] * len(received)
            + specs,
            out_specs=[held()] * len(heights),
            scratch_shapes=[pltpu.SemaphoreType.DMA((len(heights),))] * first,
        ),
        out_shape=[pltpu.VMEM((height, width), tokens.dtype) for height in heights],
        compiler_params=SMALL,
        cost_estimate=BRIEF,
        name=name,
    )(index, (in_hbm if first else in_vmem)(tokens), *[in_vmem(r) for r in received], *extra)


class Relay:
    def __init__(self, index_of, index, tokens):
        self.index_of, self.index, self.tokens = index_of, index, tokens

    def call(self, kernel, heights, received, waits, name):
        kernel = functools.partial(kernel, self.index_of)
        return hop_call(kernel, self.index, self.tokens, heights, received, waits, name)

    def first(self, waits=()):
        inward, left = self.call(first_hop_kernel, (BLK, BLK), (), waits, "first_hop")
        self.received = (
            lax.ppermute(inward, "dp", [(3, 2), (0, 1)]),
            lax.ppermute(left, "dp", [(2, 1)]),
        )
        return inward

    def second(self, waits=()):
        outer, middle = self.call(
            second_hop_kernel, (BLK, BLK), self.received, waits, "second_hop"
        )
        self.received = (
            lax.ppermute(outer, "dp", [(1, 0), (0, 1), (3, 2)]),
            lax.ppermute(middle, "dp", [(2, 1), (1, 2)]),
        )
        return outer

    def settle(self, waits=()):
        homes = self.call(settle_kernel, CHUNK_ROWS, self.received, waits, "settle")
        self.arrived = [self.spread(home) for home in homes]

    def spread(self, home):
        outer = lax.ppermute(home, "dp", [(0, 1), (1, 0), (2, 3), (3, 2)])
        inner = lax.ppermute(home, "dp", [(1, 2), (2, 1)])
        outer_2 = lax.ppermute(inner, "dp", [(1, 0), (2, 3)])
        inner_2 = lax.ppermute(outer, "dp", [(1, 2), (2, 1)])
        outer_3 = lax.ppermute(inner_2, "dp", [(1, 0), (2, 3)])
        return home, outer, inner, inner_2, outer_2, outer_3

    def rows(self, chunk, waits=(), far=()):
        arrived = self.arrived[chunk]
        count, width = arrived[0].shape
        specs, extra = after(waits, far)
        return pl.pallas_call(
            functools.partial(collect_kernel, self.index_of, count),
            grid_spec=pltpu.PrefetchScalarGridSpec(
                num_scalar_prefetch=1,
                grid=(1,),
                in_specs=[held()] * len(arrived) + specs,
                out_specs=held(),
            ),
            out_shape=pltpu.VMEM((4 * count, width), self.tokens.dtype),
            compiler_params=SMALL,
            cost_estimate=BRIEF,
            name="collect",
        )(self.index, *[in_vmem(a) for a in arrived], *extra)


def load_weight_kernel(w_ref, *refs):
    out_ref, sems = refs[-2:]
    streams = sems.shape[0]
    depth = w_ref.shape[0] // streams
    copies = [
        pltpu.make_async_copy(
            w_ref.at[pl.ds(i * depth, depth)], out_ref.at[pl.ds(i * depth, depth)], sems.at[i]
        )
        for i in range(streams)
    ]
    for copy in copies:
        copy.start()
    for copy in copies:
        copy.wait()


def load_weight(weight, waits):
    specs, extra = after(waits)
    return pl.pallas_call(
        load_weight_kernel,
        grid=(1,),
        in_specs=[pl.BlockSpec(memory_space=pl.ANY)] + specs,
        out_specs=pl.BlockSpec(memory_space=pl.ANY),
        out_shape=pltpu.VMEM(weight.shape, weight.dtype),
        scratch_shapes=[pltpu.SemaphoreType.DMA((4,))],
        compiler_params=SMALL,
        cost_estimate=BRIEF,
        name="load_weight",
    )(in_hbm(weight), *extra)


def split_product_kernel(each, half, first, tile, rows_ref, w_ref, *refs):
    send_own_ref, send_ref, own_ref, other_ref = refs[-4:]
    for n in range(own_ref.shape[1] // tile):
        total = jnp.dot(
            rows_ref[...],
            w_ref[:, first + n * tile : first + (n + 1) * tile],
            preferred_element_type=jnp.float32,
        )
        columns = slice(n * tile, (n + 1) * tile)
        send_own_ref[:, columns] = total[:each].astype(send_own_ref.dtype)
        send_ref[:, columns] = total[each:half].astype(send_ref.dtype)
        own_ref[:, columns] = total[half : half + each]
        other_ref[:, columns] = total[half + each :]


def split_product(shape, rows, weight, part, part_count, waits):
    half = rows.shape[0] // 2
    each = half // shape.chips
    width = weight.shape[1] // part_count
    specs, extra = after(waits)
    return pl.pallas_call(
        functools.partial(split_product_kernel, each, half, part * width, min(512, width)),
        grid=(1,),
        in_specs=[held(), held()] + specs,
        out_specs=[held()] * 4,
        out_shape=[
            pltpu.VMEM((each, width), jnp.bfloat16),
            pltpu.VMEM((half - each, width), jnp.bfloat16),
            pltpu.VMEM((each, width), jnp.float32),
            pltpu.VMEM((half - each, width), jnp.float32),
        ],
        compiler_params=SMALL,
        cost_estimate=BRIEF,
        name="split_product",
    )(in_vmem(rows), in_vmem(weight), *extra)


def leaving_kernel(other_ref, arrived_ref, *refs):
    total = other_ref[...] + arrived_ref[...].astype(jnp.float32)
    refs[-1][...] = total.astype(refs[-1].dtype)


def leaving(other, arrived, waits):
    specs, extra = after(waits)
    return pl.pallas_call(
        leaving_kernel,
        grid=(1,),
        in_specs=[held(), held()] + specs,
        out_specs=held(),
        out_shape=pltpu.VMEM(other.shape, arrived.dtype),
        compiler_params=SMALL,
        cost_estimate=BRIEF,
        name="leaving",
    )(in_vmem(other), in_vmem(arrived), *extra)


def narrow_kernel(index_of, index_ref, tokens_ref, down_ref, cot_ref, up_ref, *refs):
    send_ref, keep_ref, back_ref, low, tokens, down, cot, up, sems = refs[-9:]
    index = index_of(index_ref)
    pairs = [(tokens_ref, tokens), (down_ref, down), (cot_ref, cot)]
    for i in range(index.per_part):
        adapter = index.owner(index.block(0, 0, i))
        pairs.append((up_ref.at[adapter], up.at[i]))
    copies = [
        pltpu.make_async_copy(source, target, sems.at[j])
        for j, (source, target) in enumerate(pairs)
    ]
    for copy in copies:
        copy.start()
    for copy in copies[:2]:
        copy.wait()
    for m in range(CAP):
        low[m] = lax.dot_general(
            down[0],
            tokens[m * BLK : (m + 1) * BLK],
            LAST,
            preferred_element_type=jnp.float32,
        )
    for core_bit, out_ref in ((1, send_ref), (0, keep_ref)):
        for chip_bits in range(index.chips):
            for i in range(index.per_part):
                block = index.block(core_bit, chip_bits, i)
                mine = index.owner(block) == index.place
                out_ref[chip_bits, i] = jnp.where(mine, low[index.slot(block)], 0.0)
    for copy in copies[2:]:
        copy.wait()
    for i in range(index.per_part):
        back_ref[i] = lax.dot_general(
            up[i], cot[i * BLK : (i + 1) * BLK], LAST, preferred_element_type=jnp.float32
        )


def narrow(index_of, index, shape, tokens, down, cotangent, up, waits):
    rank = up.shape[1]
    one = (shape.per_part, rank, BLK)
    outs = [(shape.chips,) + one, (shape.chips,) + one, one]
    operands = (tokens, down, cotangent, up)
    specs, extra = after(waits)
    return pl.pallas_call(
        functools.partial(narrow_kernel, index_of),
        grid_spec=pltpu.PrefetchScalarGridSpec(
            num_scalar_prefetch=1,
            grid=(1,),
            in_specs=[pl.BlockSpec(memory_space=pl.ANY)] * len(operands) + specs,
            out_specs=[held()] * len(outs),
            scratch_shapes=[
                pltpu.VMEM((CAP, rank, BLK), jnp.float32),
                pltpu.VMEM(tokens.shape, tokens.dtype),
                pltpu.VMEM(down.shape, down.dtype),
                pltpu.VMEM(cotangent.shape, cotangent.dtype),
                pltpu.VMEM((shape.per_part,) + up.shape[1:], up.dtype),
                pltpu.SemaphoreType.DMA((3 + shape.per_part,)),
            ],
        ),
        out_shape=[pltpu.VMEM(o, jnp.float32) for o in outs],
        compiler_params=SMALL,
        cost_estimate=BRIEF,
        name="narrow",
    )(index, *[in_hbm(o) for o in operands], *extra)


def merge_kernel(keep_ref, arrived_ref, back_ref, *refs):
    out_ref = refs[-1]
    total = keep_ref[0] + arrived_ref[0]
    for ref in refs[:-1][: keep_ref.shape[0] - 1]:
        total = total + ref[...]
    out_ref[0] = total
    out_ref[1] = back_ref[...]


def merge(keep, arrived, back, others, waits):
    specs, extra = after(waits)
    operands = (keep, arrived, back, *others)
    out = (2,) + back.shape
    return pl.pallas_call(
        merge_kernel,
        grid=(1,),
        in_specs=[whole(o.shape) for o in operands] + specs,
        out_specs=whole(out),
        out_shape=shape_of(out, jnp.float32),
        compiler_params=SMALL,
        cost_estimate=BRIEF,
        name="merge",
    )(*operands, *extra)


def pieces_kernel(index_of, count, index_ref, cot_ref, sum_ref, *refs):
    more_refs, (low_ref, back_ref, piece_ref) = refs[:count], refs[-3:]
    index = index_of(index_ref)
    level = [sum_ref[...]] + [ref[...] for ref in more_refs]
    while len(level) > 1:
        level = [level[j] + level[j + 1] for j in range(0, len(level), 2)]
    for i in range(index.per_part):
        live = index.live_rows(index.block(0, 0, i))
        keep = lax.broadcasted_iota(jnp.int32, low_ref.shape[1:], 1) < live
        lowered = jnp.where(keep, level[0][0, i], 0.0).astype(low_ref.dtype)
        low_ref[i] = lowered
        back_ref[i] = jnp.where(keep, level[0][1, i], 0.0).astype(back_ref.dtype)
        piece_ref[i] = jnp.dot(
            lowered, cot_ref[i * BLK : (i + 1) * BLK], preferred_element_type=jnp.float32
        ).astype(piece_ref.dtype)


def make_pieces(index_of, index, shape, total, more, cotangent, waits):
    _, per_part, rank, _ = total.shape
    width = cotangent.shape[1]
    outs = [(per_part, rank, BLK), (per_part, rank, BLK), (per_part, rank, width)]
    operands = (cotangent, total, *more)
    specs, extra = after(waits)
    return pl.pallas_call(
        functools.partial(pieces_kernel, index_of, len(more)),
        grid_spec=pltpu.PrefetchScalarGridSpec(
            num_scalar_prefetch=1,
            grid=(1,),
            in_specs=[whole(o.shape) for o in operands] + specs,
            out_specs=[whole(o) for o in outs],
        ),
        out_shape=[shape_of(o, jnp.bfloat16) for o in outs],
        compiler_params=SMALL,
        cost_estimate=BRIEF,
        name="pieces",
    )(index, *operands, *extra)


def down_gradient_kernel(index_of, index_ref, tokens_ref, *refs):
    back_refs, out_ref = refs[:-1], refs[-1]
    index = index_of(index_ref)
    out_ref[...] = jnp.zeros_like(out_ref)
    for core_bit in range(CORES):
        for chip_bits in range(index.chips):
            for i in range(index.per_part):
                block = index.block(core_bit, chip_bits, i)
                back_ref = back_refs[core_bit * index.chips + chip_bits]

                @pl.when(index.owner(block) == index.place)
                def _(block=block, back_ref=back_ref, i=i):
                    at = pl.multiple_of(index.slot(block) * BLK, BLK)
                    out_ref[0] += adapter_scale * jnp.dot(
                        back_ref[i],
                        tokens_ref[pl.ds(at, BLK)],
                        preferred_element_type=jnp.float32,
                    )


def down_gradient(index_of, index, tokens, backs):
    out = (1, backs[0].shape[1], tokens.shape[1])
    operands = (in_vmem(tokens), *backs)
    return pl.pallas_call(
        functools.partial(down_gradient_kernel, index_of),
        grid_spec=pltpu.PrefetchScalarGridSpec(
            num_scalar_prefetch=1,
            grid=(1,),
            in_specs=[held()] + [whole(o.shape) for o in backs],
            out_specs=whole(out),
        ),
        out_shape=shape_of(out, jnp.float32),
        compiler_params=SMALL,
        cost_estimate=BRIEF,
        name="down_gradient",
    )(index, *operands)


def up_gradient_kernel(index_of, index_ref, *refs):
    piece_refs, out_ref = refs[:-1], refs[-1]
    index = index_of(index_ref)

    def of_device(core_bit, chip_bits, adapter):
        total = None
        for i in range(index.per_part):
            mine = index.owner(index.block(core_bit, chip_bits, i)) == adapter
            piece = piece_refs[core_bit * index.chips + chip_bits][i].astype(jnp.float32)
            term = jnp.where(mine, piece, 0.0)
            total = term if total is None else total + term
        return total

    for adapter in range(index.adapters):
        level = [
            of_device(0, j, adapter) + of_device(1, j, adapter) for j in range(index.chips)
        ]
        while len(level) > 1:
            level = [level[j] + level[j + 1] for j in range(0, len(level), 2)]
        out_ref[adapter] = adapter_scale * level[0]


def up_gradient(index_of, index, adapter_count, pieces):
    per_part, rank, width = pieces[0].shape
    tile = 1024
    out = (adapter_count, rank, width)
    return pl.pallas_call(
        functools.partial(up_gradient_kernel, index_of),
        grid_spec=pltpu.PrefetchScalarGridSpec(
            num_scalar_prefetch=1,
            grid=(width // tile,),
            in_specs=[pl.BlockSpec((per_part, rank, tile), lambda n, _: (0, 0, n))] * len(pieces),
            out_specs=pl.BlockSpec((adapter_count, rank, tile), lambda n, _: (0, 0, n)),
        ),
        out_shape=shape_of(out, jnp.float32),
        compiler_params=SMALL,
        cost_estimate=BRIEF,
        name="up_gradient",
    )(index, *pieces)


def finish_kernel(index_of, index_ref, low_ref, *refs):
    index = index_of(index_ref)
    up_refs, sum_refs, out_ref = refs[: index.per_part], refs[index.per_part : -1], refs[-1]
    per_chunk = len(sum_refs) // len(CHUNK_ROWS)
    for i in range(index.per_part):
        block = index.block(0, 0, i)
        live = index.live_rows(block)
        side = lax.dot_general(
            low_ref[i],
            up_refs[i][0],
            (((0,), (0,)), ((), ())),
            preferred_element_type=jnp.float32,
        )
        start = 0
        for c, count in enumerate(CHUNK_ROWS):
            total = adapter_scale * side[start : start + count]
            for ref in sum_refs[c * per_chunk : (c + 1) * per_chunk]:
                total = total + ref[i * count : (i + 1) * count].astype(jnp.float32)
            keep = start + lax.broadcasted_iota(jnp.int32, total.shape, 0) < live
            at = i * BLK + start
            out_ref[at : at + count] = jnp.where(keep, total, 0.0).astype(out_ref.dtype)
            start += count


def finish(index_of, index, lowered, up, sums, part, projected, far):
    per_part = lowered.shape[0]
    _, rank, width = up.shape
    tile = min(1024, width // PARTS)
    tiles = width // PARTS // tile
    first = part * tiles
    out = (per_part * BLK, width)

    def factor(i):
        def at(n, index_ref):
            index = index_of(index_ref)
            return (index.owner(index.block(0, 0, i)), 0, first + n)

        return pl.BlockSpec((1, rank, tile), at)

    flat = [term for chunk in sums for term in chunk]
    specs = [
        pl.BlockSpec((per_part * count, tile), lambda n, _: (0, n))
        for chunk, count in zip(sums, CHUNK_ROWS)
        for _ in chunk
    ]
    operands = [index, lowered, *[up] * per_part, *flat]
    more, extra = after((), far)
    aliases = {}
    if projected is not None:
        aliases = {len(operands): 0}
        more, extra = [pl.BlockSpec(memory_space=pl.ANY)] + more, [projected] + extra

    def kernel(*refs):
        finish_kernel(index_of, *refs[: len(operands)], refs[-1])

    return pl.pallas_call(
        kernel,
        grid_spec=pltpu.PrefetchScalarGridSpec(
            num_scalar_prefetch=1,
            grid=(tiles,),
            in_specs=[whole(lowered.shape)] + [factor(i) for i in range(per_part)] + specs + more,
            out_specs=pl.BlockSpec((out[0], tile), lambda n, _: (0, first + n)),
        ),
        out_shape=shape_of(out, jnp.bfloat16),
        input_output_aliases=aliases,
        compiler_params=SMALL,
        cost_estimate=BRIEF,
        name="finish",
    )(*operands, *extra)


def per_device(
    tokens,
    cotangent,
    frozen_up_weight,
    adapter_down_factor,
    adapter_up_factor,
    tokens_per_adapter,
    adapter_of_block,
    slot_of_block,
):
    owners = lax.axis_size("dp")
    parts = lax.axis_size("tensor")
    chips = parts // CORES
    block_count = adapter_of_block.shape[0]
    adapter_count = adapter_up_factor.shape[0]
    width_dev = tokens.shape[1]
    index_of = functools.partial(
        Index, block_count=block_count, adapter_count=adapter_count, parts=parts
    )
    shape = index_of(None)
    index = Index.pack(adapter_of_block, slot_of_block, tokens_per_adapter)

    def to_other_core(value):
        return lax.ppermute(value, "tensor", [(i, i ^ 1) for i in range(parts)])

    def to_chip(value, k):
        return lax.ppermute(value, "tensor", [(i, i ^ (k * CORES)) for i in range(parts)])

    def across_dp(value, k):
        return lax.ppermute(value, "dp", [(i, i ^ k) for i in range(owners)])

    def same_core(value):
        return [value] + [to_chip(value, k) for k in range(1, chips)]

    def with_other_core(values):
        return values + [to_other_core(v) for v in values]

    def small_products(waits):
        return narrow(
            index_of,
            index,
            shape,
            tokens,
            jnp.swapaxes(adapter_down_factor, 1, 2),
            cotangent,
            adapter_up_factor,
            waits,
        )

    def over_parts(send, keep):
        arrived = to_other_core(send)
        return arrived, [to_chip(keep[k] + arrived[k], k) for k in range(1, chips)]

    def over_dp(total):
        k = owners // 2
        while k > 1:
            total = total + across_dp(total, k)
            k //= 2
        return total, [across_dp(total, 1)]

    if owners == 4 and block_count == 4:
        relay = Relay(index_of, index, tokens)
        sent = relay.first()
        send, keep, back = small_products([sent])
        arrived, others = over_parts(send, keep)
        total, more = over_dp(merge(keep, arrived, back, others, []))
        relay.second([total])
        lowered, back_rows, pieces = make_pieces(
            index_of, index, shape, total, more, cotangent, []
        )
        relay.settle(more)
        weight = load_weight(frozen_up_weight, relay.arrived[-1][1:3])
        pieces = with_other_core(same_core(pieces))
        back_rows = with_other_core(same_core(back_rows))
        ahead = [v for chunk in relay.arrived[1:] for v in chunk[3:5]]
        ahead.append(weight)
        chunks = [lambda waits: relay.rows(0, ahead)]
        chunks += [functools.partial(relay.rows, c) for c in range(1, len(CHUNK_ROWS))]
    else:
        weight = load_weight(frozen_up_weight, [])
        send, keep, back = small_products([])
        arrived, others = over_parts(send, keep)
        total, more = over_dp(merge(keep, arrived, back, others, []))
        lowered, back_rows, pieces = make_pieces(
            index_of, index, shape, total, more, cotangent, []
        )
        pieces = with_other_core(same_core(pieces))
        back_rows = with_other_core(same_core(back_rows))
        every_slot = lax.all_gather(
            tokens.reshape(CAP, BLK, width_dev), "dp", axis=0, tiled=True
        )
        part = lax.axis_index("tensor")
        devices = jnp.arange(parts, dtype=jnp.int32)
        order = (devices // chips ^ 1) + (devices % chips) * CORES ^ part
        blocks = (order[:, None] * shape.per_part + jnp.arange(shape.per_part)).reshape(-1)
        picked = every_slot[adapter_of_block[blocks] * CAP + slot_of_block[blocks]]
        starts = [sum(CHUNK_ROWS[:c]) for c in range(len(CHUNK_ROWS))]
        chunks = [
            lambda waits, s=s, count=count: picked[:, s : s + count].reshape(-1, width_dev)
            for s, count in zip(starts, CHUNK_ROWS)
        ]
    def summed(rows, part, waits, late=()):
        each = rows.shape[0] // parts
        send_own, send, own, other = split_product(shape, rows, weight, part, PARTS, waits)
        outgoing = leaving(other, to_other_core(send), late)
        across = [to_chip(outgoing[(k - 1) * each : k * each], k) for k in range(1, chips)]
        return [own, to_other_core(send_own)] + across, outgoing

    first = chunks[0](())
    first_0 = summed(first, 0, pieces[1:chips])
    second = chunks[1](())
    first_1 = summed(first, 1, [second])
    second_0 = summed(second, 0, back_rows[1:chips], first_0[0][2:])
    second_1 = summed(second, 1, [*back_rows[chips:], *pieces[chips:]], first_1[0][2:])
    sums = [[first_0[0], first_1[0]], [second_0[0], second_1[0]]]
    up_grad = up_gradient(index_of, index, adapter_count, pieces)
    down_grad = down_gradient(index_of, index, tokens, back_rows)
    projected = None
    for part in range(PARTS):
        projected = finish(
            index_of,
            index,
            lowered,
            adapter_up_factor,
            [done[part] for done in sums],
            part,
            projected,
            [] if projected is not None else [up_grad, down_grad],
        )
    return (projected, jnp.swapaxes(down_grad, 1, 2), up_grad)


def solution(mesh):
    return jax.shard_map(
        per_device,
        mesh=mesh,
        in_specs=(
            P(("groups", "dp"), "tensor"),
            P(("groups", "tensor"), "dp"),
            P("tensor", "dp"),
            P(("groups", "dp"), "tensor", None),
            P("groups", None, "dp"),
            P("groups"),
            P("groups"),
            P("groups"),
        ),
        out_specs=(
            P(("groups", "tensor"), "dp"),
            P(("groups", "dp"), "tensor", None),
            P("groups", None, "dp"),
        ),
        check_vma=False,
    )
```

```python
import functools

import jax
import jax.numpy as jnp
from jax import lax
from jax.experimental import pallas as pl
from jax.experimental.pallas import tpu as pltpu
from jax.sharding import PartitionSpec as P

BLK = 128
CAP = 3
CORES = 2
CHUNK_ROWS = (64, 64)
PARTS = 2
SMALL = pltpu.CompilerParams(vmem_limit_bytes=12 * 2**20)

adapter_scale = 0.5

LAST = (((1,), (1,)), ((), ()))


class Index:
    def __init__(self, ref, block_count, adapter_count, parts):
        self.ref = ref
        self.blocks, self.adapters, self.parts = block_count, adapter_count, parts
        self.chips = parts // CORES
        self.per_part = block_count // parts

    @staticmethod
    def pack(adapter_of_block, slot_of_block, tokens_per_adapter):
        place = jnp.stack([lax.axis_index("dp"), lax.axis_index("tensor")]).astype(jnp.int32)
        return jnp.concatenate([adapter_of_block, slot_of_block, tokens_per_adapter, place])

    def owner(self, block):
        return self.ref[block]

    def slot(self, block):
        return self.ref[self.blocks + block]

    def tokens(self, adapter):
        return self.ref[2 * self.blocks + adapter]

    @property
    def place(self):
        return self.ref[2 * self.blocks + self.adapters]

    @property
    def part(self):
        return self.ref[2 * self.blocks + self.adapters + 1]

    def block(self, core_bit, chip_bits, i):
        return (self.part ^ (chip_bits * CORES + core_bit)) * self.per_part + i

    def position(self, block):
        bits = (block // self.per_part) ^ self.part
        half = (1 - bits % CORES) * self.chips + bits // CORES
        return half * self.per_part + block % self.per_part

    def live_rows(self, block):
        adapter = self.owner(block)
        first = jnp.int32(0)
        for a in range(self.adapters):
            count = (self.tokens(a) + BLK - 1) // BLK
            first = first + jnp.where(a < adapter, count, 0)
        return self.tokens(adapter) - (block - first) * BLK


def in_vmem(value):
    return pltpu.with_memory_space_constraint(value, pltpu.VMEM)


def in_hbm(value):
    return pltpu.with_memory_space_constraint(value, pltpu.HBM)


def held():
    return pl.BlockSpec(memory_space=pltpu.VMEM)


def whole(shape):
    return pl.BlockSpec(shape, lambda *_: (0,) * len(shape))


def shape_of(shape, dtype):
    return jax.ShapeDtypeStruct(shape, dtype)


BRIEF = pl.CostEstimate(flops=1, bytes_accessed=1, transcendentals=0)


def own_rows(index, block, tokens_ref, out_ref, start=0):
    at = pl.multiple_of(index.slot(block) * BLK + start, 16)
    out_ref[...] = tokens_ref[pl.ds(at, out_ref.shape[0])]


def first_hop_kernel(index_of, index_ref, tokens_ref, *refs):
    a_ref, b_ref, sems = refs[-3:]
    index = index_of(index_ref)
    copies = [
        pltpu.make_async_copy(
            tokens_ref.at[pl.ds(pl.multiple_of(index.slot(block) * BLK, BLK), BLK)],
            out_ref,
            sems.at[i],
        )
        for i, (block, out_ref) in enumerate(
            ((jnp.where(index.place == 0, 2, 1), a_ref), (0, b_ref))
        )
    ]
    for copy in copies:
        copy.start()
    for copy in copies:
        copy.wait()


def second_hop_kernel(index_of, index_ref, tokens_ref, a_ref, b_ref, *refs):
    x_ref, y_ref = refs[-2:]
    index = index_of(index_ref)
    place = index.place
    outer = jnp.where(place == 0, 1, jnp.where(place == 1, 0, 2))
    middle = jnp.where(place == 1, 2, 1)
    own_rows(index, outer, tokens_ref, x_ref)
    own_rows(index, middle, tokens_ref, y_ref)

    @pl.when((place == 1) & (index.owner(0) != 1))
    def _():
        x_ref[...] = b_ref[...]

    @pl.when(((place == 1) | (place == 2)) & (index.owner(middle) != place))
    def _():
        y_ref[...] = a_ref[...]


def settle_kernel(index_of, index_ref, tokens_ref, x_ref, y_ref, *refs):
    out_refs = refs[-len(CHUNK_ROWS) :]
    index = index_of(index_ref)
    place = index.place
    owner = index.owner(place)
    mine = owner == place
    edge = (place == 0) | ((place == 1) & (owner == 0)) | ((place == 2) & (owner == 3))
    start = 0
    for out_ref in out_refs:
        rows = slice(start, start + out_ref.shape[0])
        own_rows(index, place, tokens_ref, out_ref, start)

        @pl.when(jnp.logical_not(mine) & edge)
        def _(out_ref=out_ref, rows=rows):
            out_ref[...] = x_ref[rows]

        @pl.when(jnp.logical_not(mine | edge))
        def _(out_ref=out_ref, rows=rows):
            out_ref[...] = y_ref[rows]

        start += out_ref.shape[0]


def collect_kernel(index_of, count, index_ref, home_ref, outer_ref, *refs):
    inner_refs, outer_refs, out_ref = refs[:2], refs[2:4], refs[-1]
    index = index_of(index_ref)
    place = index.place

    def put(block, ref):
        at = pl.multiple_of(index.position(block) * count, 16)
        out_ref[pl.ds(at, count)] = ref[...]

    put(place, home_ref)
    put(place ^ 1, outer_ref)
    middle = (place == 1) | (place == 2)

    @pl.when(middle)
    def _():
        put(3 - place, inner_refs[0])
        put(place ^ 2, inner_refs[1])

    @pl.when(jnp.logical_not(middle))
    def _():
        put(place ^ 2, outer_refs[0])
        put(3 - place, outer_refs[1])


def after(values, far=()):
    specs = [
        pl.BlockSpec((1,) * (v.ndim - 2) + (16, 128), lambda *_, n=v.ndim: (0,) * n) for v in values
    ] + [pl.BlockSpec(memory_space=pl.ANY)] * len(far)
    return specs, [*values, *(in_hbm(v) for v in far)]


def hop_call(kernel, index, tokens, heights, received, waits, name):
    specs, extra = after(waits)
    width = tokens.shape[1]
    first = not received
    return pl.pallas_call(
        kernel,
        grid_spec=pltpu.PrefetchScalarGridSpec(
            num_scalar_prefetch=1,
            grid=(1,),
            in_specs=[pl.BlockSpec(memory_space=pl.ANY) if first else held()]
            + [held()] * len(received)
            + specs,
            out_specs=[held()] * len(heights),
            scratch_shapes=[pltpu.SemaphoreType.DMA((len(heights),))] * first,
        ),
        out_shape=[pltpu.VMEM((height, width), tokens.dtype) for height in heights],
        compiler_params=SMALL,
        cost_estimate=BRIEF,
        name=name,
    )(index, (in_hbm if first else in_vmem)(tokens), *[in_vmem(r) for r in received], *extra)


class Relay:
    def __init__(self, index_of, index, tokens):
        self.index_of, self.index, self.tokens = index_of, index, tokens

    def call(self, kernel, heights, received, waits, name):
        kernel = functools.partial(kernel, self.index_of)
        return hop_call(kernel, self.index, self.tokens, heights, received, waits, name)

    def first(self, waits=()):
        inward, left = self.call(first_hop_kernel, (BLK, BLK), (), waits, "first_hop")
        self.received = (
            lax.ppermute(inward, "dp", [(3, 2), (0, 1)]),
            lax.ppermute(left, "dp", [(2, 1)]),
        )
        return inward

    def second(self, waits=()):
        outer, middle = self.call(
            second_hop_kernel, (BLK, BLK), self.received, waits, "second_hop"
        )
        self.received = (
            lax.ppermute(outer, "dp", [(1, 0), (0, 1), (3, 2)]),
            lax.ppermute(middle, "dp", [(2, 1), (1, 2)]),
        )
        return outer

    def settle(self, waits=()):
        homes = self.call(settle_kernel, CHUNK_ROWS, self.received, waits, "settle")
        self.arrived = [self.spread(home) for home in homes]

    def spread(self, home):
        outer = lax.ppermute(home, "dp", [(0, 1), (1, 0), (2, 3), (3, 2)])
        inner = lax.ppermute(home, "dp", [(1, 2), (2, 1)])
        outer_2 = lax.ppermute(inner, "dp", [(1, 0), (2, 3)])
        inner_2 = lax.ppermute(outer, "dp", [(1, 2), (2, 1)])
        outer_3 = lax.ppermute(inner_2, "dp", [(1, 0), (2, 3)])
        return home, outer, inner, inner_2, outer_2, outer_3

    def rows(self, chunk, waits=(), far=()):
        arrived = self.arrived[chunk]
        count, width = arrived[0].shape
        specs, extra = after(waits, far)
        return pl.pallas_call(
            functools.partial(collect_kernel, self.index_of, count),
            grid_spec=pltpu.PrefetchScalarGridSpec(
                num_scalar_prefetch=1,
                grid=(1,),
                in_specs=[held()] * len(arrived) + specs,
                out_specs=held(),
            ),
            out_shape=pltpu.VMEM((4 * count, width), self.tokens.dtype),
            compiler_params=SMALL,
            cost_estimate=BRIEF,
            name="collect",
        )(self.index, *[in_vmem(a) for a in arrived], *extra)


def load_weight_kernel(w_ref, *refs):
    out_ref, sems = refs[-2:]
    streams = sems.shape[0]
    depth = w_ref.shape[0] // streams
    copies = [
        pltpu.make_async_copy(
            w_ref.at[pl.ds(i * depth, depth)], out_ref.at[pl.ds(i * depth, depth)], sems.at[i]
        )
        for i in range(streams)
    ]
    for copy in copies:
        copy.start()
    for copy in copies:
        copy.wait()


def load_weight(weight, waits):
    specs, extra = after(waits)
    return pl.pallas_call(
        load_weight_kernel,
        grid=(1,),
        in_specs=[pl.BlockSpec(memory_space=pl.ANY)] + specs,
        out_specs=pl.BlockSpec(memory_space=pl.ANY),
        out_shape=pltpu.VMEM(weight.shape, weight.dtype),
        scratch_shapes=[pltpu.SemaphoreType.DMA((4,))],
        compiler_params=SMALL,
        cost_estimate=BRIEF,
        name="load_weight",
    )(in_hbm(weight), *extra)


def split_product_kernel(each, half, first, tile, rows_ref, w_ref, *refs):
    send_own_ref, send_ref, own_ref, other_ref = refs[-4:]
    for n in range(own_ref.shape[1] // tile):
        total = jnp.dot(
            rows_ref[...],
            w_ref[:, first + n * tile : first + (n + 1) * tile],
            preferred_element_type=jnp.float32,
        )
        columns = slice(n * tile, (n + 1) * tile)
        send_own_ref[:, columns] = total[:each].astype(send_own_ref.dtype)
        send_ref[:, columns] = total[each:half].astype(send_ref.dtype)
        own_ref[:, columns] = total[half : half + each]
        other_ref[:, columns] = total[half + each :]


def split_product(shape, rows, weight, part, part_count, waits):
    half = rows.shape[0] // 2
    each = half // shape.chips
    width = weight.shape[1] // part_count
    specs, extra = after(waits)
    return pl.pallas_call(
        functools.partial(split_product_kernel, each, half, part * width, min(512, width)),
        grid=(1,),
        in_specs=[held(), held()] + specs,
        out_specs=[held()] * 4,
        out_shape=[
            pltpu.VMEM((each, width), jnp.bfloat16),
            pltpu.VMEM((half - each, width), jnp.bfloat16),
            pltpu.VMEM((each, width), jnp.float32),
            pltpu.VMEM((half - each, width), jnp.float32),
        ],
        compiler_params=SMALL,
        cost_estimate=BRIEF,
        name="split_product",
    )(in_vmem(rows), in_vmem(weight), *extra)


def run_copies(pairs, sems):
    copies = [
        pltpu.make_async_copy(source, target, sems.at[j])
        for j, (source, target) in enumerate(pairs)
    ]
    for copy in copies:
        copy.start()
    for copy in copies:
        copy.wait()


def narrow_kernel(index_of, index_ref, tokens_ref, down_ref, *refs):
    send_ref, keep_ref, low, tokens, down, sems = refs[-6:]
    index = index_of(index_ref)
    run_copies([(tokens_ref, tokens), (down_ref, down)], sems)
    for m in range(CAP):
        low[m] = lax.dot_general(
            down[0],
            tokens[m * BLK : (m + 1) * BLK],
            LAST,
            preferred_element_type=jnp.float32,
        )
    for core_bit, out_ref in ((1, send_ref), (0, keep_ref)):
        for chip_bits in range(index.chips):
            for i in range(index.per_part):
                block = index.block(core_bit, chip_bits, i)
                mine = index.owner(block) == index.place
                out_ref[chip_bits, i] = jnp.where(mine, low[index.slot(block)], 0.0)


def narrow(index_of, index, shape, tokens, down, rank, waits):
    out = (shape.chips, shape.per_part, rank, BLK)
    specs, extra = after(waits)
    return pl.pallas_call(
        functools.partial(narrow_kernel, index_of),
        grid_spec=pltpu.PrefetchScalarGridSpec(
            num_scalar_prefetch=1,
            grid=(1,),
            in_specs=[pl.BlockSpec(memory_space=pl.ANY)] * 2 + specs,
            out_specs=[held()] * 2,
            scratch_shapes=[
                pltpu.VMEM((CAP, rank, BLK), jnp.float32),
                pltpu.VMEM(tokens.shape, tokens.dtype),
                pltpu.VMEM(down.shape, down.dtype),
                pltpu.SemaphoreType.DMA((2,)),
            ],
        ),
        out_shape=[pltpu.VMEM(out, jnp.float32)] * 2,
        compiler_params=SMALL,
        cost_estimate=BRIEF,
        name="narrow",
    )(index, in_hbm(tokens), in_hbm(down), *extra)


def backward_kernel(index_of, index_ref, cot_ref, up_ref, *refs):
    back_ref, cot, up, sems = refs[-4:]
    index = index_of(index_ref)
    pairs = [(cot_ref, cot)]
    for i in range(index.per_part):
        pairs.append((up_ref.at[index.owner(index.block(0, 0, i))], up.at[i]))
    run_copies(pairs, sems)
    for i in range(index.per_part):
        back_ref[i] = lax.dot_general(
            up[i], cot[i * BLK : (i + 1) * BLK], LAST, preferred_element_type=jnp.float32
        )


def backward(index_of, index, shape, cotangent, up, waits):
    specs, extra = after(waits)
    return pl.pallas_call(
        functools.partial(backward_kernel, index_of),
        grid_spec=pltpu.PrefetchScalarGridSpec(
            num_scalar_prefetch=1,
            grid=(1,),
            in_specs=[pl.BlockSpec(memory_space=pl.ANY)] * 2 + specs,
            out_specs=held(),
            scratch_shapes=[
                pltpu.VMEM(cotangent.shape, cotangent.dtype),
                pltpu.VMEM((shape.per_part,) + up.shape[1:], up.dtype),
                pltpu.SemaphoreType.DMA((1 + shape.per_part,)),
            ],
        ),
        out_shape=pltpu.VMEM((shape.per_part, up.shape[1], BLK), jnp.float32),
        compiler_params=SMALL,
        cost_estimate=BRIEF,
        name="backward",
    )(index, in_hbm(cotangent), in_hbm(up), *extra)


def merge_kernel(keep_ref, arrived_ref, back_ref, *refs):
    out_ref = refs[-1]
    total = keep_ref[0] + arrived_ref[0]
    for ref in refs[:-1][: keep_ref.shape[0] - 1]:
        total = total + ref[...]
    out_ref[0] = total
    out_ref[1] = back_ref[...]


def merge(keep, arrived, back, others, waits):
    specs, extra = after(waits)
    operands = (keep, arrived, back, *others)
    out = (2,) + back.shape
    return pl.pallas_call(
        merge_kernel,
        grid=(1,),
        in_specs=[whole(o.shape) for o in operands] + specs,
        out_specs=whole(out),
        out_shape=shape_of(out, jnp.float32),
        compiler_params=SMALL,
        cost_estimate=BRIEF,
        name="merge",
    )(*operands, *extra)


def pieces_kernel(index_of, count, index_ref, cot_ref, sum_ref, *refs):
    more_refs, (low_ref, back_ref, piece_ref) = refs[:count], refs[-3:]
    index = index_of(index_ref)
    level = [sum_ref[...]] + [ref[...] for ref in more_refs]
    while len(level) > 1:
        level = [level[j] + level[j + 1] for j in range(0, len(level), 2)]
    for i in range(index.per_part):
        live = index.live_rows(index.block(0, 0, i))
        keep = lax.broadcasted_iota(jnp.int32, low_ref.shape[1:], 1) < live
        lowered = jnp.where(keep, level[0][0, i], 0.0).astype(low_ref.dtype)
        low_ref[i] = lowered
        back_ref[i] = jnp.where(keep, level[0][1, i], 0.0).astype(back_ref.dtype)
        piece_ref[i] = jnp.dot(
            lowered, cot_ref[i * BLK : (i + 1) * BLK], preferred_element_type=jnp.float32
        ).astype(piece_ref.dtype)


def make_pieces(index_of, index, shape, total, more, cotangent, waits):
    _, per_part, rank, _ = total.shape
    width = cotangent.shape[1]
    outs = [(per_part, rank, BLK), (per_part, rank, BLK), (per_part, rank, width)]
    operands = (cotangent, total, *more)
    specs, extra = after(waits)
    return pl.pallas_call(
        functools.partial(pieces_kernel, index_of, len(more)),
        grid_spec=pltpu.PrefetchScalarGridSpec(
            num_scalar_prefetch=1,
            grid=(1,),
            in_specs=[whole(o.shape) for o in operands] + specs,
            out_specs=[whole(o) for o in outs],
        ),
        out_shape=[shape_of(o, jnp.bfloat16) for o in outs],
        compiler_params=SMALL,
        cost_estimate=BRIEF,
        name="pieces",
    )(index, *operands, *extra)


def down_gradient_kernel(index_of, index_ref, tokens_ref, *refs):
    back_refs, out_ref = refs[:-1], refs[-1]
    index = index_of(index_ref)
    out_ref[...] = jnp.zeros_like(out_ref)
    for core_bit in range(CORES):
        for chip_bits in range(index.chips):
            for i in range(index.per_part):
                block = index.block(core_bit, chip_bits, i)
                back_ref = back_refs[core_bit * index.chips + chip_bits]

                @pl.when(index.owner(block) == index.place)
                def _(block=block, back_ref=back_ref, i=i):
                    at = pl.multiple_of(index.slot(block) * BLK, BLK)
                    out_ref[0] += adapter_scale * jnp.dot(
                        back_ref[i],
                        tokens_ref[pl.ds(at, BLK)],
                        preferred_element_type=jnp.float32,
                    )


def down_gradient(index_of, index, tokens, backs):
    out = (1, backs[0].shape[1], tokens.shape[1])
    operands = (in_vmem(tokens), *backs)
    return pl.pallas_call(
        functools.partial(down_gradient_kernel, index_of),
        grid_spec=pltpu.PrefetchScalarGridSpec(
            num_scalar_prefetch=1,
            grid=(1,),
            in_specs=[held()] + [whole(o.shape) for o in backs],
            out_specs=whole(out),
        ),
        out_shape=shape_of(out, jnp.float32),
        compiler_params=SMALL,
        cost_estimate=BRIEF,
        name="down_gradient",
    )(index, *operands)


def up_gradient_kernel(index_of, index_ref, *refs):
    piece_refs, out_ref = refs[:-1], refs[-1]
    index = index_of(index_ref)

    def of_device(core_bit, chip_bits, adapter):
        total = None
        for i in range(index.per_part):
            mine = index.owner(index.block(core_bit, chip_bits, i)) == adapter
            piece = piece_refs[core_bit * index.chips + chip_bits][i].astype(jnp.float32)
            term = jnp.where(mine, piece, 0.0)
            total = term if total is None else total + term
        return total

    for adapter in range(index.adapters):
        level = [
            of_device(0, j, adapter) + of_device(1, j, adapter) for j in range(index.chips)
        ]
        while len(level) > 1:
            level = [level[j] + level[j + 1] for j in range(0, len(level), 2)]
        out_ref[adapter] = adapter_scale * level[0]


def up_gradient(index_of, index, adapter_count, pieces):
    per_part, rank, width = pieces[0].shape
    tile = 1024
    out = (adapter_count, rank, width)
    return pl.pallas_call(
        functools.partial(up_gradient_kernel, index_of),
        grid_spec=pltpu.PrefetchScalarGridSpec(
            num_scalar_prefetch=1,
            grid=(width // tile,),
            in_specs=[pl.BlockSpec((per_part, rank, tile), lambda n, _: (0, 0, n))] * len(pieces),
            out_specs=pl.BlockSpec((adapter_count, rank, tile), lambda n, _: (0, 0, n)),
        ),
        out_shape=shape_of(out, jnp.float32),
        compiler_params=SMALL,
        cost_estimate=BRIEF,
        name="up_gradient",
    )(index, *pieces)


def finish_kernel(index_of, index_ref, low_ref, *refs):
    index = index_of(index_ref)
    up_refs, sum_refs, out_ref = refs[: index.per_part], refs[index.per_part : -1], refs[-1]
    per_chunk = len(sum_refs) // len(CHUNK_ROWS)
    for i in range(index.per_part):
        block = index.block(0, 0, i)
        live = index.live_rows(block)
        side = lax.dot_general(
            low_ref[i],
            up_refs[i][0],
            (((0,), (0,)), ((), ())),
            preferred_element_type=jnp.float32,
        )
        start = 0
        for c, count in enumerate(CHUNK_ROWS):
            total = adapter_scale * side[start : start + count]
            for ref in sum_refs[c * per_chunk : (c + 1) * per_chunk]:
                total = total + ref[i * count : (i + 1) * count].astype(jnp.float32)
            keep = start + lax.broadcasted_iota(jnp.int32, total.shape, 0) < live
            at = i * BLK + start
            out_ref[at : at + count] = jnp.where(keep, total, 0.0).astype(out_ref.dtype)
            start += count


def finish(index_of, index, lowered, up, sums, part, projected, far):
    per_part = lowered.shape[0]
    _, rank, width = up.shape
    tile = min(1024, width // PARTS)
    tiles = width // PARTS // tile
    first = part * tiles
    out = (per_part * BLK, width)

    def factor(i):
        def at(n, index_ref):
            index = index_of(index_ref)
            return (index.owner(index.block(0, 0, i)), 0, first + n)

        return pl.BlockSpec((1, rank, tile), at)

    flat = [term for chunk in sums for term in chunk]
    specs = [
        pl.BlockSpec((per_part * count, tile), lambda n, _: (0, n))
        for chunk, count in zip(sums, CHUNK_ROWS)
        for _ in chunk
    ]
    operands = [index, lowered, *[up] * per_part, *flat]
    more, extra = after((), far)
    aliases = {}
    if projected is not None:
        aliases = {len(operands): 0}
        more, extra = [pl.BlockSpec(memory_space=pl.ANY)] + more, [projected] + extra

    def kernel(*refs):
        finish_kernel(index_of, *refs[: len(operands)], refs[-1])

    return pl.pallas_call(
        kernel,
        grid_spec=pltpu.PrefetchScalarGridSpec(
            num_scalar_prefetch=1,
            grid=(tiles,),
            in_specs=[whole(lowered.shape)] + [factor(i) for i in range(per_part)] + specs + more,
            out_specs=pl.BlockSpec((out[0], tile), lambda n, _: (0, first + n)),
        ),
        out_shape=shape_of(out, jnp.bfloat16),
        input_output_aliases=aliases,
        compiler_params=SMALL,
        cost_estimate=BRIEF,
        name="finish",
    )(*operands, *extra)


def per_device(
    tokens,
    cotangent,
    frozen_up_weight,
    adapter_down_factor,
    adapter_up_factor,
    tokens_per_adapter,
    adapter_of_block,
    slot_of_block,
):
    owners = lax.axis_size("dp")
    parts = lax.axis_size("tensor")
    chips = parts // CORES
    block_count = adapter_of_block.shape[0]
    adapter_count = adapter_up_factor.shape[0]
    width_dev = tokens.shape[1]
    index_of = functools.partial(
        Index, block_count=block_count, adapter_count=adapter_count, parts=parts
    )
    shape = index_of(None)
    index = Index.pack(adapter_of_block, slot_of_block, tokens_per_adapter)

    def to_other_core(value):
        return lax.ppermute(value, "tensor", [(i, i ^ 1) for i in range(parts)])

    def to_chip(value, k):
        return lax.ppermute(value, "tensor", [(i, i ^ (k * CORES)) for i in range(parts)])

    def across_dp(value, k):
        return lax.ppermute(value, "dp", [(i, i ^ k) for i in range(owners)])

    def same_core(value):
        return [value] + [to_chip(value, k) for k in range(1, chips)]

    def with_other_core(values):
        return values + [to_other_core(v) for v in values]

    def small_products(waits):
        down = jnp.swapaxes(adapter_down_factor, 1, 2)
        rank = adapter_up_factor.shape[1]
        send, keep = narrow(index_of, index, shape, tokens, down, rank, waits)
        back = backward(index_of, index, shape, cotangent, adapter_up_factor, [send])
        return send, keep, back

    def over_parts(send, keep):
        arrived = to_other_core(send)
        return arrived, [to_chip(keep[k] + arrived[k], k) for k in range(1, chips)]

    def over_dp(total):
        k = owners // 2
        while k > 1:
            total = total + across_dp(total, k)
            k //= 2
        return total, [across_dp(total, 1)]

    if owners == 4 and block_count == 4:
        relay = Relay(index_of, index, tokens)
        sent = relay.first()
        send, keep, back = small_products([sent])
        arrived, others = over_parts(send, keep)
        total, more = over_dp(merge(keep, arrived, back, others, []))
        relay.second([total])
        lowered, back_rows, pieces = make_pieces(
            index_of, index, shape, total, more, cotangent, []
        )
        relay.settle(more)
        weight = load_weight(frozen_up_weight, relay.arrived[-1][1:3])
        pieces = with_other_core(same_core(pieces))
        back_rows = with_other_core(same_core(back_rows))
        ahead = [v for chunk in relay.arrived[1:] for v in chunk[3:5]]
        ahead.append(weight)
        chunks = [lambda waits: relay.rows(0, ahead)]
        chunks += [functools.partial(relay.rows, c) for c in range(1, len(CHUNK_ROWS))]
    else:
        weight = load_weight(frozen_up_weight, [])
        send, keep, back = small_products([])
        arrived, others = over_parts(send, keep)
        total, more = over_dp(merge(keep, arrived, back, others, []))
        lowered, back_rows, pieces = make_pieces(
            index_of, index, shape, total, more, cotangent, []
        )
        pieces = with_other_core(same_core(pieces))
        back_rows = with_other_core(same_core(back_rows))
        every_slot = lax.all_gather(
            tokens.reshape(CAP, BLK, width_dev), "dp", axis=0, tiled=True
        )
        part = lax.axis_index("tensor")
        devices = jnp.arange(parts, dtype=jnp.int32)
        order = (devices // chips ^ 1) + (devices % chips) * CORES ^ part
        blocks = (order[:, None] * shape.per_part + jnp.arange(shape.per_part)).reshape(-1)
        picked = every_slot[adapter_of_block[blocks] * CAP + slot_of_block[blocks]]
        starts = [sum(CHUNK_ROWS[:c]) for c in range(len(CHUNK_ROWS))]
        chunks = [
            lambda waits, s=s, count=count: picked[:, s : s + count].reshape(-1, width_dev)
            for s, count in zip(starts, CHUNK_ROWS)
        ]
    def summed(rows, part, waits):
        each = rows.shape[0] // parts
        send_own, send, own, other = split_product(shape, rows, weight, part, PARTS, waits)
        outgoing = (other + to_other_core(send).astype(jnp.float32)).astype(jnp.bfloat16)
        across = [to_chip(outgoing[(k - 1) * each : k * each], k) for k in range(1, chips)]
        return [own, to_other_core(send_own)] + across, outgoing

    sums, ready = [], ()
    waits = [pieces[1:chips], ()]
    for chunk in chunks:
        rows = chunk(ready)
        done = [summed(rows, part, waits[part]) for part in range(PARTS)]
        sums.append([terms for terms, _ in done])
        ready = [done[0][1]]
        waits = [
            [*sums[-1][0][2:], *back_rows[1:chips]],
            [*back_rows[chips:], *pieces[chips:]],
        ]
    up_grad = up_gradient(index_of, index, adapter_count, pieces)
    down_grad = down_gradient(index_of, index, tokens, back_rows)
    projected = None
    for part in range(PARTS):
        projected = finish(
            index_of,
            index,
            lowered,
            adapter_up_factor,
            [done[part] for done in sums],
            part,
            projected,
            [] if projected is not None else [up_grad, down_grad],
        )
    return (projected, jnp.swapaxes(down_grad, 1, 2), up_grad)


def solution(mesh):
    return jax.shard_map(
        per_device,
        mesh=mesh,
        in_specs=(
            P(("groups", "dp"), "tensor"),
            P(("groups", "tensor"), "dp"),
            P("tensor", "dp"),
            P(("groups", "dp"), "tensor", None),
            P("groups", None, "dp"),
            P("groups"),
            P("groups"),
            P("groups"),
        ),
        out_specs=(
            P(("groups", "tensor"), "dp"),
            P(("groups", "dp"), "tensor", None),
            P("groups", None, "dp"),
        ),
        check_vma=False,
    )
```

```python
import functools

import jax
import jax.numpy as jnp
from jax import lax
from jax.experimental import pallas as pl
from jax.experimental.pallas import tpu as pltpu
from jax.sharding import PartitionSpec as P

BLK = 128
CAP = 3
CORES = 2
CHUNK_ROWS = (64, 64)
PARTS = 2
SMALL = pltpu.CompilerParams(vmem_limit_bytes=12 * 2**20)

adapter_scale = 0.5

LAST = (((1,), (1,)), ((), ()))


class Index:
    def __init__(self, ref, block_count, adapter_count, parts):
        self.ref = ref
        self.blocks, self.adapters, self.parts = block_count, adapter_count, parts
        self.chips = parts // CORES
        self.per_part = block_count // parts

    @staticmethod
    def pack(adapter_of_block, slot_of_block, tokens_per_adapter):
        place = jnp.stack([lax.axis_index("dp"), lax.axis_index("tensor")]).astype(jnp.int32)
        return jnp.concatenate([adapter_of_block, slot_of_block, tokens_per_adapter, place])

    def owner(self, block):
        return self.ref[block]

    def slot(self, block):
        return self.ref[self.blocks + block]

    def tokens(self, adapter):
        return self.ref[2 * self.blocks + adapter]

    @property
    def place(self):
        return self.ref[2 * self.blocks + self.adapters]

    @property
    def part(self):
        return self.ref[2 * self.blocks + self.adapters + 1]

    def block(self, core_bit, chip_bits, i):
        return (self.part ^ (chip_bits * CORES + core_bit)) * self.per_part + i

    def position(self, block):
        bits = (block // self.per_part) ^ self.part
        half = (1 - bits % CORES) * self.chips + bits // CORES
        return half * self.per_part + block % self.per_part

    def live_rows(self, block):
        adapter = self.owner(block)
        first = jnp.int32(0)
        for a in range(self.adapters):
            count = (self.tokens(a) + BLK - 1) // BLK
            first = first + jnp.where(a < adapter, count, 0)
        return self.tokens(adapter) - (block - first) * BLK


def in_vmem(value):
    return pltpu.with_memory_space_constraint(value, pltpu.VMEM)


def in_hbm(value):
    return pltpu.with_memory_space_constraint(value, pltpu.HBM)


def held():
    return pl.BlockSpec(memory_space=pltpu.VMEM)


def whole(shape):
    return pl.BlockSpec(shape, lambda *_: (0,) * len(shape))


def shape_of(shape, dtype):
    return jax.ShapeDtypeStruct(shape, dtype)


BRIEF = pl.CostEstimate(flops=1, bytes_accessed=1, transcendentals=0)


def own_rows(index, block, tokens_ref, out_ref, start=0):
    at = pl.multiple_of(index.slot(block) * BLK + start, 16)
    out_ref[...] = tokens_ref[pl.ds(at, out_ref.shape[0])]


def first_hop_kernel(index_of, index_ref, tokens_ref, *refs):
    a_ref, b_ref, sems = refs[-3:]
    index = index_of(index_ref)
    copies = [
        pltpu.make_async_copy(
            tokens_ref.at[pl.ds(pl.multiple_of(index.slot(block) * BLK, BLK), BLK)],
            out_ref,
            sems.at[i],
        )
        for i, (block, out_ref) in enumerate(
            ((jnp.where(index.place == 0, 2, 1), a_ref), (0, b_ref))
        )
    ]
    for copy in copies:
        copy.start()
    for copy in copies:
        copy.wait()


def second_hop_kernel(index_of, index_ref, tokens_ref, a_ref, b_ref, *refs):
    x_ref, y_ref = refs[-2:]
    index = index_of(index_ref)
    place = index.place
    outer = jnp.where(place == 0, 1, jnp.where(place == 1, 0, 2))
    middle = jnp.where(place == 1, 2, 1)
    own_rows(index, outer, tokens_ref, x_ref)
    own_rows(index, middle, tokens_ref, y_ref)

    @pl.when((place == 1) & (index.owner(0) != 1))
    def _():
        x_ref[...] = b_ref[...]

    @pl.when(((place == 1) | (place == 2)) & (index.owner(middle) != place))
    def _():
        y_ref[...] = a_ref[...]


def settle_kernel(index_of, index_ref, tokens_ref, x_ref, y_ref, *refs):
    out_refs = refs[-len(CHUNK_ROWS) :]
    index = index_of(index_ref)
    place = index.place
    owner = index.owner(place)
    mine = owner == place
    edge = (place == 0) | ((place == 1) & (owner == 0)) | ((place == 2) & (owner == 3))
    start = 0
    for out_ref in out_refs:
        rows = slice(start, start + out_ref.shape[0])
        own_rows(index, place, tokens_ref, out_ref, start)

        @pl.when(jnp.logical_not(mine) & edge)
        def _(out_ref=out_ref, rows=rows):
            out_ref[...] = x_ref[rows]

        @pl.when(jnp.logical_not(mine | edge))
        def _(out_ref=out_ref, rows=rows):
            out_ref[...] = y_ref[rows]

        start += out_ref.shape[0]


def collect_kernel(index_of, count, index_ref, home_ref, outer_ref, *refs):
    inner_refs, outer_refs, out_ref = refs[:2], refs[2:4], refs[-1]
    index = index_of(index_ref)
    place = index.place

    def put(block, ref):
        at = pl.multiple_of(index.position(block) * count, 16)
        out_ref[pl.ds(at, count)] = ref[...]

    put(place, home_ref)
    put(place ^ 1, outer_ref)
    middle = (place == 1) | (place == 2)

    @pl.when(middle)
    def _():
        put(3 - place, inner_refs[0])
        put(place ^ 2, inner_refs[1])

    @pl.when(jnp.logical_not(middle))
    def _():
        put(place ^ 2, outer_refs[0])
        put(3 - place, outer_refs[1])


def after(values, far=()):
    specs = [
        pl.BlockSpec((1,) * (v.ndim - 2) + (16, 128), lambda *_, n=v.ndim: (0,) * n) for v in values
    ] + [pl.BlockSpec(memory_space=pl.ANY)] * len(far)
    return specs, [*values, *(in_hbm(v) for v in far)]


def hop_call(kernel, index, tokens, heights, received, waits, name):
    specs, extra = after(waits)
    width = tokens.shape[1]
    first = not received
    return pl.pallas_call(
        kernel,
        grid_spec=pltpu.PrefetchScalarGridSpec(
            num_scalar_prefetch=1,
            grid=(1,),
            in_specs=[pl.BlockSpec(memory_space=pl.ANY) if first else held()]
            + [held()] * len(received)
            + specs,
            out_specs=[held()] * len(heights),
            scratch_shapes=[pltpu.SemaphoreType.DMA((len(heights),))] * first,
        ),
        out_shape=[pltpu.VMEM((height, width), tokens.dtype) for height in heights],
        compiler_params=SMALL,
        cost_estimate=BRIEF,
        name=name,
    )(index, (in_hbm if first else in_vmem)(tokens), *[in_vmem(r) for r in received], *extra)


class Relay:
    def __init__(self, index_of, index, tokens):
        self.index_of, self.index, self.tokens = index_of, index, tokens

    def call(self, kernel, heights, received, waits, name):
        kernel = functools.partial(kernel, self.index_of)
        return hop_call(kernel, self.index, self.tokens, heights, received, waits, name)

    def first(self, waits=()):
        inward, left = self.call(first_hop_kernel, (BLK, BLK), (), waits, "first_hop")
        self.received = (
            lax.ppermute(inward, "dp", [(3, 2), (0, 1)]),
            lax.ppermute(left, "dp", [(2, 1)]),
        )
        return inward

    def second(self, waits=()):
        outer, middle = self.call(
            second_hop_kernel, (BLK, BLK), self.received, waits, "second_hop"
        )
        self.received = (
            lax.ppermute(outer, "dp", [(1, 0), (0, 1), (3, 2)]),
            lax.ppermute(middle, "dp", [(2, 1), (1, 2)]),
        )
        return outer

    def settle(self, waits=()):
        homes = self.call(settle_kernel, CHUNK_ROWS, self.received, waits, "settle")
        self.arrived = [self.spread(home) for home in homes]

    def spread(self, home):
        outer = lax.ppermute(home, "dp", [(0, 1), (1, 0), (2, 3), (3, 2)])
        inner = lax.ppermute(home, "dp", [(1, 2), (2, 1)])
        outer_2 = lax.ppermute(inner, "dp", [(1, 0), (2, 3)])
        inner_2 = lax.ppermute(outer, "dp", [(1, 2), (2, 1)])
        outer_3 = lax.ppermute(inner_2, "dp", [(1, 0), (2, 3)])
        return home, outer, inner, inner_2, outer_2, outer_3

    def rows(self, chunk, waits=(), far=()):
        arrived = self.arrived[chunk]
        count, width = arrived[0].shape
        specs, extra = after(waits, far)
        return pl.pallas_call(
            functools.partial(collect_kernel, self.index_of, count),
            grid_spec=pltpu.PrefetchScalarGridSpec(
                num_scalar_prefetch=1,
                grid=(1,),
                in_specs=[held()] * len(arrived) + specs,
                out_specs=held(),
            ),
            out_shape=pltpu.VMEM((4 * count, width), self.tokens.dtype),
            compiler_params=SMALL,
            cost_estimate=BRIEF,
            name="collect",
        )(self.index, *[in_vmem(a) for a in arrived], *extra)


def load_weight_kernel(w_ref, *refs):
    out_ref, sems = refs[-2:]
    streams = sems.shape[0]
    depth = w_ref.shape[0] // streams
    copies = [
        pltpu.make_async_copy(
            w_ref.at[pl.ds(i * depth, depth)], out_ref.at[pl.ds(i * depth, depth)], sems.at[i]
        )
        for i in range(streams)
    ]
    for copy in copies:
        copy.start()
    for copy in copies:
        copy.wait()


def load_weight(weight, waits):
    specs, extra = after(waits)
    return pl.pallas_call(
        load_weight_kernel,
        grid=(1,),
        in_specs=[pl.BlockSpec(memory_space=pl.ANY)] + specs,
        out_specs=pl.BlockSpec(memory_space=pl.ANY),
        out_shape=pltpu.VMEM(weight.shape, weight.dtype),
        scratch_shapes=[pltpu.SemaphoreType.DMA((4,))],
        compiler_params=SMALL,
        cost_estimate=BRIEF,
        name="load_weight",
    )(in_hbm(weight), *extra)


def split_product_kernel(each, half, first, tile, rows_ref, w_ref, *refs):
    send_own_ref, send_ref, own_ref, other_ref = refs[-4:]
    for n in range(own_ref.shape[1] // tile):
        total = jnp.dot(
            rows_ref[...],
            w_ref[:, first + n * tile : first + (n + 1) * tile],
            preferred_element_type=jnp.float32,
        )
        columns = slice(n * tile, (n + 1) * tile)
        send_own_ref[:, columns] = total[:each].astype(send_own_ref.dtype)
        send_ref[:, columns] = total[each:half].astype(send_ref.dtype)
        own_ref[:, columns] = total[half : half + each]
        other_ref[:, columns] = total[half + each :]


def split_product(shape, rows, weight, part, part_count, waits):
    half = rows.shape[0] // 2
    each = half // shape.chips
    width = weight.shape[1] // part_count
    specs, extra = after(waits)
    return pl.pallas_call(
        functools.partial(split_product_kernel, each, half, part * width, min(512, width)),
        grid=(1,),
        in_specs=[held(), held()] + specs,
        out_specs=[held()] * 4,
        out_shape=[
            pltpu.VMEM((each, width), jnp.bfloat16),
            pltpu.VMEM((half - each, width), jnp.bfloat16),
            pltpu.VMEM((each, width), jnp.float32),
            pltpu.VMEM((half - each, width), jnp.float32),
        ],
        compiler_params=SMALL,
        cost_estimate=BRIEF,
        name="split_product",
    )(in_vmem(rows), in_vmem(weight), *extra)


def narrow_kernel(index_of, index_ref, tokens_ref, down_ref, cot_ref, up_ref, *refs):
    send_ref, keep_ref, back_ref, low, tokens, down, cot, up, sems = refs[-9:]
    index = index_of(index_ref)
    pairs = [(tokens_ref, tokens), (down_ref, down), (cot_ref, cot)]
    for i in range(index.per_part):
        adapter = index.owner(index.block(0, 0, i))
        pairs.append((up_ref.at[adapter], up.at[i]))
    copies = [
        pltpu.make_async_copy(source, target, sems.at[j])
        for j, (source, target) in enumerate(pairs)
    ]
    for copy in copies:
        copy.start()
    for copy in copies[:2]:
        copy.wait()
    for m in range(CAP):
        low[m] = lax.dot_general(
            down[0],
            tokens[m * BLK : (m + 1) * BLK],
            LAST,
            preferred_element_type=jnp.float32,
        )
    for core_bit, out_ref in ((1, send_ref), (0, keep_ref)):
        for chip_bits in range(index.chips):
            for i in range(index.per_part):
                block = index.block(core_bit, chip_bits, i)
                mine = index.owner(block) == index.place
                out_ref[chip_bits, i] = jnp.where(mine, low[index.slot(block)], 0.0)
    for copy in copies[2:]:
        copy.wait()
    for i in range(index.per_part):
        back_ref[i] = lax.dot_general(
            up[i], cot[i * BLK : (i + 1) * BLK], LAST, preferred_element_type=jnp.float32
        )


def narrow(index_of, index, shape, tokens, down, cotangent, up, waits):
    rank = up.shape[1]
    one = (shape.per_part, rank, BLK)
    outs = [(shape.chips,) + one, (shape.chips,) + one, one]
    operands = (tokens, down, cotangent, up)
    specs, extra = after(waits)
    return pl.pallas_call(
        functools.partial(narrow_kernel, index_of),
        grid_spec=pltpu.PrefetchScalarGridSpec(
            num_scalar_prefetch=1,
            grid=(1,),
            in_specs=[pl.BlockSpec(memory_space=pl.ANY)] * len(operands) + specs,
            out_specs=[held()] * len(outs),
            scratch_shapes=[
                pltpu.VMEM((CAP, rank, BLK), jnp.float32),
                pltpu.VMEM(tokens.shape, tokens.dtype),
                pltpu.VMEM(down.shape, down.dtype),
                pltpu.VMEM(cotangent.shape, cotangent.dtype),
                pltpu.VMEM((shape.per_part,) + up.shape[1:], up.dtype),
                pltpu.SemaphoreType.DMA((3 + shape.per_part,)),
            ],
        ),
        out_shape=[pltpu.VMEM(o, jnp.float32) for o in outs],
        compiler_params=SMALL,
        cost_estimate=BRIEF,
        name="narrow",
    )(index, *[in_hbm(o) for o in operands], *extra)


def merge_kernel(keep_ref, arrived_ref, back_ref, *refs):
    out_ref = refs[-1]
    total = keep_ref[0] + arrived_ref[0]
    for ref in refs[:-1][: keep_ref.shape[0] - 1]:
        total = total + ref[...]
    out_ref[0] = total
    out_ref[1] = back_ref[...]


def merge(keep, arrived, back, others, waits):
    specs, extra = after(waits)
    operands = (keep, arrived, back, *others)
    out = (2,) + back.shape
    return pl.pallas_call(
        merge_kernel,
        grid=(1,),
        in_specs=[whole(o.shape) for o in operands] + specs,
        out_specs=whole(out),
        out_shape=shape_of(out, jnp.float32),
        compiler_params=SMALL,
        cost_estimate=BRIEF,
        name="merge",
    )(*operands, *extra)


def pieces_kernel(index_of, count, index_ref, cot_ref, sum_ref, *refs):
    more_refs, (low_ref, back_ref, piece_ref) = refs[:count], refs[-3:]
    index = index_of(index_ref)
    level = [sum_ref[...]] + [ref[...] for ref in more_refs]
    while len(level) > 1:
        level = [level[j] + level[j + 1] for j in range(0, len(level), 2)]
    for i in range(index.per_part):
        live = index.live_rows(index.block(0, 0, i))
        keep = lax.broadcasted_iota(jnp.int32, low_ref.shape[1:], 1) < live
        lowered = jnp.where(keep, level[0][0, i], 0.0).astype(low_ref.dtype)
        low_ref[i] = lowered
        back_ref[i] = jnp.where(keep, level[0][1, i], 0.0).astype(back_ref.dtype)
        piece_ref[i] = jnp.dot(
            lowered, cot_ref[i * BLK : (i + 1) * BLK], preferred_element_type=jnp.float32
        ).astype(piece_ref.dtype)


def make_pieces(index_of, index, shape, total, more, cotangent, waits):
    _, per_part, rank, _ = total.shape
    width = cotangent.shape[1]
    outs = [(per_part, rank, BLK), (per_part, rank, BLK), (per_part, rank, width)]
    operands = (cotangent, total, *more)
    specs, extra = after(waits)
    return pl.pallas_call(
        functools.partial(pieces_kernel, index_of, len(more)),
        grid_spec=pltpu.PrefetchScalarGridSpec(
            num_scalar_prefetch=1,
            grid=(1,),
            in_specs=[whole(o.shape) for o in operands] + specs,
            out_specs=[whole(o) for o in outs],
        ),
        out_shape=[shape_of(o, jnp.bfloat16) for o in outs],
        compiler_params=SMALL,
        cost_estimate=BRIEF,
        name="pieces",
    )(index, *operands, *extra)


def down_gradient_kernel(index_of, index_ref, tokens_ref, *refs):
    back_refs, out_ref = refs[:-1], refs[-1]
    index = index_of(index_ref)
    out_ref[...] = jnp.zeros_like(out_ref)
    for core_bit in range(CORES):
        for chip_bits in range(index.chips):
            for i in range(index.per_part):
                block = index.block(core_bit, chip_bits, i)
                back_ref = back_refs[core_bit * index.chips + chip_bits]

                @pl.when(index.owner(block) == index.place)
                def _(block=block, back_ref=back_ref, i=i):
                    at = pl.multiple_of(index.slot(block) * BLK, BLK)
                    out_ref[0] += adapter_scale * jnp.dot(
                        back_ref[i],
                        tokens_ref[pl.ds(at, BLK)],
                        preferred_element_type=jnp.float32,
                    )


def down_gradient(index_of, index, tokens, backs):
    out = (1, backs[0].shape[1], tokens.shape[1])
    operands = (in_vmem(tokens), *backs)
    return pl.pallas_call(
        functools.partial(down_gradient_kernel, index_of),
        grid_spec=pltpu.PrefetchScalarGridSpec(
            num_scalar_prefetch=1,
            grid=(1,),
            in_specs=[held()] + [whole(o.shape) for o in backs],
            out_specs=whole(out),
        ),
        out_shape=shape_of(out, jnp.float32),
        compiler_params=SMALL,
        cost_estimate=BRIEF,
        name="down_gradient",
    )(index, *operands)


def up_gradient_kernel(index_of, index_ref, *refs):
    piece_refs, out_ref = refs[:-1], refs[-1]
    index = index_of(index_ref)

    def of_device(core_bit, chip_bits, adapter):
        total = None
        for i in range(index.per_part):
            mine = index.owner(index.block(core_bit, chip_bits, i)) == adapter
            piece = piece_refs[core_bit * index.chips + chip_bits][i].astype(jnp.float32)
            term = jnp.where(mine, piece, 0.0)
            total = term if total is None else total + term
        return total

    for adapter in range(index.adapters):
        level = [
            of_device(0, j, adapter) + of_device(1, j, adapter) for j in range(index.chips)
        ]
        while len(level) > 1:
            level = [level[j] + level[j + 1] for j in range(0, len(level), 2)]
        out_ref[adapter] = adapter_scale * level[0]


def up_gradient(index_of, index, adapter_count, pieces):
    per_part, rank, width = pieces[0].shape
    tile = 1024
    out = (adapter_count, rank, width)
    return pl.pallas_call(
        functools.partial(up_gradient_kernel, index_of),
        grid_spec=pltpu.PrefetchScalarGridSpec(
            num_scalar_prefetch=1,
            grid=(width // tile,),
            in_specs=[pl.BlockSpec((per_part, rank, tile), lambda n, _: (0, 0, n))] * len(pieces),
            out_specs=pl.BlockSpec((adapter_count, rank, tile), lambda n, _: (0, 0, n)),
        ),
        out_shape=shape_of(out, jnp.float32),
        compiler_params=SMALL,
        cost_estimate=BRIEF,
        name="up_gradient",
    )(index, *pieces)


def finish_kernel(index_of, index_ref, low_ref, *refs):
    index = index_of(index_ref)
    up_refs, sum_refs, out_ref = refs[: index.per_part], refs[index.per_part : -1], refs[-1]
    per_chunk = len(sum_refs) // len(CHUNK_ROWS)
    tile = out_ref.shape[1]
    columns = pl.ds(pl.multiple_of(pl.program_id(0) * tile, tile), tile)
    for i in range(index.per_part):
        block = index.block(0, 0, i)
        live = index.live_rows(block)
        side = lax.dot_general(
            low_ref[i],
            up_refs[i][0],
            (((0,), (0,)), ((), ())),
            preferred_element_type=jnp.float32,
        )
        start = 0
        for c, count in enumerate(CHUNK_ROWS):
            total = adapter_scale * side[start : start + count]
            for ref in sum_refs[c * per_chunk : (c + 1) * per_chunk]:
                total = total + ref[i * count : (i + 1) * count, columns].astype(jnp.float32)
            keep = start + lax.broadcasted_iota(jnp.int32, total.shape, 0) < live
            at = i * BLK + start
            out_ref[at : at + count] = jnp.where(keep, total, 0.0).astype(out_ref.dtype)
            start += count


def finish(index_of, index, lowered, up, sums, part, projected, far):
    per_part = lowered.shape[0]
    _, rank, width = up.shape
    tile = min(1024, width // PARTS)
    tiles = width // PARTS // tile
    first = part * tiles
    out = (per_part * BLK, width)

    def factor(i):
        def at(n, index_ref):
            index = index_of(index_ref)
            return (index.owner(index.block(0, 0, i)), 0, first + n)

        return pl.BlockSpec((1, rank, tile), at)

    flat = [term for chunk in sums for term in chunk]
    specs = [held()] * len(flat)
    operands = [index, lowered, *[up] * per_part, *[in_vmem(term) for term in flat]]
    more, extra = after((), far)
    aliases = {}
    if projected is not None:
        aliases = {len(operands): 0}
        more, extra = [pl.BlockSpec(memory_space=pl.ANY)] + more, [projected] + extra

    def kernel(*refs):
        finish_kernel(index_of, *refs[: len(operands)], refs[-1])

    return pl.pallas_call(
        kernel,
        grid_spec=pltpu.PrefetchScalarGridSpec(
            num_scalar_prefetch=1,
            grid=(tiles,),
            in_specs=[whole(lowered.shape)] + [factor(i) for i in range(per_part)] + specs + more,
            out_specs=pl.BlockSpec((out[0], tile), lambda n, _: (0, first + n)),
        ),
        out_shape=shape_of(out, jnp.bfloat16),
        input_output_aliases=aliases,
        compiler_params=SMALL,
        cost_estimate=BRIEF,
        name="finish",
    )(*operands, *extra)


def per_device(
    tokens,
    cotangent,
    frozen_up_weight,
    adapter_down_factor,
    adapter_up_factor,
    tokens_per_adapter,
    adapter_of_block,
    slot_of_block,
):
    owners = lax.axis_size("dp")
    parts = lax.axis_size("tensor")
    chips = parts // CORES
    block_count = adapter_of_block.shape[0]
    adapter_count = adapter_up_factor.shape[0]
    width_dev = tokens.shape[1]
    index_of = functools.partial(
        Index, block_count=block_count, adapter_count=adapter_count, parts=parts
    )
    shape = index_of(None)
    index = Index.pack(adapter_of_block, slot_of_block, tokens_per_adapter)

    def to_other_core(value):
        return lax.ppermute(value, "tensor", [(i, i ^ 1) for i in range(parts)])

    def to_chip(value, k):
        return lax.ppermute(value, "tensor", [(i, i ^ (k * CORES)) for i in range(parts)])

    def across_dp(value, k):
        return lax.ppermute(value, "dp", [(i, i ^ k) for i in range(owners)])

    def same_core(value):
        return [value] + [to_chip(value, k) for k in range(1, chips)]

    def with_other_core(values):
        return values + [to_other_core(v) for v in values]

    def small_products(waits):
        return narrow(
            index_of,
            index,
            shape,
            tokens,
            jnp.swapaxes(adapter_down_factor, 1, 2),
            cotangent,
            adapter_up_factor,
            waits,
        )

    def over_parts(send, keep):
        arrived = to_other_core(send)
        return arrived, [to_chip(keep[k] + arrived[k], k) for k in range(1, chips)]

    def over_dp(total):
        k = owners // 2
        while k > 1:
            total = total + across_dp(total, k)
            k //= 2
        return total, [across_dp(total, 1)]

    if owners == 4 and block_count == 4:
        relay = Relay(index_of, index, tokens)
        sent = relay.first()
        send, keep, back = small_products([sent])
        arrived, others = over_parts(send, keep)
        total, more = over_dp(merge(keep, arrived, back, others, []))
        relay.second([total])
        lowered, back_rows, pieces = make_pieces(
            index_of, index, shape, total, more, cotangent, []
        )
        relay.settle(more)
        weight = load_weight(frozen_up_weight, relay.arrived[-1][1:3])
        pieces = with_other_core(same_core(pieces))
        back_rows = with_other_core(same_core(back_rows))
        ahead = [v for chunk in relay.arrived[1:] for v in chunk[3:5]]
        ahead.append(weight)
        chunks = [lambda waits: relay.rows(0, ahead)]
        chunks += [functools.partial(relay.rows, c) for c in range(1, len(CHUNK_ROWS))]
    else:
        weight = load_weight(frozen_up_weight, [])
        send, keep, back = small_products([])
        arrived, others = over_parts(send, keep)
        total, more = over_dp(merge(keep, arrived, back, others, []))
        lowered, back_rows, pieces = make_pieces(
            index_of, index, shape, total, more, cotangent, []
        )
        pieces = with_other_core(same_core(pieces))
        back_rows = with_other_core(same_core(back_rows))
        every_slot = lax.all_gather(
            tokens.reshape(CAP, BLK, width_dev), "dp", axis=0, tiled=True
        )
        part = lax.axis_index("tensor")
        devices = jnp.arange(parts, dtype=jnp.int32)
        order = (devices // chips ^ 1) + (devices % chips) * CORES ^ part
        blocks = (order[:, None] * shape.per_part + jnp.arange(shape.per_part)).reshape(-1)
        picked = every_slot[adapter_of_block[blocks] * CAP + slot_of_block[blocks]]
        starts = [sum(CHUNK_ROWS[:c]) for c in range(len(CHUNK_ROWS))]
        chunks = [
            lambda waits, s=s, count=count: picked[:, s : s + count].reshape(-1, width_dev)
            for s, count in zip(starts, CHUNK_ROWS)
        ]
    def summed(rows, part, waits):
        each = rows.shape[0] // parts
        send_own, send, own, other = split_product(shape, rows, weight, part, PARTS, waits)
        outgoing = (other + to_other_core(send).astype(jnp.float32)).astype(jnp.bfloat16)
        across = [to_chip(outgoing[(k - 1) * each : k * each], k) for k in range(1, chips)]
        return [own, to_other_core(send_own)] + across, outgoing

    sums, ready = [], ()
    waits = [pieces[1:chips], ()]
    for chunk in chunks:
        rows = chunk(ready)
        done = [summed(rows, part, waits[part]) for part in range(PARTS)]
        sums.append([terms for terms, _ in done])
        ready = [done[0][1]]
        waits = [
            [*sums[-1][0][2:], *back_rows[1:chips]],
            [*back_rows[chips:], *pieces[chips:]],
        ]
    up_grad = up_gradient(index_of, index, adapter_count, pieces)
    down_grad = down_gradient(index_of, index, tokens, back_rows)
    projected = None
    for part in range(PARTS):
        projected = finish(
            index_of,
            index,
            lowered,
            adapter_up_factor,
            [done[part] for done in sums],
            part,
            projected,
            [] if projected is not None else [up_grad, down_grad],
        )
    return (projected, jnp.swapaxes(down_grad, 1, 2), up_grad)


def solution(mesh):
    return jax.shard_map(
        per_device,
        mesh=mesh,
        in_specs=(
            P(("groups", "dp"), "tensor"),
            P(("groups", "tensor"), "dp"),
            P("tensor", "dp"),
            P(("groups", "dp"), "tensor", None),
            P("groups", None, "dp"),
            P("groups"),
            P("groups"),
            P("groups"),
        ),
        out_specs=(
            P(("groups", "tensor"), "dp"),
            P(("groups", "dp"), "tensor", None),
            P("groups", None, "dp"),
        ),
        check_vma=False,
    )
```

```python
import functools

import jax
import jax.numpy as jnp
from jax import lax
from jax.experimental import pallas as pl
from jax.experimental.pallas import tpu as pltpu
from jax.sharding import PartitionSpec as P

BLK = 128
CAP = 3
CORES = 2
CHUNK_ROWS = (64, 64)
PARTS = 2
SMALL = pltpu.CompilerParams(vmem_limit_bytes=12 * 2**20)

adapter_scale = 0.5

LAST = (((1,), (1,)), ((), ()))


class Index:
    def __init__(self, ref, block_count, adapter_count, parts):
        self.ref = ref
        self.blocks, self.adapters, self.parts = block_count, adapter_count, parts
        self.chips = parts // CORES
        self.per_part = block_count // parts

    @staticmethod
    def pack(adapter_of_block, slot_of_block, tokens_per_adapter):
        place = jnp.stack([lax.axis_index("dp"), lax.axis_index("tensor")]).astype(jnp.int32)
        return jnp.concatenate([adapter_of_block, slot_of_block, tokens_per_adapter, place])

    def owner(self, block):
        return self.ref[block]

    def slot(self, block):
        return self.ref[self.blocks + block]

    def tokens(self, adapter):
        return self.ref[2 * self.blocks + adapter]

    @property
    def place(self):
        return self.ref[2 * self.blocks + self.adapters]

    @property
    def part(self):
        return self.ref[2 * self.blocks + self.adapters + 1]

    def block(self, core_bit, chip_bits, i):
        return (self.part ^ (chip_bits * CORES + core_bit)) * self.per_part + i

    def position(self, block):
        bits = (block // self.per_part) ^ self.part
        half = (1 - bits % CORES) * self.chips + bits // CORES
        return half * self.per_part + block % self.per_part

    def live_rows(self, block):
        adapter = self.owner(block)
        first = jnp.int32(0)
        for a in range(self.adapters):
            count = (self.tokens(a) + BLK - 1) // BLK
            first = first + jnp.where(a < adapter, count, 0)
        return self.tokens(adapter) - (block - first) * BLK


def in_vmem(value):
    return pltpu.with_memory_space_constraint(value, pltpu.VMEM)


def in_hbm(value):
    return pltpu.with_memory_space_constraint(value, pltpu.HBM)


def held():
    return pl.BlockSpec(memory_space=pltpu.VMEM)


def whole(shape):
    return pl.BlockSpec(shape, lambda *_: (0,) * len(shape))


def shape_of(shape, dtype):
    return jax.ShapeDtypeStruct(shape, dtype)


BRIEF = pl.CostEstimate(flops=1, bytes_accessed=1, transcendentals=0)


def own_rows(index, block, tokens_ref, out_ref, start=0):
    at = pl.multiple_of(index.slot(block) * BLK + start, 16)
    out_ref[...] = tokens_ref[pl.ds(at, out_ref.shape[0])]


def first_hop_kernel(index_of, index_ref, tokens_ref, *refs):
    a_ref, b_ref, sems = refs[-3:]
    index = index_of(index_ref)
    copies = [
        pltpu.make_async_copy(
            tokens_ref.at[pl.ds(pl.multiple_of(index.slot(block) * BLK, BLK), BLK)],
            out_ref,
            sems.at[i],
        )
        for i, (block, out_ref) in enumerate(
            ((jnp.where(index.place == 0, 2, 1), a_ref), (0, b_ref))
        )
    ]
    for copy in copies:
        copy.start()
    for copy in copies:
        copy.wait()


def second_hop_kernel(index_of, index_ref, tokens_ref, a_ref, b_ref, *refs):
    x_ref, y_ref = refs[-2:]
    index = index_of(index_ref)
    place = index.place
    outer = jnp.where(place == 0, 1, jnp.where(place == 1, 0, 2))
    middle = jnp.where(place == 1, 2, 1)
    own_rows(index, outer, tokens_ref, x_ref)
    own_rows(index, middle, tokens_ref, y_ref)

    @pl.when((place == 1) & (index.owner(0) != 1))
    def _():
        x_ref[...] = b_ref[...]

    @pl.when(((place == 1) | (place == 2)) & (index.owner(middle) != place))
    def _():
        y_ref[...] = a_ref[...]


def settle_kernel(index_of, index_ref, tokens_ref, x_ref, y_ref, *refs):
    out_refs = refs[-len(CHUNK_ROWS) :]
    index = index_of(index_ref)
    place = index.place
    owner = index.owner(place)
    mine = owner == place
    edge = (place == 0) | ((place == 1) & (owner == 0)) | ((place == 2) & (owner == 3))
    start = 0
    for out_ref in out_refs:
        rows = slice(start, start + out_ref.shape[0])
        own_rows(index, place, tokens_ref, out_ref, start)

        @pl.when(jnp.logical_not(mine) & edge)
        def _(out_ref=out_ref, rows=rows):
            out_ref[...] = x_ref[rows]

        @pl.when(jnp.logical_not(mine | edge))
        def _(out_ref=out_ref, rows=rows):
            out_ref[...] = y_ref[rows]

        start += out_ref.shape[0]


def collect_kernel(index_of, count, index_ref, home_ref, outer_ref, *refs):
    inner_refs, outer_refs, out_ref = refs[:2], refs[2:4], refs[-1]
    index = index_of(index_ref)
    place = index.place

    def put(block, ref):
        at = pl.multiple_of(index.position(block) * count, 16)
        out_ref[pl.ds(at, count)] = ref[...]

    put(place, home_ref)
    put(place ^ 1, outer_ref)
    middle = (place == 1) | (place == 2)

    @pl.when(middle)
    def _():
        put(3 - place, inner_refs[0])
        put(place ^ 2, inner_refs[1])

    @pl.when(jnp.logical_not(middle))
    def _():
        put(place ^ 2, outer_refs[0])
        put(3 - place, outer_refs[1])


def after(values, far=()):
    specs = [
        pl.BlockSpec((1,) * (v.ndim - 2) + (16, 128), lambda *_, n=v.ndim: (0,) * n) for v in values
    ] + [pl.BlockSpec(memory_space=pl.ANY)] * len(far)
    return specs, [*values, *(in_hbm(v) for v in far)]


def hop_call(kernel, index, tokens, heights, received, waits, name):
    specs, extra = after(waits)
    width = tokens.shape[1]
    first = not received
    return pl.pallas_call(
        kernel,
        grid_spec=pltpu.PrefetchScalarGridSpec(
            num_scalar_prefetch=1,
            grid=(1,),
            in_specs=[pl.BlockSpec(memory_space=pl.ANY) if first else held()]
            + [held()] * len(received)
            + specs,
            out_specs=[held()] * len(heights),
            scratch_shapes=[pltpu.SemaphoreType.DMA((len(heights),))] * first,
        ),
        out_shape=[pltpu.VMEM((height, width), tokens.dtype) for height in heights],
        compiler_params=SMALL,
        cost_estimate=BRIEF,
        name=name,
    )(index, (in_hbm if first else in_vmem)(tokens), *[in_vmem(r) for r in received], *extra)


class Relay:
    def __init__(self, index_of, index, tokens):
        self.index_of, self.index, self.tokens = index_of, index, tokens

    def call(self, kernel, heights, received, waits, name):
        kernel = functools.partial(kernel, self.index_of)
        return hop_call(kernel, self.index, self.tokens, heights, received, waits, name)

    def first(self, waits=()):
        inward, left = self.call(first_hop_kernel, (BLK, BLK), (), waits, "first_hop")
        self.received = (
            lax.ppermute(inward, "dp", [(3, 2), (0, 1)]),
            lax.ppermute(left, "dp", [(2, 1)]),
        )
        return inward

    def second(self, waits=()):
        outer, middle = self.call(
            second_hop_kernel, (BLK, BLK), self.received, waits, "second_hop"
        )
        self.received = (
            lax.ppermute(outer, "dp", [(1, 0), (0, 1), (3, 2)]),
            lax.ppermute(middle, "dp", [(2, 1), (1, 2)]),
        )
        return outer

    def settle(self, waits=()):
        homes = self.call(settle_kernel, CHUNK_ROWS, self.received, waits, "settle")
        self.arrived = [self.spread(home) for home in homes]

    def spread(self, home):
        outer = lax.ppermute(home, "dp", [(0, 1), (1, 0), (2, 3), (3, 2)])
        inner = lax.ppermute(home, "dp", [(1, 2), (2, 1)])
        outer_2 = lax.ppermute(inner, "dp", [(1, 0), (2, 3)])
        inner_2 = lax.ppermute(outer, "dp", [(1, 2), (2, 1)])
        outer_3 = lax.ppermute(inner_2, "dp", [(1, 0), (2, 3)])
        return home, outer, inner, inner_2, outer_2, outer_3

    def rows(self, chunk, waits=(), far=()):
        arrived = self.arrived[chunk]
        count, width = arrived[0].shape
        specs, extra = after(waits, far)
        return pl.pallas_call(
            functools.partial(collect_kernel, self.index_of, count),
            grid_spec=pltpu.PrefetchScalarGridSpec(
                num_scalar_prefetch=1,
                grid=(1,),
                in_specs=[held()] * len(arrived) + specs,
                out_specs=held(),
            ),
            out_shape=pltpu.VMEM((4 * count, width), self.tokens.dtype),
            compiler_params=SMALL,
            cost_estimate=BRIEF,
            name="collect",
        )(self.index, *[in_vmem(a) for a in arrived], *extra)


def load_weight_kernel(w_ref, *refs):
    out_ref, sems = refs[-2:]
    streams = sems.shape[0]
    depth = w_ref.shape[0] // streams
    copies = [
        pltpu.make_async_copy(
            w_ref.at[pl.ds(i * depth, depth)], out_ref.at[pl.ds(i * depth, depth)], sems.at[i]
        )
        for i in range(streams)
    ]
    for copy in copies:
        copy.start()
    for copy in copies:
        copy.wait()


def load_weight(weight, waits):
    specs, extra = after(waits)
    return pl.pallas_call(
        load_weight_kernel,
        grid=(1,),
        in_specs=[pl.BlockSpec(memory_space=pl.ANY)] + specs,
        out_specs=pl.BlockSpec(memory_space=pl.ANY),
        out_shape=pltpu.VMEM(weight.shape, weight.dtype),
        scratch_shapes=[pltpu.SemaphoreType.DMA((4,))],
        compiler_params=SMALL,
        cost_estimate=BRIEF,
        name="load_weight",
    )(in_hbm(weight), *extra)


def split_product_kernel(each, half, first, tile, rows_ref, w_ref, *refs):
    send_own_ref, send_ref, own_ref, other_ref = refs[-4:]
    for n in range(own_ref.shape[1] // tile):
        total = jnp.dot(
            rows_ref[...],
            w_ref[:, first + n * tile : first + (n + 1) * tile],
            preferred_element_type=jnp.float32,
        )
        columns = slice(n * tile, (n + 1) * tile)
        send_own_ref[:, columns] = total[:each].astype(send_own_ref.dtype)
        send_ref[:, columns] = total[each:half].astype(send_ref.dtype)
        own_ref[:, columns] = total[half : half + each]
        other_ref[:, columns] = total[half + each :]


def split_product(shape, rows, weight, part, part_count, waits):
    half = rows.shape[0] // 2
    each = half // shape.chips
    width = weight.shape[1] // part_count
    specs, extra = after(waits)
    return pl.pallas_call(
        functools.partial(split_product_kernel, each, half, part * width, min(512, width)),
        grid=(1,),
        in_specs=[held(), held()] + specs,
        out_specs=[held()] * 4,
        out_shape=[
            pltpu.VMEM((each, width), jnp.bfloat16),
            pltpu.VMEM((half - each, width), jnp.bfloat16),
            pltpu.VMEM((each, width), jnp.float32),
            pltpu.VMEM((half - each, width), jnp.float32),
        ],
        compiler_params=SMALL,
        cost_estimate=BRIEF,
        name="split_product",
    )(in_vmem(rows), in_vmem(weight), *extra)


def run_copies(pairs, sems):
    copies = [
        pltpu.make_async_copy(source, target, sems.at[j])
        for j, (source, target) in enumerate(pairs)
    ]
    for copy in copies:
        copy.start()
    for copy in copies:
        copy.wait()


def narrow_kernel(index_of, index_ref, tokens_ref, down_ref, *refs):
    send_ref, keep_ref, low, tokens, down, sems = refs[-6:]
    index = index_of(index_ref)
    run_copies([(tokens_ref, tokens), (down_ref, down)], sems)
    for m in range(CAP):
        low[m] = lax.dot_general(
            down[0],
            tokens[m * BLK : (m + 1) * BLK],
            LAST,
            preferred_element_type=jnp.float32,
        )
    for core_bit, out_ref in ((1, send_ref), (0, keep_ref)):
        for chip_bits in range(index.chips):
            for i in range(index.per_part):
                block = index.block(core_bit, chip_bits, i)
                mine = index.owner(block) == index.place
                out_ref[chip_bits, i] = jnp.where(mine, low[index.slot(block)], 0.0)


def narrow(index_of, index, shape, tokens, down, rank, waits):
    out = (shape.chips, shape.per_part, rank, BLK)
    specs, extra = after(waits)
    return pl.pallas_call(
        functools.partial(narrow_kernel, index_of),
        grid_spec=pltpu.PrefetchScalarGridSpec(
            num_scalar_prefetch=1,
            grid=(1,),
            in_specs=[pl.BlockSpec(memory_space=pl.ANY)] * 2 + specs,
            out_specs=[held()] * 2,
            scratch_shapes=[
                pltpu.VMEM((CAP, rank, BLK), jnp.float32),
                pltpu.VMEM(tokens.shape, tokens.dtype),
                pltpu.VMEM(down.shape, down.dtype),
                pltpu.SemaphoreType.DMA((2,)),
            ],
        ),
        out_shape=[pltpu.VMEM(out, jnp.float32)] * 2,
        compiler_params=SMALL,
        cost_estimate=BRIEF,
        name="narrow",
    )(index, in_hbm(tokens), in_hbm(down), *extra)


def backward_kernel(index_of, index_ref, cot_ref, up_ref, *refs):
    back_ref, cot, up, sems = refs[-4:]
    index = index_of(index_ref)
    pairs = [(cot_ref, cot)]
    for i in range(index.per_part):
        pairs.append((up_ref.at[index.owner(index.block(0, 0, i))], up.at[i]))
    run_copies(pairs, sems)
    for i in range(index.per_part):
        back_ref[i] = lax.dot_general(
            up[i], cot[i * BLK : (i + 1) * BLK], LAST, preferred_element_type=jnp.float32
        )


def backward(index_of, index, shape, cotangent, up, waits):
    specs, extra = after(waits)
    return pl.pallas_call(
        functools.partial(backward_kernel, index_of),
        grid_spec=pltpu.PrefetchScalarGridSpec(
            num_scalar_prefetch=1,
            grid=(1,),
            in_specs=[pl.BlockSpec(memory_space=pl.ANY)] * 2 + specs,
            out_specs=held(),
            scratch_shapes=[
                pltpu.VMEM(cotangent.shape, cotangent.dtype),
                pltpu.VMEM((shape.per_part,) + up.shape[1:], up.dtype),
                pltpu.SemaphoreType.DMA((1 + shape.per_part,)),
            ],
        ),
        out_shape=pltpu.VMEM((shape.per_part, up.shape[1], BLK), jnp.float32),
        compiler_params=SMALL,
        cost_estimate=BRIEF,
        name="backward",
    )(index, in_hbm(cotangent), in_hbm(up), *extra)


def merge_kernel(keep_ref, arrived_ref, back_ref, *refs):
    out_ref = refs[-1]
    total = keep_ref[0] + arrived_ref[0]
    for ref in refs[:-1][: keep_ref.shape[0] - 1]:
        total = total + ref[...]
    out_ref[0] = total
    out_ref[1] = back_ref[...]


def merge(keep, arrived, back, others, waits):
    specs, extra = after(waits)
    operands = (keep, arrived, back, *others)
    out = (2,) + back.shape
    return pl.pallas_call(
        merge_kernel,
        grid=(1,),
        in_specs=[whole(o.shape) for o in operands] + specs,
        out_specs=whole(out),
        out_shape=shape_of(out, jnp.float32),
        compiler_params=SMALL,
        cost_estimate=BRIEF,
        name="merge",
    )(*operands, *extra)


def pieces_kernel(index_of, count, index_ref, cot_ref, sum_ref, *refs):
    more_refs, (low_ref, back_ref, piece_ref) = refs[:count], refs[-3:]
    index = index_of(index_ref)
    level = [sum_ref[...]] + [ref[...] for ref in more_refs]
    while len(level) > 1:
        level = [level[j] + level[j + 1] for j in range(0, len(level), 2)]
    for i in range(index.per_part):
        live = index.live_rows(index.block(0, 0, i))
        keep = lax.broadcasted_iota(jnp.int32, low_ref.shape[1:], 1) < live
        lowered = jnp.where(keep, level[0][0, i], 0.0).astype(low_ref.dtype)
        low_ref[i] = lowered
        back_ref[i] = jnp.where(keep, level[0][1, i], 0.0).astype(back_ref.dtype)
        piece_ref[i] = jnp.dot(
            lowered, cot_ref[i * BLK : (i + 1) * BLK], preferred_element_type=jnp.float32
        ).astype(piece_ref.dtype)


def make_pieces(index_of, index, shape, total, more, cotangent, waits):
    _, per_part, rank, _ = total.shape
    width = cotangent.shape[1]
    outs = [(per_part, rank, BLK), (per_part, rank, BLK), (per_part, rank, width)]
    operands = (cotangent, total, *more)
    specs, extra = after(waits)
    return pl.pallas_call(
        functools.partial(pieces_kernel, index_of, len(more)),
        grid_spec=pltpu.PrefetchScalarGridSpec(
            num_scalar_prefetch=1,
            grid=(1,),
            in_specs=[whole(o.shape) for o in operands] + specs,
            out_specs=[whole(o) for o in outs],
        ),
        out_shape=[shape_of(o, jnp.bfloat16) for o in outs],
        compiler_params=SMALL,
        cost_estimate=BRIEF,
        name="pieces",
    )(index, *operands, *extra)


def down_gradient_kernel(index_of, index_ref, tokens_ref, *refs):
    back_refs, out_ref = refs[:-1], refs[-1]
    index = index_of(index_ref)
    out_ref[...] = jnp.zeros_like(out_ref)
    for core_bit in range(CORES):
        for chip_bits in range(index.chips):
            for i in range(index.per_part):
                block = index.block(core_bit, chip_bits, i)
                back_ref = back_refs[core_bit * index.chips + chip_bits]

                @pl.when(index.owner(block) == index.place)
                def _(block=block, back_ref=back_ref, i=i):
                    at = pl.multiple_of(index.slot(block) * BLK, BLK)
                    out_ref[0] += adapter_scale * jnp.dot(
                        back_ref[i],
                        tokens_ref[pl.ds(at, BLK)],
                        preferred_element_type=jnp.float32,
                    )


def down_gradient(index_of, index, tokens, backs):
    out = (1, backs[0].shape[1], tokens.shape[1])
    operands = (in_vmem(tokens), *backs)
    return pl.pallas_call(
        functools.partial(down_gradient_kernel, index_of),
        grid_spec=pltpu.PrefetchScalarGridSpec(
            num_scalar_prefetch=1,
            grid=(1,),
            in_specs=[held()] + [whole(o.shape) for o in backs],
            out_specs=whole(out),
        ),
        out_shape=shape_of(out, jnp.float32),
        compiler_params=SMALL,
        cost_estimate=BRIEF,
        name="down_gradient",
    )(index, *operands)


def up_gradient_kernel(index_of, index_ref, *refs):
    piece_refs, out_ref = refs[:-1], refs[-1]
    index = index_of(index_ref)

    def of_device(core_bit, chip_bits, adapter):
        total = None
        for i in range(index.per_part):
            mine = index.owner(index.block(core_bit, chip_bits, i)) == adapter
            piece = piece_refs[core_bit * index.chips + chip_bits][i].astype(jnp.float32)
            term = jnp.where(mine, piece, 0.0)
            total = term if total is None else total + term
        return total

    for adapter in range(index.adapters):
        level = [
            of_device(0, j, adapter) + of_device(1, j, adapter) for j in range(index.chips)
        ]
        while len(level) > 1:
            level = [level[j] + level[j + 1] for j in range(0, len(level), 2)]
        out_ref[adapter] = adapter_scale * level[0]


def up_gradient(index_of, index, adapter_count, pieces):
    per_part, rank, width = pieces[0].shape
    tile = 1024
    out = (adapter_count, rank, width)
    return pl.pallas_call(
        functools.partial(up_gradient_kernel, index_of),
        grid_spec=pltpu.PrefetchScalarGridSpec(
            num_scalar_prefetch=1,
            grid=(width // tile,),
            in_specs=[pl.BlockSpec((per_part, rank, tile), lambda n, _: (0, 0, n))] * len(pieces),
            out_specs=pl.BlockSpec((adapter_count, rank, tile), lambda n, _: (0, 0, n)),
        ),
        out_shape=shape_of(out, jnp.float32),
        compiler_params=SMALL,
        cost_estimate=BRIEF,
        name="up_gradient",
    )(index, *pieces)


def finish_kernel(index_of, index_ref, low_ref, *refs):
    index = index_of(index_ref)
    up_refs, sum_refs, out_ref = refs[: index.per_part], refs[index.per_part : -1], refs[-1]
    per_chunk = len(sum_refs) // len(CHUNK_ROWS)
    for i in range(index.per_part):
        block = index.block(0, 0, i)
        live = index.live_rows(block)
        side = lax.dot_general(
            low_ref[i],
            up_refs[i][0],
            (((0,), (0,)), ((), ())),
            preferred_element_type=jnp.float32,
        )
        start = 0
        for c, count in enumerate(CHUNK_ROWS):
            total = adapter_scale * side[start : start + count]
            for ref in sum_refs[c * per_chunk : (c + 1) * per_chunk]:
                total = total + ref[i * count : (i + 1) * count].astype(jnp.float32)
            keep = start + lax.broadcasted_iota(jnp.int32, total.shape, 0) < live
            at = i * BLK + start
            out_ref[at : at + count] = jnp.where(keep, total, 0.0).astype(out_ref.dtype)
            start += count


def finish(index_of, index, lowered, up, sums, part, projected, far):
    per_part = lowered.shape[0]
    _, rank, width = up.shape
    tile = min(1024, width // PARTS)
    tiles = width // PARTS // tile
    first = part * tiles
    out = (per_part * BLK, width)

    def factor(i):
        def at(n, index_ref):
            index = index_of(index_ref)
            return (index.owner(index.block(0, 0, i)), 0, first + n)

        return pl.BlockSpec((1, rank, tile), at)

    flat = [term for chunk in sums for term in chunk]
    specs = [
        pl.BlockSpec((per_part * count, tile), lambda n, _: (0, n))
        for chunk, count in zip(sums, CHUNK_ROWS)
        for _ in chunk
    ]
    operands = [index, lowered, *[up] * per_part, *flat]
    more, extra = after((), far)
    aliases = {}
    if projected is not None:
        aliases = {len(operands): 0}
        more, extra = [pl.BlockSpec(memory_space=pl.ANY)] + more, [projected] + extra

    def kernel(*refs):
        finish_kernel(index_of, *refs[: len(operands)], refs[-1])

    return pl.pallas_call(
        kernel,
        grid_spec=pltpu.PrefetchScalarGridSpec(
            num_scalar_prefetch=1,
            grid=(tiles,),
            in_specs=[whole(lowered.shape)] + [factor(i) for i in range(per_part)] + specs + more,
            out_specs=pl.BlockSpec((out[0], tile), lambda n, _: (0, first + n)),
        ),
        out_shape=shape_of(out, jnp.bfloat16),
        input_output_aliases=aliases,
        compiler_params=SMALL,
        cost_estimate=BRIEF,
        name="finish",
    )(*operands, *extra)


def per_device(
    tokens,
    cotangent,
    frozen_up_weight,
    adapter_down_factor,
    adapter_up_factor,
    tokens_per_adapter,
    adapter_of_block,
    slot_of_block,
):
    owners = lax.axis_size("dp")
    parts = lax.axis_size("tensor")
    chips = parts // CORES
    block_count = adapter_of_block.shape[0]
    adapter_count = adapter_up_factor.shape[0]
    width_dev = tokens.shape[1]
    index_of = functools.partial(
        Index, block_count=block_count, adapter_count=adapter_count, parts=parts
    )
    shape = index_of(None)
    index = Index.pack(adapter_of_block, slot_of_block, tokens_per_adapter)

    def to_other_core(value):
        return lax.ppermute(value, "tensor", [(i, i ^ 1) for i in range(parts)])

    def to_chip(value, k):
        return lax.ppermute(value, "tensor", [(i, i ^ (k * CORES)) for i in range(parts)])

    def across_dp(value, k):
        return lax.ppermute(value, "dp", [(i, i ^ k) for i in range(owners)])

    def same_core(value):
        return [value] + [to_chip(value, k) for k in range(1, chips)]

    def with_other_core(values):
        return values + [to_other_core(v) for v in values]

    def small_products(waits):
        down = jnp.swapaxes(adapter_down_factor, 1, 2)
        rank = adapter_up_factor.shape[1]
        send, keep = narrow(index_of, index, shape, tokens, down, rank, waits)
        back = backward(index_of, index, shape, cotangent, adapter_up_factor, [send])
        return send, keep, back

    def over_parts(send, keep):
        arrived = to_other_core(send)
        return arrived, [to_chip(keep[k] + arrived[k], k) for k in range(1, chips)]

    def over_dp(total):
        k = 1
        while 2 * k < owners:
            total = total + across_dp(total, k)
            k *= 2
        return total, [across_dp(total, k)]

    if owners == 4 and block_count == 4:
        relay = Relay(index_of, index, tokens)
        sent = relay.first()
        send, keep, back = small_products([sent])
        arrived, others = over_parts(send, keep)
        total, more = over_dp(merge(keep, arrived, back, others, []))
        relay.second([total])
        lowered, back_rows, pieces = make_pieces(
            index_of, index, shape, total, more, cotangent, []
        )
        relay.settle(more)
        weight = load_weight(frozen_up_weight, relay.arrived[-1][1:3])
        pieces = with_other_core(same_core(pieces))
        back_rows = with_other_core(same_core(back_rows))
        ahead = [v for chunk in relay.arrived[1:] for v in chunk[3:5]]
        ahead.append(weight)
        chunks = [lambda waits: relay.rows(0, ahead)]
        chunks += [functools.partial(relay.rows, c) for c in range(1, len(CHUNK_ROWS))]
    else:
        weight = load_weight(frozen_up_weight, [])
        send, keep, back = small_products([])
        arrived, others = over_parts(send, keep)
        total, more = over_dp(merge(keep, arrived, back, others, []))
        lowered, back_rows, pieces = make_pieces(
            index_of, index, shape, total, more, cotangent, []
        )
        pieces = with_other_core(same_core(pieces))
        back_rows = with_other_core(same_core(back_rows))
        every_slot = lax.all_gather(
            tokens.reshape(CAP, BLK, width_dev), "dp", axis=0, tiled=True
        )
        part = lax.axis_index("tensor")
        devices = jnp.arange(parts, dtype=jnp.int32)
        order = (devices // chips ^ 1) + (devices % chips) * CORES ^ part
        blocks = (order[:, None] * shape.per_part + jnp.arange(shape.per_part)).reshape(-1)
        picked = every_slot[adapter_of_block[blocks] * CAP + slot_of_block[blocks]]
        starts = [sum(CHUNK_ROWS[:c]) for c in range(len(CHUNK_ROWS))]
        chunks = [
            lambda waits, s=s, count=count: picked[:, s : s + count].reshape(-1, width_dev)
            for s, count in zip(starts, CHUNK_ROWS)
        ]
    def summed(rows, part, waits):
        each = rows.shape[0] // parts
        send_own, send, own, other = split_product(shape, rows, weight, part, PARTS, waits)
        outgoing = (other + to_other_core(send).astype(jnp.float32)).astype(jnp.bfloat16)
        across = [to_chip(outgoing[(k - 1) * each : k * each], k) for k in range(1, chips)]
        return [own, to_other_core(send_own)] + across, outgoing

    sums, ready = [], ()
    waits = [pieces[1:chips], ()]
    for chunk in chunks:
        rows = chunk(ready)
        done = [summed(rows, part, waits[part]) for part in range(PARTS)]
        sums.append([terms for terms, _ in done])
        ready = [done[0][1]]
        waits = [
            [*sums[-1][0][2:], *back_rows[1:chips]],
            [*back_rows[chips:], *pieces[chips:]],
        ]
    up_grad = up_gradient(index_of, index, adapter_count, pieces)
    down_grad = down_gradient(index_of, index, tokens, back_rows)
    projected = None
    for part in range(PARTS):
        projected = finish(
            index_of,
            index,
            lowered,
            adapter_up_factor,
            [done[part] for done in sums],
            part,
            projected,
            [] if projected is not None else [up_grad, down_grad],
        )
    return (projected, jnp.swapaxes(down_grad, 1, 2), up_grad)


def solution(mesh):
    return jax.shard_map(
        per_device,
        mesh=mesh,
        in_specs=(
            P(("groups", "dp"), "tensor"),
            P(("groups", "tensor"), "dp"),
            P("tensor", "dp"),
            P(("groups", "dp"), "tensor", None),
            P("groups", None, "dp"),
            P("groups"),
            P("groups"),
            P("groups"),
        ),
        out_specs=(
            P(("groups", "tensor"), "dp"),
            P(("groups", "dp"), "tensor", None),
            P("groups", None, "dp"),
        ),
        check_vma=False,
    )
```
